32 devices in a mesh: ctx: 8 (over y, x, core), fsdp: 4 (over z).
Axes of the slice: x: 2, y: 2, z: 4, core: 2. Of those that a mesh axis runs over, the one named last changes fastest.
Arguments:
- inputs: bfloat16 [4, 1024, 768], P('fsdp', 'ctx'), may hold values from -6 to 6
- cotangent: bfloat16 [4, 1024, 768], P('fsdp', 'ctx'), may hold values from -6 to 6
- first_gain: bfloat16 [768], P('fsdp'), may hold values from 0.5 to 1.5
- first_shift: bfloat16 [768], P('fsdp'), may hold values from -1.75 to 1.75
- input_weight: bfloat16 [768, 2304], P('fsdp'), may hold values from -0.3125 to 0.3125
- query_bias: bfloat16 [768], P('fsdp'), may hold values from -1.75 to 1.75
- value_bias: bfloat16 [768], P('fsdp'), may hold values from -1.75 to 1.75
- output_weight: bfloat16 [768, 768], P('fsdp'), may hold values from -0.625 to 0.625
- output_bias: bfloat16 [768], P('fsdp'), may hold values from -1.75 to 1.75
- second_gain: bfloat16 [768], P('fsdp'), may hold values from 0.5 to 1.5
- second_shift: bfloat16 [768], P('fsdp'), may hold values from -1.75 to 1.75
- expand_weight: bfloat16 [768, 3072], P('fsdp'), may hold values from -0.21875 to 0.21875
- expand_bias: bfloat16 [3072], P('fsdp'), may hold values from -1.75 to 1.75
- contract_weight: bfloat16 [3072, 768], P('fsdp'), may hold values from -0.21875 to 0.21875
- contract_bias: bfloat16 [768], P('fsdp'), may hold values from -1.75 to 1.75
Outputs:
- outputs: bfloat16 [4, 1024, 768], P('fsdp', 'ctx')
- delta_inputs: bfloat16 [4, 1024, 768], P('fsdp', 'ctx')
- delta_first_gain: float32 [768], P('fsdp')
- delta_first_shift: float32 [768], P('fsdp')
- delta_input_weight: float32 [768, 2304], P('fsdp')
- delta_query_bias: float32 [768], P('fsdp')
- delta_value_bias: float32 [768], P('fsdp')
- delta_output_weight: float32 [768, 768], P('fsdp')
- delta_output_bias: float32 [768], P('fsdp')
- delta_second_gain: float32 [768], P('fsdp')
- delta_second_shift: float32 [768], P('fsdp')
- delta_expand_weight: float32 [768, 3072], P('fsdp')
- delta_expand_bias: float32 [3072], P('fsdp')
- delta_contract_weight: float32 [3072, 768], P('fsdp')
- delta_contract_bias: float32 [768], P('fsdp')
The draws below stay inside these ranges and needn't reach their ends.
All inputs are finite; a program needn't handle non-finite values.
Results may differ from the reference program's by a relative error of at most 0.022.
Values may be sent and summed in bfloat16 or wider, within the bound.
No kernel may reach another device: no remote copies, remote signals or barrier semaphores. Data moves between devices by JAX's collectives and lax.ppermute only.
A program may use at most 128 MiB of HBM per device.

```python
import jax
import jax.numpy as jnp
from jax import lax

D = 768
HEADS = 12
HEAD = 64
FF = 3072
LEN = 1024
SEQS = 4


def shard_levels(rng, shape, shards, low, largest):
    factor_of, own = 1.0, jax.random.fold_in(rng, 6)
    for position, shards_of in shards:
        heights = jnp.exp(jax.random.uniform(jax.random.fold_in(own, position), (shards_of,), jnp.float32, low / len(shards), largest / len(shards)))
        factor_of = factor_of * jnp.repeat(heights, shape[position] // shards_of).reshape([-1 if axis == position else 1 for axis in range(len(shape))])
    return factor_of


def normal_values(own_key, shape, width, reach, shards=(), kind=jnp.bfloat16):
    values = width * jax.random.normal(own_key, shape, jnp.float32)
    if shards:
        values = values * shard_levels(own_key, shape, shards, -0.22, 0.18)
    return jnp.clip(values, -reach, reach).astype(kind)


def setup_inputs(seed: int = 0) -> dict:
    key_of = jax.random.split(jax.random.key(seed), 16)
    return {
        "inputs": normal_values(key_of[0], (SEQS, LEN, D), 1.0, 6.0, ((0, 4), (1, 8))),
        "cotangent": normal_values(key_of[1], (SEQS, LEN, D), 1.0, 6.0, ((0, 4), (1, 8))),
        "first_gain": jnp.clip(1.0 + 0.1 * jax.random.normal(key_of[2], (D,), jnp.float32), 0.5, 1.5).astype(jnp.bfloat16),
        "first_shift": normal_values(key_of[3], (D,), 0.3, 1.75, ((0, 4),)),
        "input_weight": normal_values(key_of[4], (D, 3 * D), (D // 2) ** -0.5, 0.3125, ((0, 4),)),
        "query_bias": normal_values(key_of[5], (D,), 0.3, 1.75, ((0, 4),)),
        "value_bias": normal_values(key_of[6], (D,), 0.3, 1.75, ((0, 4),)),
        "output_weight": normal_values(key_of[7], (D, D), (D // 8) ** -0.5, 0.625, ((0, 4),)),
        "output_bias": normal_values(key_of[8], (D,), 0.3, 1.75, ((0, 4),)),
        "second_gain": jnp.clip(1.0 + 0.1 * jax.random.normal(key_of[9], (D,), jnp.float32), 0.5, 1.5).astype(jnp.bfloat16),
        "second_shift": normal_values(key_of[10], (D,), 0.3, 1.75, ((0, 4),)),
        "expand_weight": normal_values(key_of[11], (D, FF), D ** -0.5, 0.21875, ((0, 4),)),
        "expand_bias": normal_values(key_of[12], (FF,), 0.3, 1.75, ((0, 4),)),
        "contract_weight": normal_values(key_of[13], (FF, D), (FF // 4) ** -0.5, 0.21875, ((0, 4),)),
        "contract_bias": normal_values(key_of[14], (D,), 0.3, 1.75, ((0, 4),)),
    }


@jax.custom_vjp
def low(v):
    return lax.optimization_barrier(v.astype(jnp.bfloat16)).astype(jnp.float32)

@jax.custom_vjp
def low_back(v):
    return v

def low_keep(v):
    return (low(v), None)

def low_pass(kept, grad):
    return (grad,)

def back_keep(v):
    return (v, None)

def back_low(kept, grad):
    return (low(grad),)
low.defvjp(low_keep, low_pass)
low_back.defvjp(back_keep, back_low)
NORM_EPS = 1e-05
MASK_FILL = -1e+30
GELU_COEF = 0.7978845608028654

def norm_rows(values, gain_vec, shift_vec):
    center = values - lax.optimization_barrier(jnp.mean(values, axis=-1, keepdims=True))
    spread = lax.optimization_barrier(jnp.mean(center * center, axis=-1, keepdims=True))
    return center * lax.rsqrt(spread + NORM_EPS) * gain_vec + shift_vec

def gelu_tanh(values):
    return 0.5 * values * (1.0 + jnp.tanh(GELU_COEF * (values + 0.044715 * values * values * values)))

def matmul(left, right):
    return jnp.dot(left, right, precision=lax.Precision.HIGHEST, preferred_element_type=jnp.float32)

def attend_block(query_block, block_start, keys_all, values_all):
    block_rows = query_block.shape[0]
    score_scale = HEAD ** (-0.5)
    scores = jnp.einsum('qhd,khd->hqk', query_block, keys_all, precision=lax.Precision.HIGHEST) * score_scale
    scores = low_back(scores)
    query_place = block_start + jnp.arange(block_rows, dtype=jnp.int32)
    key_place = jnp.arange(keys_all.shape[0], dtype=jnp.int32)
    allowed = key_place[None, None, :] <= query_place[None, :, None]
    masked = jnp.where(allowed, scores, MASK_FILL)
    row_peak = lax.optimization_barrier(jnp.max(masked, axis=-1, keepdims=True))
    weights = jnp.exp(masked - row_peak)
    chances = weights / lax.optimization_barrier(jnp.sum(weights, axis=-1, keepdims=True))
    return jnp.einsum('hqk,khd->qhd', low(chances), values_all, precision=lax.Precision.HIGHEST)

def attention(queries, keys_all, values_all):
    query_heads = queries.reshape(LEN, HEADS, HEAD)
    key_heads = keys_all.reshape(LEN, HEADS, HEAD)
    value_heads = values_all.reshape(LEN, HEADS, HEAD)
    block_size = 512 if LEN % 512 == 0 else LEN
    block_count = LEN // block_size
    blocks = query_heads.reshape(block_count, block_size, HEADS, HEAD)
    starts = jnp.arange(block_count, dtype=jnp.int32) * block_size
    checked = jax.checkpoint(attend_block)

    def one_block(block_item):
        return checked(block_item[0], block_item[1], key_heads, value_heads)
    result = lax.map(one_block, (blocks, starts))
    return result.reshape(LEN, D)

def layer(seq_input, parameters):
    first_gain, first_shift, input_weight, query_bias, value_bias, output_weight, output_bias, second_gain, second_shift, expand_weight, expand_bias, contract_weight, contract_bias = parameters
    hidden_one = low(norm_rows(seq_input, first_gain, first_shift))
    projected = matmul(hidden_one, input_weight)
    queries = low(low_back(projected[:, :D] + query_bias))
    keys_all = low(low_back(projected[:, D:2 * D]))
    values_all = low(low_back(projected[:, 2 * D:] + value_bias))
    attended = low(low_back(attention(queries, keys_all, values_all)))
    branch_one = low_back(matmul(attended, output_weight) + output_bias)
    middle = seq_input + branch_one
    hidden_two = low(norm_rows(middle, second_gain, second_shift))
    inner_pre = low_back(matmul(hidden_two, expand_weight) + expand_bias)
    activated = low(gelu_tanh(inner_pre))
    branch_two = low_back(matmul(activated, contract_weight) + contract_bias)
    return middle + branch_two

def reference(inputs, cotangent, first_gain, first_shift, input_weight, query_bias, value_bias, output_weight, output_bias, second_gain, second_shift, expand_weight, expand_bias, contract_weight, contract_bias):
    parameters = tuple((item.astype(jnp.float32) for item in (first_gain, first_shift, input_weight, query_bias, value_bias, output_weight, output_bias, second_gain, second_shift, expand_weight, expand_bias, contract_weight, contract_bias)))

    def one_sequence(carried, seq_item):
        seq_input, seq_slope = seq_item
        result, pull_back = jax.vjp(layer, seq_input.astype(jnp.float32), parameters)
        input_slope, param_slopes = pull_back(seq_slope.astype(jnp.float32))
        carried = jax.tree.map(jnp.add, carried, param_slopes)
        return (carried, (result.astype(jnp.bfloat16), input_slope.astype(jnp.bfloat16)))
    zero_slopes = tuple((jnp.zeros_like(item) for item in parameters))
    totals, (outputs, delta_inputs) = lax.scan(one_sequence, zero_slopes, (inputs, cotangent))
    delta_first_gain, delta_first_shift, delta_input_weight, delta_query_bias, delta_value_bias, delta_output_weight, delta_output_bias, delta_second_gain, delta_second_shift, delta_expand_weight, delta_expand_bias, delta_contract_weight, delta_contract_bias = totals
    return (outputs, delta_inputs, delta_first_gain, delta_first_shift, delta_input_weight, delta_query_bias, delta_value_bias, delta_output_weight, delta_output_bias, delta_second_gain, delta_second_shift, delta_expand_weight, delta_expand_bias, delta_contract_weight, delta_contract_bias)
```

```python
import jax
import jax.numpy as jnp
from jax import lax
from jax.sharding import PartitionSpec as P

HEADS = 12
GROUPS = 4

NORM_EPS = 1e-05
MASK_FILL = -1e30
GELU_COEF = 0.7978845608028654
GELU_CUBE = 0.044715

BF = jnp.bfloat16
F32 = jnp.float32


def mm(left, right):
    return jnp.dot(left, right, preferred_element_type=F32)


def mm_lt(left, right):
    return lax.dot_general(left, right, (((0,), (0,)), ((), ())), preferred_element_type=F32)


def mm_rt(left, right):
    return lax.dot_general(left, right, (((1,), (1,)), ((), ())), preferred_element_type=F32)


def send(value, axis, flip):
    count = lax.axis_size(axis)
    return lax.ppermute(value, axis, [(s, s ^ flip) for s in range(count)])


def gather_flips(value, axis, count, stride):
    return [value] + [send(value, axis, i * stride) for i in range(1, count)]


def swap_flips(pieces, axis, stride):
    return [pieces[0]] + [send(p, axis, i * stride) for i, p in enumerate(pieces) if i]


def pick(stacked, place):
    return lax.dynamic_index_in_dim(stacked, place, axis=0, keepdims=False)


def in_order(pieces, me):
    stacked = jnp.stack(pieces)
    return jnp.stack([pick(stacked, me ^ j) for j in range(len(pieces))])


def norm_stats(values):
    center = values - jnp.mean(values, axis=-1, keepdims=True)
    spread = jnp.mean(center * center, axis=-1, keepdims=True)
    rate = lax.rsqrt(spread + NORM_EPS)
    return center * rate, rate


def norm_back(slope, gain, hat, rate):
    scaled = slope * gain
    return rate * (
        scaled
        - jnp.mean(scaled, axis=-1, keepdims=True)
        - hat * jnp.mean(scaled * hat, axis=-1, keepdims=True)
    )


def total(parts):
    out = parts[0].astype(F32)
    for part in parts[1:]:
        out = out + part.astype(F32)
    return out


def shards(
    inputs,
    cotangent,
    first_gain,
    first_shift,
    input_weight,
    query_bias,
    value_bias,
    output_weight,
    output_bias,
    second_gain,
    second_shift,
    expand_weight,
    expand_bias,
    contract_weight,
    contract_bias,
):
    tok, width = inputs.shape[1:]
    ctx, zs = lax.axis_size("ctx"), lax.axis_size("fsdp")
    ks = ctx // GROUPS
    where = lax.axis_index("ctx")
    g, k = where // ks, where % ks
    z = lax.axis_index("fsdp")
    rows_z = width // zs
    heads_here = HEADS // GROUPS
    head = width // HEADS
    cols = width // GROUPS
    ff = expand_weight.shape[1]
    ff_z = ff // zs
    ff_g = ff_z // GROUPS
    mine = GROUPS * tok
    scale = head ** (-0.5)

    x_own = inputs[0]
    slope_own = cotangent[0]

    x_rows = gather_flips(x_own, "ctx", GROUPS, ks)
    x_more = [[send(b, "ctx", j) for b in x_rows] for j in range(1, ks)]

    smalls = jnp.concatenate(
        [
            first_gain,
            first_shift,
            query_bias,
            value_bias,
            output_bias,
            second_gain,
            second_shift,
            contract_bias,
            expand_bias,
        ]
    )
    smalls_all = in_order(gather_flips(smalls, "fsdp", zs, 1), z).astype(F32)

    def small(i):
        return smalls_all[:, i * rows_z : (i + 1) * rows_z].reshape(width)

    gain_one, shift_one, q_bias, v_bias, o_bias, gain_two, shift_two, c_bias = [
        small(i) for i in range(8)
    ]
    e_bias = pick(
        smalls_all[:, 8 * rows_z :].reshape(zs, GROUPS, ff_g).transpose(1, 0, 2), g
    ).reshape(zs * ff_g)
    q_bias = pick(q_bias.reshape(GROUPS, cols), g)
    v_bias = pick(v_bias.reshape(GROUPS, cols), g)

    in_slice = lax.dynamic_index_in_dim(
        input_weight.reshape(rows_z, 3, GROUPS, cols), g, axis=2, keepdims=False
    ).reshape(rows_z, 3 * cols)
    in_w = in_order(gather_flips(in_slice, "fsdp", zs, 1), z).reshape(width, 3 * cols)

    slope_rows = jnp.concatenate(gather_flips(slope_own, "ctx", GROUPS, ks))

    out_w = in_order(gather_flips(output_weight, "fsdp", zs, 1), z).reshape(GROUPS, cols, width)
    out_w = jnp.concatenate([pick(out_w, g ^ i) for i in range(GROUPS)])
    e_slice = lax.dynamic_index_in_dim(
        expand_weight.reshape(rows_z, zs, GROUPS, ff_g), g, axis=2, keepdims=False
    ).reshape(rows_z, zs * ff_g)
    c_slice = pick(contract_weight.reshape(GROUPS, ff_g, width), g)
    exp_w = in_order(gather_flips(e_slice, "fsdp", zs, 1), z).reshape(width, zs * ff_g)
    con_w = in_order(gather_flips(c_slice, "fsdp", zs, 1), z).reshape(zs * ff_g, width)

    x_mine = jnp.concatenate(x_rows).astype(F32)
    hat_one, _ = norm_stats(x_mine)
    h1 = (hat_one * gain_one + shift_one).astype(BF)
    more = [jnp.concatenate(bs).astype(F32) for bs in x_more]
    h1_all = jnp.concatenate(
        [h1] + [(norm_stats(v)[0] * gain_one + shift_one).astype(BF) for v in more]
    )
    queries = (mm(h1, in_w[:, :cols]) + q_bias).astype(BF)
    kv = mm(h1_all, in_w[:, cols:])
    keys = kv[:, :cols].astype(BF)
    values = (kv[:, cols:] + v_bias).astype(BF)

    def to_heads(flat):
        return flat.reshape(flat.shape[0], heads_here, head).transpose(1, 0, 2)

    def from_heads(split):
        return split.transpose(1, 0, 2).reshape(split.shape[1], cols)

    qh, kh, vh = to_heads(queries), to_heads(keys), to_heads(values)
    steps = jnp.arange(tok, dtype=jnp.int32)
    q_place = jnp.concatenate([((g ^ i) * ks + k) * tok + steps for i in range(GROUPS)])
    k_place = jnp.concatenate(
        [((g ^ i) * ks + (k ^ j)) * tok + steps for j in range(ks) for i in range(GROUPS)]
    )
    scores = jnp.einsum("hqd,hkd->hqk", qh, kh, preferred_element_type=F32) * scale
    scores = jnp.where((k_place[None, :] <= q_place[:, None])[None], scores, MASK_FILL)
    peak = jnp.max(scores, axis=-1, keepdims=True)
    weights = jnp.exp(scores - peak)
    mass = jnp.sum(weights, axis=-1, keepdims=True)
    chances = weights / mass
    chances_low = chances.astype(BF)
    att_full = jnp.einsum("hqk,hkd->hqd", chances_low, vh, preferred_element_type=F32)
    att_rows = from_heads(att_full).astype(BF)

    att = jnp.concatenate(
        swap_flips([att_rows[i * tok : (i + 1) * tok] for i in range(GROUPS)], "ctx", ks), axis=1
    )
    x_f = x_own.astype(F32)
    middle = x_f + mm(att, out_w) + o_bias
    hat_two, rate_two = norm_stats(middle)
    h2 = (hat_two * gain_two + shift_two).astype(BF)
    h2_rows = jnp.concatenate(gather_flips(h2, "ctx", GROUPS, ks))

    slope_act = mm_rt(slope_rows, con_w)
    inner = mm(h2_rows, exp_w) + e_bias
    cube = GELU_COEF * (inner + GELU_CUBE * inner * inner * inner)
    tanh = jnp.tanh(cube)
    act = (0.5 * inner * (1.0 + tanh)).astype(BF)
    gelu_slope = 0.5 * (1.0 + tanh) + 0.5 * inner * (1.0 - tanh * tanh) * GELU_COEF * (
        1.0 + 3.0 * GELU_CUBE * inner * inner
    )
    slope_inner = (slope_act * gelu_slope).astype(BF)
    sh2_part = mm_rt(slope_inner, exp_w).astype(BF)
    sh2 = total(
        swap_flips([sh2_part[i * tok : (i + 1) * tok] for i in range(GROUPS)], "ctx", ks)
    )
    out_part = mm(act, con_w).astype(BF)
    out_sum = total(
        swap_flips([out_part[i * tok : (i + 1) * tok] for i in range(GROUPS)], "ctx", ks)
    )
    outputs = (middle + out_sum + c_bias).astype(BF)[None]

    slope_f = slope_own.astype(F32)
    d_gain_two = jnp.sum(sh2 * hat_two, axis=0)
    d_shift_two = jnp.sum(sh2, axis=0)
    slope_middle = slope_f + norm_back(sh2, gain_two, hat_two, rate_two)
    slope_branch = slope_middle.astype(BF)
    slope_att = mm_rt(slope_branch, out_w).astype(BF)
    datt = jnp.concatenate(
        swap_flips([slope_att[:, i * cols : (i + 1) * cols] for i in range(GROUPS)], "ctx", ks)
    )

    def over_k(grad):
        parts = grad.reshape(zs, ks, grad.shape[1] // ks, grad.shape[2]).astype(BF)
        pieces = [lax.dynamic_index_in_dim(parts, k ^ j, axis=1, keepdims=False) for j in range(ks)]
        return total(swap_flips(pieces, "ctx", 1))

    def over_z(grad):
        parts = grad.astype(BF)
        return total(swap_flips([pick(parts, z ^ i) for i in range(zs)], "fsdp", 1))

    def over_ctx(grad):
        low = grad.astype(BF)
        got = [gather_flips(p, "ctx", ks, 1) for p in gather_flips(low, "ctx", GROUPS, ks)]
        got = [in_order(p, k).reshape(ks * low.shape[0], low.shape[1]) for p in got]
        return in_order(got, g).astype(F32)

    d_con = mm_lt(act, slope_rows).reshape(zs, ff_g, width)
    d_exp = mm_lt(h2_rows, slope_inner).reshape(zs, rows_z, zs * ff_g)
    s_con = over_ctx(over_z(over_k(d_con)))
    s_exp = over_ctx(over_z(over_k(d_exp)))
    d_con_w = s_con.reshape(ff_z, width)
    d_exp_w = s_exp.reshape(GROUPS, rows_z, zs, ff_g).transpose(1, 2, 0, 3).reshape(rows_z, ff)

    d_out = mm_lt(att, slope_branch).reshape(GROUPS, cols, width)
    d_out = in_order([d_out[i] for i in range(GROUPS)], g).reshape(
        zs, GROUPS, rows_z // GROUPS, width
    )
    d_out = d_out.astype(BF)
    d_out = total(
        swap_flips(
            [lax.dynamic_index_in_dim(d_out, g ^ i, axis=1, keepdims=False) for i in range(GROUPS)],
            "ctx",
            ks,
        )
    )
    d_out_w = over_ctx(over_z(over_k(d_out))).reshape(rows_z, width)

    dh = to_heads(datt)
    diag = jnp.sum(dh.astype(F32) * att_full, axis=-1, keepdims=True)
    slope_chances = jnp.einsum("hqd,hkd->hqk", dh, vh, preferred_element_type=F32)
    slope_scores = (chances * (slope_chances - diag)).astype(BF)
    dq = jnp.einsum("hqk,hkd->hqd", slope_scores, kh, preferred_element_type=F32) * scale
    dk = jnp.einsum("hqk,hqd->hkd", slope_scores, qh, preferred_element_type=F32) * scale
    dv = jnp.einsum("hqk,hqd->hkd", chances_low, dh, preferred_element_type=F32)
    dkv = jnp.concatenate([from_heads(dk), from_heads(dv)], axis=1)
    dkv = total(
        swap_flips([dkv[j * mine : (j + 1) * mine].astype(BF) for j in range(ks)], "ctx", 1)
    )
    slope_project = jnp.concatenate([from_heads(dq), dkv], axis=1).astype(BF)
    sh1_part = mm_rt(slope_project, in_w)
    sh1_low = sh1_part.astype(BF)
    sh1 = total(swap_flips([sh1_low[i * tok : (i + 1) * tok] for i in range(GROUPS)], "ctx", ks))
    hat_own, rate_own = norm_stats(x_f)
    delta_inputs = (slope_middle + norm_back(sh1, gain_one, hat_own, rate_own)).astype(BF)[None]

    d_in = mm_lt(h1, slope_project).reshape(zs, rows_z, 3 * cols)
    s_in = over_ctx(over_z(over_k(d_in)))
    d_in_w = (
        s_in.reshape(GROUPS, rows_z, 3, cols).transpose(1, 2, 0, 3).reshape(rows_z, 3 * width)
    )

    def at_group(vec, lead):
        parts = vec.reshape(lead, 1, -1)
        spot = (jnp.arange(GROUPS) == g).astype(F32)[None, :, None]
        return (parts * spot).reshape(-1)

    sums = jnp.sum(slope_project.astype(F32), axis=0)
    vectors = [
        jnp.sum(sh1_part * hat_one, axis=0),
        jnp.sum(sh1_part, axis=0),
        at_group(sums[:cols], 1),
        at_group(sums[2 * cols :], 1),
        jnp.sum(slope_branch.astype(F32), axis=0),
        d_gain_two,
        d_shift_two,
        jnp.sum(slope_f, axis=0),
    ]
    packed = jnp.concatenate(
        [v.reshape(zs, rows_z) for v in vectors]
        + [at_group(jnp.sum(slope_inner.astype(F32), axis=0), zs).reshape(zs, ff_z)],
        axis=1,
    )
    packed = total(swap_flips([pick(packed, z ^ i) for i in range(zs)], "fsdp", 1))
    flip = 1
    while flip < ctx:
        packed = packed + send(packed, "ctx", flip)
        flip *= 2

    def vec(i):
        return packed[i * rows_z : (i + 1) * rows_z]

    return (
        outputs,
        delta_inputs,
        vec(0),
        vec(1),
        d_in_w,
        vec(2),
        vec(3),
        d_out_w,
        vec(4),
        vec(5),
        vec(6),
        d_exp_w,
        packed[8 * rows_z :],
        d_con_w,
        vec(7),
    )


def solution(mesh):
    row, vec, mat = P("fsdp", "ctx", None), P("fsdp"), P("fsdp", None)
    placed = (row, row, vec, vec, mat, vec, vec, mat, vec, vec, vec, mat, vec, mat, vec)
    return jax.shard_map(
        shards,
        mesh=mesh,
        in_specs=placed,
        out_specs=placed,
        check_vma=False,
    )
```

```python
import functools

import jax
import jax.numpy as jnp
from jax import lax
from jax.experimental import pallas as pl
from jax.experimental.pallas import tpu as pltpu
from jax.sharding import Mesh, PartitionSpec as P

HEADS = 12
GROUPS = 4

NORM_EPS = 1e-05
MASK_FILL = -1e30
GELU_COEF = 0.7978845608028654
GELU_CUBE = 0.044715

BF = jnp.bfloat16
F32 = jnp.float32


def mm(left, right):
    return jnp.dot(left, right, preferred_element_type=F32)


def mm_lt(left, right):
    return lax.dot_general(left, right, (((0,), (0,)), ((), ())), preferred_element_type=F32)


def mm_rt(left, right):
    return lax.dot_general(left, right, (((1,), (1,)), ((), ())), preferred_element_type=F32)


def send(value, axis, flip):
    count = lax.axis_size(axis)
    return lax.ppermute(value, axis, [(s, s ^ flip) for s in range(count)])


def gather_flips(value, axis):
    return [value] + [send(value, axis, i) for i in range(1, lax.axis_size(axis))]


def swap_flips(pieces, axis):
    return [pieces[0]] + [send(p, axis, i) for i, p in enumerate(pieces) if i]


def pick(stacked, place):
    return lax.dynamic_index_in_dim(stacked, place, axis=0, keepdims=False)


def in_order(pieces, me):
    stacked = jnp.stack(pieces)
    return jnp.stack([pick(stacked, me ^ j) for j in range(len(pieces))])


def norm_stats(values):
    center = values - jnp.mean(values, axis=-1, keepdims=True)
    spread = jnp.mean(center * center, axis=-1, keepdims=True)
    rate = lax.rsqrt(spread + NORM_EPS)
    return center * rate, rate


def norm_back(slope, gain, hat, rate):
    scaled = slope * gain
    return rate * (
        scaled
        - jnp.mean(scaled, axis=-1, keepdims=True)
        - hat * jnp.mean(scaled * hat, axis=-1, keepdims=True)
    )


def total(parts):
    out = parts[0].astype(F32)
    for part in parts[1:]:
        out = out + part.astype(F32)
    return out


def cut_columns(source, cut, parts, i):
    wide = cut.shape[1] // parts
    for part in range(parts):
        low = (part * GROUPS + i) * wide
        cut[:, part * wide : (part + 1) * wide] = source[:, low : low + wide]


def cut_kernel(parts, place, in_ref, exp_ref, con_ref, out_ref, in_cut, exp_cut, con_cut, out_cut):
    con_cut[...] = con_ref[...]
    out_cut[...] = out_ref[...]
    for i in range(GROUPS):

        @pl.when(place[0] == i)
        def _():
            cut_columns(in_ref, in_cut, 3, i)
            cut_columns(exp_ref, exp_cut, parts, i)


def cut_weights(g, k, ks, zs, in_w, exp_w, con_w, out_w):
    rows = in_w.shape[0] // ks
    ff_rows = con_w.shape[0] // (GROUPS * ks)
    in_cols, exp_cols = in_w.shape[1] // GROUPS, exp_w.shape[1] // GROUPS
    width = out_w.shape[1]
    if rows % 16 == 0 and ff_rows % 16 == 0:
        by_k = lambda i, place: (place[1], 0)
        by_g = lambda i, place: (place[0] * ks + place[1], 0)
        whole = lambda i, place: (0, 0)
        shapes = [(rows, in_cols), (rows, exp_cols), (ff_rows, width), (rows, width)]
        return pl.pallas_call(
            functools.partial(cut_kernel, zs),
            grid_spec=pltpu.PrefetchScalarGridSpec(
                num_scalar_prefetch=1,
                grid=(1,),
                in_specs=[
                    pl.BlockSpec((rows, in_w.shape[1]), by_k),
                    pl.BlockSpec((rows, exp_w.shape[1]), by_k),
                    pl.BlockSpec((ff_rows, width), by_g),
                    pl.BlockSpec((rows, width), by_k),
                ],
                out_specs=[pl.BlockSpec(s, whole) for s in shapes],
            ),
            out_shape=[jax.ShapeDtypeStruct(s, BF) for s in shapes],
            compiler_params=pltpu.CompilerParams(vmem_limit_bytes=16 * 2**20),
        )(jnp.stack([g, k]).astype(jnp.int32), in_w, exp_w, con_w, out_w)

    def cut(weight, parts):
        half = pick(weight.reshape(ks, rows, -1), k)
        wide = weight.shape[1] // (parts * GROUPS)
        return lax.dynamic_index_in_dim(
            half.reshape(rows, parts, GROUPS, wide), g, axis=2, keepdims=False
        ).reshape(rows, parts * wide)

    return (
        cut(in_w, 3),
        cut(exp_w, zs),
        pick(con_w.reshape(GROUPS * ks, ff_rows, width), g * ks + k),
        pick(out_w.reshape(ks, rows, width), k),
    )


def weave_kernel(parts, pieces, out):
    wide = pieces.shape[2] // parts
    for i in range(GROUPS):
        for part in range(parts):
            low = (part * GROUPS + i) * wide
            out[:, low : low + wide] = pieces[i, :, part * wide : (part + 1) * wide].astype(F32)


def weave(pieces, parts):
    rows, cols = pieces.shape[1], pieces.shape[2]
    step = 32
    return pl.pallas_call(
        functools.partial(weave_kernel, parts),
        grid=(rows // step,),
        in_specs=[pl.BlockSpec((GROUPS, step, cols), lambda i: (0, i, 0))],
        out_specs=pl.BlockSpec((step, GROUPS * cols), lambda i: (i, 0)),
        out_shape=jax.ShapeDtypeStruct((rows, GROUPS * cols), F32),
        compiler_params=pltpu.CompilerParams(vmem_limit_bytes=16 * 2**20),
    )(pieces)


def shards(
    inputs,
    cotangent,
    first_gain,
    first_shift,
    input_weight,
    query_bias,
    value_bias,
    output_weight,
    output_bias,
    second_gain,
    second_shift,
    expand_weight,
    expand_bias,
    contract_weight,
    contract_bias,
):
    tok, width = inputs.shape[1:]
    ks, zs = lax.axis_size("core"), lax.axis_size("fsdp")
    g, k, z = lax.axis_index("grp"), lax.axis_index("core"), lax.axis_index("fsdp")
    rows_z = width // zs
    heads_here = HEADS // GROUPS
    head = width // HEADS
    cols = width // GROUPS
    ff = expand_weight.shape[1]
    ff_z = ff // zs
    ff_g = ff_z // GROUPS
    mine = GROUPS * tok
    scale = head ** (-0.5)

    x_own = inputs[0]
    slope_own = cotangent[0]

    x_rows = gather_flips(x_own, "grp")
    x_more = [[send(b, "core", j) for b in x_rows] for j in range(1, ks)]

    smalls = jnp.concatenate(
        [
            first_gain,
            first_shift,
            query_bias,
            value_bias,
            output_bias,
            second_gain,
            second_shift,
            contract_bias,
            expand_bias,
        ]
    )
    smalls_all = in_order(gather_flips(smalls, "fsdp"), z).astype(F32)

    def small(i):
        return smalls_all[:, i * rows_z : (i + 1) * rows_z].reshape(width)

    gain_one, shift_one, q_bias, v_bias, o_bias, gain_two, shift_two, c_bias = [
        small(i) for i in range(8)
    ]
    e_bias = pick(
        smalls_all[:, 8 * rows_z :].reshape(zs, GROUPS, ff_g).transpose(1, 0, 2), g
    ).reshape(zs * ff_g)
    q_bias = pick(q_bias.reshape(GROUPS, cols), g)
    v_bias = pick(v_bias.reshape(GROUPS, cols), g)

    in_cut, exp_cut, con_cut, out_cut = cut_weights(
        g, k, ks, zs, input_weight, expand_weight, contract_weight, output_weight
    )
    in_half = in_order(gather_flips(in_cut, "fsdp"), z)
    in_w = jnp.stack(in_order(gather_flips(in_half, "core"), k), axis=1).reshape(width, 3 * cols)

    slope_rows = jnp.concatenate(gather_flips(slope_own, "grp"))

    def whole(cut):
        return lax.all_gather(cut, ("fsdp", "core"), axis=0, tiled=True)

    out_w = whole(out_cut)
    con_w = whole(con_cut)
    exp_w = whole(exp_cut)
    out_w = out_w.reshape(GROUPS, cols, width)
    out_w = jnp.concatenate([pick(out_w, g ^ i) for i in range(GROUPS)])

    x_mine = jnp.concatenate(x_rows).astype(F32)
    hat_one, _ = norm_stats(x_mine)
    h1 = (hat_one * gain_one + shift_one).astype(BF)
    more = [jnp.concatenate(bs).astype(F32) for bs in x_more]
    h1_all = jnp.concatenate(
        [h1] + [(norm_stats(v)[0] * gain_one + shift_one).astype(BF) for v in more]
    )
    queries = (mm(h1, in_w[:, :cols]) + q_bias).astype(BF)
    kv = mm(h1_all, in_w[:, cols:])
    keys = kv[:, :cols].astype(BF)
    values = (kv[:, cols:] + v_bias).astype(BF)

    def to_heads(flat):
        return flat.reshape(flat.shape[0], heads_here, head).transpose(1, 0, 2)

    def from_heads(split):
        return split.transpose(1, 0, 2).reshape(split.shape[1], cols)

    qh, kh, vh = to_heads(queries), to_heads(keys), to_heads(values)
    steps = jnp.arange(tok, dtype=jnp.int32)
    q_place = jnp.concatenate([((g ^ i) * ks + k) * tok + steps for i in range(GROUPS)])
    k_place = jnp.concatenate(
        [((g ^ i) * ks + (k ^ j)) * tok + steps for j in range(ks) for i in range(GROUPS)]
    )
    scores = jnp.einsum("hqd,hkd->hqk", qh, kh, preferred_element_type=F32) * scale
    scores = jnp.where((k_place[None, :] <= q_place[:, None])[None], scores, MASK_FILL)
    peak = jnp.max(scores, axis=-1, keepdims=True)
    weights = jnp.exp(scores - peak)
    mass = jnp.sum(weights, axis=-1, keepdims=True)
    chances = weights / mass
    chances_low = chances.astype(BF)
    att_full = jnp.einsum("hqk,hkd->hqd", chances_low, vh, preferred_element_type=F32)
    att_rows = from_heads(att_full).astype(BF)

    att = jnp.concatenate(
        swap_flips([att_rows[i * tok : (i + 1) * tok] for i in range(GROUPS)], "grp"), axis=1
    )
    x_f = x_own.astype(F32)
    middle = x_f + mm(att, out_w) + o_bias
    hat_two, rate_two = norm_stats(middle)
    h2 = (hat_two * gain_two + shift_two).astype(BF)
    h2_rows = jnp.concatenate(gather_flips(h2, "grp"))

    slope_act = mm_rt(slope_rows, con_w)
    inner = mm(h2_rows, exp_w) + e_bias
    cube = GELU_COEF * (inner + GELU_CUBE * inner * inner * inner)
    tanh = jnp.tanh(cube)
    act = (0.5 * inner * (1.0 + tanh)).astype(BF)
    gelu_slope = 0.5 * (1.0 + tanh) + 0.5 * inner * (1.0 - tanh * tanh) * GELU_COEF * (
        1.0 + 3.0 * GELU_CUBE * inner * inner
    )
    slope_inner = (slope_act * gelu_slope).astype(BF)
    sh2_part = mm_rt(slope_inner, exp_w).astype(BF)
    sh2 = total(
        swap_flips([sh2_part[i * tok : (i + 1) * tok] for i in range(GROUPS)], "grp")
    )
    out_part = mm(act, con_w).astype(BF)
    out_sum = total(
        swap_flips([out_part[i * tok : (i + 1) * tok] for i in range(GROUPS)], "grp")
    )
    outputs = (middle + out_sum + c_bias).astype(BF)[None]

    slope_f = slope_own.astype(F32)
    d_gain_two = jnp.sum(sh2 * hat_two, axis=0)
    d_shift_two = jnp.sum(sh2, axis=0)
    slope_middle = slope_f + norm_back(sh2, gain_two, hat_two, rate_two)
    slope_branch = slope_middle.astype(BF)
    slope_att = mm_rt(slope_branch, out_w).astype(BF)
    datt = jnp.concatenate(
        swap_flips([slope_att[:, i * cols : (i + 1) * cols] for i in range(GROUPS)], "grp")
    )

    def reduced(grad, axes):
        return lax.psum_scatter(grad.astype(BF), axes, scatter_dimension=0, tiled=True)

    def spread(grad):
        return lax.all_gather(grad, ("grp", "core"), axis=0, tiled=True)

    d_con = reduced(mm_lt(act, slope_rows), ("fsdp", "core"))
    d_exp = reduced(mm_lt(h2_rows, slope_inner), ("fsdp", "core"))
    d_con_w = spread(d_con).astype(F32)
    d_exp_w = weave(spread(d_exp).reshape(GROUPS, rows_z, zs * ff_g), zs)

    d_out = mm_lt(att, slope_branch).reshape(GROUPS, cols, width)
    d_out = in_order([d_out[i] for i in range(GROUPS)], g).reshape(width, width)
    d_out_w = spread(reduced(d_out, ("fsdp", "grp", "core"))).astype(F32)

    dh = to_heads(datt)
    diag = jnp.sum(dh.astype(F32) * att_full, axis=-1, keepdims=True)
    slope_chances = jnp.einsum("hqd,hkd->hqk", dh, vh, preferred_element_type=F32)
    slope_scores = (chances * (slope_chances - diag)).astype(BF)
    dq = jnp.einsum("hqk,hkd->hqd", slope_scores, kh, preferred_element_type=F32) * scale
    dk = jnp.einsum("hqk,hqd->hkd", slope_scores, qh, preferred_element_type=F32) * scale
    dv = jnp.einsum("hqk,hqd->hkd", chances_low, dh, preferred_element_type=F32)
    dkv = jnp.concatenate([from_heads(dk), from_heads(dv)], axis=1)
    dkv = total(
        swap_flips([dkv[j * mine : (j + 1) * mine].astype(BF) for j in range(ks)], "core")
    )
    slope_project = jnp.concatenate([from_heads(dq), dkv], axis=1).astype(BF)
    sh1_part = mm_rt(slope_project, in_w)
    sh1_low = sh1_part.astype(BF)
    sh1 = total(swap_flips([sh1_low[i * tok : (i + 1) * tok] for i in range(GROUPS)], "grp"))
    hat_own, rate_own = norm_stats(x_f)
    delta_inputs = (slope_middle + norm_back(sh1, gain_one, hat_own, rate_own)).astype(BF)[None]

    def at_group(vec, lead):
        parts = vec.reshape(lead, 1, -1)
        spot = (jnp.arange(GROUPS) == g).astype(F32)[None, :, None]
        return (parts * spot).reshape(-1)

    sums = jnp.sum(slope_project.astype(F32), axis=0)
    vectors = [
        jnp.sum(sh1_part * hat_one, axis=0),
        jnp.sum(sh1_part, axis=0),
        at_group(sums[:cols], 1),
        at_group(sums[2 * cols :], 1),
        jnp.sum(slope_branch.astype(F32), axis=0),
        d_gain_two,
        d_shift_two,
        jnp.sum(slope_f, axis=0),
    ]
    packed = jnp.concatenate(
        [v.reshape(zs, rows_z) for v in vectors]
        + [at_group(jnp.sum(slope_inner.astype(F32), axis=0), zs).reshape(zs, ff_z)],
        axis=1,
    )
    count = packed.shape[1]
    extra = -(-count // (3 * cols * ks))
    packed = jnp.pad(packed, ((0, 0), (0, extra * ks * 3 * cols - count)))
    d_in = mm_lt(h1, slope_project).astype(BF).reshape(zs, ks, rows_z // ks, 3 * cols)
    d_in = jnp.concatenate([d_in, packed.astype(BF).reshape(zs, ks, extra, 3 * cols)], axis=2)
    pieces = [lax.dynamic_index_in_dim(d_in, k ^ j, axis=1, keepdims=False) for j in range(ks)]
    d_in = total(swap_flips(pieces, "core")).astype(BF)
    d_in = total(swap_flips([pick(d_in, z ^ i) for i in range(zs)], "fsdp")).astype(BF)
    d_in = in_order(gather_flips(d_in, "grp"), g)
    d_in = in_order(gather_flips(d_in, "core"), k)
    packed = jnp.sum(d_in[:, :, rows_z // ks :].astype(F32), axis=1).reshape(-1)
    d_in = d_in[:, :, : rows_z // ks].transpose(1, 0, 2, 3).reshape(GROUPS, rows_z, 3 * cols)
    d_in_w = weave(d_in, 3)

    def vec(i):
        return packed[i * rows_z : (i + 1) * rows_z]

    return (
        outputs,
        delta_inputs,
        vec(0),
        vec(1),
        d_in_w,
        vec(2),
        vec(3),
        d_out_w,
        vec(4),
        vec(5),
        vec(6),
        d_exp_w,
        packed[8 * rows_z : 8 * rows_z + ff_z],
        d_con_w,
        vec(7),
    )


def solution(mesh):
    ctx, zs = mesh.shape["ctx"], mesh.shape["fsdp"]
    axes = ("grp", "core", "fsdp")
    split = Mesh(mesh.devices.reshape(GROUPS, ctx // GROUPS, zs), axes)
    row, vec, mat = P("fsdp", ("grp", "core"), None), P("fsdp"), P("fsdp", None)
    placed = (row, row, vec, vec, mat, vec, vec, mat, vec, vec, vec, mat, vec, mat, vec)
    return jax.shard_map(
        shards,
        mesh=split,
        in_specs=placed,
        out_specs=placed,
        check_vma=False,
    )
```

```python
import functools

import jax
import jax.numpy as jnp
from jax import lax
from jax.experimental import pallas as pl
from jax.experimental.pallas import tpu as pltpu
from jax.sharding import Mesh, PartitionSpec as P

HEADS = 12
GROUPS = 4

NORM_EPS = 1e-05
MASK_FILL = -1e30
GELU_COEF = 0.7978845608028654
GELU_CUBE = 0.044715

BF = jnp.bfloat16
F32 = jnp.float32


def mm(left, right):
    return jnp.dot(left, right, preferred_element_type=F32)


def mm_lt(left, right):
    return lax.dot_general(left, right, (((0,), (0,)), ((), ())), preferred_element_type=F32)


def mm_rt(left, right):
    return lax.dot_general(left, right, (((1,), (1,)), ((), ())), preferred_element_type=F32)


def send(value, axis, flip):
    count = lax.axis_size(axis)
    return lax.ppermute(value, axis, [(s, s ^ flip) for s in range(count)])


def gather_flips(value, axis):
    return [value] + [send(value, axis, i) for i in range(1, lax.axis_size(axis))]


def swap_flips(pieces, axis):
    return [pieces[0]] + [send(p, axis, i) for i, p in enumerate(pieces) if i]


def pick(stacked, place):
    return lax.dynamic_index_in_dim(stacked, place, axis=0, keepdims=False)


def in_order(pieces, me):
    stacked = jnp.stack(pieces)
    return jnp.stack([pick(stacked, me ^ j) for j in range(len(pieces))])


def norm_stats(values):
    center = values - jnp.mean(values, axis=-1, keepdims=True)
    spread = jnp.mean(center * center, axis=-1, keepdims=True)
    rate = lax.rsqrt(spread + NORM_EPS)
    return center * rate, rate


def norm_back(slope, gain, hat, rate):
    scaled = slope * gain
    return rate * (
        scaled
        - jnp.mean(scaled, axis=-1, keepdims=True)
        - hat * jnp.mean(scaled * hat, axis=-1, keepdims=True)
    )


def total(parts):
    out = parts[0].astype(F32)
    for part in parts[1:]:
        out = out + part.astype(F32)
    return out


def cut_columns(source, cut, parts, i):
    wide = cut.shape[1] // parts
    for part in range(parts):
        low = (part * GROUPS + i) * wide
        cut[:, part * wide : (part + 1) * wide] = source[:, low : low + wide]


def cut_kernel(parts, place, source, cut):
    for i in range(GROUPS):

        @pl.when(place[0] == i)
        def _():
            cut_columns(source, cut, parts, i)


def cut_weight(weight, parts, g, k, ks):
    rows = weight.shape[0] // ks
    cols = weight.shape[1] // GROUPS
    if rows % 16 == 0:
        return pl.pallas_call(
            functools.partial(cut_kernel, parts),
            grid_spec=pltpu.PrefetchScalarGridSpec(
                num_scalar_prefetch=1,
                grid=(1,),
                in_specs=[pl.BlockSpec((rows, weight.shape[1]), lambda i, place: (place[1], 0))],
                out_specs=pl.BlockSpec((rows, cols), lambda i, place: (0, 0)),
            ),
            out_shape=jax.ShapeDtypeStruct((rows, cols), BF),
            compiler_params=pltpu.CompilerParams(vmem_limit_bytes=8 * 2**20),
        )(jnp.stack([g, k]).astype(jnp.int32), weight)
    half = pick(weight.reshape(ks, rows, -1), k)
    return lax.dynamic_index_in_dim(
        half.reshape(rows, parts, GROUPS, cols // parts), g, axis=2, keepdims=False
    ).reshape(rows, cols)


def weave_kernel(parts, pieces, out):
    wide = pieces.shape[2] // parts
    for i in range(GROUPS):
        for part in range(parts):
            low = (part * GROUPS + i) * wide
            out[:, low : low + wide] = pieces[i, :, part * wide : (part + 1) * wide].astype(F32)


def weave(pieces, parts):
    rows, cols = pieces.shape[1], pieces.shape[2]
    step = 32
    return pl.pallas_call(
        functools.partial(weave_kernel, parts),
        grid=(rows // step,),
        in_specs=[pl.BlockSpec((GROUPS, step, cols), lambda i: (0, i, 0))],
        out_specs=pl.BlockSpec((step, GROUPS * cols), lambda i: (i, 0)),
        out_shape=jax.ShapeDtypeStruct((rows, GROUPS * cols), F32),
        compiler_params=pltpu.CompilerParams(vmem_limit_bytes=16 * 2**20),
    )(pieces)


def unfold_kernel(parts, pieces, exp_out, con_out):
    wide = con_out.shape[2]
    part_wide = wide // parts
    for i in range(GROUPS):
        con_out[i] = pieces[i, :, wide:].astype(F32)
        for part in range(parts):
            low = (part * GROUPS + i) * part_wide
            exp_out[:, low : low + part_wide] = pieces[
                i, :, part * part_wide : (part + 1) * part_wide
            ].astype(F32)


def unfold(pieces, parts):
    rows, wide = pieces.shape[1], pieces.shape[2] // 2
    step = 32
    return pl.pallas_call(
        functools.partial(unfold_kernel, parts),
        grid=(rows // step,),
        in_specs=[pl.BlockSpec((GROUPS, step, 2 * wide), lambda i: (0, i, 0))],
        out_specs=[
            pl.BlockSpec((step, GROUPS * wide), lambda i: (i, 0)),
            pl.BlockSpec((GROUPS, step, wide), lambda i: (0, i, 0)),
        ],
        out_shape=[
            jax.ShapeDtypeStruct((rows, GROUPS * wide), F32),
            jax.ShapeDtypeStruct((GROUPS, rows, wide), F32),
        ],
        compiler_params=pltpu.CompilerParams(vmem_limit_bytes=16 * 2**20),
    )(pieces)


def hidden_kernel(
    h_a, h_b, h_c, h_d, s_a, s_b, s_c, s_d, exp_w, con_w, bias,
    act_ref, inner_ref, back_ref, out_ref, bias_ref, h_ref, s_ref, back_sum, out_sum,
):
    step = pl.program_id(0)
    tok = h_a.shape[0]

    @pl.when(step == 0)
    def _():
        for i, (h, s) in enumerate(((h_a, s_a), (h_b, s_b), (h_c, s_c), (h_d, s_d))):
            h_ref[i * tok : (i + 1) * tok, :] = h[...]
            s_ref[i * tok : (i + 1) * tok, :] = s[...]

    inner = mm(h_ref[...], exp_w[...]) + bias[...]
    square = inner * inner
    tanh = jnp.tanh(GELU_COEF * (inner + GELU_CUBE * square * inner))
    half = 0.5 + 0.5 * tanh
    act = (inner * half).astype(BF)
    gelu_slope = half + (0.5 * GELU_COEF) * inner * (1.0 - tanh * tanh) * (
        1.0 + (3.0 * GELU_CUBE) * square
    )
    slope = (mm_rt(s_ref[...], con_w[...]) * gelu_slope).astype(BF)
    act_ref[...] = act
    inner_ref[...] = slope
    bias_ref[...] = jnp.sum(slope.astype(F32), axis=0, keepdims=True)
    back = mm_rt(slope, exp_w[...])
    out = mm(act, con_w[...])

    @pl.when(step == 0)
    def _():
        back_sum[...] = back
        out_sum[...] = out

    @pl.when(step > 0)
    def _():
        back_sum[...] += back
        out_sum[...] += out

    @pl.when(step == pl.num_programs(0) - 1)
    def _():
        for i in range(GROUPS):
            back_ref[i] = back_sum[i * tok : (i + 1) * tok, :].astype(BF)
            out_ref[i] = out_sum[i * tok : (i + 1) * tok, :].astype(BF)


def hidden_part(h_rows, s_rows, exp_w, con_w, bias):
    tok, width = h_rows[0].shape
    hidden = exp_w.shape[1]
    rows = GROUPS * tok
    step = 256
    fixed = lambda i: (0, 0)
    cols = lambda i: (0, i)
    return pl.pallas_call(
        hidden_kernel,
        grid=(hidden // step,),
        in_specs=[pl.BlockSpec((tok, width), fixed)] * (2 * GROUPS)
        + [
            pl.BlockSpec((width, step), cols),
            pl.BlockSpec((step, width), lambda i: (i, 0)),
            pl.BlockSpec((1, step), cols),
        ],
        out_specs=[
            pl.BlockSpec((rows, step), cols),
            pl.BlockSpec((rows, step), cols),
            pl.BlockSpec((GROUPS, tok, width), lambda i: (0, 0, 0)),
            pl.BlockSpec((GROUPS, tok, width), lambda i: (0, 0, 0)),
            pl.BlockSpec((1, step), cols),
            pl.BlockSpec((rows, width), fixed),
            pl.BlockSpec((rows, width), fixed),
        ],
        out_shape=[
            jax.ShapeDtypeStruct((rows, hidden), BF),
            jax.ShapeDtypeStruct((rows, hidden), BF),
            jax.ShapeDtypeStruct((GROUPS, tok, width), BF),
            jax.ShapeDtypeStruct((GROUPS, tok, width), BF),
            jax.ShapeDtypeStruct((1, hidden), F32),
            jax.ShapeDtypeStruct((rows, width), BF),
            jax.ShapeDtypeStruct((rows, width), BF),
        ],
        scratch_shapes=[pltpu.VMEM((rows, width), F32), pltpu.VMEM((rows, width), F32)],
        compiler_params=pltpu.CompilerParams(vmem_limit_bytes=40 * 2**20),
        cost_estimate=pl.CostEstimate(
            flops=8 * rows * width * hidden, bytes_accessed=12 * rows * width, transcendentals=0
        ),
    )(*h_rows, *s_rows, exp_w, con_w, bias)


def hidden_grad_kernel(h_ref, inner_ref, act_ref, s_ref, out_ref):
    wide = inner_ref.shape[1]
    out_ref[:, :wide] = mm_lt(h_ref[...], inner_ref[...]).astype(BF)
    out_ref[:, wide:] = mm_lt(act_ref[...], s_ref[...]).astype(BF)


def hidden_grads(h_rows, slope_inner, act, s_rows):
    rows, width = h_rows.shape
    hidden = act.shape[1]
    step = 256
    cols = lambda i: (0, i)
    fixed = lambda i: (0, 0)
    return pl.pallas_call(
        hidden_grad_kernel,
        grid=(width // step,),
        in_specs=[
            pl.BlockSpec((rows, step), cols),
            pl.BlockSpec((rows, hidden), fixed),
            pl.BlockSpec((rows, step), cols),
            pl.BlockSpec((rows, width), fixed),
        ],
        out_specs=pl.BlockSpec((step, hidden + width), lambda i: (i, 0)),
        out_shape=jax.ShapeDtypeStruct((width, hidden + width), BF),
        compiler_params=pltpu.CompilerParams(vmem_limit_bytes=40 * 2**20),
        cost_estimate=pl.CostEstimate(
            flops=4 * rows * width * hidden, bytes_accessed=12 * rows * width, transcendentals=0
        ),
    )(h_rows, slope_inner, act, s_rows)


def shards(
    inputs,
    cotangent,
    first_gain,
    first_shift,
    input_weight,
    query_bias,
    value_bias,
    output_weight,
    output_bias,
    second_gain,
    second_shift,
    expand_weight,
    expand_bias,
    contract_weight,
    contract_bias,
):
    tok, width = inputs.shape[1:]
    ks, zs = lax.axis_size("core"), lax.axis_size("fsdp")
    g, k, z = lax.axis_index("grp"), lax.axis_index("core"), lax.axis_index("fsdp")
    rows_z = width // zs
    heads_here = HEADS // GROUPS
    head = width // HEADS
    cols = width // GROUPS
    ff = expand_weight.shape[1]
    ff_z = ff // zs
    ff_g = ff_z // GROUPS
    mine = GROUPS * tok
    scale = head ** (-0.5)

    x_own = inputs[0]
    slope_own = cotangent[0]

    x_rows = gather_flips(x_own, "grp")
    in_cut = cut_weight(input_weight, 3, g, k, ks)
    in_pieces = gather_flips(in_cut, "fsdp")
    x_more = [[send(b, "core", j) for b in x_rows] for j in range(1, ks)]

    smalls = jnp.concatenate(
        [
            first_gain,
            first_shift,
            query_bias,
            value_bias,
            output_bias,
            second_gain,
            second_shift,
            contract_bias,
            expand_bias,
        ]
    )
    smalls_all = in_order(gather_flips(smalls, "fsdp"), z).astype(F32)

    def small(i):
        return smalls_all[:, i * rows_z : (i + 1) * rows_z].reshape(width)

    gain_one, shift_one, q_bias, v_bias, o_bias, gain_two, shift_two, c_bias = [
        small(i) for i in range(8)
    ]
    e_bias = pick(
        smalls_all[:, 8 * rows_z :].reshape(zs, GROUPS, ff_g).transpose(1, 0, 2), g
    ).reshape(zs * ff_g)
    q_bias = pick(q_bias.reshape(GROUPS, cols), g)
    v_bias = pick(v_bias.reshape(GROUPS, cols), g)

    in_half = in_order(in_pieces, z)
    in_w = jnp.stack(in_order(gather_flips(in_half, "core"), k), axis=1).reshape(width, 3 * cols)

    def whole(cut):
        return lax.all_gather(cut, ("fsdp", "core"), axis=0, tiled=True)

    out_w = whole(pick(output_weight.reshape(ks, rows_z // ks, width), k))
    con_w = whole(pick(contract_weight.reshape(GROUPS * ks, ff_g // ks, width), g * ks + k))
    exp_w = whole(cut_weight(expand_weight, zs, g, k, ks))
    out_w = out_w.reshape(GROUPS, cols, width)
    out_w = jnp.concatenate([pick(out_w, g ^ i) for i in range(GROUPS)])
    slope_late, _ = lax.optimization_barrier((slope_own, x_rows[-1]))
    slope_rows = gather_flips(slope_late, "grp")

    x_mine = jnp.concatenate(x_rows).astype(F32)
    hat_one, _ = norm_stats(x_mine)
    h1 = (hat_one * gain_one + shift_one).astype(BF)
    more = [jnp.concatenate(bs).astype(F32) for bs in x_more]
    h1_all = jnp.concatenate(
        [h1] + [(norm_stats(v)[0] * gain_one + shift_one).astype(BF) for v in more]
    )
    queries = (mm(h1, in_w[:, :cols]) + q_bias).astype(BF)
    kv = mm(h1_all, in_w[:, cols:])
    keys = kv[:, :cols].astype(BF)
    values = (kv[:, cols:] + v_bias).astype(BF)

    def to_heads(flat):
        return flat.reshape(flat.shape[0], heads_here, head).transpose(1, 0, 2)

    def from_heads(split):
        return split.transpose(1, 0, 2).reshape(split.shape[1], cols)

    qh, kh, vh = to_heads(queries), to_heads(keys), to_heads(values)
    steps = jnp.arange(tok, dtype=jnp.int32)
    q_place = jnp.concatenate([((g ^ i) * ks + k) * tok + steps for i in range(GROUPS)])
    k_place = jnp.concatenate(
        [((g ^ i) * ks + (k ^ j)) * tok + steps for j in range(ks) for i in range(GROUPS)]
    )
    scores = jnp.einsum("hqd,hkd->hqk", qh, kh, preferred_element_type=F32) * scale
    scores = jnp.where((k_place[None, :] <= q_place[:, None])[None], scores, MASK_FILL)
    peak = jnp.max(scores, axis=-1, keepdims=True)
    weights = jnp.exp(scores - peak)
    mass = jnp.sum(weights, axis=-1, keepdims=True)
    chances = weights / mass
    chances_low = chances.astype(BF)
    att_full = jnp.einsum("hqk,hkd->hqd", chances_low, vh, preferred_element_type=F32)
    att_rows = from_heads(att_full).astype(BF)

    att = jnp.concatenate(
        swap_flips([att_rows[i * tok : (i + 1) * tok] for i in range(GROUPS)], "grp"), axis=1
    )
    x_f = x_own.astype(F32)
    middle = x_f + mm(att, out_w) + o_bias
    hat_two, rate_two = norm_stats(middle)
    h2 = (hat_two * gain_two + shift_two).astype(BF)
    h2_rows = gather_flips(h2, "grp")

    act, slope_inner, sh2_part, out_part, d_exp_b, h2_all, slope_all = hidden_part(
        h2_rows, slope_rows, exp_w, con_w, e_bias[None]
    )
    sh2 = total(swap_flips([sh2_part[i] for i in range(GROUPS)], "grp"))

    def spread(grad):
        return lax.all_gather(grad, ("grp", "core"), axis=0, tiled=True)

    d_hidden = lax.psum_scatter(
        hidden_grads(h2_all, slope_inner, act, slope_all),
        ("fsdp", "core"),
        scatter_dimension=0,
        tiled=True,
    )
    d_exp_w, d_con_w = unfold(spread(d_hidden).reshape(GROUPS, rows_z, -1), zs)
    d_con_w = d_con_w.reshape(ff_z, width)

    slope_f = slope_own.astype(F32)
    d_gain_two = jnp.sum(sh2 * hat_two, axis=0)
    d_shift_two = jnp.sum(sh2, axis=0)
    slope_middle = slope_f + norm_back(sh2, gain_two, hat_two, rate_two)
    slope_branch = slope_middle.astype(BF)
    slope_att = mm_rt(slope_branch, out_w).astype(BF)
    datt = jnp.concatenate(
        swap_flips([slope_att[:, i * cols : (i + 1) * cols] for i in range(GROUPS)], "grp")
    )

    d_out = mm_lt(att, slope_branch).astype(BF).reshape(GROUPS, cols, width)
    d_out = in_order([d_out[i] for i in range(GROUPS)], g)
    d_out = d_out.reshape(zs, GROUPS, ks, rows_z // GROUPS // ks, width)
    pieces = [lax.dynamic_index_in_dim(d_out, k ^ j, axis=2, keepdims=False) for j in range(ks)]
    d_out = total(swap_flips(pieces, "core")).astype(BF)
    pieces = [lax.dynamic_index_in_dim(d_out, g ^ i, axis=1, keepdims=False) for i in range(GROUPS)]
    d_out = total(swap_flips(pieces, "grp")).astype(BF)
    third = d_out.shape[1] // 3
    tail = d_out[:, :, 3 * cols :]
    d_out = jnp.concatenate(
        [
            d_out[:, :, : 3 * cols],
            jnp.concatenate([tail[:, i * third : (i + 1) * third] for i in range(3)], axis=2),
        ],
        axis=1,
    )

    dh = to_heads(datt)
    diag = jnp.sum(dh.astype(F32) * att_full, axis=-1, keepdims=True)
    slope_chances = jnp.einsum("hqd,hkd->hqk", dh, vh, preferred_element_type=F32)
    slope_scores = (chances * (slope_chances - diag)).astype(BF)
    dq = jnp.einsum("hqk,hkd->hqd", slope_scores, kh, preferred_element_type=F32) * scale
    dk = jnp.einsum("hqk,hqd->hkd", slope_scores, qh, preferred_element_type=F32) * scale
    dv = jnp.einsum("hqk,hqd->hkd", chances_low, dh, preferred_element_type=F32)
    dkv = jnp.concatenate([from_heads(dk), from_heads(dv)], axis=1)
    dkv = total(
        swap_flips([dkv[j * mine : (j + 1) * mine].astype(BF) for j in range(ks)], "core")
    )
    slope_project = jnp.concatenate([from_heads(dq), dkv], axis=1).astype(BF)
    sh1_part = mm_rt(slope_project, in_w)
    sh1_low = sh1_part.astype(BF)
    sh1 = total(swap_flips([sh1_low[i * tok : (i + 1) * tok] for i in range(GROUPS)], "grp"))
    hat_own, rate_own = norm_stats(x_f)
    delta_inputs = (slope_middle + norm_back(sh1, gain_one, hat_own, rate_own)).astype(BF)[None]

    def at_group(vec, lead):
        parts = vec.reshape(lead, 1, -1)
        spot = (jnp.arange(GROUPS) == g).astype(F32)[None, :, None]
        return (parts * spot).reshape(-1)

    sums = jnp.sum(slope_project.astype(F32), axis=0)
    vectors = [
        jnp.sum(sh1_part * hat_one, axis=0),
        jnp.sum(sh1_part, axis=0),
        at_group(sums[:cols], 1),
        at_group(sums[2 * cols :], 1),
        jnp.sum(slope_branch.astype(F32), axis=0),
        d_gain_two,
        d_shift_two,
        jnp.sum(slope_f, axis=0),
    ]
    packed = jnp.concatenate(
        [v.reshape(zs, rows_z) for v in vectors]
        + [at_group(d_exp_b, zs).reshape(zs, ff_z)],
        axis=1,
    )
    count = packed.shape[1]
    extra = -(-count // (3 * cols * ks))
    packed = jnp.pad(packed, ((0, 0), (0, extra * ks * 3 * cols - count)))
    d_in = mm_lt(h1, slope_project).astype(BF).reshape(zs, ks, rows_z // ks, 3 * cols)
    d_in = jnp.concatenate([d_in, packed.astype(BF).reshape(zs, ks, extra, 3 * cols)], axis=2)
    pieces = [lax.dynamic_index_in_dim(d_in, k ^ j, axis=1, keepdims=False) for j in range(ks)]
    d_in = total(swap_flips(pieces, "core")).astype(BF)
    d_in = jnp.concatenate([d_in, d_out], axis=1)
    out_late, _ = lax.optimization_barrier((out_part, d_in))
    out_sum = total(swap_flips([out_late[i] for i in range(GROUPS)], "grp"))
    outputs = (middle + out_sum + c_bias).astype(BF)[None]
    d_in = total(swap_flips([pick(d_in, z ^ i) for i in range(zs)], "fsdp")).astype(BF)
    d_in = in_order(gather_flips(d_in, "grp"), g)
    d_in = in_order(gather_flips(d_in, "core"), k)
    own = rows_z // ks
    packed = jnp.sum(d_in[:, :, own : own + extra].astype(F32), axis=1).reshape(-1)
    d_out = d_in[:, :, own + extra :].transpose(1, 0, 2, 3)
    tail = d_out[:, :, 3 * third :].reshape(GROUPS, ks, third, 3, width - 3 * cols)
    d_out_w = (
        jnp.concatenate(
            [
                d_out[:, :, : 3 * third],
                jnp.concatenate([tail[:, :, :, i] for i in range(3)], axis=2),
            ],
            axis=3,
        )
        .reshape(rows_z, width)
        .astype(F32)
    )
    d_in = d_in[:, :, :own].transpose(1, 0, 2, 3).reshape(GROUPS, rows_z, 3 * cols)
    d_in_w = weave(d_in, 3)

    def vec(i):
        return packed[i * rows_z : (i + 1) * rows_z]

    return (
        outputs,
        delta_inputs,
        vec(0),
        vec(1),
        d_in_w,
        vec(2),
        vec(3),
        d_out_w,
        vec(4),
        vec(5),
        vec(6),
        d_exp_w,
        packed[8 * rows_z : 8 * rows_z + ff_z],
        d_con_w,
        vec(7),
    )


def solution(mesh):
    ctx, zs = mesh.shape["ctx"], mesh.shape["fsdp"]
    axes = ("grp", "core", "fsdp")
    split = Mesh(mesh.devices.reshape(GROUPS, ctx // GROUPS, zs), axes)
    row, vec, mat = P("fsdp", ("grp", "core"), None), P("fsdp"), P("fsdp", None)
    placed = (row, row, vec, vec, mat, vec, vec, mat, vec, vec, vec, mat, vec, mat, vec)
    return jax.shard_map(
        shards,
        mesh=split,
        in_specs=placed,
        out_specs=placed,
        check_vma=False,
    )
```

```python
import functools

import jax
import jax.numpy as jnp
from jax import lax
from jax.experimental import pallas as pl
from jax.experimental.pallas import tpu as pltpu
from jax.sharding import Mesh, PartitionSpec as P

HEADS = 12
GROUPS = 4

NORM_EPS = 1e-05
MASK_FILL = -1e30
GELU_COEF = 0.7978845608028654
GELU_CUBE = 0.044715

BF = jnp.bfloat16
F32 = jnp.float32


def mm(left, right):
    return jnp.dot(left, right, preferred_element_type=F32)


def mm_lt(left, right):
    return lax.dot_general(left, right, (((0,), (0,)), ((), ())), preferred_element_type=F32)


def mm_rt(left, right):
    return lax.dot_general(left, right, (((1,), (1,)), ((), ())), preferred_element_type=F32)


def send(value, axis, flip):
    count = lax.axis_size(axis)
    return lax.ppermute(value, axis, [(s, s ^ flip) for s in range(count)])


def gather_flips(value, axis):
    return [value] + [send(value, axis, i) for i in range(1, lax.axis_size(axis))]


def swap_flips(pieces, axis):
    return [pieces[0]] + [send(p, axis, i) for i, p in enumerate(pieces) if i]


def pick(stacked, place):
    return lax.dynamic_index_in_dim(stacked, place, axis=0, keepdims=False)


def in_order(pieces, me):
    stacked = jnp.stack(pieces)
    return jnp.stack([pick(stacked, me ^ j) for j in range(len(pieces))])


def norm_stats(values):
    center = values - jnp.mean(values, axis=-1, keepdims=True)
    spread = jnp.mean(center * center, axis=-1, keepdims=True)
    rate = lax.rsqrt(spread + NORM_EPS)
    return center * rate, rate


def norm_back(slope, gain, hat, rate):
    scaled = slope * gain
    return rate * (
        scaled
        - jnp.mean(scaled, axis=-1, keepdims=True)
        - hat * jnp.mean(scaled * hat, axis=-1, keepdims=True)
    )


def total(parts):
    out = parts[0].astype(F32)
    for part in parts[1:]:
        out = out + part.astype(F32)
    return out


def cut_columns(source, cut, parts, i):
    wide = cut.shape[1] // parts
    for part in range(parts):
        low = (part * GROUPS + i) * wide
        cut[:, part * wide : (part + 1) * wide] = source[:, low : low + wide]


def cut_kernel(parts, place, source, cut):
    for i in range(GROUPS):

        @pl.when(place[0] == i)
        def _():
            cut_columns(source, cut, parts, i)


def cut_weight(weight, parts, g, k, ks):
    rows = weight.shape[0] // ks
    cols = weight.shape[1] // GROUPS
    if rows % 16 == 0:
        return pl.pallas_call(
            functools.partial(cut_kernel, parts),
            grid_spec=pltpu.PrefetchScalarGridSpec(
                num_scalar_prefetch=1,
                grid=(1,),
                in_specs=[pl.BlockSpec((rows, weight.shape[1]), lambda i, place: (place[1], 0))],
                out_specs=pl.BlockSpec((rows, cols), lambda i, place: (0, 0)),
            ),
            out_shape=jax.ShapeDtypeStruct((rows, cols), BF),
            compiler_params=pltpu.CompilerParams(vmem_limit_bytes=8 * 2**20),
        )(jnp.stack([g, k]).astype(jnp.int32), weight)
    half = pick(weight.reshape(ks, rows, -1), k)
    return lax.dynamic_index_in_dim(
        half.reshape(rows, parts, GROUPS, cols // parts), g, axis=2, keepdims=False
    ).reshape(rows, cols)


def cut_rest_kernel(parts, place, con_ref, exp_ref, out_ref, cut):
    width = con_ref.shape[1]
    wide = exp_ref.shape[1] // GROUPS
    cut[:, :width] = con_ref[...]
    cut[:, width + wide :] = out_ref[...]
    for i in range(GROUPS):

        @pl.when(place[0] == i)
        def _():
            cut_columns(exp_ref, cut.at[:, width : width + wide], parts, i)


def cut_rest(con_w, exp_w, out_w, parts, g, k, ks):
    width = out_w.shape[1]
    rows, ff_rows = out_w.shape[0] // ks, con_w.shape[0] // (GROUPS * ks)
    wide = exp_w.shape[1] // GROUPS
    if rows % 16 == 0 and rows == ff_rows:
        by_k = lambda i, place: (place[1], 0)
        return pl.pallas_call(
            functools.partial(cut_rest_kernel, parts),
            grid_spec=pltpu.PrefetchScalarGridSpec(
                num_scalar_prefetch=1,
                grid=(1,),
                in_specs=[
                    pl.BlockSpec((rows, width), lambda i, place: (place[0] * ks + place[1], 0)),
                    pl.BlockSpec((rows, exp_w.shape[1]), by_k),
                    pl.BlockSpec((rows, width), by_k),
                ],
                out_specs=pl.BlockSpec((rows, 2 * width + wide), lambda i, place: (0, 0)),
            ),
            out_shape=jax.ShapeDtypeStruct((rows, 2 * width + wide), BF),
            compiler_params=pltpu.CompilerParams(vmem_limit_bytes=8 * 2**20),
        )(jnp.stack([g, k]).astype(jnp.int32), con_w, exp_w, out_w)
    return jnp.concatenate(
        [
            pick(con_w.reshape(GROUPS * ks, ff_rows, width), g * ks + k),
            cut_weight(exp_w, parts, g, k, ks),
            pick(out_w.reshape(ks, rows, width), k),
        ],
        axis=1,
    )


def weave_kernel(parts, pieces, out):
    wide = pieces.shape[2] // parts
    for i in range(GROUPS):
        for part in range(parts):
            low = (part * GROUPS + i) * wide
            out[:, low : low + wide] = pieces[i, :, part * wide : (part + 1) * wide].astype(F32)


def weave(pieces, parts):
    rows, cols = pieces.shape[1], pieces.shape[2]
    step = 32
    return pl.pallas_call(
        functools.partial(weave_kernel, parts),
        grid=(rows // step,),
        in_specs=[pl.BlockSpec((GROUPS, step, cols), lambda i: (0, i, 0))],
        out_specs=pl.BlockSpec((step, GROUPS * cols), lambda i: (i, 0)),
        out_shape=jax.ShapeDtypeStruct((rows, GROUPS * cols), F32),
        compiler_params=pltpu.CompilerParams(vmem_limit_bytes=16 * 2**20),
    )(pieces)


def unfold_kernel(parts, pieces, exp_out, con_out):
    wide = con_out.shape[2]
    part_wide = wide // parts
    for i in range(GROUPS):
        con_out[i] = pieces[i, :, wide:].astype(F32)
        for part in range(parts):
            low = (part * GROUPS + i) * part_wide
            exp_out[:, low : low + part_wide] = pieces[
                i, :, part * part_wide : (part + 1) * part_wide
            ].astype(F32)


def unfold(pieces, parts):
    rows, wide = pieces.shape[1], pieces.shape[2] // 2
    step = 32
    return pl.pallas_call(
        functools.partial(unfold_kernel, parts),
        grid=(rows // step,),
        in_specs=[pl.BlockSpec((GROUPS, step, 2 * wide), lambda i: (0, i, 0))],
        out_specs=[
            pl.BlockSpec((step, GROUPS * wide), lambda i: (i, 0)),
            pl.BlockSpec((GROUPS, step, wide), lambda i: (0, i, 0)),
        ],
        out_shape=[
            jax.ShapeDtypeStruct((rows, GROUPS * wide), F32),
            jax.ShapeDtypeStruct((GROUPS, rows, wide), F32),
        ],
        compiler_params=pltpu.CompilerParams(vmem_limit_bytes=16 * 2**20),
    )(pieces)


def join_rows(pieces, joined):
    tok = pieces[0].shape[0]
    for i, piece in enumerate(pieces):
        joined[i * tok : (i + 1) * tok, :] = piece[...]


def hidden_kernel(*refs):
    h_rows, s_rows = refs[:GROUPS], refs[GROUPS : 2 * GROUPS]
    (exp_w, con_w, bias, act_ref, inner_ref, back_ref, out_ref, bias_ref) = refs[2 * GROUPS : -4]
    h_ref, s_ref, back_sum, out_sum = refs[-4:]
    step = pl.program_id(0)
    tok = h_rows[0].shape[0]

    @pl.when(step == 0)
    def _():
        join_rows(h_rows, h_ref)
        join_rows(s_rows, s_ref)

    inner = mm(h_ref[...], exp_w[...]) + bias[...]
    square = inner * inner
    tanh = jnp.tanh(GELU_COEF * (inner + GELU_CUBE * square * inner))
    half = 0.5 + 0.5 * tanh
    act = (inner * half).astype(BF)
    gelu_slope = half + (0.5 * GELU_COEF) * inner * (1.0 - tanh * tanh) * (
        1.0 + (3.0 * GELU_CUBE) * square
    )
    slope = (mm_rt(s_ref[...], con_w[...]) * gelu_slope).astype(BF)
    act_ref[...] = act
    inner_ref[...] = slope
    bias_ref[...] = jnp.sum(slope.astype(F32), axis=0, keepdims=True)
    back = mm_rt(slope, exp_w[...])
    out = mm(act, con_w[...])

    @pl.when(step == 0)
    def _():
        back_sum[...] = back
        out_sum[...] = out

    @pl.when(step > 0)
    def _():
        back_sum[...] += back
        out_sum[...] += out

    @pl.when(step == pl.num_programs(0) - 1)
    def _():
        for i in range(GROUPS):
            back_ref[i] = back_sum[i * tok : (i + 1) * tok, :].astype(BF)
            out_ref[i] = out_sum[i * tok : (i + 1) * tok, :].astype(BF)


def hidden_part(h_rows, s_rows, weights, bias):
    tok, width = h_rows[0].shape
    hidden = bias.shape[1]
    rows = GROUPS * tok
    step = 256
    fixed = lambda i: (0, 0)
    cols = lambda i: (0, i)
    slots = pl.BlockSpec((GROUPS, tok, width), lambda i: (0, 0, 0))
    return pl.pallas_call(
        hidden_kernel,
        grid=(hidden // step,),
        in_specs=[pl.BlockSpec((tok, width), fixed)] * (2 * GROUPS)
        + [
            pl.BlockSpec((width, step), lambda i: (0, width // step + i)),
            pl.BlockSpec((step, width), lambda i: (i, 0)),
            pl.BlockSpec((1, step), cols),
        ],
        out_specs=[
            pl.BlockSpec((rows, step), cols),
            pl.BlockSpec((rows, step), cols),
            slots,
            slots,
            pl.BlockSpec((1, step), cols),
        ],
        out_shape=[
            jax.ShapeDtypeStruct((rows, hidden), BF),
            jax.ShapeDtypeStruct((rows, hidden), BF),
            jax.ShapeDtypeStruct((GROUPS, tok, width), BF),
            jax.ShapeDtypeStruct((GROUPS, tok, width), BF),
            jax.ShapeDtypeStruct((1, hidden), F32),
        ],
        scratch_shapes=[pltpu.VMEM((rows, width), BF)] * 2 + [pltpu.VMEM((rows, width), F32)] * 2,
        compiler_params=pltpu.CompilerParams(vmem_limit_bytes=24 * 2**20),
        cost_estimate=pl.CostEstimate(
            flops=8 * rows * width * hidden, bytes_accessed=12 * rows * width, transcendentals=0
        ),
    )(*h_rows, *s_rows, weights, weights, bias)


def hidden_grad_kernel(*refs):
    h_rows, s_rows = refs[:GROUPS], refs[GROUPS : 2 * GROUPS]
    inner_ref, act_ref, out_ref, h_ref, s_ref = refs[2 * GROUPS :]
    wide, step = inner_ref.shape[1], act_ref.shape[1]

    @pl.when(pl.program_id(0) == 0)
    def _():
        join_rows(s_rows, s_ref)

    join_rows(h_rows, h_ref)
    out_ref[:, :wide] = mm_lt(h_ref[...], inner_ref[...]).astype(BF)
    out_ref[:, wide:] = mm_lt(act_ref[...], s_ref[...]).astype(BF)


def hidden_grads(h_rows, s_rows, slope_inner, act):
    tok, width = h_rows[0].shape
    rows, hidden = act.shape
    step = 256
    cols = lambda i: (0, i)
    fixed = lambda i: (0, 0)
    return pl.pallas_call(
        hidden_grad_kernel,
        grid=(width // step,),
        in_specs=[pl.BlockSpec((tok, step), cols)] * GROUPS
        + [pl.BlockSpec((tok, width), fixed)] * GROUPS
        + [pl.BlockSpec((rows, hidden), fixed), pl.BlockSpec((rows, step), cols)],
        out_specs=pl.BlockSpec((step, hidden + width), lambda i: (i, 0)),
        out_shape=jax.ShapeDtypeStruct((width, hidden + width), BF),
        scratch_shapes=[pltpu.VMEM((rows, step), BF), pltpu.VMEM((rows, width), BF)],
        compiler_params=pltpu.CompilerParams(vmem_limit_bytes=16 * 2**20),
        cost_estimate=pl.CostEstimate(
            flops=4 * rows * width * hidden, bytes_accessed=12 * rows * width, transcendentals=0
        ),
    )(*h_rows, *s_rows, slope_inner, act)


def visible(k, tok, keys):
    row = lax.broadcasted_iota(jnp.int32, (tok, keys), 0)
    col = lax.broadcasted_iota(jnp.int32, (tok, keys), 1)
    return col <= k * tok + row


def masked_scores(query, keys, seen):
    scores = mm_rt(query, keys)
    near = keys.shape[0] - seen.shape[1]
    last = jnp.where(seen, scores[:, near:], MASK_FILL)
    return last if near == 0 else jnp.concatenate([scores[:, :near], last], axis=1)


def attend_kernel(ks, head, place, *refs):
    pieces = refs[: GROUPS * ks]
    in_w, gain, shift, q_bias, v_bias = refs[GROUPS * ks : GROUPS * ks + 5]
    slots, q_out, k_out, v_out, att_out, lse_out, h_out, hat_out, h_all = refs[GROUPS * ks + 5 :]
    g, k = place[0], place[1]
    tok, width = pieces[0].shape
    cols = q_out.shape[1]
    for j in range(ks):
        for i in range(GROUPS):
            hat, _ = norm_stats(pieces[j * GROUPS + i][...].astype(F32))
            normed = (hat * gain[...] + shift[...]).astype(BF)
            spot = pl.multiple_of(((g ^ i) * ks + (k ^ j)) * tok, tok)
            h_all[pl.ds(spot, tok), :] = normed
            if j == 0:
                spot = pl.multiple_of((g ^ i) * tok, tok)
                h_out[pl.ds(spot, tok), :] = normed
                hat_out[pl.ds(spot, tok), :] = hat.astype(BF)
    q_out[...] = (mm(h_out[...], in_w[:, :cols]) + q_bias[...]).astype(BF)
    kv = mm(h_all[...], in_w[:, cols:])
    k_out[...] = kv[:, :cols].astype(BF)
    v_out[...] = (kv[:, cols:] + v_bias[...]).astype(BF)
    seen = visible(k, tok, ks * tok)
    for h in range(cols // head):
        low, high = h * head, (h + 1) * head
        for i in range(GROUPS):
            rows = slice(i * tok, (i + 1) * tok)
            span = (i + 1) * ks * tok
            query = (q_out[rows, low:high].astype(F32) * head**-0.5).astype(BF)
            scores = masked_scores(query, k_out[:span, low:high], seen)
            peak = jnp.max(scores, axis=-1, keepdims=True)
            weights = jnp.exp(scores - peak)
            mass = jnp.sum(weights, axis=-1, keepdims=True)
            lse_out[rows, h : h + 1] = peak + jnp.log(mass)
            att = mm(weights.astype(BF), v_out[:span, low:high]) / mass
            att_out[rows, low:high] = att
    for i in range(GROUPS):
        slots[g ^ i] = att_out[i * tok : (i + 1) * tok, :].astype(BF)


def attend(g, k, ks, head, pieces, in_w, gain, shift, q_bias, v_bias):
    tok, width = pieces[0].shape
    cols = in_w.shape[1] // 3
    mine, rows = GROUPS * tok, GROUPS * ks * tok
    vmem = pl.BlockSpec(memory_space=pltpu.VMEM)
    shapes = [
        ((GROUPS, tok, cols), BF),
        ((mine, cols), BF),
        ((rows, cols), BF),
        ((rows, cols), BF),
        ((mine, cols), F32),
        ((mine, 8), F32),
        ((mine, width), BF),
        ((mine, width), BF),
    ]
    return pl.pallas_call(
        functools.partial(attend_kernel, ks, head),
        grid_spec=pltpu.PrefetchScalarGridSpec(
            num_scalar_prefetch=1,
            in_specs=[vmem] * (len(pieces) + 5),
            out_specs=[vmem] * len(shapes),
            scratch_shapes=[pltpu.VMEM((rows, width), BF)],
        ),
        out_shape=[jax.ShapeDtypeStruct(s, t) for s, t in shapes],
        compiler_params=pltpu.CompilerParams(vmem_limit_bytes=(16 if ks == 2 else 48) * 2**20),
        cost_estimate=pl.CostEstimate(
            flops=6 * rows * width * cols, bytes_accessed=4 * rows * width, transcendentals=0
        ),
    )(jnp.stack([g, k]).astype(jnp.int32), *pieces, in_w, gain, shift, q_bias, v_bias)


def attend_back_kernel(ks, head, place, *refs):
    slopes = refs[:GROUPS]
    q_ref, k_ref, v_ref, att_ref, lse_ref, dq_out, dkv_out, dk_sum, dv_sum = refs[GROUPS:]
    g, k = place[0], place[1]
    tok, cols = slopes[0].shape
    d_rows = dq_out
    for i in range(GROUPS):
        d_rows[pl.ds(pl.multiple_of((g ^ i) * tok, tok), tok), :] = slopes[i][...]
    seen = visible(k, tok, ks * tok)
    for i in reversed(range(GROUPS)):
        rows = slice(i * tok, (i + 1) * tok)
        span = (i + 1) * ks * tok
        slope_all = d_rows[rows, :]
        parts = []
        for h in range(cols // head):
            low, high = h * head, (h + 1) * head
            query = (q_ref[rows, low:high].astype(F32) * head**-0.5).astype(BF)
            keys = k_ref[:span, low:high]
            slope = slope_all[:, low:high]
            scores = masked_scores(query, keys, seen)
            chances = jnp.exp(scores - lse_ref[rows, h : h + 1])
            diag = jnp.sum(slope.astype(F32) * att_ref[rows, low:high], axis=-1, keepdims=True)
            slope_chances = mm_rt(slope, v_ref[:span, low:high])
            slope_scores = (chances * (slope_chances - diag)).astype(BF)
            parts.append(mm(slope_scores, keys) * head**-0.5)
            dk = mm_lt(slope_scores, query)
            dv = mm_lt(chances.astype(BF), slope)
            if i == GROUPS - 1:
                dk_sum[:, low:high] = dk
                dv_sum[:, low:high] = dv
            else:
                dk_sum[:span, low:high] += dk
                dv_sum[:span, low:high] += dv
        dq_out[rows, :] = jnp.concatenate(parts, axis=1).astype(BF)
    for i in range(GROUPS):
        for j in range(ks):
            spot = slice((i * ks + j) * tok, (i * ks + j + 1) * tok)
            dkv_out[k ^ j, i * tok : (i + 1) * tok, :] = jnp.concatenate(
                [dk_sum[spot, :], dv_sum[spot, :]], axis=1
            ).astype(BF)


def attend_back(g, k, ks, head, slopes, q, keys, values, att, lse):
    tok, cols = slopes[0].shape
    mine, rows = GROUPS * tok, GROUPS * ks * tok
    vmem = pl.BlockSpec(memory_space=pltpu.VMEM)
    return pl.pallas_call(
        functools.partial(attend_back_kernel, ks, head),
        grid_spec=pltpu.PrefetchScalarGridSpec(
            num_scalar_prefetch=1,
            in_specs=[vmem] * (len(slopes) + 5),
            out_specs=[vmem] * 2,
            scratch_shapes=[pltpu.VMEM((rows, cols), F32)] * 2,
        ),
        out_shape=[
            jax.ShapeDtypeStruct((mine, cols), BF),
            jax.ShapeDtypeStruct((ks, mine, 2 * cols), BF),
        ],
        compiler_params=pltpu.CompilerParams(vmem_limit_bytes=(16 if ks == 2 else 48) * 2**20),
        cost_estimate=pl.CostEstimate(
            flops=10 * mine * rows * cols, bytes_accessed=8 * rows * cols, transcendentals=0
        ),
    )(jnp.stack([g, k]).astype(jnp.int32), *slopes, q, keys, values, att, lse)


def project_back_kernel(ks, place, *refs):
    dq, dkv = refs[0], refs[1 : 1 + ks]
    h_ref, hat_ref, in_w, slots, d_in, sums, project = refs[1 + ks :]
    g = place[0]
    tok = slots.shape[1]
    cols = dq.shape[1]
    project[:, :cols] = dq[...]
    project[:, cols:] = total([part[...] for part in dkv]).astype(BF)
    back = mm_rt(project[...], in_w[...])
    for i in range(GROUPS):
        slots[g ^ i] = back[i * tok : (i + 1) * tok, :].astype(BF)
    sums[0:1, :] = jnp.sum(back * hat_ref[...].astype(F32), axis=0, keepdims=True)
    sums[1:2, :] = jnp.sum(back, axis=0, keepdims=True)
    sums[2:3, : 3 * cols] = jnp.sum(project[...].astype(F32), axis=0, keepdims=True)
    d_in[...] = mm_lt(h_ref[...], project[...]).astype(BF)


def project_back(g, k, dq, dkv, h, hat, in_w):
    mine, width = h.shape
    cols = dq.shape[1]
    vmem = pl.BlockSpec(memory_space=pltpu.VMEM)
    return pl.pallas_call(
        functools.partial(project_back_kernel, len(dkv)),
        grid_spec=pltpu.PrefetchScalarGridSpec(
            num_scalar_prefetch=1,
            in_specs=[vmem] * (len(dkv) + 4),
            out_specs=[vmem] * 3,
            scratch_shapes=[pltpu.VMEM((mine, 3 * cols), BF)],
        ),
        out_shape=[
            jax.ShapeDtypeStruct((GROUPS, mine // GROUPS, width), BF),
            jax.ShapeDtypeStruct((width, 3 * cols), BF),
            jax.ShapeDtypeStruct((8, width), F32),
        ],
        compiler_params=pltpu.CompilerParams(vmem_limit_bytes=16 * 2**20),
        cost_estimate=pl.CostEstimate(
            flops=12 * mine * width * cols, bytes_accessed=4 * mine * width, transcendentals=0
        ),
    )(jnp.stack([g, k]).astype(jnp.int32), dq, *dkv, h, hat, in_w)


def shards(
    inputs,
    cotangent,
    first_gain,
    first_shift,
    input_weight,
    query_bias,
    value_bias,
    output_weight,
    output_bias,
    second_gain,
    second_shift,
    expand_weight,
    expand_bias,
    contract_weight,
    contract_bias,
):
    tok, width = inputs.shape[1:]
    ks, zs = lax.axis_size("core"), lax.axis_size("fsdp")
    g, k, z = lax.axis_index("grp"), lax.axis_index("core"), lax.axis_index("fsdp")
    rows_z = width // zs
    heads_here = HEADS // GROUPS
    head = width // HEADS
    cols = width // GROUPS
    ff = expand_weight.shape[1]
    ff_z = ff // zs
    ff_g = ff_z // GROUPS
    mine = GROUPS * tok
    scale = head ** (-0.5)

    x_own = inputs[0]
    slope_own = cotangent[0]

    x_rows = gather_flips(x_own, "grp")
    in_cut = cut_weight(input_weight, 3, g, k, ks)
    in_pieces = gather_flips(in_cut, "fsdp")
    x_more = [[send(b, "core", j) for b in x_rows] for j in range(1, ks)]

    smalls = jnp.concatenate(
        [
            first_gain,
            first_shift,
            query_bias,
            value_bias,
            output_bias,
            second_gain,
            second_shift,
            contract_bias,
            expand_bias,
        ]
    )
    smalls_all = in_order(gather_flips(smalls, "fsdp"), z).astype(F32)

    def small(i):
        return smalls_all[:, i * rows_z : (i + 1) * rows_z].reshape(width)

    gain_one, shift_one, q_bias, v_bias, o_bias, gain_two, shift_two, c_bias = [
        small(i) for i in range(8)
    ]
    e_bias = pick(
        smalls_all[:, 8 * rows_z :].reshape(zs, GROUPS, ff_g).transpose(1, 0, 2), g
    ).reshape(zs * ff_g)
    q_bias = pick(q_bias.reshape(GROUPS, cols), g)
    v_bias = pick(v_bias.reshape(GROUPS, cols), g)

    in_half = in_order(in_pieces, z)
    in_w = jnp.stack(in_order(gather_flips(in_half, "core"), k), axis=1).reshape(width, 3 * cols)

    rest = cut_rest(contract_weight, expand_weight, output_weight, zs, g, k, ks)
    rest = lax.all_gather(rest, ("fsdp", "core"), axis=0, tiled=True)
    out_w = rest[:, width + zs * ff_g :].reshape(GROUPS, cols, width)
    out_w = jnp.concatenate([pick(out_w, g ^ i) for i in range(GROUPS)])
    slope_late, _ = lax.optimization_barrier((slope_own, x_rows[-1]))
    slope_rows = gather_flips(slope_late, "grp")

    slots, qs, keys, values, att_full, lse, h1, hat_one = attend(
        g,
        k,
        ks,
        head,
        x_rows + [b for bs in x_more for b in bs],
        in_w,
        gain_one[None],
        shift_one[None],
        q_bias[None],
        v_bias[None],
    )
    att = jnp.concatenate(swap_flips([slots[i] for i in range(GROUPS)], "grp"), axis=1)
    x_f = x_own.astype(F32)
    middle = x_f + mm(att, out_w) + o_bias
    hat_two, rate_two = norm_stats(middle)
    h2 = (hat_two * gain_two + shift_two).astype(BF)
    h2_rows = gather_flips(h2, "grp")

    act, slope_inner, sh2_part, out_part, d_exp_b = hidden_part(
        h2_rows, slope_rows, rest, e_bias[None]
    )
    sh2 = total(swap_flips([sh2_part[i] for i in range(GROUPS)], "grp"))
    d_hidden = lax.psum_scatter(
        hidden_grads(h2_rows, slope_rows, slope_inner, act),
        ("fsdp", "core"),
        scatter_dimension=0,
        tiled=True,
    )

    slope_f = slope_own.astype(F32)
    d_gain_two = jnp.sum(sh2 * hat_two, axis=0)
    d_shift_two = jnp.sum(sh2, axis=0)
    slope_middle = slope_f + norm_back(sh2, gain_two, hat_two, rate_two)
    slope_branch = slope_middle.astype(BF)
    slope_att = mm_rt(slope_branch, out_w).astype(BF)
    datt = swap_flips([slope_att[:, i * cols : (i + 1) * cols] for i in range(GROUPS)], "grp")

    d_out = mm_lt(att, slope_branch).astype(BF).reshape(GROUPS, cols, width)
    d_out = in_order([d_out[i] for i in range(GROUPS)], g)
    d_out = d_out.reshape(zs, GROUPS, ks, rows_z // GROUPS // ks, width)
    pieces = [lax.dynamic_index_in_dim(d_out, k ^ j, axis=2, keepdims=False) for j in range(ks)]
    d_out = total(swap_flips(pieces, "core")).astype(BF)
    pieces = [lax.dynamic_index_in_dim(d_out, g ^ i, axis=1, keepdims=False) for i in range(GROUPS)]
    d_out = total(swap_flips(pieces, "grp")).astype(BF)
    third = d_out.shape[1] // 3
    tail = d_out[:, :, 3 * cols :]
    d_out = jnp.concatenate(
        [
            d_out[:, :, : 3 * cols],
            jnp.concatenate([tail[:, i * third : (i + 1) * third] for i in range(3)], axis=2),
        ],
        axis=1,
    )

    datt, d_out = lax.optimization_barrier((datt, d_out))
    dq, dkv = attend_back(g, k, ks, head, datt, qs, keys, values, att_full, lse)
    dkv = swap_flips([dkv[j] for j in range(ks)], "core")
    sh1_part, d_in, sums = project_back(g, k, dq, dkv, h1, hat_one, in_w)
    sh1 = total(swap_flips([sh1_part[i] for i in range(GROUPS)], "grp"))
    hat_own, rate_own = norm_stats(x_f)
    delta_inputs = (slope_middle + norm_back(sh1, gain_one, hat_own, rate_own)).astype(BF)[None]

    def at_group(vec, lead):
        parts = vec.reshape(lead, 1, -1)
        spot = (jnp.arange(GROUPS) == g).astype(F32)[None, :, None]
        return (parts * spot).reshape(-1)

    vectors = [
        sums[0],
        sums[1],
        at_group(sums[2, :cols], 1),
        at_group(sums[2, 2 * cols : 3 * cols], 1),
        jnp.sum(slope_branch.astype(F32), axis=0),
        d_gain_two,
        d_shift_two,
        jnp.sum(slope_f, axis=0),
    ]
    packed = jnp.concatenate(
        [v.reshape(zs, rows_z) for v in vectors]
        + [at_group(d_exp_b, zs).reshape(zs, ff_z)],
        axis=1,
    )
    count = packed.shape[1]
    extra = -(-count // (3 * cols * ks))
    packed = jnp.pad(packed, ((0, 0), (0, extra * ks * 3 * cols - count)))
    d_in = d_in.reshape(zs, ks, rows_z // ks, 3 * cols)
    d_in = jnp.concatenate([d_in, packed.astype(BF).reshape(zs, ks, extra, 3 * cols)], axis=2)
    pieces = [lax.dynamic_index_in_dim(d_in, k ^ j, axis=1, keepdims=False) for j in range(ks)]
    d_in = total(swap_flips(pieces, "core")).astype(BF)
    d_in = jnp.concatenate([d_in, d_out], axis=1)
    out_late, _ = lax.optimization_barrier((out_part, d_in))
    out_sum = total(swap_flips([out_late[i] for i in range(GROUPS)], "grp"))
    outputs = (middle + out_sum + c_bias).astype(BF)[None]
    d_in = total(swap_flips([pick(d_in, z ^ i) for i in range(zs)], "fsdp")).astype(BF)
    d_in = in_order(gather_flips(d_in, "grp"), g)
    d_in = in_order(gather_flips(d_in, "core"), k)
    own = rows_z // ks
    packed = jnp.sum(d_in[:, :, own : own + extra].astype(F32), axis=1).reshape(-1)
    d_out = d_in[:, :, own + extra :].transpose(1, 0, 2, 3)
    tail = d_out[:, :, 3 * third :].reshape(GROUPS, ks, third, 3, width - 3 * cols)
    d_out_w = (
        jnp.concatenate(
            [
                d_out[:, :, : 3 * third],
                jnp.concatenate([tail[:, :, :, i] for i in range(3)], axis=2),
            ],
            axis=3,
        )
        .reshape(rows_z, width)
        .astype(F32)
    )
    d_in = d_in[:, :, :own].transpose(1, 0, 2, 3).reshape(GROUPS, rows_z, 3 * cols)
    d_in_w = weave(d_in, 3)
    d_hidden = in_order(gather_flips(d_hidden, "grp"), g)
    d_hidden = jnp.stack(in_order(gather_flips(d_hidden, "core"), k), axis=1)
    d_exp_w, d_con_w = unfold(d_hidden.reshape(GROUPS, rows_z, -1), zs)
    d_con_w = d_con_w.reshape(ff_z, width)

    def vec(i):
        return packed[i * rows_z : (i + 1) * rows_z]

    return (
        outputs,
        delta_inputs,
        vec(0),
        vec(1),
        d_in_w,
        vec(2),
        vec(3),
        d_out_w,
        vec(4),
        vec(5),
        vec(6),
        d_exp_w,
        packed[8 * rows_z : 8 * rows_z + ff_z],
        d_con_w,
        vec(7),
    )


def solution(mesh):
    ctx, zs = mesh.shape["ctx"], mesh.shape["fsdp"]
    axes = ("grp", "core", "fsdp")
    split = Mesh(mesh.devices.reshape(GROUPS, ctx // GROUPS, zs), axes)
    row, vec, mat = P("fsdp", ("grp", "core"), None), P("fsdp"), P("fsdp", None)
    placed = (row, row, vec, vec, mat, vec, vec, mat, vec, vec, vec, mat, vec, mat, vec)
    return jax.shard_map(
        shards,
        mesh=split,
        in_specs=placed,
        out_specs=placed,
        check_vma=False,
    )
```

```python
import functools

import jax
import jax.numpy as jnp
from jax import lax
from jax.experimental import pallas as pl
from jax.experimental.pallas import tpu as pltpu
from jax.sharding import Mesh, PartitionSpec as P

HEADS = 12
GROUPS = 4

NORM_EPS = 1e-05
MASK_FILL = -1e30
GELU_COEF = 0.7978845608028654
GELU_CUBE = 0.044715

BF = jnp.bfloat16
F32 = jnp.float32


def in_hbm(*values):
    return [pltpu.with_memory_space_constraint(v, pltpu.HBM) for v in values]


def mm(left, right):
    return jnp.dot(left, right, preferred_element_type=F32)


def mm_lt(left, right):
    return lax.dot_general(left, right, (((0,), (0,)), ((), ())), preferred_element_type=F32)


def mm_rt(left, right):
    return lax.dot_general(left, right, (((1,), (1,)), ((), ())), preferred_element_type=F32)


def send(value, axis, flip):
    count = lax.axis_size(axis)
    return lax.ppermute(value, axis, [(s, s ^ flip) for s in range(count)])


def gather_flips(value, axis):
    return [value] + [send(value, axis, i) for i in range(1, lax.axis_size(axis))]


def swap_flips(pieces, axis):
    return [pieces[0]] + [send(p, axis, i) for i, p in enumerate(pieces) if i]


def pick(stacked, place):
    return lax.dynamic_index_in_dim(stacked, place, axis=0, keepdims=False)


def in_order(pieces, me):
    stacked = jnp.stack(pieces)
    return jnp.stack([pick(stacked, me ^ j) for j in range(len(pieces))])


def norm_stats(values):
    center = values - jnp.mean(values, axis=-1, keepdims=True)
    spread = jnp.mean(center * center, axis=-1, keepdims=True)
    rate = lax.rsqrt(spread + NORM_EPS)
    return center * rate, rate


def norm_back(slope, gain, hat, rate):
    scaled = slope * gain
    return rate * (
        scaled
        - jnp.mean(scaled, axis=-1, keepdims=True)
        - hat * jnp.mean(scaled * hat, axis=-1, keepdims=True)
    )


def total(parts):
    out = parts[0].astype(F32)
    for part in parts[1:]:
        out = out + part.astype(F32)
    return out


def cut_columns(source, cut, parts, i):
    wide = cut.shape[1] // parts
    for part in range(parts):
        low = (part * GROUPS + i) * wide
        cut[:, part * wide : (part + 1) * wide] = source[:, low : low + wide]


def cut_kernel(parts, place, source, cut):
    for i in range(GROUPS):

        @pl.when(place[0] == i)
        def _():
            cut_columns(source, cut, parts, i)


def cut_weight(weight, parts, g, k, ks):
    rows = weight.shape[0] // ks
    cols = weight.shape[1] // GROUPS
    if rows % 16 == 0:
        return pl.pallas_call(
            functools.partial(cut_kernel, parts),
            grid_spec=pltpu.PrefetchScalarGridSpec(
                num_scalar_prefetch=1,
                grid=(1,),
                in_specs=[pl.BlockSpec((rows, weight.shape[1]), lambda i, place: (place[1], 0))],
                out_specs=pl.BlockSpec((rows, cols), lambda i, place: (0, 0)),
            ),
            out_shape=jax.ShapeDtypeStruct((rows, cols), BF),
            compiler_params=pltpu.CompilerParams(vmem_limit_bytes=8 * 2**20),
        )(jnp.stack([g, k]).astype(jnp.int32), weight)
    half = pick(weight.reshape(ks, rows, -1), k)
    return lax.dynamic_index_in_dim(
        half.reshape(rows, parts, GROUPS, cols // parts), g, axis=2, keepdims=False
    ).reshape(rows, cols)


def cut_rest_kernel(parts, place, con_ref, exp_ref, out_ref, cut):
    width = con_ref.shape[1]
    wide = exp_ref.shape[1] // GROUPS
    cut[:, :width] = con_ref[...]
    cut[:, width + wide :] = out_ref[...]
    for i in range(GROUPS):

        @pl.when(place[0] == i)
        def _():
            cut_columns(exp_ref, cut.at[:, width : width + wide], parts, i)


def cut_rest(con_w, exp_w, out_w, parts, g, k, ks):
    width = out_w.shape[1]
    rows, ff_rows = out_w.shape[0] // ks, con_w.shape[0] // (GROUPS * ks)
    wide = exp_w.shape[1] // GROUPS
    if rows % 16 == 0 and rows == ff_rows:
        by_k = lambda i, place: (place[1], 0)
        return pl.pallas_call(
            functools.partial(cut_rest_kernel, parts),
            grid_spec=pltpu.PrefetchScalarGridSpec(
                num_scalar_prefetch=1,
                grid=(1,),
                in_specs=[
                    pl.BlockSpec((rows, width), lambda i, place: (place[0] * ks + place[1], 0)),
                    pl.BlockSpec((rows, exp_w.shape[1]), by_k),
                    pl.BlockSpec((rows, width), by_k),
                ],
                out_specs=pl.BlockSpec((rows, 2 * width + wide), lambda i, place: (0, 0)),
            ),
            out_shape=jax.ShapeDtypeStruct((rows, 2 * width + wide), BF),
            compiler_params=pltpu.CompilerParams(vmem_limit_bytes=8 * 2**20),
        )(jnp.stack([g, k]).astype(jnp.int32), con_w, exp_w, out_w)
    return jnp.concatenate(
        [
            pick(con_w.reshape(GROUPS * ks, ff_rows, width), g * ks + k),
            cut_weight(exp_w, parts, g, k, ks),
            pick(out_w.reshape(ks, rows, width), k),
        ],
        axis=1,
    )


def weave_kernel(parts, pieces, out):
    wide = pieces.shape[2] // parts
    for i in range(GROUPS):
        for part in range(parts):
            low = (part * GROUPS + i) * wide
            out[:, low : low + wide] = pieces[i, :, part * wide : (part + 1) * wide].astype(F32)


def weave(pieces, parts):
    rows, cols = pieces.shape[1], pieces.shape[2]
    step = 32
    return pl.pallas_call(
        functools.partial(weave_kernel, parts),
        grid=(rows // step,),
        in_specs=[pl.BlockSpec((GROUPS, step, cols), lambda i: (0, i, 0))],
        out_specs=pl.BlockSpec((step, GROUPS * cols), lambda i: (i, 0)),
        out_shape=jax.ShapeDtypeStruct((rows, GROUPS * cols), F32),
        compiler_params=pltpu.CompilerParams(vmem_limit_bytes=16 * 2**20),
    )(pieces)


def unfold_kernel(parts, pieces, exp_out, con_out):
    wide = con_out.shape[2]
    part_wide = wide // parts
    for i in range(GROUPS):
        con_out[i] = pieces[i, :, wide:].astype(F32)
        for part in range(parts):
            low = (part * GROUPS + i) * part_wide
            exp_out[:, low : low + part_wide] = pieces[
                i, :, part * part_wide : (part + 1) * part_wide
            ].astype(F32)


def unfold(pieces, parts):
    rows, wide = pieces.shape[1], pieces.shape[2] // 2
    step = 32
    return pl.pallas_call(
        functools.partial(unfold_kernel, parts),
        grid=(rows // step,),
        in_specs=[pl.BlockSpec((GROUPS, step, 2 * wide), lambda i: (0, i, 0))],
        out_specs=[
            pl.BlockSpec((step, GROUPS * wide), lambda i: (i, 0)),
            pl.BlockSpec((GROUPS, step, wide), lambda i: (0, i, 0)),
        ],
        out_shape=[
            jax.ShapeDtypeStruct((rows, GROUPS * wide), F32),
            jax.ShapeDtypeStruct((GROUPS, rows, wide), F32),
        ],
        compiler_params=pltpu.CompilerParams(vmem_limit_bytes=16 * 2**20),
    )(pieces)


def join_rows(pieces, joined):
    tok = pieces[0].shape[0]
    for i, piece in enumerate(pieces):
        joined[i * tok : (i + 1) * tok, :] = piece[...]


def hidden_kernel(*refs):
    h_rows, s_rows = refs[:GROUPS], refs[GROUPS : 2 * GROUPS]
    (exp_w, con_w, bias, act_ref, inner_ref, back_ref, out_ref, bias_ref) = refs[2 * GROUPS : -4]
    h_ref, s_ref, back_sum, out_sum = refs[-4:]
    step = pl.program_id(0)
    tok = h_rows[0].shape[0]

    @pl.when(step == 0)
    def _():
        join_rows(h_rows, h_ref)
        join_rows(s_rows, s_ref)

    inner = mm(h_ref[...], exp_w[...]) + bias[...]
    square = inner * inner
    tanh = jnp.tanh(GELU_COEF * (inner + GELU_CUBE * square * inner))
    half = 0.5 + 0.5 * tanh
    act = (inner * half).astype(BF)
    gelu_slope = half + (0.5 * GELU_COEF) * inner * (1.0 - tanh * tanh) * (
        1.0 + (3.0 * GELU_CUBE) * square
    )
    slope = (mm_rt(s_ref[...], con_w[...]) * gelu_slope).astype(BF)
    act_ref[...] = act
    inner_ref[...] = slope
    bias_ref[...] = jnp.sum(slope.astype(F32), axis=0, keepdims=True)
    back = mm_rt(slope, exp_w[...])
    out = mm(act, con_w[...])

    @pl.when(step == 0)
    def _():
        back_sum[...] = back
        out_sum[...] = out

    @pl.when(step > 0)
    def _():
        back_sum[...] += back
        out_sum[...] += out

    @pl.when(step == pl.num_programs(0) - 1)
    def _():
        for i in range(GROUPS):
            back_ref[i] = back_sum[i * tok : (i + 1) * tok, :].astype(BF)
            out_ref[i] = out_sum[i * tok : (i + 1) * tok, :].astype(BF)


def hidden_part(h_rows, s_rows, weights, bias):
    tok, width = h_rows[0].shape
    hidden = bias.shape[1]
    rows = GROUPS * tok
    step = 256
    fixed = lambda i: (0, 0)
    cols = lambda i: (0, i)
    slots = pl.BlockSpec((GROUPS, tok, width), lambda i: (0, 0, 0))
    return pl.pallas_call(
        hidden_kernel,
        grid=(hidden // step,),
        in_specs=[pl.BlockSpec((tok, width), fixed)] * (2 * GROUPS)
        + [
            pl.BlockSpec((width, step), lambda i: (0, width // step + i)),
            pl.BlockSpec((step, width), lambda i: (i, 0)),
            pl.BlockSpec((1, step), cols),
        ],
        out_specs=[
            pl.BlockSpec((rows, step), cols),
            pl.BlockSpec((rows, step), cols),
            slots,
            slots,
            pl.BlockSpec((1, step), cols),
        ],
        out_shape=[
            jax.ShapeDtypeStruct((rows, hidden), BF),
            jax.ShapeDtypeStruct((rows, hidden), BF),
            jax.ShapeDtypeStruct((GROUPS, tok, width), BF),
            pltpu.HBM((GROUPS, tok, width), BF),
            jax.ShapeDtypeStruct((1, hidden), F32),
        ],
        scratch_shapes=[pltpu.VMEM((rows, width), BF)] * 2 + [pltpu.VMEM((rows, width), F32)] * 2,
        compiler_params=pltpu.CompilerParams(vmem_limit_bytes=24 * 2**20),
        cost_estimate=pl.CostEstimate(
            flops=8 * rows * width * hidden, bytes_accessed=12 * rows * width, transcendentals=0
        ),
    )(*h_rows, *in_hbm(*s_rows, weights, weights), bias)


def hidden_grad_kernel(*refs):
    h_rows, s_rows = refs[:GROUPS], refs[GROUPS : 2 * GROUPS]
    inner_ref, act_ref, out_ref, h_ref, s_ref = refs[2 * GROUPS :]
    wide, step = inner_ref.shape[1], act_ref.shape[1]

    @pl.when(pl.program_id(0) == 0)
    def _():
        join_rows(s_rows, s_ref)

    join_rows(h_rows, h_ref)
    out_ref[:, :wide] = mm_lt(h_ref[...], inner_ref[...]).astype(BF)
    out_ref[:, wide:] = mm_lt(act_ref[...], s_ref[...]).astype(BF)


def hidden_grads(h_rows, s_rows, slope_inner, act):
    tok, width = h_rows[0].shape
    rows, hidden = act.shape
    step = 256
    cols = lambda i: (0, i)
    fixed = lambda i: (0, 0)
    return pl.pallas_call(
        hidden_grad_kernel,
        grid=(width // step,),
        in_specs=[pl.BlockSpec((tok, step), cols)] * GROUPS
        + [pl.BlockSpec((tok, width), fixed)] * GROUPS
        + [pl.BlockSpec((rows, hidden), fixed), pl.BlockSpec((rows, step), cols)],
        out_specs=pl.BlockSpec((step, hidden + width), lambda i: (i, 0)),
        out_shape=jax.ShapeDtypeStruct((width, hidden + width), BF),
        scratch_shapes=[pltpu.VMEM((rows, step), BF), pltpu.VMEM((rows, width), BF)],
        compiler_params=pltpu.CompilerParams(vmem_limit_bytes=16 * 2**20),
        cost_estimate=pl.CostEstimate(
            flops=4 * rows * width * hidden, bytes_accessed=12 * rows * width, transcendentals=0
        ),
    )(*h_rows, *in_hbm(*s_rows), slope_inner, act)


def visible(k, tok, keys):
    row = lax.broadcasted_iota(jnp.int32, (tok, keys), 0)
    col = lax.broadcasted_iota(jnp.int32, (tok, keys), 1)
    return col <= k * tok + row


def masked_scores(query, keys, seen):
    scores = mm_rt(query, keys)
    near = keys.shape[0] - seen.shape[1]
    last = jnp.where(seen, scores[:, near:], MASK_FILL)
    return last if near == 0 else jnp.concatenate([scores[:, :near], last], axis=1)


def attend_kernel(ks, head, place, *refs):
    pieces = refs[: GROUPS * ks]
    in_w, gain, shift, q_bias, v_bias = refs[GROUPS * ks : GROUPS * ks + 5]
    slots, q_out, k_out, v_out, att_out, lse_out, h_out, hat_out, h_all = refs[GROUPS * ks + 5 :]
    g, k = place[0], place[1]
    tok, width = pieces[0].shape
    cols = q_out.shape[1]
    for j in range(ks):
        for i in range(GROUPS):
            hat, _ = norm_stats(pieces[j * GROUPS + i][...].astype(F32))
            normed = (hat * gain[...] + shift[...]).astype(BF)
            spot = pl.multiple_of(((g ^ i) * ks + (k ^ j)) * tok, tok)
            h_all[pl.ds(spot, tok), :] = normed
            if j == 0:
                spot = pl.multiple_of((g ^ i) * tok, tok)
                h_out[pl.ds(spot, tok), :] = normed
                hat_out[pl.ds(spot, tok), :] = hat.astype(BF)
    q_out[...] = (mm(h_out[...], in_w[:, :cols]) + q_bias[...]).astype(BF)
    kv = mm(h_all[...], in_w[:, cols:])
    k_out[...] = kv[:, :cols].astype(BF)
    v_out[...] = (kv[:, cols:] + v_bias[...]).astype(BF)
    seen = visible(k, tok, ks * tok)
    for h in range(cols // head):
        low, high = h * head, (h + 1) * head
        for i in range(GROUPS):
            rows = slice(i * tok, (i + 1) * tok)
            span = (i + 1) * ks * tok
            query = (q_out[rows, low:high].astype(F32) * head**-0.5).astype(BF)
            scores = masked_scores(query, k_out[:span, low:high], seen)
            peak = jnp.max(scores, axis=-1, keepdims=True)
            weights = jnp.exp(scores - peak)
            mass = jnp.sum(weights, axis=-1, keepdims=True)
            lse_out[rows, h : h + 1] = peak + jnp.log(mass)
            att = mm(weights.astype(BF), v_out[:span, low:high]) / mass
            att_out[rows, low:high] = att
    for i in range(GROUPS):
        slots[g ^ i] = att_out[i * tok : (i + 1) * tok, :].astype(BF)


def attend(g, k, ks, head, pieces, in_w, gain, shift, q_bias, v_bias):
    tok, width = pieces[0].shape
    cols = in_w.shape[1] // 3
    mine, rows = GROUPS * tok, GROUPS * ks * tok
    vmem = pl.BlockSpec(memory_space=pltpu.VMEM)
    shapes = [
        ((GROUPS, tok, cols), BF),
        ((mine, cols), BF),
        ((rows, cols), BF),
        ((rows, cols), BF),
        ((mine, cols), F32),
        ((mine, 8), F32),
        ((mine, width), BF),
        ((mine, width), BF),
    ]
    return pl.pallas_call(
        functools.partial(attend_kernel, ks, head),
        grid_spec=pltpu.PrefetchScalarGridSpec(
            num_scalar_prefetch=1,
            in_specs=[vmem] * (len(pieces) + 5),
            out_specs=[vmem] * len(shapes),
            scratch_shapes=[pltpu.VMEM((rows, width), BF)],
        ),
        out_shape=[jax.ShapeDtypeStruct(*shapes[0])] + [pltpu.HBM(s, t) for s, t in shapes[1:]],
        compiler_params=pltpu.CompilerParams(vmem_limit_bytes=(16 if ks == 2 else 48) * 2**20),
        cost_estimate=pl.CostEstimate(
            flops=6 * rows * width * cols, bytes_accessed=4 * rows * width, transcendentals=0
        ),
    )(jnp.stack([g, k]).astype(jnp.int32), *pieces, in_w, gain, shift, q_bias, v_bias)


def attend_back_kernel(ks, head, place, *refs):
    slopes = refs[:GROUPS]
    q_ref, k_ref, v_ref, att_ref, lse_ref, dq_out, dkv_out, dk_sum, dv_sum = refs[GROUPS:]
    g, k = place[0], place[1]
    tok, cols = slopes[0].shape
    d_rows = dq_out
    for i in range(GROUPS):
        d_rows[pl.ds(pl.multiple_of((g ^ i) * tok, tok), tok), :] = slopes[i][...]
    seen = visible(k, tok, ks * tok)
    for i in reversed(range(GROUPS)):
        rows = slice(i * tok, (i + 1) * tok)
        span = (i + 1) * ks * tok
        slope_all = d_rows[rows, :]
        parts = []
        for h in range(cols // head):
            low, high = h * head, (h + 1) * head
            query = (q_ref[rows, low:high].astype(F32) * head**-0.5).astype(BF)
            keys = k_ref[:span, low:high]
            slope = slope_all[:, low:high]
            scores = masked_scores(query, keys, seen)
            chances = jnp.exp(scores - lse_ref[rows, h : h + 1])
            diag = jnp.sum(slope.astype(F32) * att_ref[rows, low:high], axis=-1, keepdims=True)
            slope_chances = mm_rt(slope, v_ref[:span, low:high])
            slope_scores = (chances * (slope_chances - diag)).astype(BF)
            parts.append(mm(slope_scores, keys) * head**-0.5)
            dk = mm_lt(slope_scores, query)
            dv = mm_lt(chances.astype(BF), slope)
            if i == GROUPS - 1:
                dk_sum[:, low:high] = dk
                dv_sum[:, low:high] = dv
            else:
                dk_sum[:span, low:high] += dk
                dv_sum[:span, low:high] += dv
        dq_out[rows, :] = jnp.concatenate(parts, axis=1).astype(BF)
    for i in range(GROUPS):
        for j in range(ks):
            spot = slice((i * ks + j) * tok, (i * ks + j + 1) * tok)
            dkv_out[k ^ j, i * tok : (i + 1) * tok, :] = jnp.concatenate(
                [dk_sum[spot, :], dv_sum[spot, :]], axis=1
            ).astype(BF)


def attend_back(g, k, ks, head, slopes, q, keys, values, att, lse):
    tok, cols = slopes[0].shape
    mine, rows = GROUPS * tok, GROUPS * ks * tok
    vmem = pl.BlockSpec(memory_space=pltpu.VMEM)
    return pl.pallas_call(
        functools.partial(attend_back_kernel, ks, head),
        grid_spec=pltpu.PrefetchScalarGridSpec(
            num_scalar_prefetch=1,
            in_specs=[vmem] * (len(slopes) + 5),
            out_specs=[vmem] * 2,
            scratch_shapes=[pltpu.VMEM((rows, cols), F32)] * 2,
        ),
        out_shape=[
            jax.ShapeDtypeStruct((mine, cols), BF),
            jax.ShapeDtypeStruct((ks, mine, 2 * cols), BF),
        ],
        compiler_params=pltpu.CompilerParams(vmem_limit_bytes=(16 if ks == 2 else 48) * 2**20),
        cost_estimate=pl.CostEstimate(
            flops=10 * mine * rows * cols, bytes_accessed=8 * rows * cols, transcendentals=0
        ),
    )(jnp.stack([g, k]).astype(jnp.int32), *slopes, *in_hbm(q, keys, values, att, lse))


def project_back_kernel(ks, place, *refs):
    dq, dkv = refs[0], refs[1 : 1 + ks]
    h_ref, hat_ref, in_w, slots, d_in, sums, project = refs[1 + ks :]
    g = place[0]
    tok = slots.shape[1]
    cols = dq.shape[1]
    project[:, :cols] = dq[...]
    project[:, cols:] = total([part[...] for part in dkv]).astype(BF)
    back = mm_rt(project[...], in_w[...])
    for i in range(GROUPS):
        slots[g ^ i] = back[i * tok : (i + 1) * tok, :].astype(BF)
    sums[0:1, :] = jnp.sum(back * hat_ref[...].astype(F32), axis=0, keepdims=True)
    sums[1:2, :] = jnp.sum(back, axis=0, keepdims=True)
    sums[2:3, : 3 * cols] = jnp.sum(project[...].astype(F32), axis=0, keepdims=True)
    d_in[...] = mm_lt(h_ref[...], project[...]).astype(BF)


def project_back(g, k, dq, dkv, h, hat, in_w):
    mine, width = h.shape
    cols = dq.shape[1]
    vmem = pl.BlockSpec(memory_space=pltpu.VMEM)
    return pl.pallas_call(
        functools.partial(project_back_kernel, len(dkv)),
        grid_spec=pltpu.PrefetchScalarGridSpec(
            num_scalar_prefetch=1,
            in_specs=[vmem] * (len(dkv) + 4),
            out_specs=[vmem] * 3,
            scratch_shapes=[pltpu.VMEM((mine, 3 * cols), BF)],
        ),
        out_shape=[
            jax.ShapeDtypeStruct((GROUPS, mine // GROUPS, width), BF),
            jax.ShapeDtypeStruct((width, 3 * cols), BF),
            jax.ShapeDtypeStruct((8, width), F32),
        ],
        compiler_params=pltpu.CompilerParams(vmem_limit_bytes=16 * 2**20),
        cost_estimate=pl.CostEstimate(
            flops=12 * mine * width * cols, bytes_accessed=4 * mine * width, transcendentals=0
        ),
    )(jnp.stack([g, k]).astype(jnp.int32), dq, *dkv, *in_hbm(h, hat), in_w)


def shards(
    inputs,
    cotangent,
    first_gain,
    first_shift,
    input_weight,
    query_bias,
    value_bias,
    output_weight,
    output_bias,
    second_gain,
    second_shift,
    expand_weight,
    expand_bias,
    contract_weight,
    contract_bias,
):
    tok, width = inputs.shape[1:]
    ks, zs = lax.axis_size("core"), lax.axis_size("fsdp")
    g, k, z = lax.axis_index("grp"), lax.axis_index("core"), lax.axis_index("fsdp")
    rows_z = width // zs
    heads_here = HEADS // GROUPS
    head = width // HEADS
    cols = width // GROUPS
    ff = expand_weight.shape[1]
    ff_z = ff // zs
    ff_g = ff_z // GROUPS
    mine = GROUPS * tok
    scale = head ** (-0.5)

    x_own = inputs[0]
    slope_own = cotangent[0]

    x_rows = gather_flips(x_own, "grp")
    in_cut = cut_weight(input_weight, 3, g, k, ks)
    in_pieces = gather_flips(in_cut, "fsdp")
    x_more = [[send(b, "core", j) for b in x_rows] for j in range(1, ks)]

    smalls = jnp.concatenate(
        [
            first_gain,
            first_shift,
            query_bias,
            value_bias,
            output_bias,
            second_gain,
            second_shift,
            contract_bias,
            expand_bias,
        ]
    )
    smalls_all = in_order(gather_flips(smalls, "fsdp"), z).astype(F32)

    def small(i):
        return smalls_all[:, i * rows_z : (i + 1) * rows_z].reshape(width)

    gain_one, shift_one, q_bias, v_bias, o_bias, gain_two, shift_two, c_bias = [
        small(i) for i in range(8)
    ]
    e_bias = pick(
        smalls_all[:, 8 * rows_z :].reshape(zs, GROUPS, ff_g).transpose(1, 0, 2), g
    ).reshape(zs * ff_g)
    q_bias = pick(q_bias.reshape(GROUPS, cols), g)
    v_bias = pick(v_bias.reshape(GROUPS, cols), g)

    rest = cut_rest(contract_weight, expand_weight, output_weight, zs, g, k, ks)
    rest, in_pieces = lax.optimization_barrier((rest, in_pieces))

    in_half = in_order(in_pieces, z)
    in_w = jnp.stack(in_order(gather_flips(in_half, "core"), k), axis=1).reshape(width, 3 * cols)

    split = width + zs * ff_g
    out_pieces = gather_flips(rest[:, split:], "fsdp")
    rest_pieces = gather_flips(rest[:, :split], "fsdp")
    slope_late, x_rows = lax.optimization_barrier((slope_own, x_rows))
    slope_rows = gather_flips(slope_late, "grp")

    in_w, slope_rows = lax.optimization_barrier((in_w, slope_rows))
    slots, qs, keys, values, att_full, lse, h1, hat_one = attend(
        g,
        k,
        ks,
        head,
        x_rows + [b for bs in x_more for b in bs],
        in_w,
        gain_one[None],
        shift_one[None],
        q_bias[None],
        v_bias[None],
    )
    out_pieces, lse = lax.optimization_barrier((out_pieces, lse))

    def whole(pieces):
        half = in_order(pieces, z)
        return jnp.stack(in_order(gather_flips(half, "core"), k), axis=1).reshape(width, -1)

    out_w = whole(out_pieces).reshape(GROUPS, cols, width)
    out_w = jnp.concatenate([pick(out_w, g ^ i) for i in range(GROUPS)])
    att = jnp.concatenate(swap_flips([slots[i] for i in range(GROUPS)], "grp"), axis=1)
    x_f = x_own.astype(F32)
    middle = x_f + mm(att, out_w) + o_bias
    hat_two, rate_two = norm_stats(middle)
    h2 = (hat_two * gain_two + shift_two).astype(BF)
    h2_rows = gather_flips(h2, "grp")
    middle, rest_pieces = lax.optimization_barrier((middle, rest_pieces))
    rest = whole(rest_pieces)

    act, slope_inner, sh2_part, out_part, d_exp_b = hidden_part(
        h2_rows, slope_rows, rest, e_bias[None]
    )
    sh2 = swap_flips([sh2_part[i] for i in range(GROUPS)], "grp")
    d_hidden = hidden_grads(h2_rows, slope_rows, slope_inner, act)
    sh2, d_hidden = lax.optimization_barrier((sh2, d_hidden))
    sh2 = total(sh2)
    d_hidden = lax.psum_scatter(d_hidden, ("fsdp", "core"), scatter_dimension=0, tiled=True)

    slope_f = slope_own.astype(F32)
    d_gain_two = jnp.sum(sh2 * hat_two, axis=0)
    d_shift_two = jnp.sum(sh2, axis=0)
    slope_middle = slope_f + norm_back(sh2, gain_two, hat_two, rate_two)
    slope_branch = slope_middle.astype(BF)
    slope_att = mm_rt(slope_branch, out_w).astype(BF)
    datt = swap_flips([slope_att[:, i * cols : (i + 1) * cols] for i in range(GROUPS)], "grp")

    datt, slope_late = lax.optimization_barrier((datt, slope_branch))
    d_out = mm_lt(att, slope_late).astype(BF).reshape(GROUPS, cols, width)
    d_out = in_order([d_out[i] for i in range(GROUPS)], g)
    d_out = d_out.reshape(zs, GROUPS, rows_z // GROUPS, width)
    pieces = [lax.dynamic_index_in_dim(d_out, g ^ i, axis=1, keepdims=False) for i in range(GROUPS)]
    datt, pieces = lax.optimization_barrier((datt, pieces))
    d_out = swap_flips(pieces, "grp")

    dq, dkv = attend_back(g, k, ks, head, datt, qs, keys, values, att_full, lse)
    dkv = swap_flips([dkv[j] for j in range(ks)], "core")
    sh1_part, d_in, sums = project_back(g, k, dq, dkv, h1, hat_one, in_w)
    sh1 = total(swap_flips([sh1_part[i] for i in range(GROUPS)], "grp"))
    hat_own, rate_own = norm_stats(x_f)
    delta_inputs = (slope_middle + norm_back(sh1, gain_one, hat_own, rate_own)).astype(BF)[None]

    def at_group(vec, lead):
        parts = vec.reshape(lead, 1, -1)
        spot = (jnp.arange(GROUPS) == g).astype(F32)[None, :, None]
        return (parts * spot).reshape(-1)

    vectors = [
        sums[0],
        sums[1],
        at_group(sums[2, :cols], 1),
        at_group(sums[2, 2 * cols : 3 * cols], 1),
        jnp.sum(slope_branch.astype(F32), axis=0),
        d_gain_two,
        d_shift_two,
        jnp.sum(slope_f, axis=0),
    ]
    packed = jnp.concatenate(
        [v.reshape(zs, rows_z) for v in vectors]
        + [at_group(d_exp_b, zs).reshape(zs, ff_z)],
        axis=1,
    )
    d_out = total(d_out).astype(BF).reshape(zs, ks, -1, width)
    third = d_out.shape[2] // 3
    tail = d_out[..., 3 * cols :]
    tail = [tail[:, :, i * third : (i + 1) * third] for i in range(3)]
    d_out = jnp.concatenate([d_out[..., : 3 * cols], jnp.concatenate(tail, axis=3)], axis=2)
    count = packed.shape[1]
    extra = -(-count // (3 * cols * ks))
    packed = jnp.pad(packed, ((0, 0), (0, extra * ks * 3 * cols - count)))
    d_in = d_in.reshape(zs, ks, rows_z // ks, 3 * cols)
    packed = packed.astype(BF).reshape(zs, ks, extra, 3 * cols)
    d_in = jnp.concatenate([d_in, packed, d_out], axis=2)
    pieces = [lax.dynamic_index_in_dim(d_in, k ^ j, axis=1, keepdims=False) for j in range(ks)]
    d_in = total(swap_flips(pieces, "core")).astype(BF)
    out_late, d_in = lax.optimization_barrier((out_part, d_in))
    out_sum = total(swap_flips([out_late[i] for i in range(GROUPS)], "grp"))
    outputs = (middle + out_sum + c_bias).astype(BF)[None]
    d_in = total(swap_flips([pick(d_in, z ^ i) for i in range(zs)], "fsdp")).astype(BF)
    d_in = in_order(gather_flips(d_in, "grp"), g)
    d_in = in_order(gather_flips(d_in, "core"), k)
    own = rows_z // ks
    packed = jnp.sum(d_in[:, :, own : own + extra].astype(F32), axis=1).reshape(-1)
    d_out = d_in[:, :, own + extra :].transpose(1, 0, 2, 3)
    tail = d_out[:, :, 3 * third :].reshape(GROUPS, ks, third, 3, width - 3 * cols)
    d_out_w = (
        jnp.concatenate(
            [
                d_out[:, :, : 3 * third],
                jnp.concatenate([tail[:, :, :, i] for i in range(3)], axis=2),
            ],
            axis=3,
        )
        .reshape(rows_z, width)
        .astype(F32)
    )
    d_in = d_in[:, :, :own].transpose(1, 0, 2, 3).reshape(GROUPS, rows_z, 3 * cols)
    d_in_w = weave(d_in, 3)
    d_hidden = in_order(gather_flips(d_hidden, "grp"), g)
    d_hidden = jnp.stack(in_order(gather_flips(d_hidden, "core"), k), axis=1)
    d_exp_w, d_con_w = unfold(d_hidden.reshape(GROUPS, rows_z, -1), zs)
    d_con_w = d_con_w.reshape(ff_z, width)

    def vec(i):
        return packed[i * rows_z : (i + 1) * rows_z]

    return (
        outputs,
        delta_inputs,
        vec(0),
        vec(1),
        d_in_w,
        vec(2),
        vec(3),
        d_out_w,
        vec(4),
        vec(5),
        vec(6),
        d_exp_w,
        packed[8 * rows_z : 8 * rows_z + ff_z],
        d_con_w,
        vec(7),
    )


def solution(mesh):
    ctx, zs = mesh.shape["ctx"], mesh.shape["fsdp"]
    axes = ("grp", "core", "fsdp")
    split = Mesh(mesh.devices.reshape(GROUPS, ctx // GROUPS, zs), axes)
    row, vec, mat = P("fsdp", ("grp", "core"), None), P("fsdp"), P("fsdp", None)
    placed = (row, row, vec, vec, mat, vec, vec, mat, vec, vec, vec, mat, vec, mat, vec)
    return jax.shard_map(
        shards,
        mesh=split,
        in_specs=placed,
        out_specs=placed,
        check_vma=False,
    )
```

```python
import functools

import jax
import jax.numpy as jnp
from jax import lax
from jax.experimental import pallas as pl
from jax.experimental.pallas import tpu as pltpu
from jax.sharding import Mesh, PartitionSpec as P

HEADS = 12
GROUPS = 4

NORM_EPS = 1e-05
MASK_FILL = -1e30
GELU_COEF = 0.7978845608028654
GELU_CUBE = 0.044715

SHORT = pl.CostEstimate(flops=1, bytes_accessed=1, transcendentals=0)

BF = jnp.bfloat16
F32 = jnp.float32


def in_hbm(*values):
    return [pltpu.with_memory_space_constraint(v, pltpu.HBM) for v in values]


def mm(left, right):
    return jnp.dot(left, right, preferred_element_type=F32)


def mm_lt(left, right):
    return lax.dot_general(left, right, (((0,), (0,)), ((), ())), preferred_element_type=F32)


def mm_rt(left, right):
    return lax.dot_general(left, right, (((1,), (1,)), ((), ())), preferred_element_type=F32)


def send(value, axis, flip):
    count = lax.axis_size(axis)
    return lax.ppermute(value, axis, [(s, s ^ flip) for s in range(count)])


def gather_flips(value, axis):
    return [value] + [send(value, axis, i) for i in range(1, lax.axis_size(axis))]


def swap_flips(pieces, axis):
    return [pieces[0]] + [send(p, axis, i) for i, p in enumerate(pieces) if i]


def pick(stacked, place):
    return lax.dynamic_index_in_dim(stacked, place, axis=0, keepdims=False)


def in_order(pieces, me):
    stacked = jnp.stack(pieces)
    return jnp.stack([pick(stacked, me ^ j) for j in range(len(pieces))])


def norm_stats(values):
    center = values - jnp.mean(values, axis=-1, keepdims=True)
    spread = jnp.mean(center * center, axis=-1, keepdims=True)
    rate = lax.rsqrt(spread + NORM_EPS)
    return center * rate, rate


def norm_back(slope, gain, hat, rate):
    scaled = slope * gain
    return rate * (
        scaled
        - jnp.mean(scaled, axis=-1, keepdims=True)
        - hat * jnp.mean(scaled * hat, axis=-1, keepdims=True)
    )


def total(parts):
    out = parts[0].astype(F32)
    for part in parts[1:]:
        out = out + part.astype(F32)
    return out


def cut_columns(source, cut, parts, i):
    wide = cut.shape[1] // parts
    for part in range(parts):
        low = (part * GROUPS + i) * wide
        cut[:, part * wide : (part + 1) * wide] = source[:, low : low + wide]


def cut_kernel(parts, place, source, cut):
    for i in range(GROUPS):

        @pl.when(place[0] == i)
        def _():
            cut_columns(source, cut, parts, i)


def cut_weight(weight, parts, g, k, ks):
    rows = weight.shape[0] // ks
    cols = weight.shape[1] // GROUPS
    if rows % 16 == 0:
        return pl.pallas_call(
            functools.partial(cut_kernel, parts),
            grid_spec=pltpu.PrefetchScalarGridSpec(
                num_scalar_prefetch=1,
                grid=(1,),
                in_specs=[pl.BlockSpec((rows, weight.shape[1]), lambda i, place: (place[1], 0))],
                out_specs=pl.BlockSpec((rows, cols), lambda i, place: (0, 0)),
            ),
            out_shape=jax.ShapeDtypeStruct((rows, cols), BF),
            compiler_params=pltpu.CompilerParams(vmem_limit_bytes=8 * 2**20),
        )(jnp.stack([g, k]).astype(jnp.int32), weight)
    half = pick(weight.reshape(ks, rows, -1), k)
    return lax.dynamic_index_in_dim(
        half.reshape(rows, parts, GROUPS, cols // parts), g, axis=2, keepdims=False
    ).reshape(rows, cols)


def cut_first_kernel(place, *refs):
    source, vectors, cut, held = refs[0], refs[1:-2], refs[-2], refs[-1]
    rows, wide = source.shape
    unit = vectors[0].shape[0]
    per = cut.shape[1] // unit
    held[...] = jnp.zeros_like(held)
    spot = 0
    for vector in vectors:
        row = vector[...].astype(F32).reshape(1, vector.shape[0])
        for part in range(vector.shape[0] // unit):
            col = spot % per * unit
            held[spot // per : spot // per + 1, col : col + unit] = row[
                :, part * unit : (part + 1) * unit
            ]
            spot += 1
    cut[rows:, :] = held[...].astype(BF)
    for i in range(GROUPS):

        @pl.when(place[0] == i)
        def _():
            cut_columns(source, cut.at[:rows, :], 3, i)


def cut_first(weight, vectors, g, k, ks):
    rows, cols = weight.shape[0] // ks, weight.shape[1] // GROUPS
    return pl.pallas_call(
        cut_first_kernel,
        grid_spec=pltpu.PrefetchScalarGridSpec(
            num_scalar_prefetch=1,
            grid=(1,),
            in_specs=[pl.BlockSpec((rows, weight.shape[1]), lambda i, place: (place[1], 0))]
            + [pl.BlockSpec(v.shape, lambda i, place: (0,)) for v in vectors],
            out_specs=pl.BlockSpec((rows + 16, cols), lambda i, place: (0, 0)),
            scratch_shapes=[pltpu.VMEM((16, cols), F32)],
        ),
        out_shape=jax.ShapeDtypeStruct((rows + 16, cols), BF),
        compiler_params=pltpu.CompilerParams(vmem_limit_bytes=8 * 2**20),
    )(jnp.stack([g, k]).astype(jnp.int32), weight, *vectors)


def table_kernel(unit, place, *refs):
    pieces, out, held = refs[:-2], refs[-2], refs[-1]
    zs = len(pieces)
    per = held.shape[2] // unit
    cols = out.shape[1] // GROUPS
    for i, piece in enumerate(pieces):
        held[place[1] ^ i] = piece[...].astype(F32)

    def unpack(row, slot):
        for zz in range(zs):
            col = slot % per * unit
            out[row : row + 1, zz * unit : (zz + 1) * unit] = held[
                zz, slot // per : slot // per + 1, col : col + unit
            ]

    out[...] = jnp.zeros_like(out)
    for slot in range(8):
        unpack(slot + 8 if slot in (2, 3) else slot, slot)
    for i in range(GROUPS):

        @pl.when(place[0] == i)
        def _():
            unpack(8, 8 + i)
            out[2:4, :cols] = out[10:12, i * cols : (i + 1) * cols]


def vector_table(pieces, unit, width, g, z):
    rows, cols = pieces[0].shape
    return pl.pallas_call(
        functools.partial(table_kernel, unit),
        grid_spec=pltpu.PrefetchScalarGridSpec(
            num_scalar_prefetch=1,
            grid=(1,),
            in_specs=[pl.BlockSpec((16, cols), lambda i, place: (rows // 16 - 1, 0))] * len(pieces),
            out_specs=pl.BlockSpec((16, width), lambda i, place: (0, 0)),
            scratch_shapes=[pltpu.VMEM((len(pieces), 16, cols), F32)],
        ),
        out_shape=jax.ShapeDtypeStruct((16, width), F32),
        compiler_params=pltpu.CompilerParams(vmem_limit_bytes=8 * 2**20),
    )(jnp.stack([g, z]).astype(jnp.int32), *pieces)


def pack_kernel(zs, stride, unit, place, sums, out_bias, gain, shift, con_bias, exp_bias, out):
    per = out.shape[1] // unit
    cols = out.shape[1] // 3

    def put(zz, slot, value):
        row, col = zz * stride + slot // per, slot % per * unit
        out[row : row + 1, col : col + unit] = value

    out[...] = jnp.zeros_like(out)
    whole = [(0, sums, 0), (1, sums, 1), (4, out_bias, 0), (5, gain, 0), (6, shift, 0), (7, con_bias, 0)]
    for slot, source, row in whole:
        for zz in range(zs):
            put(zz, slot, source[row : row + 1, zz * unit : (zz + 1) * unit])
    for i in range(GROUPS):

        @pl.when(place[0] == i)
        def _():
            for zz in range(zs):
                put(zz, 8 + i, exp_bias[:, zz * unit : (zz + 1) * unit])
            for part in range(cols // unit):
                zz = i * cols // unit + part
                low = part * unit
                put(zz, 2, sums[2:3, low : low + unit])
                put(zz, 3, sums[2:3, 2 * cols + low : 2 * cols + low + unit])


def pack_vectors(g, zs, stride, unit, sums, *vectors):
    wide = 3 * (vectors[0].shape[1] // GROUPS)
    vmem = pl.BlockSpec(memory_space=pltpu.VMEM)
    return pl.pallas_call(
        functools.partial(pack_kernel, zs, stride, unit),
        grid_spec=pltpu.PrefetchScalarGridSpec(
            num_scalar_prefetch=1, in_specs=[vmem] * (1 + len(vectors)), out_specs=vmem
        ),
        out_shape=jax.ShapeDtypeStruct((zs * stride, wide), F32),
        compiler_params=pltpu.CompilerParams(vmem_limit_bytes=8 * 2**20),
    )(jnp.stack([g]).astype(jnp.int32), sums, *vectors)


def cut_rest_kernel(parts, place, con_ref, exp_ref, out_ref, cut):
    width = con_ref.shape[1]
    wide = exp_ref.shape[1] // GROUPS
    cut[:, :width] = con_ref[...]
    cut[:, width + wide :] = out_ref[...]
    for i in range(GROUPS):

        @pl.when(place[0] == i)
        def _():
            cut_columns(exp_ref, cut.at[:, width : width + wide], parts, i)


def cut_rest(con_w, exp_w, out_w, parts, g, k, ks):
    width = out_w.shape[1]
    rows, ff_rows = out_w.shape[0] // ks, con_w.shape[0] // (GROUPS * ks)
    wide = exp_w.shape[1] // GROUPS
    if rows % 16 == 0 and rows == ff_rows:
        by_k = lambda i, place: (place[1], 0)
        return pl.pallas_call(
            functools.partial(cut_rest_kernel, parts),
            grid_spec=pltpu.PrefetchScalarGridSpec(
                num_scalar_prefetch=1,
                grid=(1,),
                in_specs=[
                    pl.BlockSpec((rows, width), lambda i, place: (place[0] * ks + place[1], 0)),
                    pl.BlockSpec((rows, exp_w.shape[1]), by_k),
                    pl.BlockSpec((rows, width), by_k),
                ],
                out_specs=pl.BlockSpec((rows, 2 * width + wide), lambda i, place: (0, 0)),
            ),
            out_shape=jax.ShapeDtypeStruct((rows, 2 * width + wide), BF),
            compiler_params=pltpu.CompilerParams(vmem_limit_bytes=8 * 2**20),
        )(jnp.stack([g, k]).astype(jnp.int32), con_w, exp_w, out_w)
    return jnp.concatenate(
        [
            pick(con_w.reshape(GROUPS * ks, ff_rows, width), g * ks + k),
            cut_weight(exp_w, parts, g, k, ks),
            pick(out_w.reshape(ks, rows, width), k),
        ],
        axis=1,
    )


def weave_kernel(parts, pieces, out):
    wide = pieces.shape[2] // parts
    for i in range(GROUPS):
        for part in range(parts):
            low = (part * GROUPS + i) * wide
            out[:, low : low + wide] = pieces[i, :, part * wide : (part + 1) * wide].astype(F32)


def weave(pieces, parts):
    rows, cols = pieces.shape[1], pieces.shape[2]
    step = 32
    return pl.pallas_call(
        functools.partial(weave_kernel, parts),
        grid=(rows // step,),
        in_specs=[pl.BlockSpec((GROUPS, step, cols), lambda i: (0, i, 0))],
        out_specs=pl.BlockSpec((step, GROUPS * cols), lambda i: (i, 0)),
        out_shape=jax.ShapeDtypeStruct((rows, GROUPS * cols), F32),
        compiler_params=pltpu.CompilerParams(vmem_limit_bytes=16 * 2**20),
    )(pieces)


def unfold_kernel(parts, pieces, exp_out, con_out):
    wide = con_out.shape[2]
    part_wide = wide // parts
    for i in range(GROUPS):
        con_out[i] = pieces[i, :, wide:].astype(F32)
        for part in range(parts):
            low = (part * GROUPS + i) * part_wide
            exp_out[:, low : low + part_wide] = pieces[
                i, :, part * part_wide : (part + 1) * part_wide
            ].astype(F32)


def unfold(pieces, parts):
    rows, wide = pieces.shape[1], pieces.shape[2] // 2
    step = 32
    return pl.pallas_call(
        functools.partial(unfold_kernel, parts),
        grid=(rows // step,),
        in_specs=[pl.BlockSpec((GROUPS, step, 2 * wide), lambda i: (0, i, 0))],
        out_specs=[
            pl.BlockSpec((step, GROUPS * wide), lambda i: (i, 0)),
            pl.BlockSpec((GROUPS, step, wide), lambda i: (0, i, 0)),
        ],
        out_shape=[
            jax.ShapeDtypeStruct((rows, GROUPS * wide), F32),
            jax.ShapeDtypeStruct((GROUPS, rows, wide), F32),
        ],
        compiler_params=pltpu.CompilerParams(vmem_limit_bytes=16 * 2**20),
    )(pieces)


def join_rows(pieces, joined):
    tok = pieces[0].shape[0]
    for i, piece in enumerate(pieces):
        joined[i * tok : (i + 1) * tok, :] = piece[...]


def hidden_kernel(*refs):
    h_rows, s_rows = refs[:GROUPS], refs[GROUPS : 2 * GROUPS]
    (exp_w, con_w, bias, act_ref, inner_ref, back_ref, out_ref, bias_ref) = refs[2 * GROUPS : -4]
    h_ref, s_ref, back_sum, out_sum = refs[-4:]
    step = pl.program_id(0)
    tok = h_rows[0].shape[0]

    @pl.when(step == 0)
    def _():
        join_rows(h_rows, h_ref)
        join_rows(s_rows, s_ref)

    inner = mm(h_ref[...], exp_w[...]) + bias[8:9, :]
    square = inner * inner
    tanh = jnp.tanh(GELU_COEF * (inner + GELU_CUBE * square * inner))
    half = 0.5 + 0.5 * tanh
    act = (inner * half).astype(BF)
    gelu_slope = half + (0.5 * GELU_COEF) * inner * (1.0 - tanh * tanh) * (
        1.0 + (3.0 * GELU_CUBE) * square
    )
    slope = (mm_rt(s_ref[...], con_w[...]) * gelu_slope).astype(BF)
    act_ref[...] = act
    inner_ref[...] = slope
    bias_ref[...] = jnp.sum(slope.astype(F32), axis=0, keepdims=True)
    back = mm_rt(slope, exp_w[...])
    out = mm(act, con_w[...])

    @pl.when(step == 0)
    def _():
        back_sum[...] = back
        out_sum[...] = out

    @pl.when(step > 0)
    def _():
        back_sum[...] += back
        out_sum[...] += out

    @pl.when(step == pl.num_programs(0) - 1)
    def _():
        for i in range(GROUPS):
            back_ref[i] = back_sum[i * tok : (i + 1) * tok, :].astype(BF)
            out_ref[i] = out_sum[i * tok : (i + 1) * tok, :].astype(BF)


def hidden_part(h_rows, s_rows, weights, table):
    tok, width = h_rows[0].shape
    hidden = weights.shape[1] - width
    rows = GROUPS * tok
    step = 256
    fixed = lambda i: (0, 0)
    cols = lambda i: (0, i)
    slots = pl.BlockSpec((GROUPS, tok, width), lambda i: (0, 0, 0))
    return pl.pallas_call(
        hidden_kernel,
        grid=(hidden // step,),
        in_specs=[pl.BlockSpec((tok, width), fixed)] * (2 * GROUPS)
        + [
            pl.BlockSpec((width, step), lambda i: (0, width // step + i)),
            pl.BlockSpec((step, width), lambda i: (i, 0)),
            pl.BlockSpec((16, step), cols),
        ],
        out_specs=[
            pl.BlockSpec((rows, step), cols),
            pl.BlockSpec((rows, step), cols),
            slots,
            slots,
            pl.BlockSpec((1, step), cols),
        ],
        out_shape=[
            jax.ShapeDtypeStruct((rows, hidden), BF),
            jax.ShapeDtypeStruct((rows, hidden), BF),
            jax.ShapeDtypeStruct((GROUPS, tok, width), BF),
            pltpu.HBM((GROUPS, tok, width), BF),
            jax.ShapeDtypeStruct((1, hidden), F32),
        ],
        scratch_shapes=[pltpu.VMEM((rows, width), BF)] * 2 + [pltpu.VMEM((rows, width), F32)] * 2,
        compiler_params=pltpu.CompilerParams(vmem_limit_bytes=24 * 2**20),
        cost_estimate=SHORT,
    )(*h_rows, *in_hbm(*s_rows, weights, weights), table)


def hidden_grad_kernel(*refs):
    h_rows, s_rows = refs[:GROUPS], refs[GROUPS : 2 * GROUPS]
    inner_ref, act_ref, out_ref, h_ref, s_ref = refs[2 * GROUPS :]
    wide, step = inner_ref.shape[1], act_ref.shape[1]

    @pl.when(pl.program_id(0) == 0)
    def _():
        join_rows(s_rows, s_ref)

    join_rows(h_rows, h_ref)
    out_ref[:, :wide] = mm_lt(h_ref[...], inner_ref[...]).astype(BF)
    out_ref[:, wide:] = mm_lt(act_ref[...], s_ref[...]).astype(BF)


def hidden_grads(h_rows, s_rows, slope_inner, act):
    tok, width = h_rows[0].shape
    rows, hidden = act.shape
    step = 256
    cols = lambda i: (0, i)
    fixed = lambda i: (0, 0)
    return pl.pallas_call(
        hidden_grad_kernel,
        grid=(width // step,),
        in_specs=[pl.BlockSpec((tok, step), cols)] * GROUPS
        + [pl.BlockSpec((tok, width), fixed)] * GROUPS
        + [pl.BlockSpec((rows, hidden), fixed), pl.BlockSpec((rows, step), cols)],
        out_specs=pl.BlockSpec((step, hidden + width), lambda i: (i, 0)),
        out_shape=jax.ShapeDtypeStruct((width, hidden + width), BF),
        scratch_shapes=[pltpu.VMEM((rows, step), BF), pltpu.VMEM((rows, width), BF)],
        compiler_params=pltpu.CompilerParams(vmem_limit_bytes=16 * 2**20),
        cost_estimate=SHORT,
    )(*h_rows, *in_hbm(*s_rows), slope_inner, act)


def visible(k, tok, keys):
    row = lax.broadcasted_iota(jnp.int32, (tok, keys), 0)
    col = lax.broadcasted_iota(jnp.int32, (tok, keys), 1)
    return col <= k * tok + row


def masked_scores(query, keys, seen):
    scores = mm_rt(query, keys)
    near = keys.shape[0] - seen.shape[1]
    last = jnp.where(seen, scores[:, near:], MASK_FILL)
    return last if near == 0 else jnp.concatenate([scores[:, :near], last], axis=1)


def attend_kernel(ks, head, place, *refs):
    pieces = refs[: GROUPS * ks]
    in_w, table = refs[GROUPS * ks : GROUPS * ks + 2]
    slots, q_out, k_out, v_out, att_out, lse_out, h_out, hat_out, h_all = refs[GROUPS * ks + 2 :]
    g, k = place[0], place[1]
    tok, width = pieces[0].shape
    cols = q_out.shape[1]
    gain, shift = table[0:1, :], table[1:2, :]
    for j in range(ks):
        for i in range(GROUPS):
            hat, _ = norm_stats(pieces[j * GROUPS + i][...].astype(F32))
            normed = (hat * gain + shift).astype(BF)
            spot = pl.multiple_of(((g ^ i) * ks + (k ^ j)) * tok, tok)
            h_all[pl.ds(spot, tok), :] = normed
            if j == 0:
                spot = pl.multiple_of((g ^ i) * tok, tok)
                h_out[pl.ds(spot, tok), :] = normed
                hat_out[pl.ds(spot, tok), :] = hat.astype(BF)
    q_out[...] = (mm(h_out[...], in_w[:, :cols]) + table[2:3, :cols]).astype(BF)
    kv = mm(h_all[...], in_w[:, cols:])
    k_out[...] = kv[:, :cols].astype(BF)
    v_out[...] = (kv[:, cols:] + table[3:4, :cols]).astype(BF)
    seen = visible(k, tok, ks * tok)
    for h in range(cols // head):
        low, high = h * head, (h + 1) * head
        for i in range(GROUPS):
            rows = slice(i * tok, (i + 1) * tok)
            span = (i + 1) * ks * tok
            query = (q_out[rows, low:high].astype(F32) * head**-0.5).astype(BF)
            scores = masked_scores(query, k_out[:span, low:high], seen)
            peak = jnp.max(scores, axis=-1, keepdims=True)
            weights = jnp.exp(scores - peak)
            mass = jnp.sum(weights, axis=-1, keepdims=True)
            lse_out[rows, h : h + 1] = peak + jnp.log(mass)
            att = mm(weights.astype(BF), v_out[:span, low:high]) / mass
            att_out[rows, low:high] = att
    for i in range(GROUPS):
        slots[g ^ i] = att_out[i * tok : (i + 1) * tok, :].astype(BF)


def attend(g, k, ks, head, pieces, in_w, table):
    tok, width = pieces[0].shape
    cols = in_w.shape[1] // 3
    mine, rows = GROUPS * tok, GROUPS * ks * tok
    vmem = pl.BlockSpec(memory_space=pltpu.VMEM)
    shapes = [
        ((GROUPS, tok, cols), BF),
        ((mine, cols), BF),
        ((rows, cols), BF),
        ((rows, cols), BF),
        ((mine, cols), F32),
        ((mine, 8), F32),
        ((mine, width), BF),
        ((mine, width), BF),
    ]
    return pl.pallas_call(
        functools.partial(attend_kernel, ks, head),
        grid_spec=pltpu.PrefetchScalarGridSpec(
            num_scalar_prefetch=1,
            in_specs=[vmem] * (len(pieces) + 2),
            out_specs=[vmem] * len(shapes),
            scratch_shapes=[pltpu.VMEM((rows, width), BF)],
        ),
        out_shape=[jax.ShapeDtypeStruct(*shapes[0])] + [pltpu.HBM(s, t) for s, t in shapes[1:]],
        compiler_params=pltpu.CompilerParams(vmem_limit_bytes=(16 if ks == 2 else 48) * 2**20),
        cost_estimate=SHORT,
    )(jnp.stack([g, k]).astype(jnp.int32), *pieces, in_w, table)


def attend_back_kernel(ks, head, place, *refs):
    slopes = refs[:GROUPS]
    q_ref, k_ref, v_ref, att_ref, lse_ref, dq_out, dkv_out, dk_sum, dv_sum = refs[GROUPS:]
    g, k = place[0], place[1]
    tok, cols = slopes[0].shape
    d_rows = dq_out
    for i in range(GROUPS):
        d_rows[pl.ds(pl.multiple_of((g ^ i) * tok, tok), tok), :] = slopes[i][...]
    seen = visible(k, tok, ks * tok)
    for i in reversed(range(GROUPS)):
        rows = slice(i * tok, (i + 1) * tok)
        span = (i + 1) * ks * tok
        slope_all = d_rows[rows, :]
        parts = []
        for h in range(cols // head):
            low, high = h * head, (h + 1) * head
            query = (q_ref[rows, low:high].astype(F32) * head**-0.5).astype(BF)
            keys = k_ref[:span, low:high]
            slope = slope_all[:, low:high]
            scores = masked_scores(query, keys, seen)
            chances = jnp.exp(scores - lse_ref[rows, h : h + 1])
            diag = jnp.sum(slope.astype(F32) * att_ref[rows, low:high], axis=-1, keepdims=True)
            slope_chances = mm_rt(slope, v_ref[:span, low:high])
            slope_scores = (chances * (slope_chances - diag)).astype(BF)
            parts.append(mm(slope_scores, keys) * head**-0.5)
            dk = mm_lt(slope_scores, query)
            dv = mm_lt(chances.astype(BF), slope)
            if i == GROUPS - 1:
                dk_sum[:, low:high] = dk
                dv_sum[:, low:high] = dv
            else:
                dk_sum[:span, low:high] += dk
                dv_sum[:span, low:high] += dv
        dq_out[rows, :] = jnp.concatenate(parts, axis=1).astype(BF)
    for i in range(GROUPS):
        for j in range(ks):
            spot = slice((i * ks + j) * tok, (i * ks + j + 1) * tok)
            dkv_out[k ^ j, i * tok : (i + 1) * tok, :] = jnp.concatenate(
                [dk_sum[spot, :], dv_sum[spot, :]], axis=1
            ).astype(BF)


def attend_back(g, k, ks, head, slopes, q, keys, values, att, lse):
    tok, cols = slopes[0].shape
    mine, rows = GROUPS * tok, GROUPS * ks * tok
    vmem = pl.BlockSpec(memory_space=pltpu.VMEM)
    return pl.pallas_call(
        functools.partial(attend_back_kernel, ks, head),
        grid_spec=pltpu.PrefetchScalarGridSpec(
            num_scalar_prefetch=1,
            in_specs=[vmem] * (len(slopes) + 5),
            out_specs=[vmem] * 2,
            scratch_shapes=[pltpu.VMEM((rows, cols), F32)] * 2,
        ),
        out_shape=[
            jax.ShapeDtypeStruct((mine, cols), BF),
            jax.ShapeDtypeStruct((ks, mine, 2 * cols), BF),
        ],
        compiler_params=pltpu.CompilerParams(vmem_limit_bytes=(16 if ks == 2 else 48) * 2**20),
        cost_estimate=SHORT,
    )(jnp.stack([g, k]).astype(jnp.int32), *slopes, *in_hbm(q, keys, values, att, lse))


def project_back_kernel(ks, place, *refs):
    dq, dkv = refs[0], refs[1 : 1 + ks]
    h_ref, hat_ref, in_w, slots, d_in, sums, project = refs[1 + ks :]
    g = place[0]
    tok = slots.shape[1]
    cols = dq.shape[1]
    project[:, :cols] = dq[...]
    project[:, cols:] = total([part[...] for part in dkv]).astype(BF)
    back = mm_rt(project[...], in_w[...])
    for i in range(GROUPS):
        slots[g ^ i] = back[i * tok : (i + 1) * tok, :].astype(BF)
    sums[0:1, :] = jnp.sum(back * hat_ref[...].astype(F32), axis=0, keepdims=True)
    sums[1:2, :] = jnp.sum(back, axis=0, keepdims=True)
    sums[2:3, : 3 * cols] = jnp.sum(project[...].astype(F32), axis=0, keepdims=True)
    d_in[...] = mm_lt(h_ref[...], project[...]).astype(BF)


def project_back(g, k, dq, dkv, h, hat, in_w):
    mine, width = h.shape
    cols = dq.shape[1]
    vmem = pl.BlockSpec(memory_space=pltpu.VMEM)
    return pl.pallas_call(
        functools.partial(project_back_kernel, len(dkv)),
        grid_spec=pltpu.PrefetchScalarGridSpec(
            num_scalar_prefetch=1,
            in_specs=[vmem] * (len(dkv) + 4),
            out_specs=[vmem] * 3,
            scratch_shapes=[pltpu.VMEM((mine, 3 * cols), BF)],
        ),
        out_shape=[
            jax.ShapeDtypeStruct((GROUPS, mine // GROUPS, width), BF),
            jax.ShapeDtypeStruct((width, 3 * cols), BF),
            jax.ShapeDtypeStruct((8, width), F32),
        ],
        compiler_params=pltpu.CompilerParams(vmem_limit_bytes=16 * 2**20),
        cost_estimate=SHORT,
    )(jnp.stack([g, k]).astype(jnp.int32), dq, *dkv, *in_hbm(h, hat), in_w)


def shards(
    inputs,
    cotangent,
    first_gain,
    first_shift,
    input_weight,
    query_bias,
    value_bias,
    output_weight,
    output_bias,
    second_gain,
    second_shift,
    expand_weight,
    expand_bias,
    contract_weight,
    contract_bias,
):
    tok, width = inputs.shape[1:]
    ks, zs = lax.axis_size("core"), lax.axis_size("fsdp")
    g, k, z = lax.axis_index("grp"), lax.axis_index("core"), lax.axis_index("fsdp")
    rows_z = width // zs
    heads_here = HEADS // GROUPS
    head = width // HEADS
    cols = width // GROUPS
    ff = expand_weight.shape[1]
    ff_z = ff // zs
    ff_g = ff_z // GROUPS
    mine = GROUPS * tok
    scale = head ** (-0.5)

    x_own = inputs[0]
    slope_own = cotangent[0]

    x_rows = gather_flips(x_own, "grp")

    smalls = [first_gain, first_shift, query_bias, value_bias, output_bias]
    smalls += [second_gain, second_shift, contract_bias, expand_bias]
    own = rows_z // ks
    aligned = own % 16 == 0
    if aligned:
        in_pieces = gather_flips(cut_first(input_weight, smalls, g, k, ks), "fsdp")
    else:
        in_pieces = gather_flips(cut_weight(input_weight, 3, g, k, ks), "fsdp")
    in_pieces, x_rows = lax.optimization_barrier((in_pieces, x_rows))
    x_more = [[send(b, "core", j) for b in x_rows] for j in range(1, ks)]
    if aligned:
        table = vector_table(in_pieces, rows_z, width, g, z)
    else:
        got = in_order(gather_flips(jnp.concatenate(smalls), "fsdp"), z).astype(F32)
        vectors = [got[:, i * rows_z : (i + 1) * rows_z].reshape(width) for i in range(8)]
        for i in (2, 3):
            vectors[i] = jnp.tile(pick(vectors[i].reshape(GROUPS, cols), g), GROUPS)
        got = got[:, 8 * rows_z :].reshape(zs, GROUPS, ff_g)
        vectors.append(lax.dynamic_index_in_dim(got, g, axis=1, keepdims=False).reshape(width))
        table = jnp.pad(jnp.stack(vectors), ((0, 7), (0, 0)))
    o_bias, gain_two, shift_two, c_bias = [table[i : i + 1] for i in range(4, 8)]

    con_raw, exp_raw, out_raw, slope_late, in_pieces = lax.optimization_barrier(
        (contract_weight, expand_weight, output_weight, slope_own, in_pieces)
    )
    in_half = in_order([p[:own] for p in in_pieces], z)
    in_w = jnp.stack(in_order(gather_flips(in_half, "core"), k), axis=1).reshape(width, 3 * cols)
    rest = cut_rest(con_raw, exp_raw, out_raw, zs, g, k, ks)
    split = width + zs * ff_g
    out_pieces = gather_flips(rest[:, split:], "fsdp")
    rest = lax.all_gather(rest[:, :split], ("fsdp", "core"), axis=0, tiled=True)

    slope_rows = gather_flips(slope_late, "grp")
    out_pieces, slope_rows, x_more = lax.optimization_barrier((out_pieces, slope_rows, x_more))
    half = in_order(out_pieces, z)
    out_w = jnp.stack(in_order(gather_flips(half, "core"), k), axis=1)
    out_w = out_w.reshape(GROUPS, cols, width)
    out_w = jnp.concatenate([pick(out_w, g ^ i) for i in range(GROUPS)])
    in_w, out_w = lax.optimization_barrier((in_w, out_w))
    slots, qs, keys, values, att_full, lse, h1, hat_one = attend(
        g, k, ks, head, x_rows + [b for bs in x_more for b in bs], in_w, table
    )
    att = jnp.concatenate(swap_flips([slots[i] for i in range(GROUPS)], "grp"), axis=1)
    x_f = x_own.astype(F32)
    middle = x_f + mm(att, out_w) + o_bias
    hat_two, rate_two = norm_stats(middle)
    h2 = (hat_two * gain_two + shift_two).astype(BF)
    h2_rows = gather_flips(h2, "grp")

    act, slope_inner, sh2_part, out_part, d_exp_b = hidden_part(
        h2_rows, slope_rows, rest, table
    )
    sh2 = swap_flips([sh2_part[i] for i in range(GROUPS)], "grp")
    d_hidden = hidden_grads(h2_rows, slope_rows, slope_inner, act)
    sh2, d_hidden = lax.optimization_barrier((sh2, d_hidden))
    sh2 = total(sh2)
    d_hidden = lax.psum_scatter(d_hidden, ("fsdp", "core"), scatter_dimension=0, tiled=True)

    slope_f = slope_own.astype(F32)
    d_gain_two = jnp.sum(sh2 * hat_two, axis=0, keepdims=True)
    d_shift_two = jnp.sum(sh2, axis=0, keepdims=True)
    slope_middle = slope_f + norm_back(sh2, gain_two, hat_two, rate_two)
    slope_branch = slope_middle.astype(BF)
    slope_att = mm_rt(slope_branch, out_w).astype(BF)
    datt = swap_flips([slope_att[:, i * cols : (i + 1) * cols] for i in range(GROUPS)], "grp")

    datt, slope_late = lax.optimization_barrier((datt, slope_branch))
    d_out = mm_lt(att, slope_late).astype(BF).reshape(GROUPS, cols, width)
    d_out = in_order([d_out[i] for i in range(GROUPS)], g)
    d_out = d_out.reshape(zs, GROUPS, rows_z // GROUPS, width)
    pieces = [lax.dynamic_index_in_dim(d_out, g ^ i, axis=1, keepdims=False) for i in range(GROUPS)]
    datt, pieces = lax.optimization_barrier((datt, pieces))
    d_out = swap_flips(pieces, "grp")

    dq, dkv = attend_back(g, k, ks, head, datt, qs, keys, values, att_full, lse)
    dkv = swap_flips([dkv[j] for j in range(ks)], "core")
    sh1_part, d_in, sums = project_back(g, k, dq, dkv, h1, hat_one, in_w)
    sh1 = swap_flips([sh1_part[i] for i in range(GROUPS)], "grp")
    sh1, out_late = lax.optimization_barrier((sh1, out_part))
    sh1 = total(sh1)
    out_sum = swap_flips([out_late[i] for i in range(GROUPS)], "grp")
    hat_own, rate_own = norm_stats(x_f)
    delta_inputs = (slope_middle + norm_back(sh1, table[0:1], hat_own, rate_own)).astype(BF)[None]

    extra = -(-(12 * rows_z) // (3 * cols * ks))
    packed = pack_vectors(
        g,
        zs,
        extra * ks,
        rows_z,
        sums,
        jnp.sum(slope_branch.astype(F32), axis=0, keepdims=True),
        d_gain_two,
        d_shift_two,
        jnp.sum(slope_f, axis=0, keepdims=True),
        d_exp_b,
    )
    d_out = total(d_out).astype(BF).reshape(zs, ks, -1, width)
    third = d_out.shape[2] // 3
    tail = d_out[..., 3 * cols :]
    tail = [tail[:, :, i * third : (i + 1) * third] for i in range(3)]
    d_out = jnp.concatenate([d_out[..., : 3 * cols], jnp.concatenate(tail, axis=3)], axis=2)
    d_in = jnp.concatenate(
        [
            d_in.reshape(zs, ks, own, 3 * cols),
            packed.astype(BF).reshape(zs, ks, extra, 3 * cols),
            d_out,
        ],
        axis=2,
    )
    pieces = [lax.dynamic_index_in_dim(d_in, k ^ j, axis=1, keepdims=False) for j in range(ks)]
    d_in = total(swap_flips(pieces, "core")).astype(BF)
    d_in = swap_flips([pick(d_in, z ^ i) for i in range(zs)], "fsdp")
    d_hidden = gather_flips(d_hidden, "grp")
    d_in, d_hidden, out_sum = lax.optimization_barrier((d_in, d_hidden, out_sum))
    d_in = in_order(gather_flips(total(d_in).astype(BF), "grp"), g)
    d_in = in_order(gather_flips(d_in, "core"), k)
    outputs = (middle + total(out_sum) + c_bias).astype(BF)[None]
    d_hidden = in_order(d_hidden, g)
    d_hidden = jnp.stack(in_order(gather_flips(d_hidden, "core"), k), axis=1)
    d_exp_w, d_con_w = unfold(d_hidden.reshape(GROUPS, rows_z, -1), zs)
    d_con_w = d_con_w.reshape(ff_z, width)
    packed = jnp.sum(d_in[:, :, own : own + extra].astype(F32), axis=1).reshape(-1)
    d_out = d_in[:, :, own + extra :].transpose(1, 0, 2, 3)
    tail = d_out[:, :, 3 * third :].reshape(GROUPS, ks, third, 3, width - 3 * cols)
    d_out_w = (
        jnp.concatenate(
            [
                d_out[:, :, : 3 * third],
                jnp.concatenate([tail[:, :, :, i] for i in range(3)], axis=2),
            ],
            axis=3,
        )
        .reshape(rows_z, width)
        .astype(F32)
    )
    d_in_w = weave(
        d_in[:, :, :own].transpose(1, 0, 2, 3).reshape(GROUPS, rows_z, 3 * cols), 3
    )

    def vec(i):
        return packed[i * rows_z : (i + 1) * rows_z]

    return (
        outputs,
        delta_inputs,
        vec(0),
        vec(1),
        d_in_w,
        vec(2),
        vec(3),
        d_out_w,
        vec(4),
        vec(5),
        vec(6),
        d_exp_w,
        packed[8 * rows_z : 8 * rows_z + ff_z],
        d_con_w,
        vec(7),
    )


def solution(mesh):
    ctx, zs = mesh.shape["ctx"], mesh.shape["fsdp"]
    axes = ("grp", "core", "fsdp")
    split = Mesh(mesh.devices.reshape(GROUPS, ctx // GROUPS, zs), axes)
    row, vec, mat = P("fsdp", ("grp", "core"), None), P("fsdp"), P("fsdp", None)
    placed = (row, row, vec, vec, mat, vec, vec, mat, vec, vec, vec, mat, vec, mat, vec)
    return jax.shard_map(
        shards,
        mesh=split,
        in_specs=placed,
        out_specs=placed,
        check_vma=False,
    )
```

```python
import functools

import jax
import jax.numpy as jnp
from jax import lax
from jax.experimental import pallas as pl
from jax.experimental.pallas import tpu as pltpu
from jax.sharding import Mesh, PartitionSpec as P

HEADS = 12
GROUPS = 4

NORM_EPS = 1e-05
MASK_FILL = -1e30
GELU_COEF = 0.7978845608028654
GELU_CUBE = 0.044715

SHORT = pl.CostEstimate(flops=1, bytes_accessed=1, transcendentals=0)
LONG = pl.CostEstimate(flops=8 * 10**9, bytes_accessed=1, transcendentals=0)

BF = jnp.bfloat16
F32 = jnp.float32


def in_hbm(*values):
    return [pltpu.with_memory_space_constraint(v, pltpu.HBM) for v in values]


def mm(left, right):
    return jnp.dot(left, right, preferred_element_type=F32)


def mm_lt(left, right):
    return lax.dot_general(left, right, (((0,), (0,)), ((), ())), preferred_element_type=F32)


def mm_rt(left, right):
    return lax.dot_general(left, right, (((1,), (1,)), ((), ())), preferred_element_type=F32)


def send(value, axis, flip):
    count = lax.axis_size(axis)
    return lax.ppermute(value, axis, [(s, s ^ flip) for s in range(count)])


def gather_flips(value, axis):
    return [value] + [send(value, axis, i) for i in range(1, lax.axis_size(axis))]


def swap_flips(pieces, axis):
    return [pieces[0]] + [send(p, axis, i) for i, p in enumerate(pieces) if i]


def pick(stacked, place):
    return lax.dynamic_index_in_dim(stacked, place, axis=0, keepdims=False)


def in_order(pieces, me):
    stacked = jnp.stack(pieces)
    return jnp.stack([pick(stacked, me ^ j) for j in range(len(pieces))])


def norm_stats(values):
    center = values - jnp.mean(values, axis=-1, keepdims=True)
    spread = jnp.mean(center * center, axis=-1, keepdims=True)
    rate = lax.rsqrt(spread + NORM_EPS)
    return center * rate, rate


def norm_back(slope, gain, hat, rate):
    scaled = slope * gain
    return rate * (
        scaled
        - jnp.mean(scaled, axis=-1, keepdims=True)
        - hat * jnp.mean(scaled * hat, axis=-1, keepdims=True)
    )


def total(parts):
    out = parts[0].astype(F32)
    for part in parts[1:]:
        out = out + part.astype(F32)
    return out


def cut_columns(source, cut, parts, i):
    wide = cut.shape[1] // parts
    for part in range(parts):
        low = (part * GROUPS + i) * wide
        cut[:, part * wide : (part + 1) * wide] = source[:, low : low + wide]


def cut_kernel(parts, place, source, cut):
    for i in range(GROUPS):

        @pl.when(place[0] == i)
        def _():
            cut_columns(source, cut, parts, i)


def cut_weight(weight, parts, g, k, ks):
    rows = weight.shape[0] // ks
    cols = weight.shape[1] // GROUPS
    if rows % 16 == 0:
        return pl.pallas_call(
            functools.partial(cut_kernel, parts),
            grid_spec=pltpu.PrefetchScalarGridSpec(
                num_scalar_prefetch=1,
                grid=(1,),
                in_specs=[pl.BlockSpec((rows, weight.shape[1]), lambda i, place: (place[1], 0))],
                out_specs=pl.BlockSpec((rows, cols), lambda i, place: (0, 0)),
            ),
            out_shape=jax.ShapeDtypeStruct((rows, cols), BF),
            compiler_params=pltpu.CompilerParams(vmem_limit_bytes=8 * 2**20),
        )(jnp.stack([g, k]).astype(jnp.int32), weight)
    half = pick(weight.reshape(ks, rows, -1), k)
    return lax.dynamic_index_in_dim(
        half.reshape(rows, parts, GROUPS, cols // parts), g, axis=2, keepdims=False
    ).reshape(rows, cols)


def cut_first_kernel(place, *refs):
    source, other, vectors, cut, held = refs[0], refs[1], refs[2:-2], refs[-2], refs[-1]
    rows = source.shape[0]
    third, cols = rows // 3, cut.shape[1]
    cut[rows + 16 : 2 * rows + 16, :] = other[:, :cols]
    over = other.shape[1] - cols
    for part in range(3):
        cut[2 * rows + 16 :, part * over : (part + 1) * over] = other[
            part * third : (part + 1) * third, cols:
        ]
    unit = vectors[0].shape[0]
    per = cut.shape[1] // unit
    held[...] = jnp.zeros_like(held)
    spot = 0
    for vector in vectors:
        row = vector[...].astype(F32).reshape(1, vector.shape[0])
        for part in range(vector.shape[0] // unit):
            col = spot % per * unit
            held[spot // per : spot // per + 1, col : col + unit] = row[
                :, part * unit : (part + 1) * unit
            ]
            spot += 1
    cut[rows : rows + 16, :] = held[...].astype(BF)
    for i in range(GROUPS):

        @pl.when(place[0] == i)
        def _():
            cut_columns(source, cut.at[:rows, :], 3, i)


def cut_first(weight, other, vectors, g, k, ks):
    rows, cols = weight.shape[0] // ks, weight.shape[1] // GROUPS
    tall = 2 * rows + 16 + rows // 3
    by_k = lambda i, place: (place[1], 0)
    return pl.pallas_call(
        cut_first_kernel,
        grid_spec=pltpu.PrefetchScalarGridSpec(
            num_scalar_prefetch=1,
            grid=(1,),
            in_specs=[
                pl.BlockSpec((rows, weight.shape[1]), by_k),
                pl.BlockSpec((rows, other.shape[1]), by_k),
            ]
            + [pl.BlockSpec(v.shape, lambda i, place: (0,)) for v in vectors],
            out_specs=pl.BlockSpec((tall, cols), lambda i, place: (0, 0)),
            scratch_shapes=[pltpu.VMEM((16, cols), F32)],
        ),
        out_shape=jax.ShapeDtypeStruct((tall, cols), BF),
        compiler_params=pltpu.CompilerParams(vmem_limit_bytes=8 * 2**20),
        cost_estimate=SHORT,
    )(jnp.stack([g, k]).astype(jnp.int32), *in_hbm(weight, other, *vectors))


def both_weights_kernel(rows, place, *refs):
    pieces, in_w, out_w = refs[:-2], refs[-2], refs[-1]
    zs, ks = in_w.shape[:2]
    third, cols = rows // 3, in_w.shape[3]
    over = out_w.shape[3] - cols
    low = rows + 16
    for j in range(ks):
        for i in range(zs):
            piece = pieces[j * zs + i]
            in_w[place[1] ^ i, place[2] ^ j] = piece[:rows, :]
            spot = (place[1] ^ i ^ place[0], place[2] ^ j)
            out_w[spot[0], spot[1], :, :cols] = piece[low : low + rows, :]
            for part in range(3):
                out_w[spot[0], spot[1], part * third : (part + 1) * third, cols:] = piece[
                    low + rows :, part * over : (part + 1) * over
                ]


def both_weights(pieces, g, z, k, rows, width):
    ks, zs = len(pieces), len(pieces[0])
    cols = pieces[0][0].shape[1]
    vmem = pl.BlockSpec(memory_space=pltpu.VMEM)
    shapes = [(zs, ks, rows, cols), (zs, ks, rows, width)]
    in_w, out_w = pl.pallas_call(
        functools.partial(both_weights_kernel, rows),
        grid_spec=pltpu.PrefetchScalarGridSpec(
            num_scalar_prefetch=1, in_specs=[vmem] * (zs * ks), out_specs=[vmem] * 2
        ),
        out_shape=[jax.ShapeDtypeStruct(s, BF) for s in shapes],
        compiler_params=pltpu.CompilerParams(vmem_limit_bytes=16 * 2**20),
        cost_estimate=SHORT,
    )(jnp.stack([g, z, k]).astype(jnp.int32), *[p for group in pieces for p in group])
    return in_w.reshape(width, cols), out_w.reshape(width, width)


def table_kernel(unit, place, *refs):
    pieces, out, held = refs[:-2], refs[-2], refs[-1]
    zs = len(pieces)
    per = held.shape[2] // unit
    cols = out.shape[1] // GROUPS
    for i, piece in enumerate(pieces):
        held[place[1] ^ i] = piece[...].astype(F32)

    def unpack(row, slot):
        for zz in range(zs):
            col = slot % per * unit
            out[row : row + 1, zz * unit : (zz + 1) * unit] = held[
                zz, slot // per : slot // per + 1, col : col + unit
            ]

    out[...] = jnp.zeros_like(out)
    for slot in range(8):
        unpack(slot + 8 if slot in (2, 3) else slot, slot)
    for i in range(GROUPS):

        @pl.when(place[0] == i)
        def _():
            unpack(8, 8 + i)
            out[2:4, :cols] = out[10:12, i * cols : (i + 1) * cols]


def vector_table(pieces, below, unit, width, g, z):
    cols = pieces[0].shape[1]
    return pl.pallas_call(
        functools.partial(table_kernel, unit),
        grid_spec=pltpu.PrefetchScalarGridSpec(
            num_scalar_prefetch=1,
            grid=(1,),
            in_specs=[pl.BlockSpec((16, cols), lambda i, place: (below // 16, 0))] * len(pieces),
            out_specs=pl.BlockSpec((16, width), lambda i, place: (0, 0)),
            scratch_shapes=[pltpu.VMEM((len(pieces), 16, cols), F32)],
        ),
        out_shape=jax.ShapeDtypeStruct((16, width), F32),
        compiler_params=pltpu.CompilerParams(vmem_limit_bytes=8 * 2**20),
    )(jnp.stack([g, z]).astype(jnp.int32), *pieces)


def pack_kernel(zs, stride, unit, place, sums, out_bias, gain, shift, con_bias, exp_bias, out):
    per = out.shape[1] // unit
    cols = out.shape[1] // 3

    def put(zz, slot, value):
        row, col = zz * stride + slot // per, slot % per * unit
        out[row : row + 1, col : col + unit] = value

    out[...] = jnp.zeros_like(out)
    whole = [(0, sums, 0), (1, sums, 1), (4, out_bias, 0), (5, gain, 0), (6, shift, 0), (7, con_bias, 0)]
    for slot, source, row in whole:
        for zz in range(zs):
            put(zz, slot, source[row : row + 1, zz * unit : (zz + 1) * unit])
    for i in range(GROUPS):

        @pl.when(place[0] == i)
        def _():
            for zz in range(zs):
                put(zz, 8 + i, exp_bias[:, zz * unit : (zz + 1) * unit])
            for part in range(cols // unit):
                zz = i * cols // unit + part
                low = part * unit
                put(zz, 2, sums[2:3, low : low + unit])
                put(zz, 3, sums[2:3, 2 * cols + low : 2 * cols + low + unit])


def pack_vectors(g, zs, stride, unit, sums, *vectors):
    wide = 3 * (vectors[0].shape[1] // GROUPS)
    vmem = pl.BlockSpec(memory_space=pltpu.VMEM)
    return pl.pallas_call(
        functools.partial(pack_kernel, zs, stride, unit),
        grid_spec=pltpu.PrefetchScalarGridSpec(
            num_scalar_prefetch=1, in_specs=[vmem] * (1 + len(vectors)), out_specs=vmem
        ),
        out_shape=jax.ShapeDtypeStruct((zs * stride, wide), F32),
        compiler_params=pltpu.CompilerParams(vmem_limit_bytes=8 * 2**20),
    )(jnp.stack([g]).astype(jnp.int32), sums, *vectors)


def cut_rest_kernel(parts, place, con_ref, exp_ref, cut):
    width = con_ref.shape[1]
    cut[:, :width] = con_ref[...]
    for i in range(GROUPS):

        @pl.when(place[0] == i)
        def _():
            cut_columns(exp_ref, cut.at[:, width:], parts, i)


def cut_rest(con_w, exp_w, parts, g, k, ks):
    width = con_w.shape[1]
    rows, ff_rows = exp_w.shape[0] // ks, con_w.shape[0] // (GROUPS * ks)
    wide = exp_w.shape[1] // GROUPS
    if rows % 16 == 0 and rows == ff_rows:
        return pl.pallas_call(
            functools.partial(cut_rest_kernel, parts),
            grid_spec=pltpu.PrefetchScalarGridSpec(
                num_scalar_prefetch=1,
                grid=(1,),
                in_specs=[
                    pl.BlockSpec((rows, width), lambda i, place: (place[0] * ks + place[1], 0)),
                    pl.BlockSpec((rows, exp_w.shape[1]), lambda i, place: (place[1], 0)),
                ],
                out_specs=pl.BlockSpec((rows, width + wide), lambda i, place: (0, 0)),
            ),
            out_shape=jax.ShapeDtypeStruct((rows, width + wide), BF),
            compiler_params=pltpu.CompilerParams(vmem_limit_bytes=8 * 2**20),
        )(jnp.stack([g, k]).astype(jnp.int32), *in_hbm(con_w, exp_w))
    return jnp.concatenate(
        [
            pick(con_w.reshape(GROUPS * ks, ff_rows, width), g * ks + k),
            cut_weight(exp_w, parts, g, k, ks),
        ],
        axis=1,
    )


def assemble_kernel(rows, place, *refs):
    pieces, out = refs[:-1], refs[-1]
    zs = out.shape[0]
    for j in range(out.shape[1]):
        for i in range(zs):
            out[place[0] ^ i, place[1] ^ j] = pieces[j * zs + i][:rows, :]


def assemble(pieces, first, k, rows):
    ks, zs = len(pieces), len(pieces[0])
    cols = pieces[0][0].shape[1]
    shape = (zs, ks, rows, cols)
    if rows % 16:
        parts = [in_order([p[:rows] for p in group], first) for group in pieces]
        return jnp.stack(in_order(parts, k), axis=1).reshape(zs, ks * rows, cols)
    vmem = pl.BlockSpec(memory_space=pltpu.VMEM)
    out = pl.pallas_call(
        functools.partial(assemble_kernel, rows),
        grid_spec=pltpu.PrefetchScalarGridSpec(
            num_scalar_prefetch=1, in_specs=[vmem] * (zs * ks), out_specs=vmem
        ),
        out_shape=jax.ShapeDtypeStruct(shape, BF),
        compiler_params=pltpu.CompilerParams(vmem_limit_bytes=8 * 2**20),
        cost_estimate=SHORT,
    )(jnp.stack([first, k]).astype(jnp.int32), *[p for group in pieces for p in group])
    return out.reshape(zs, ks * rows, cols)


def weave_kernel(parts, pieces, out):
    wide = pieces.shape[2] // parts
    for i in range(GROUPS):
        for part in range(parts):
            low = (part * GROUPS + i) * wide
            out[:, low : low + wide] = pieces[i, :, part * wide : (part + 1) * wide].astype(F32)


def weave(pieces, parts):
    rows, cols = pieces.shape[1], pieces.shape[2]
    step = 32
    return pl.pallas_call(
        functools.partial(weave_kernel, parts),
        grid=(rows // step,),
        in_specs=[pl.BlockSpec((GROUPS, step, cols), lambda i: (0, i, 0))],
        out_specs=pl.BlockSpec((step, GROUPS * cols), lambda i: (i, 0)),
        out_shape=jax.ShapeDtypeStruct((rows, GROUPS * cols), F32),
        compiler_params=pltpu.CompilerParams(vmem_limit_bytes=16 * 2**20),
    )(pieces)


def unfold_kernel(parts, ks, place, *refs):
    pieces, (exp_out, con_out, held) = refs[:-3], refs[-3:]
    wide = con_out.shape[3]
    part_wide = wide // parts
    for j in range(ks):
        for i in range(GROUPS):
            held[place[0] ^ i] = pieces[j * GROUPS + i][...]
        spot = place[1] ^ j
        for i in range(GROUPS):
            con_out[i, spot] = held[i, :, wide:].astype(F32)
            for part in range(parts):
                low = (part * GROUPS + i) * part_wide
                exp_out[spot, :, low : low + part_wide] = held[
                    i, :, part * part_wide : (part + 1) * part_wide
                ].astype(F32)


def unfold(pieces, parts, g, k):
    ks = len(pieces)
    rows, wide = pieces[0][0].shape[0], pieces[0][0].shape[1] // 2
    step = rows // 2 if rows % 32 == 0 else rows
    shapes = [(ks, rows, GROUPS * wide), (GROUPS, ks, rows, wide)]
    exp, con = pl.pallas_call(
        functools.partial(unfold_kernel, parts, ks),
        grid_spec=pltpu.PrefetchScalarGridSpec(
            num_scalar_prefetch=1,
            grid=(rows // step,),
            in_specs=[pl.BlockSpec((step, 2 * wide), lambda i, place: (i, 0))] * (ks * GROUPS),
            out_specs=[
                pl.BlockSpec((ks, step, GROUPS * wide), lambda i, place: (0, i, 0)),
                pl.BlockSpec((GROUPS, ks, step, wide), lambda i, place: (0, 0, i, 0)),
            ],
            scratch_shapes=[pltpu.VMEM((GROUPS, step, 2 * wide), BF)],
        ),
        out_shape=[jax.ShapeDtypeStruct(s, F32) for s in shapes],
        compiler_params=pltpu.CompilerParams(vmem_limit_bytes=20 * 2**20),
        cost_estimate=SHORT,
    )(jnp.stack([g, k]).astype(jnp.int32), *[p for group in pieces for p in group])
    return exp.reshape(ks * rows, -1), con.reshape(-1, wide)


def join_rows(pieces, joined):
    tok = joined.shape[0] // GROUPS
    for i, piece in enumerate(pieces):
        joined[i * tok : (i + 1) * tok, :] = piece[...].reshape(tok, joined.shape[1])


def hidden_kernel(*refs):
    h_rows, s_rows = refs[:GROUPS], refs[GROUPS : 2 * GROUPS]
    (exp_w, con_w, bias, act_ref, inner_ref, back_ref, out_ref, bias_ref) = refs[2 * GROUPS : -4]
    h_ref, s_ref, back_sum, out_sum = refs[-4:]
    step = pl.program_id(0)
    tok = h_rows[0].shape[0]

    @pl.when(step == 0)
    def _():
        join_rows(h_rows, h_ref)
        join_rows(s_rows, s_ref)

    inner = mm(h_ref[...], exp_w[...]) + bias[8:9, :]
    square = inner * inner
    tanh = jnp.tanh(GELU_COEF * (inner + GELU_CUBE * square * inner))
    half = 0.5 + 0.5 * tanh
    act = (inner * half).astype(BF)
    gelu_slope = half + (0.5 * GELU_COEF) * inner * (1.0 - tanh * tanh) * (
        1.0 + (3.0 * GELU_CUBE) * square
    )
    slope = (mm_rt(s_ref[...], con_w[...]) * gelu_slope).astype(BF)
    act_ref[...] = act
    inner_ref[...] = slope
    bias_ref[...] = jnp.sum(slope.astype(F32), axis=0, keepdims=True)
    back = mm_rt(slope, exp_w[...])
    out = mm(act, con_w[...])

    @pl.when(step == 0)
    def _():
        back_sum[...] = back
        out_sum[...] = out

    @pl.when(step > 0)
    def _():
        back_sum[...] += back
        out_sum[...] += out

    @pl.when(step == pl.num_programs(0) - 1)
    def _():
        for i in range(GROUPS):
            back_ref[i] = back_sum[i * tok : (i + 1) * tok, :].astype(BF)
            out_ref[i] = out_sum[i * tok : (i + 1) * tok, :].astype(BF)


def hidden_part(h_rows, s_rows, weights, table):
    tok, width = h_rows[0].shape
    hidden = weights.shape[1] - width
    rows = GROUPS * tok
    step = 256
    fixed = lambda i: (0, 0)
    cols = lambda i: (0, i)
    slots = pl.BlockSpec((GROUPS, tok, width), lambda i: (0, 0, 0))
    return pl.pallas_call(
        hidden_kernel,
        grid=(hidden // step,),
        in_specs=[pl.BlockSpec((tok, width), fixed)] * GROUPS
        + [pl.BlockSpec((1, tok, width), lambda i: (1, 0, 0))] * GROUPS
        + [
            pl.BlockSpec((width, step), lambda i: (0, width // step + i)),
            pl.BlockSpec((step, width), lambda i: (i, 0)),
            pl.BlockSpec((16, step), cols),
        ],
        out_specs=[
            pl.BlockSpec((rows, step), cols),
            pl.BlockSpec((rows, step), cols),
            slots,
            slots,
            pl.BlockSpec((1, step), cols),
        ],
        out_shape=[
            jax.ShapeDtypeStruct((rows, hidden), BF),
            jax.ShapeDtypeStruct((rows, hidden), BF),
            jax.ShapeDtypeStruct((GROUPS, tok, width), BF),
            pltpu.HBM((GROUPS, tok, width), BF),
            jax.ShapeDtypeStruct((1, hidden), F32),
        ],
        scratch_shapes=[pltpu.VMEM((rows, width), BF)] * 2 + [pltpu.VMEM((rows, width), F32)] * 2,
        compiler_params=pltpu.CompilerParams(vmem_limit_bytes=24 * 2**20),
        cost_estimate=SHORT,
    )(*h_rows, *in_hbm(*s_rows, weights, weights), table)


def hidden_grad_kernel(*refs):
    h_rows, s_rows = refs[:GROUPS], refs[GROUPS : 2 * GROUPS]
    inner_ref, act_ref, out_ref, h_ref, s_ref = refs[2 * GROUPS :]
    wide, step = inner_ref.shape[1], act_ref.shape[1]

    @pl.when(pl.program_id(0) == 0)
    def _():
        join_rows(s_rows, s_ref)

    join_rows(h_rows, h_ref)
    out_ref[:, :wide] = mm_lt(h_ref[...], inner_ref[...]).astype(BF)
    out_ref[:, wide:] = mm_lt(act_ref[...], s_ref[...]).astype(BF)


def hidden_grads(h_rows, s_rows, slope_inner, act):
    tok, width = h_rows[0].shape
    rows, hidden = act.shape
    step = 256
    cols = lambda i: (0, i)
    fixed = lambda i: (0, 0)
    return pl.pallas_call(
        hidden_grad_kernel,
        grid=(width // step,),
        in_specs=[pl.BlockSpec((tok, step), cols)] * GROUPS
        + [pl.BlockSpec((1, tok, width), lambda i: (1, 0, 0))] * GROUPS
        + [pl.BlockSpec((rows, hidden), fixed), pl.BlockSpec((rows, step), cols)],
        out_specs=pl.BlockSpec((step, hidden + width), lambda i: (i, 0)),
        out_shape=jax.ShapeDtypeStruct((width, hidden + width), BF),
        scratch_shapes=[pltpu.VMEM((rows, step), BF), pltpu.VMEM((rows, width), BF)],
        compiler_params=pltpu.CompilerParams(vmem_limit_bytes=16 * 2**20),
        cost_estimate=LONG,
    )(*h_rows, *in_hbm(*s_rows), slope_inner, act)


def visible(k, tok, keys):
    row = lax.broadcasted_iota(jnp.int32, (tok, keys), 0)
    col = lax.broadcasted_iota(jnp.int32, (tok, keys), 1)
    return col <= k * tok + row


def masked_scores(query, keys, seen):
    scores = mm_rt(query, keys)
    near = keys.shape[0] - seen.shape[1]
    last = jnp.where(seen, scores[:, near:], MASK_FILL)
    return last if near == 0 else jnp.concatenate([scores[:, :near], last], axis=1)


def attend_kernel(ks, head, place, *refs):
    pieces = refs[: GROUPS * ks]
    in_w, table = refs[GROUPS * ks : GROUPS * ks + 2]
    slots, q_out, k_out, v_out, att_out, lse_out, h_out, hat_out, h_all = refs[GROUPS * ks + 2 :]
    g, k = place[0], place[1]
    tok, width = pieces[-1].shape
    cols = q_out.shape[1]
    gain, shift = table[0:1, :], table[1:2, :]
    for j in range(ks):
        for i in range(GROUPS):
            piece = pieces[j * GROUPS + i]
            hat, _ = norm_stats((piece[...] if j else piece[0]).astype(F32))
            normed = (hat * gain + shift).astype(BF)
            spot = pl.multiple_of(((g ^ i) * ks + (k ^ j)) * tok, tok)
            h_all[pl.ds(spot, tok), :] = normed
            if j == 0:
                spot = pl.multiple_of((g ^ i) * tok, tok)
                h_out[pl.ds(spot, tok), :] = normed
                hat_out[pl.ds(spot, tok), :] = hat.astype(BF)
    q_out[...] = (mm(h_out[...], in_w[:, :cols]) + table[2:3, :cols]).astype(BF)
    kv = mm(h_all[...], in_w[:, cols:])
    k_out[...] = kv[:, :cols].astype(BF)
    v_out[...] = (kv[:, cols:] + table[3:4, :cols]).astype(BF)
    seen = visible(k, tok, ks * tok)
    for h in range(cols // head):
        low, high = h * head, (h + 1) * head
        for i in range(GROUPS):
            rows = slice(i * tok, (i + 1) * tok)
            span = (i + 1) * ks * tok
            query = (q_out[rows, low:high].astype(F32) * head**-0.5).astype(BF)
            scores = masked_scores(query, k_out[:span, low:high], seen)
            peak = jnp.max(scores, axis=-1, keepdims=True)
            weights = jnp.exp(scores - peak)
            mass = jnp.sum(weights, axis=-1, keepdims=True)
            lse_out[rows, h : h + 1] = peak + jnp.log(mass)
            att = mm(weights.astype(BF), v_out[:span, low:high]) / mass
            att_out[rows, low:high] = att
    for i in range(GROUPS):
        slots[g ^ i] = att_out[i * tok : (i + 1) * tok, :].astype(BF)


def attend(g, k, ks, head, both, more, in_w, table):
    tok, width = both[0].shape[1:]
    cols = in_w.shape[1] // 3
    mine, rows = GROUPS * tok, GROUPS * ks * tok
    vmem = pl.BlockSpec(memory_space=pltpu.VMEM)
    shapes = [
        ((GROUPS, tok, cols), BF),
        ((mine, cols), BF),
        ((rows, cols), BF),
        ((rows, cols), BF),
        ((mine, cols), F32),
        ((mine, 8), F32),
        ((mine, width), BF),
        ((mine, width), BF),
    ]
    return pl.pallas_call(
        functools.partial(attend_kernel, ks, head),
        grid_spec=pltpu.PrefetchScalarGridSpec(
            num_scalar_prefetch=1,
            in_specs=[pl.BlockSpec((1, tok, width), lambda i, place: (0, 0, 0))] * GROUPS
            + [vmem] * (len(more) + 2),
            grid=(1,),
            out_specs=[vmem] * len(shapes),
            scratch_shapes=[pltpu.VMEM((rows, width), BF)],
        ),
        out_shape=[jax.ShapeDtypeStruct(*shapes[0])] + [pltpu.HBM(s, t) for s, t in shapes[1:]],
        compiler_params=pltpu.CompilerParams(vmem_limit_bytes=(16 if ks == 2 else 48) * 2**20),
        cost_estimate=SHORT,
    )(jnp.stack([g, k]).astype(jnp.int32), *both, *more, in_w, table)


def attend_back_kernel(ks, head, place, *refs):
    slopes = refs[:GROUPS]
    q_ref, k_ref, v_ref, att_ref, lse_ref, dq_out, dkv_out, dk_sum, dv_sum = refs[GROUPS:]
    g, k = place[0], place[1]
    tok, cols = slopes[0].shape
    d_rows = dq_out
    for i in range(GROUPS):
        d_rows[pl.ds(pl.multiple_of((g ^ i) * tok, tok), tok), :] = slopes[i][...]
    seen = visible(k, tok, ks * tok)
    for i in reversed(range(GROUPS)):
        rows = slice(i * tok, (i + 1) * tok)
        span = (i + 1) * ks * tok
        slope_all = d_rows[rows, :]
        parts = []
        for h in range(cols // head):
            low, high = h * head, (h + 1) * head
            query = (q_ref[rows, low:high].astype(F32) * head**-0.5).astype(BF)
            keys = k_ref[:span, low:high]
            slope = slope_all[:, low:high]
            scores = masked_scores(query, keys, seen)
            chances = jnp.exp(scores - lse_ref[rows, h : h + 1])
            diag = jnp.sum(slope.astype(F32) * att_ref[rows, low:high], axis=-1, keepdims=True)
            slope_chances = mm_rt(slope, v_ref[:span, low:high])
            slope_scores = (chances * (slope_chances - diag)).astype(BF)
            parts.append(mm(slope_scores, keys) * head**-0.5)
            dk = mm_lt(slope_scores, query)
            dv = mm_lt(chances.astype(BF), slope)
            if i == GROUPS - 1:
                dk_sum[:, low:high] = dk
                dv_sum[:, low:high] = dv
            else:
                dk_sum[:span, low:high] += dk
                dv_sum[:span, low:high] += dv
        dq_out[rows, :] = jnp.concatenate(parts, axis=1).astype(BF)
    for i in range(GROUPS):
        for j in range(ks):
            spot = slice((i * ks + j) * tok, (i * ks + j + 1) * tok)
            dkv_out[k ^ j, i * tok : (i + 1) * tok, :] = jnp.concatenate(
                [dk_sum[spot, :], dv_sum[spot, :]], axis=1
            ).astype(BF)


def attend_back(g, k, ks, head, slopes, q, keys, values, att, lse):
    tok, cols = slopes[0].shape
    mine, rows = GROUPS * tok, GROUPS * ks * tok
    vmem = pl.BlockSpec(memory_space=pltpu.VMEM)
    return pl.pallas_call(
        functools.partial(attend_back_kernel, ks, head),
        grid_spec=pltpu.PrefetchScalarGridSpec(
            num_scalar_prefetch=1,
            in_specs=[vmem] * (len(slopes) + 5),
            out_specs=[vmem] * 2,
            scratch_shapes=[pltpu.VMEM((rows, cols), F32)] * 2,
        ),
        out_shape=[
            jax.ShapeDtypeStruct((mine, cols), BF),
            jax.ShapeDtypeStruct((ks, mine, 2 * cols), BF),
        ],
        compiler_params=pltpu.CompilerParams(vmem_limit_bytes=(16 if ks == 2 else 48) * 2**20),
        cost_estimate=LONG,
    )(jnp.stack([g, k]).astype(jnp.int32), *slopes, *in_hbm(q, keys, values, att, lse))


def project_back_kernel(ks, place, *refs):
    dq, dkv = refs[0], refs[1 : 1 + ks]
    h_ref, hat_ref, in_w, slots, d_in, sums, project = refs[1 + ks :]
    g = place[0]
    tok = slots.shape[1]
    cols = dq.shape[1]
    project[:, :cols] = dq[...]
    project[:, cols:] = total([part[...] for part in dkv]).astype(BF)
    back = mm_rt(project[...], in_w[...])
    for i in range(GROUPS):
        slots[g ^ i] = back[i * tok : (i + 1) * tok, :].astype(BF)
    sums[0:1, :] = jnp.sum(back * hat_ref[...].astype(F32), axis=0, keepdims=True)
    sums[1:2, :] = jnp.sum(back, axis=0, keepdims=True)
    sums[2:3, : 3 * cols] = jnp.sum(project[...].astype(F32), axis=0, keepdims=True)
    d_in[...] = mm_lt(h_ref[...], project[...]).astype(BF)


def project_back(g, k, dq, dkv, h, hat, in_w):
    mine, width = h.shape
    cols = dq.shape[1]
    vmem = pl.BlockSpec(memory_space=pltpu.VMEM)
    return pl.pallas_call(
        functools.partial(project_back_kernel, len(dkv)),
        grid_spec=pltpu.PrefetchScalarGridSpec(
            num_scalar_prefetch=1,
            in_specs=[vmem] * (len(dkv) + 4),
            out_specs=[vmem] * 3,
            scratch_shapes=[pltpu.VMEM((mine, 3 * cols), BF)],
        ),
        out_shape=[
            jax.ShapeDtypeStruct((GROUPS, mine // GROUPS, width), BF),
            jax.ShapeDtypeStruct((width, 3 * cols), BF),
            jax.ShapeDtypeStruct((8, width), F32),
        ],
        compiler_params=pltpu.CompilerParams(vmem_limit_bytes=16 * 2**20),
        cost_estimate=SHORT,
    )(jnp.stack([g, k]).astype(jnp.int32), dq, *dkv, *in_hbm(h, hat), in_w)


def shards(
    inputs,
    cotangent,
    first_gain,
    first_shift,
    input_weight,
    query_bias,
    value_bias,
    output_weight,
    output_bias,
    second_gain,
    second_shift,
    expand_weight,
    expand_bias,
    contract_weight,
    contract_bias,
):
    tok, width = inputs.shape[1:]
    ks, zs = lax.axis_size("core"), lax.axis_size("fsdp")
    g, k, z = lax.axis_index("grp"), lax.axis_index("core"), lax.axis_index("fsdp")
    rows_z = width // zs
    heads_here = HEADS // GROUPS
    head = width // HEADS
    cols = width // GROUPS
    ff = expand_weight.shape[1]
    ff_z = ff // zs
    ff_g = ff_z // GROUPS
    mine = GROUPS * tok
    scale = head ** (-0.5)

    x_own = inputs[0]
    slope_own = cotangent[0]

    smalls = [first_gain, first_shift, query_bias, value_bias, output_bias]
    smalls += [second_gain, second_shift, contract_bias, expand_bias]
    own = rows_z // ks
    aligned = own % 48 == 0 and zs == GROUPS
    if aligned:
        cut = cut_first(input_weight, output_weight, smalls, g, k, ks)
    else:
        cut = cut_weight(input_weight, 3, g, k, ks)
    pieces = gather_flips(cut, "fsdp")
    rows_both = gather_flips(jnp.concatenate([inputs, cotangent]), "grp")
    pieces, rows_both, con_raw, exp_raw = lax.optimization_barrier(
        (pieces, rows_both, contract_weight, expand_weight)
    )
    x_more = [send(b[0], "core", j) for j in range(1, ks) for b in rows_both]
    more = [[send(b, "core", j) for b in pieces] for j in range(1, ks)]
    if aligned:
        table = vector_table(pieces, own, rows_z, width, g, z)
        in_w, out_w = both_weights([pieces] + more, g, z, k, own, width)
    else:
        in_w = assemble([pieces] + more, z, k, own).reshape(width, 3 * cols)
        out_w = gather_flips(pick(output_weight.reshape(ks, own, width), k), "fsdp")
        out_more = [[send(b, "core", j) for b in out_w] for j in range(1, ks)]
        out_w = assemble([out_w] + out_more, z, k, own).reshape(GROUPS, cols, width)
        out_w = jnp.concatenate([pick(out_w, g ^ i) for i in range(GROUPS)])
        got = in_order(gather_flips(jnp.concatenate(smalls), "fsdp"), z).astype(F32)
        vectors = [got[:, i * rows_z : (i + 1) * rows_z].reshape(width) for i in range(8)]
        for i in (2, 3):
            vectors[i] = jnp.tile(pick(vectors[i].reshape(GROUPS, cols), g), GROUPS)
        got = got[:, 8 * rows_z :].reshape(zs, GROUPS, ff_g)
        vectors.append(lax.dynamic_index_in_dim(got, g, axis=1, keepdims=False).reshape(width))
        table = jnp.pad(jnp.stack(vectors), ((0, 7), (0, 0)))
    o_bias, gain_two, shift_two, c_bias = [table[i : i + 1] for i in range(4, 8)]

    rest = cut_rest(con_raw, exp_raw, zs, g, k, ks)
    rest = lax.all_gather(rest, ("fsdp", "core"), axis=0, tiled=True)

    slots, qs, keys, values, att_full, lse, h1, hat_one = attend(
        g, k, ks, head, rows_both, x_more, in_w, table
    )
    att = jnp.concatenate(swap_flips([slots[i] for i in range(GROUPS)], "grp"), axis=1)
    x_f = x_own.astype(F32)
    middle = x_f + mm(att, out_w) + o_bias
    hat_two, rate_two = norm_stats(middle)
    h2 = (hat_two * gain_two + shift_two).astype(BF)
    h2_rows = gather_flips(h2, "grp")

    act, slope_inner, sh2_part, out_part, d_exp_b = hidden_part(
        h2_rows, rows_both, rest, table
    )
    sh2 = swap_flips([sh2_part[i] for i in range(GROUPS)], "grp")
    d_hidden = hidden_grads(h2_rows, rows_both, slope_inner, act)
    sh2, d_hidden = lax.optimization_barrier((sh2, d_hidden))
    sh2 = total(sh2)
    d_hidden = lax.psum_scatter(d_hidden, ("fsdp", "core"), scatter_dimension=0, tiled=True)

    slope_f = slope_own.astype(F32)
    d_gain_two = jnp.sum(sh2 * hat_two, axis=0, keepdims=True)
    d_shift_two = jnp.sum(sh2, axis=0, keepdims=True)
    slope_middle = slope_f + norm_back(sh2, gain_two, hat_two, rate_two)
    slope_branch = slope_middle.astype(BF)
    slope_att = mm_rt(slope_branch, out_w).astype(BF)
    datt = swap_flips([slope_att[:, i * cols : (i + 1) * cols] for i in range(GROUPS)], "grp")

    datt, slope_late = lax.optimization_barrier((datt, slope_branch))
    d_out = mm_lt(att, slope_late).astype(BF).reshape(GROUPS, cols, width)
    d_out = in_order([d_out[i] for i in range(GROUPS)], g)
    d_out = d_out.reshape(zs, GROUPS, ks, own // GROUPS, width)
    pieces = [lax.dynamic_index_in_dim(d_out, k ^ j, axis=2, keepdims=False) for j in range(ks)]
    datt, pieces = lax.optimization_barrier((datt, pieces))
    d_out = swap_flips(pieces, "core")

    dq, dkv = attend_back(g, k, ks, head, datt, qs, keys, values, att_full, lse)
    dkv = swap_flips([dkv[j] for j in range(ks)], "core")
    dkv, d_out = lax.optimization_barrier((dkv, d_out))
    d_out = total(d_out).astype(BF)
    pieces = [lax.dynamic_index_in_dim(d_out, g ^ i, axis=1, keepdims=False) for i in range(GROUPS)]
    dkv, pieces = lax.optimization_barrier((dkv, pieces))
    d_out = swap_flips(pieces, "grp")
    sh1_part, d_in, sums = project_back(g, k, dq, dkv, h1, hat_one, in_w)
    sh1 = swap_flips([sh1_part[i] for i in range(GROUPS)], "grp")
    sh1, d_out = lax.optimization_barrier((sh1, d_out))
    sh1 = total(sh1)
    hat_own, rate_own = norm_stats(x_f)
    delta_inputs = (slope_middle + norm_back(sh1, table[0:1], hat_own, rate_own)).astype(BF)[None]

    extra = -(-(12 * rows_z) // (3 * cols * ks))
    packed = pack_vectors(
        g,
        zs,
        extra * ks,
        rows_z,
        sums,
        jnp.sum(slope_branch.astype(F32), axis=0, keepdims=True),
        d_gain_two,
        d_shift_two,
        jnp.sum(slope_f, axis=0, keepdims=True),
        d_exp_b,
    )
    d_out = total(d_out).astype(BF)
    third = d_out.shape[1] // 3
    tail = d_out[..., 3 * cols :]
    tail = [tail[:, i * third : (i + 1) * third] for i in range(3)]
    d_out = jnp.concatenate([d_out[..., : 3 * cols], jnp.concatenate(tail, axis=2)], axis=1)
    d_in = jnp.concatenate(
        [
            d_in.reshape(zs, ks, own, 3 * cols),
            packed.astype(BF).reshape(zs, ks, extra, 3 * cols),
        ],
        axis=2,
    )
    pieces = [lax.dynamic_index_in_dim(d_in, k ^ j, axis=1, keepdims=False) for j in range(ks)]
    d_in = total(swap_flips(pieces, "core")).astype(BF)
    d_in = jnp.concatenate([d_in, d_out], axis=1)
    d_in = swap_flips([pick(d_in, z ^ i) for i in range(zs)], "fsdp")
    d_hidden = gather_flips(d_hidden, "grp")
    d_in, d_hidden = lax.optimization_barrier((d_in, d_hidden))
    d_in = gather_flips(total(d_in).astype(BF), "grp")
    d_hidden = [d_hidden] + [[send(p, "core", j) for p in d_hidden] for j in range(1, ks)]
    d_exp_w, d_con_w = unfold(d_hidden, zs, g, k)
    d_in, d_exp_w, d_con_w, out_part = lax.optimization_barrier((d_in, d_exp_w, d_con_w, out_part))
    out_sum = swap_flips([out_part[i] for i in range(GROUPS)], "grp")
    d_in = in_order(gather_flips(in_order(d_in, g), "core"), k)
    outputs = (middle + total(out_sum) + c_bias).astype(BF)[None]
    packed = jnp.sum(d_in[:, :, own : own + extra].astype(F32), axis=1).reshape(-1)
    d_out = d_in[:, :, own + extra :].transpose(1, 0, 2, 3)
    tail = d_out[:, :, 3 * third :].reshape(GROUPS, ks, third, 3, width - 3 * cols)
    d_out_w = (
        jnp.concatenate(
            [
                d_out[:, :, : 3 * third],
                jnp.concatenate([tail[:, :, :, i] for i in range(3)], axis=2),
            ],
            axis=3,
        )
        .reshape(rows_z, width)
        .astype(F32)
    )
    d_in_w = weave(
        d_in[:, :, :own].transpose(1, 0, 2, 3).reshape(GROUPS, rows_z, 3 * cols), 3
    )

    def vec(i):
        return packed[i * rows_z : (i + 1) * rows_z]

    return (
        outputs,
        delta_inputs,
        vec(0),
        vec(1),
        d_in_w,
        vec(2),
        vec(3),
        d_out_w,
        vec(4),
        vec(5),
        vec(6),
        d_exp_w,
        packed[8 * rows_z : 8 * rows_z + ff_z],
        d_con_w,
        vec(7),
    )


def solution(mesh):
    ctx, zs = mesh.shape["ctx"], mesh.shape["fsdp"]
    axes = ("grp", "core", "fsdp")
    split = Mesh(mesh.devices.reshape(GROUPS, ctx // GROUPS, zs), axes)
    row, vec, mat = P("fsdp", ("grp", "core"), None), P("fsdp"), P("fsdp", None)
    placed = (row, row, vec, vec, mat, vec, vec, mat, vec, vec, vec, mat, vec, mat, vec)
    return jax.shard_map(
        shards,
        mesh=split,
        in_specs=placed,
        out_specs=placed,
        check_vma=False,
    )
```

```python
import functools

import jax
import jax.numpy as jnp
from jax import lax
from jax.experimental import pallas as pl
from jax.experimental.pallas import tpu as pltpu
from jax.sharding import Mesh, PartitionSpec as P

HEADS = 12
GROUPS = 4

NORM_EPS = 1e-05
MASK_FILL = -1e30
GELU_COEF = 0.7978845608028654
GELU_CUBE = 0.044715

SHORT = pl.CostEstimate(flops=1, bytes_accessed=1, transcendentals=0)
LONG = pl.CostEstimate(flops=8 * 10**9, bytes_accessed=1, transcendentals=0)

BF = jnp.bfloat16
F32 = jnp.float32


def in_hbm(*values):
    return [pltpu.with_memory_space_constraint(v, pltpu.HBM) for v in values]


def mm(left, right):
    return jnp.dot(left, right, preferred_element_type=F32)


def mm_lt(left, right):
    return lax.dot_general(left, right, (((0,), (0,)), ((), ())), preferred_element_type=F32)


def mm_rt(left, right):
    return lax.dot_general(left, right, (((1,), (1,)), ((), ())), preferred_element_type=F32)


def send(value, axis, flip):
    count = lax.axis_size(axis)
    return lax.ppermute(value, axis, [(s, s ^ flip) for s in range(count)])


def gather_flips(value, axis):
    return [value] + [send(value, axis, i) for i in range(1, lax.axis_size(axis))]


def swap_flips(pieces, axis):
    return [pieces[0]] + [send(p, axis, i) for i, p in enumerate(pieces) if i]


def pick(stacked, place):
    return lax.dynamic_index_in_dim(stacked, place, axis=0, keepdims=False)


def in_order(pieces, me):
    stacked = jnp.stack(pieces)
    return jnp.stack([pick(stacked, me ^ j) for j in range(len(pieces))])


def norm_stats(values):
    center = values - jnp.mean(values, axis=-1, keepdims=True)
    spread = jnp.mean(center * center, axis=-1, keepdims=True)
    rate = lax.rsqrt(spread + NORM_EPS)
    return center * rate, rate


def norm_back(slope, gain, hat, rate):
    scaled = slope * gain
    return rate * (
        scaled
        - jnp.mean(scaled, axis=-1, keepdims=True)
        - hat * jnp.mean(scaled * hat, axis=-1, keepdims=True)
    )


def total(parts):
    out = parts[0].astype(F32)
    for part in parts[1:]:
        out = out + part.astype(F32)
    return out


def cut_columns(source, cut, parts, i):
    wide = cut.shape[1] // parts
    for part in range(parts):
        low = (part * GROUPS + i) * wide
        cut[:, part * wide : (part + 1) * wide] = source[:, low : low + wide]


def cut_kernel(parts, place, source, cut):
    for i in range(GROUPS):

        @pl.when(place[0] == i)
        def _():
            cut_columns(source, cut, parts, i)


def cut_weight(weight, parts, g, k, ks):
    rows = weight.shape[0] // ks
    cols = weight.shape[1] // GROUPS
    if rows % 16 == 0:
        return pl.pallas_call(
            functools.partial(cut_kernel, parts),
            grid_spec=pltpu.PrefetchScalarGridSpec(
                num_scalar_prefetch=1,
                grid=(1,),
                in_specs=[pl.BlockSpec((rows, weight.shape[1]), lambda i, place: (place[1], 0))],
                out_specs=pl.BlockSpec((rows, cols), lambda i, place: (0, 0)),
            ),
            out_shape=jax.ShapeDtypeStruct((rows, cols), BF),
            compiler_params=pltpu.CompilerParams(vmem_limit_bytes=8 * 2**20),
        )(jnp.stack([g, k]).astype(jnp.int32), weight)
    half = pick(weight.reshape(ks, rows, -1), k)
    return lax.dynamic_index_in_dim(
        half.reshape(rows, parts, GROUPS, cols // parts), g, axis=2, keepdims=False
    ).reshape(rows, cols)


def cut_first_kernel(place, *refs):
    source, other, vectors, cut, held = refs[0], refs[1], refs[2:-2], refs[-2], refs[-1]
    rows = source.shape[0]
    third, cols = rows // 3, cut.shape[1]
    cut[rows + 16 : 2 * rows + 16, :] = other[:, :cols]
    over = other.shape[1] - cols
    for part in range(3):
        cut[2 * rows + 16 :, part * over : (part + 1) * over] = other[
            part * third : (part + 1) * third, cols:
        ]
    unit = vectors[0].shape[0]
    per = cut.shape[1] // unit
    held[...] = jnp.zeros_like(held)
    spot = 0
    for vector in vectors:
        row = vector[...].astype(F32).reshape(1, vector.shape[0])
        for part in range(vector.shape[0] // unit):
            col = spot % per * unit
            held[spot // per : spot // per + 1, col : col + unit] = row[
                :, part * unit : (part + 1) * unit
            ]
            spot += 1
    cut[rows : rows + 16, :] = held[...].astype(BF)
    for i in range(GROUPS):

        @pl.when(place[0] == i)
        def _():
            cut_columns(source, cut.at[:rows, :], 3, i)


def cut_first(weight, other, vectors, g, k, ks):
    rows, cols = weight.shape[0] // ks, weight.shape[1] // GROUPS
    tall = 2 * rows + 16 + rows // 3
    by_k = lambda i, place: (place[1], 0)
    return pl.pallas_call(
        cut_first_kernel,
        grid_spec=pltpu.PrefetchScalarGridSpec(
            num_scalar_prefetch=1,
            grid=(1,),
            in_specs=[
                pl.BlockSpec((rows, weight.shape[1]), by_k),
                pl.BlockSpec((rows, other.shape[1]), by_k),
            ]
            + [pl.BlockSpec(v.shape, lambda i, place: (0,)) for v in vectors],
            out_specs=pl.BlockSpec((tall, cols), lambda i, place: (0, 0)),
            scratch_shapes=[pltpu.VMEM((16, cols), F32)],
        ),
        out_shape=jax.ShapeDtypeStruct((tall, cols), BF),
        compiler_params=pltpu.CompilerParams(vmem_limit_bytes=8 * 2**20),
        cost_estimate=SHORT,
    )(jnp.stack([g, k]).astype(jnp.int32), *in_hbm(weight, other, *vectors))


def both_weights_kernel(rows, place, *refs):
    pieces, in_w, out_w = refs[:-2], refs[-2], refs[-1]
    zs, ks = in_w.shape[:2]
    third, cols = rows // 3, in_w.shape[3]
    over = out_w.shape[3] - cols
    low = rows + 16
    for j in range(ks):
        for i in range(zs):
            piece = pieces[j * zs + i]
            in_w[place[1] ^ i, place[2] ^ j] = piece[:rows, :]
            spot = (place[1] ^ i ^ place[0], place[2] ^ j)
            out_w[spot[0], spot[1], :, :cols] = piece[low : low + rows, :]
            for part in range(3):
                out_w[spot[0], spot[1], part * third : (part + 1) * third, cols:] = piece[
                    low + rows :, part * over : (part + 1) * over
                ]


def both_weights(pieces, g, z, k, rows, width):
    ks, zs = len(pieces), len(pieces[0])
    cols = pieces[0][0].shape[1]
    vmem = pl.BlockSpec(memory_space=pltpu.VMEM)
    shapes = [(zs, ks, rows, cols), (zs, ks, rows, width)]
    in_w, out_w = pl.pallas_call(
        functools.partial(both_weights_kernel, rows),
        grid_spec=pltpu.PrefetchScalarGridSpec(
            num_scalar_prefetch=1, in_specs=[vmem] * (zs * ks), out_specs=[vmem] * 2
        ),
        out_shape=[jax.ShapeDtypeStruct(s, BF) for s in shapes],
        compiler_params=pltpu.CompilerParams(vmem_limit_bytes=16 * 2**20),
        cost_estimate=SHORT,
    )(jnp.stack([g, z, k]).astype(jnp.int32), *[p for group in pieces for p in group])
    return in_w.reshape(width, cols), out_w.reshape(width, width)


def table_kernel(unit, place, *refs):
    pieces, out, held = refs[:-2], refs[-2], refs[-1]
    zs = len(pieces)
    per = held.shape[2] // unit
    cols = out.shape[1] // GROUPS
    for i, piece in enumerate(pieces):
        held[place[1] ^ i] = piece[...].astype(F32)

    def unpack(row, slot):
        for zz in range(zs):
            col = slot % per * unit
            out[row : row + 1, zz * unit : (zz + 1) * unit] = held[
                zz, slot // per : slot // per + 1, col : col + unit
            ]

    out[...] = jnp.zeros_like(out)
    for slot in range(8):
        unpack(slot + 8 if slot in (2, 3) else slot, slot)
    for i in range(GROUPS):

        @pl.when(place[0] == i)
        def _():
            unpack(8, 8 + i)
            out[2:4, :cols] = out[10:12, i * cols : (i + 1) * cols]


def vector_table(pieces, below, unit, width, g, z):
    cols = pieces[0].shape[1]
    return pl.pallas_call(
        functools.partial(table_kernel, unit),
        grid_spec=pltpu.PrefetchScalarGridSpec(
            num_scalar_prefetch=1,
            grid=(1,),
            in_specs=[pl.BlockSpec((16, cols), lambda i, place: (below // 16, 0))] * len(pieces),
            out_specs=pl.BlockSpec((16, width), lambda i, place: (0, 0)),
            scratch_shapes=[pltpu.VMEM((len(pieces), 16, cols), F32)],
        ),
        out_shape=jax.ShapeDtypeStruct((16, width), F32),
        compiler_params=pltpu.CompilerParams(vmem_limit_bytes=8 * 2**20),
    )(jnp.stack([g, z]).astype(jnp.int32), *pieces)


def pack_kernel(zs, stride, unit, place, sums, out_bias, gain, shift, con_bias, exp_bias, out):
    per = out.shape[1] // unit
    cols = out.shape[1] // 3

    def put(zz, slot, value):
        row, col = zz * stride + slot // per, slot % per * unit
        out[row : row + 1, col : col + unit] = value

    out[...] = jnp.zeros_like(out)
    whole = [(0, sums, 0), (1, sums, 1), (4, out_bias, 0), (5, gain, 0), (6, shift, 0), (7, con_bias, 0)]
    for slot, source, row in whole:
        for zz in range(zs):
            put(zz, slot, source[row : row + 1, zz * unit : (zz + 1) * unit])
    for i in range(GROUPS):

        @pl.when(place[0] == i)
        def _():
            for zz in range(zs):
                put(zz, 8 + i, exp_bias[:, zz * unit : (zz + 1) * unit])
            for part in range(cols // unit):
                zz = i * cols // unit + part
                low = part * unit
                put(zz, 2, sums[2:3, low : low + unit])
                put(zz, 3, sums[2:3, 2 * cols + low : 2 * cols + low + unit])


def pack_vectors(g, zs, stride, unit, sums, *vectors):
    wide = 3 * (vectors[0].shape[1] // GROUPS)
    vmem = pl.BlockSpec(memory_space=pltpu.VMEM)
    return pl.pallas_call(
        functools.partial(pack_kernel, zs, stride, unit),
        grid_spec=pltpu.PrefetchScalarGridSpec(
            num_scalar_prefetch=1, in_specs=[vmem] * (1 + len(vectors)), out_specs=vmem
        ),
        out_shape=jax.ShapeDtypeStruct((zs * stride, wide), F32),
        compiler_params=pltpu.CompilerParams(vmem_limit_bytes=8 * 2**20),
    )(jnp.stack([g]).astype(jnp.int32), sums, *vectors)


def cut_rest_kernel(parts, place, con_ref, exp_ref, cut):
    width = con_ref.shape[1]
    cut[:, :width] = con_ref[...]
    for i in range(GROUPS):

        @pl.when(place[0] == i)
        def _():
            cut_columns(exp_ref, cut.at[:, width:], parts, i)


def cut_rest(con_w, exp_w, parts, g, k, ks):
    width = con_w.shape[1]
    rows, ff_rows = exp_w.shape[0] // ks, con_w.shape[0] // (GROUPS * ks)
    wide = exp_w.shape[1] // GROUPS
    if rows % 16 == 0 and rows == ff_rows:
        return pl.pallas_call(
            functools.partial(cut_rest_kernel, parts),
            grid_spec=pltpu.PrefetchScalarGridSpec(
                num_scalar_prefetch=1,
                grid=(1,),
                in_specs=[
                    pl.BlockSpec((rows, width), lambda i, place: (place[0] * ks + place[1], 0)),
                    pl.BlockSpec((rows, exp_w.shape[1]), lambda i, place: (place[1], 0)),
                ],
                out_specs=pl.BlockSpec((rows, width + wide), lambda i, place: (0, 0)),
            ),
            out_shape=jax.ShapeDtypeStruct((rows, width + wide), BF),
            compiler_params=pltpu.CompilerParams(vmem_limit_bytes=8 * 2**20),
        )(jnp.stack([g, k]).astype(jnp.int32), *in_hbm(con_w, exp_w))
    return jnp.concatenate(
        [
            pick(con_w.reshape(GROUPS * ks, ff_rows, width), g * ks + k),
            cut_weight(exp_w, parts, g, k, ks),
        ],
        axis=1,
    )


def assemble_kernel(rows, place, *refs):
    pieces, out = refs[:-1], refs[-1]
    zs = out.shape[0]
    for j in range(out.shape[1]):
        for i in range(zs):
            out[place[0] ^ i, place[1] ^ j] = pieces[j * zs + i][:rows, :]


def assemble(pieces, first, k, rows):
    ks, zs = len(pieces), len(pieces[0])
    cols = pieces[0][0].shape[1]
    shape = (zs, ks, rows, cols)
    if rows % 16:
        parts = [in_order([p[:rows] for p in group], first) for group in pieces]
        return jnp.stack(in_order(parts, k), axis=1).reshape(zs, ks * rows, cols)
    vmem = pl.BlockSpec(memory_space=pltpu.VMEM)
    out = pl.pallas_call(
        functools.partial(assemble_kernel, rows),
        grid_spec=pltpu.PrefetchScalarGridSpec(
            num_scalar_prefetch=1, in_specs=[vmem] * (zs * ks), out_specs=vmem
        ),
        out_shape=jax.ShapeDtypeStruct(shape, BF),
        compiler_params=pltpu.CompilerParams(vmem_limit_bytes=8 * 2**20),
        cost_estimate=SHORT,
    )(jnp.stack([first, k]).astype(jnp.int32), *[p for group in pieces for p in group])
    return out.reshape(zs, ks * rows, cols)


def weave_kernel(parts, pieces, out):
    wide = pieces.shape[2] // parts
    for i in range(GROUPS):
        for part in range(parts):
            low = (part * GROUPS + i) * wide
            out[:, low : low + wide] = pieces[i, :, part * wide : (part + 1) * wide].astype(F32)


def weave(pieces, parts):
    rows, cols = pieces.shape[1], pieces.shape[2]
    step = 32
    return pl.pallas_call(
        functools.partial(weave_kernel, parts),
        grid=(rows // step,),
        in_specs=[pl.BlockSpec((GROUPS, step, cols), lambda i: (0, i, 0))],
        out_specs=pl.BlockSpec((step, GROUPS * cols), lambda i: (i, 0)),
        out_shape=jax.ShapeDtypeStruct((rows, GROUPS * cols), F32),
        compiler_params=pltpu.CompilerParams(vmem_limit_bytes=16 * 2**20),
    )(pieces)


def unfold_kernel(parts, ks, place, *refs):
    pieces, (exp_out, con_out, held) = refs[:-3], refs[-3:]
    wide = con_out.shape[3]
    part_wide = wide // parts
    for j in range(ks):
        for i in range(GROUPS):
            held[place[0] ^ i] = pieces[j * GROUPS + i][...]
        spot = place[1] ^ j
        for i in range(GROUPS):
            con_out[i, spot] = held[i, :, wide:].astype(F32)
            for part in range(parts):
                low = (part * GROUPS + i) * part_wide
                exp_out[spot, :, low : low + part_wide] = held[
                    i, :, part * part_wide : (part + 1) * part_wide
                ].astype(F32)


def unfold(pieces, parts, g, k):
    ks = len(pieces)
    rows, wide = pieces[0][0].shape[0], pieces[0][0].shape[1] // 2
    step = rows // 2 if rows % 32 == 0 else rows
    shapes = [(ks, rows, GROUPS * wide), (GROUPS, ks, rows, wide)]
    exp, con = pl.pallas_call(
        functools.partial(unfold_kernel, parts, ks),
        grid_spec=pltpu.PrefetchScalarGridSpec(
            num_scalar_prefetch=1,
            grid=(rows // step,),
            in_specs=[pl.BlockSpec((step, 2 * wide), lambda i, place: (i, 0))] * (ks * GROUPS),
            out_specs=[
                pl.BlockSpec((ks, step, GROUPS * wide), lambda i, place: (0, i, 0)),
                pl.BlockSpec((GROUPS, ks, step, wide), lambda i, place: (0, 0, i, 0)),
            ],
            scratch_shapes=[pltpu.VMEM((GROUPS, step, 2 * wide), BF)],
        ),
        out_shape=[jax.ShapeDtypeStruct(s, F32) for s in shapes],
        compiler_params=pltpu.CompilerParams(vmem_limit_bytes=20 * 2**20),
        cost_estimate=SHORT,
    )(jnp.stack([g, k]).astype(jnp.int32), *[p for group in pieces for p in group])
    return exp.reshape(ks * rows, -1), con.reshape(-1, wide)


def join_rows(pieces, joined):
    tok = joined.shape[0] // GROUPS
    for i, piece in enumerate(pieces):
        joined[i * tok : (i + 1) * tok, :] = piece[...].reshape(tok, joined.shape[1])


def hidden_kernel(*refs):
    h_rows, s_rows = refs[:GROUPS], refs[GROUPS : 2 * GROUPS]
    exp_w, con_w, bias, act_ref, inner_ref = refs[2 * GROUPS : 2 * GROUPS + 5]
    back_ref = refs[2 * GROUPS + 5 : 3 * GROUPS + 5]
    out_ref = refs[3 * GROUPS + 5 : 4 * GROUPS + 5]
    bias_ref = refs[4 * GROUPS + 5]
    h_ref, s_ref, back_sum, out_sum = refs[-4:]
    step = pl.program_id(0)
    tok = h_rows[0].shape[0]

    @pl.when(step == 0)
    def _():
        join_rows(h_rows, h_ref)
        join_rows(s_rows, s_ref)

    inner = mm(h_ref[...], exp_w[...]) + bias[8:9, :]
    square = inner * inner
    tanh = jnp.tanh(GELU_COEF * (inner + GELU_CUBE * square * inner))
    half = 0.5 + 0.5 * tanh
    act = (inner * half).astype(BF)
    gelu_slope = half + (0.5 * GELU_COEF) * inner * (1.0 - tanh * tanh) * (
        1.0 + (3.0 * GELU_CUBE) * square
    )
    slope = (mm_rt(s_ref[...], con_w[...]) * gelu_slope).astype(BF)
    act_ref[...] = act
    inner_ref[...] = slope
    bias_ref[...] = jnp.sum(slope.astype(F32), axis=0, keepdims=True)
    back = mm_rt(slope, exp_w[...])
    out = mm(act, con_w[...])

    @pl.when(step == 0)
    def _():
        back_sum[...] = back
        out_sum[...] = out

    @pl.when(step > 0)
    def _():
        back_sum[...] += back
        out_sum[...] += out

    @pl.when(step == pl.num_programs(0) - 1)
    def _():
        for i in range(GROUPS):
            back_ref[i][...] = back_sum[i * tok : (i + 1) * tok, :].astype(BF)
            out_ref[i][...] = out_sum[i * tok : (i + 1) * tok, :].astype(BF)


def hidden_part(h_rows, s_rows, weights, table):
    tok, width = h_rows[0].shape
    hidden = weights.shape[1] - width
    rows = GROUPS * tok
    step = 256
    fixed = lambda i: (0, 0)
    cols = lambda i: (0, i)
    slots = [pl.BlockSpec((tok, width), fixed)] * GROUPS
    got = pl.pallas_call(
        hidden_kernel,
        grid=(hidden // step,),
        in_specs=[pl.BlockSpec((tok, width), fixed)] * GROUPS
        + [pl.BlockSpec((1, tok, width), lambda i: (1, 0, 0))] * GROUPS
        + [
            pl.BlockSpec((width, step), lambda i: (0, width // step + i)),
            pl.BlockSpec((step, width), lambda i: (i, 0)),
            pl.BlockSpec((16, step), cols),
        ],
        out_specs=[
            pl.BlockSpec((rows, step), cols),
            pl.BlockSpec((rows, step), cols),
            *slots,
            *slots,
            pl.BlockSpec((1, step), cols),
        ],
        out_shape=[
            jax.ShapeDtypeStruct((rows, hidden), BF),
            jax.ShapeDtypeStruct((rows, hidden), BF),
            *[jax.ShapeDtypeStruct((tok, width), BF)] * GROUPS,
            *[pltpu.HBM((tok, width), BF)] * GROUPS,
            jax.ShapeDtypeStruct((1, hidden), F32),
        ],
        scratch_shapes=[pltpu.VMEM((rows, width), BF)] * 2 + [pltpu.VMEM((rows, width), F32)] * 2,
        compiler_params=pltpu.CompilerParams(vmem_limit_bytes=24 * 2**20),
        cost_estimate=SHORT,
    )(*h_rows, *in_hbm(*s_rows, weights, weights), table)
    return got[0], got[1], got[2 : 2 + GROUPS], got[2 + GROUPS : 2 + 2 * GROUPS], got[-1]


def hidden_grad_kernel(*refs):
    h_rows, s_rows = refs[:GROUPS], refs[GROUPS : 2 * GROUPS]
    inner_ref, act_ref, out_ref, h_ref, s_ref = refs[2 * GROUPS :]
    wide, step = inner_ref.shape[1], act_ref.shape[1]

    @pl.when(pl.program_id(0) == 0)
    def _():
        join_rows(s_rows, s_ref)

    join_rows(h_rows, h_ref)
    out_ref[:, :wide] = mm_lt(h_ref[...], inner_ref[...]).astype(BF)
    out_ref[:, wide:] = mm_lt(act_ref[...], s_ref[...]).astype(BF)


def hidden_grads(h_rows, s_rows, slope_inner, act):
    tok, width = h_rows[0].shape
    rows, hidden = act.shape
    step = 256
    cols = lambda i: (0, i)
    fixed = lambda i: (0, 0)
    return pl.pallas_call(
        hidden_grad_kernel,
        grid=(width // step,),
        in_specs=[pl.BlockSpec((tok, step), cols)] * GROUPS
        + [pl.BlockSpec((1, tok, width), lambda i: (1, 0, 0))] * GROUPS
        + [pl.BlockSpec((rows, hidden), fixed), pl.BlockSpec((rows, step), cols)],
        out_specs=pl.BlockSpec((step, hidden + width), lambda i: (i, 0)),
        out_shape=jax.ShapeDtypeStruct((width, hidden + width), BF),
        scratch_shapes=[pltpu.VMEM((rows, step), BF), pltpu.VMEM((rows, width), BF)],
        compiler_params=pltpu.CompilerParams(vmem_limit_bytes=16 * 2**20),
        cost_estimate=LONG,
    )(*h_rows, *in_hbm(*s_rows), slope_inner, act)


def visible(k, tok, keys):
    row = lax.broadcasted_iota(jnp.int32, (tok, keys), 0)
    col = lax.broadcasted_iota(jnp.int32, (tok, keys), 1)
    return col <= k * tok + row


def masked_scores(query, keys, seen):
    scores = mm_rt(query, keys)
    near = keys.shape[0] - seen.shape[1]
    last = jnp.where(seen, scores[:, near:], MASK_FILL)
    return last if near == 0 else jnp.concatenate([scores[:, :near], last], axis=1)


def attend_kernel(ks, head, place, *refs):
    pieces = refs[: GROUPS * ks]
    in_w, table = refs[GROUPS * ks : GROUPS * ks + 2]
    slots = refs[GROUPS * ks + 2 : GROUPS * ks + 2 + GROUPS]
    q_out, k_out, v_out, att_out, lse_out, h_out, hat_out, h_all = refs[GROUPS * ks + 2 + GROUPS :]
    g, k = place[0], place[1]
    tok, width = pieces[-1].shape
    cols = q_out.shape[1]
    gain, shift = table[0:1, :], table[1:2, :]
    for j in range(ks):
        for i in range(GROUPS):
            piece = pieces[j * GROUPS + i]
            hat, _ = norm_stats((piece[...] if j else piece[0]).astype(F32))
            normed = (hat * gain + shift).astype(BF)
            spot = pl.multiple_of(((g ^ i) * ks + (k ^ j)) * tok, tok)
            h_all[pl.ds(spot, tok), :] = normed
            if j == 0:
                spot = pl.multiple_of((g ^ i) * tok, tok)
                h_out[pl.ds(spot, tok), :] = normed
                hat_out[pl.ds(spot, tok), :] = hat.astype(BF)
    q_out[...] = (mm(h_out[...], in_w[:, :cols]) + table[2:3, :cols]).astype(BF)
    kv = mm(h_all[...], in_w[:, cols:])
    k_out[...] = kv[:, :cols].astype(BF)
    v_out[...] = (kv[:, cols:] + table[3:4, :cols]).astype(BF)
    seen = visible(k, tok, ks * tok)
    for h in range(cols // head):
        low, high = h * head, (h + 1) * head
        for i in range(GROUPS):
            rows = slice(i * tok, (i + 1) * tok)
            span = (i + 1) * ks * tok
            query = (q_out[rows, low:high].astype(F32) * head**-0.5).astype(BF)
            scores = masked_scores(query, k_out[:span, low:high], seen)
            peak = jnp.max(scores, axis=-1, keepdims=True)
            weights = jnp.exp(scores - peak)
            mass = jnp.sum(weights, axis=-1, keepdims=True)
            lse_out[rows, h : h + 1] = peak + jnp.log(mass)
            att = mm(weights.astype(BF), v_out[:span, low:high]) / mass
            att_out[rows, low:high] = att
    for i in range(GROUPS):
        slots[i][...] = att_out[pl.ds(pl.multiple_of((g ^ i) * tok, tok), tok), :].astype(BF)


def attend(g, k, ks, head, both, more, in_w, table):
    tok, width = both[0].shape[1:]
    cols = in_w.shape[1] // 3
    mine, rows = GROUPS * tok, GROUPS * ks * tok
    vmem = pl.BlockSpec(memory_space=pltpu.VMEM)
    shapes = [
        *[((tok, cols), BF)] * GROUPS,
        ((mine, cols), BF),
        ((rows, cols), BF),
        ((rows, cols), BF),
        ((mine, cols), F32),
        ((mine, 8), F32),
        ((mine, width), BF),
        ((mine, width), BF),
    ]
    return pl.pallas_call(
        functools.partial(attend_kernel, ks, head),
        grid_spec=pltpu.PrefetchScalarGridSpec(
            num_scalar_prefetch=1,
            in_specs=[pl.BlockSpec((1, tok, width), lambda i, place: (0, 0, 0))] * GROUPS
            + [vmem] * (len(more) + 2),
            grid=(1,),
            out_specs=[vmem] * len(shapes),
            scratch_shapes=[pltpu.VMEM((rows, width), BF)],
        ),
        out_shape=[jax.ShapeDtypeStruct(s, t) for s, t in shapes[:GROUPS]]
        + [pltpu.HBM(s, t) for s, t in shapes[GROUPS:]],
        compiler_params=pltpu.CompilerParams(vmem_limit_bytes=(16 if ks == 2 else 48) * 2**20),
        cost_estimate=SHORT,
    )(jnp.stack([g, k]).astype(jnp.int32), *both, *more, in_w, table)


def attend_back_kernel(ks, head, first, place, *refs):
    slopes = refs[:GROUPS]
    q_ref, k_ref, v_ref, att_ref, lse_ref, dq_out, dkv_out = refs[GROUPS : GROUPS + 7]
    dk_sum, dv_sum, slope_rows = refs[GROUPS + 7 :]
    g, k = place[0], place[1]
    tok = slopes[0].shape[0]
    heads = dq_out.shape[1] // head
    for i in range(GROUPS):
        slope_rows[pl.ds(pl.multiple_of((g ^ i) * tok, tok), tok), :] = slopes[i][...]
    seen = visible(k, tok, ks * tok)
    for i in reversed(range(GROUPS)):
        rows = slice(i * tok, (i + 1) * tok)
        span = (i + 1) * ks * tok
        for h in range(heads):
            low, high = (first + h) * head, (first + h + 1) * head
            to = slice(h * head, (h + 1) * head)
            query = (q_ref[rows, low:high].astype(F32) * head**-0.5).astype(BF)
            keys = k_ref[:span, low:high]
            slope = slope_rows[rows, low:high]
            scores = masked_scores(query, keys, seen)
            chances = jnp.exp(scores - lse_ref[rows, first + h : first + h + 1])
            diag = jnp.sum(slope.astype(F32) * att_ref[rows, low:high], axis=-1, keepdims=True)
            slope_chances = mm_rt(slope, v_ref[:span, low:high])
            slope_scores = (chances * (slope_chances - diag)).astype(BF)
            dq_out[rows, to] = (mm(slope_scores, keys) * head**-0.5).astype(BF)
            dk = mm_lt(slope_scores, query)
            dv = mm_lt(chances.astype(BF), slope)
            if i == GROUPS - 1:
                dk_sum[:, to] = dk
                dv_sum[:, to] = dv
            else:
                dk_sum[:span, to] += dk
                dv_sum[:span, to] += dv
    for i in range(GROUPS):
        for j in range(ks):
            spot = slice((i * ks + j) * tok, (i * ks + j + 1) * tok)
            dkv_out[k ^ j, i * tok : (i + 1) * tok, :] = jnp.concatenate(
                [dk_sum[spot, :], dv_sum[spot, :]], axis=1
            ).astype(BF)


def attend_back(g, k, ks, head, first, heads, slopes, q, keys, values, att, lse):
    tok, cols = slopes[0].shape
    mine, rows = GROUPS * tok, GROUPS * ks * tok
    wide = heads * head
    vmem = pl.BlockSpec(memory_space=pltpu.VMEM)
    return pl.pallas_call(
        functools.partial(attend_back_kernel, ks, head, first),
        grid_spec=pltpu.PrefetchScalarGridSpec(
            num_scalar_prefetch=1,
            in_specs=[vmem] * (len(slopes) + 5),
            out_specs=[vmem] * 2,
            scratch_shapes=[pltpu.VMEM((rows, wide), F32)] * 2 + [pltpu.VMEM((mine, cols), BF)],
        ),
        out_shape=[
            jax.ShapeDtypeStruct((mine, wide), BF),
            jax.ShapeDtypeStruct((ks, mine, 2 * wide), BF),
        ],
        compiler_params=pltpu.CompilerParams(vmem_limit_bytes=(16 if ks == 2 else 48) * 2**20),
        cost_estimate=LONG,
    )(jnp.stack([g, k]).astype(jnp.int32), *slopes, *in_hbm(q, keys, values, att, lse))


def project_back_kernel(ks, parts, place, *refs):
    count = len(parts)
    dq, dkv = refs[:count], refs[count : count + count * ks]
    h_ref, hat_ref, in_w = refs[count * (ks + 1) : count * (ks + 1) + 3]
    slots, (d_in, sums, project, back) = refs[-GROUPS - 4 : -4], refs[-4:]
    g = place[0]
    tok = slots[0].shape[0]
    cols = sum(parts)
    low = 0
    for n, wide in enumerate(parts):
        project[:, low : low + wide] = dq[n][...]
        both = total([dkv[n * ks + j][...] for j in range(ks)]).astype(BF)
        project[:, cols + low : cols + low + wide] = both[:, :wide]
        project[:, 2 * cols + low : 2 * cols + low + wide] = both[:, wide:]
        low += wide
    back[...] = mm_rt(project[...], in_w[...])
    for i in range(GROUPS):
        slots[i][...] = back[pl.ds(pl.multiple_of((g ^ i) * tok, tok), tok), :].astype(BF)
    sums[0:1, :] = jnp.sum(back[...] * hat_ref[...].astype(F32), axis=0, keepdims=True)
    sums[1:2, :] = jnp.sum(back[...], axis=0, keepdims=True)
    sums[2:3, : 3 * cols] = jnp.sum(project[...].astype(F32), axis=0, keepdims=True)
    d_in[...] = mm_lt(h_ref[...], project[...]).astype(BF)


def project_back(g, dq, dkv, h, hat, in_w):
    mine, width = h.shape
    parts = [part.shape[1] for part in dq]
    cols = sum(parts)
    ks = len(dkv[0])
    vmem = pl.BlockSpec(memory_space=pltpu.VMEM)
    got = pl.pallas_call(
        functools.partial(project_back_kernel, ks, parts),
        grid_spec=pltpu.PrefetchScalarGridSpec(
            num_scalar_prefetch=1,
            in_specs=[vmem] * (len(dq) * (ks + 1) + 3),
            out_specs=[vmem] * (GROUPS + 2),
            scratch_shapes=[pltpu.VMEM((mine, 3 * cols), BF), pltpu.VMEM((mine, width), F32)],
        ),
        out_shape=[jax.ShapeDtypeStruct((mine // GROUPS, width), BF)] * GROUPS
        + [
            jax.ShapeDtypeStruct((width, 3 * cols), BF),
            jax.ShapeDtypeStruct((8, width), F32),
        ],
        compiler_params=pltpu.CompilerParams(vmem_limit_bytes=16 * 2**20),
        cost_estimate=SHORT,
    )(
        jnp.stack([g]).astype(jnp.int32),
        *dq,
        *[p for pieces in dkv for p in pieces],
        *in_hbm(h, hat),
        in_w,
    )
    return got[:GROUPS], got[GROUPS], got[GROUPS + 1]


def shards(
    inputs,
    cotangent,
    first_gain,
    first_shift,
    input_weight,
    query_bias,
    value_bias,
    output_weight,
    output_bias,
    second_gain,
    second_shift,
    expand_weight,
    expand_bias,
    contract_weight,
    contract_bias,
):
    tok, width = inputs.shape[1:]
    ks, zs = lax.axis_size("core"), lax.axis_size("fsdp")
    g, k, z = lax.axis_index("grp"), lax.axis_index("core"), lax.axis_index("fsdp")
    rows_z = width // zs
    heads_here = HEADS // GROUPS
    head = width // HEADS
    cols = width // GROUPS
    ff = expand_weight.shape[1]
    ff_z = ff // zs
    ff_g = ff_z // GROUPS
    mine = GROUPS * tok
    scale = head ** (-0.5)

    x_own = inputs[0]
    slope_own = cotangent[0]

    smalls = [first_gain, first_shift, query_bias, value_bias, output_bias]
    smalls += [second_gain, second_shift, contract_bias, expand_bias]
    own = rows_z // ks
    aligned = own % 48 == 0 and zs == GROUPS
    if aligned:
        cut = cut_first(input_weight, output_weight, smalls, g, k, ks)
    else:
        cut = cut_weight(input_weight, 3, g, k, ks)
    pieces = gather_flips(cut, "fsdp")
    rows_both = gather_flips(jnp.concatenate([inputs, cotangent]), "grp")
    pieces, rows_both, con_raw, exp_raw = lax.optimization_barrier(
        (pieces, rows_both, contract_weight, expand_weight)
    )
    x_more = [send(b[0], "core", j) for j in range(1, ks) for b in rows_both]
    more = [[send(b, "core", j) for b in pieces] for j in range(1, ks)]
    if aligned:
        table = vector_table(pieces, own, rows_z, width, g, z)
        in_w, out_w = both_weights([pieces] + more, g, z, k, own, width)
    else:
        in_w = assemble([pieces] + more, z, k, own).reshape(width, 3 * cols)
        out_w = gather_flips(pick(output_weight.reshape(ks, own, width), k), "fsdp")
        out_more = [[send(b, "core", j) for b in out_w] for j in range(1, ks)]
        out_w = assemble([out_w] + out_more, z, k, own).reshape(GROUPS, cols, width)
        out_w = jnp.concatenate([pick(out_w, g ^ i) for i in range(GROUPS)])
        got = in_order(gather_flips(jnp.concatenate(smalls), "fsdp"), z).astype(F32)
        vectors = [got[:, i * rows_z : (i + 1) * rows_z].reshape(width) for i in range(8)]
        for i in (2, 3):
            vectors[i] = jnp.tile(pick(vectors[i].reshape(GROUPS, cols), g), GROUPS)
        got = got[:, 8 * rows_z :].reshape(zs, GROUPS, ff_g)
        vectors.append(lax.dynamic_index_in_dim(got, g, axis=1, keepdims=False).reshape(width))
        table = jnp.pad(jnp.stack(vectors), ((0, 7), (0, 0)))
    o_bias, gain_two, shift_two, c_bias = [table[i : i + 1] for i in range(4, 8)]

    rest = cut_rest(con_raw, exp_raw, zs, g, k, ks)
    rest = lax.all_gather(rest, ("fsdp", "core"), axis=0, tiled=True)

    *slots, qs, keys, values, att_full, lse, h1, hat_one = attend(
        g, k, ks, head, rows_both, x_more, in_w, table
    )
    att = jnp.concatenate(swap_flips(slots, "grp"), axis=1)
    x_f = x_own.astype(F32)
    middle = x_f + mm(att, out_w) + o_bias
    hat_two, rate_two = norm_stats(middle)
    h2 = (hat_two * gain_two + shift_two).astype(BF)
    h2_rows = gather_flips(h2, "grp")

    act, slope_inner, sh2_part, out_part, d_exp_b = hidden_part(
        h2_rows, rows_both, rest, table
    )
    sh2 = swap_flips(sh2_part, "grp")
    d_hidden = hidden_grads(h2_rows, rows_both, slope_inner, act)
    sh2, d_hidden = lax.optimization_barrier((sh2, d_hidden))
    sh2 = total(sh2)
    d_hidden = lax.psum_scatter(d_hidden, ("fsdp", "core"), scatter_dimension=0, tiled=True)

    slope_f = slope_own.astype(F32)
    d_gain_two = jnp.sum(sh2 * hat_two, axis=0, keepdims=True)
    d_shift_two = jnp.sum(sh2, axis=0, keepdims=True)
    slope_middle = slope_f + norm_back(sh2, gain_two, hat_two, rate_two)
    slope_branch = slope_middle.astype(BF)
    slope_att = mm_rt(slope_branch, out_w).astype(BF)
    datt = swap_flips([slope_att[:, i * cols : (i + 1) * cols] for i in range(GROUPS)], "grp")

    datt, slope_late, out_part = lax.optimization_barrier((datt, slope_branch, out_part))
    out_sum = swap_flips(out_part, "grp")
    d_out = mm_lt(att, slope_late).astype(BF).reshape(GROUPS, cols, width)
    d_out = in_order([d_out[i] for i in range(GROUPS)], g)
    d_out = d_out.reshape(zs, GROUPS, ks, own // GROUPS, width)
    pieces = [lax.dynamic_index_in_dim(d_out, k ^ j, axis=2, keepdims=False) for j in range(ks)]
    datt, pieces = lax.optimization_barrier((datt, pieces))
    d_out = swap_flips(pieces, "core")

    kept = (qs, keys, values, att_full, lse)
    split = (heads_here + 1) // 2
    dq, dkv = attend_back(g, k, ks, head, 0, split, datt, *kept)
    dq, dkv = [dq], [swap_flips([dkv[j] for j in range(ks)], "core")]
    datt, d_out, out_sum = lax.optimization_barrier((datt, d_out, out_sum))
    d_out = total(d_out).astype(BF)
    pieces = [lax.dynamic_index_in_dim(d_out, g ^ i, axis=1, keepdims=False) for i in range(GROUPS)]
    datt, pieces = lax.optimization_barrier((datt, pieces))
    d_out = swap_flips(pieces, "grp")
    more = attend_back(g, k, ks, head, split, heads_here - split, datt, *kept)
    dq.append(more[0])
    dkv.append(swap_flips([more[1][j] for j in range(ks)], "core"))
    sh1_part, d_in, sums = project_back(g, dq, dkv, h1, hat_one, in_w)
    sh1 = total(swap_flips(sh1_part, "grp"))
    hat_own, rate_own = norm_stats(x_f)
    delta_inputs = (slope_middle + norm_back(sh1, table[0:1], hat_own, rate_own)).astype(BF)[None]

    extra = -(-(12 * rows_z) // (3 * cols * ks))
    packed = pack_vectors(
        g,
        zs,
        extra * ks,
        rows_z,
        sums,
        jnp.sum(slope_branch.astype(F32), axis=0, keepdims=True),
        d_gain_two,
        d_shift_two,
        jnp.sum(slope_f, axis=0, keepdims=True),
        d_exp_b,
    )
    d_out = total(d_out).astype(BF)
    third = d_out.shape[1] // 3
    tail = d_out[..., 3 * cols :]
    tail = [tail[:, i * third : (i + 1) * third] for i in range(3)]
    d_out = jnp.concatenate([d_out[..., : 3 * cols], jnp.concatenate(tail, axis=2)], axis=1)
    d_in = jnp.concatenate(
        [
            d_in.reshape(zs, ks, own, 3 * cols),
            packed.astype(BF).reshape(zs, ks, extra, 3 * cols),
        ],
        axis=2,
    )
    pieces = [lax.dynamic_index_in_dim(d_in, k ^ j, axis=1, keepdims=False) for j in range(ks)]
    d_in = total(swap_flips(pieces, "core")).astype(BF)
    d_in = jnp.concatenate([d_in, d_out], axis=1)
    pieces = lax.optimization_barrier([pick(d_in, z ^ i) for i in range(zs)])
    d_in = swap_flips(pieces, "fsdp")
    d_hidden = gather_flips(d_hidden, "grp")
    d_in, d_hidden = lax.optimization_barrier((d_in, d_hidden))
    d_in = gather_flips(total(d_in).astype(BF), "grp")
    d_hidden = [d_hidden] + [[send(p, "core", j) for p in d_hidden] for j in range(1, ks)]
    d_exp_w, d_con_w = unfold(d_hidden, zs, g, k)
    d_in, d_exp_w, d_con_w = lax.optimization_barrier((d_in, d_exp_w, d_con_w))
    d_in = in_order(gather_flips(in_order(d_in, g), "core"), k)
    outputs = (middle + total(out_sum) + c_bias).astype(BF)[None]
    packed = jnp.sum(d_in[:, :, own : own + extra].astype(F32), axis=1).reshape(-1)
    d_out = d_in[:, :, own + extra :].transpose(1, 0, 2, 3)
    tail = d_out[:, :, 3 * third :].reshape(GROUPS, ks, third, 3, width - 3 * cols)
    d_out_w = (
        jnp.concatenate(
            [
                d_out[:, :, : 3 * third],
                jnp.concatenate([tail[:, :, :, i] for i in range(3)], axis=2),
            ],
            axis=3,
        )
        .reshape(rows_z, width)
        .astype(F32)
    )
    d_in_w = weave(
        d_in[:, :, :own].transpose(1, 0, 2, 3).reshape(GROUPS, rows_z, 3 * cols), 3
    )

    def vec(i):
        return packed[i * rows_z : (i + 1) * rows_z]

    return (
        outputs,
        delta_inputs,
        vec(0),
        vec(1),
        d_in_w,
        vec(2),
        vec(3),
        d_out_w,
        vec(4),
        vec(5),
        vec(6),
        d_exp_w,
        packed[8 * rows_z : 8 * rows_z + ff_z],
        d_con_w,
        vec(7),
    )


def solution(mesh):
    ctx, zs = mesh.shape["ctx"], mesh.shape["fsdp"]
    axes = ("grp", "core", "fsdp")
    split = Mesh(mesh.devices.reshape(GROUPS, ctx // GROUPS, zs), axes)
    row, vec, mat = P("fsdp", ("grp", "core"), None), P("fsdp"), P("fsdp", None)
    placed = (row, row, vec, vec, mat, vec, vec, mat, vec, vec, vec, mat, vec, mat, vec)
    return jax.shard_map(
        shards,
        mesh=split,
        in_specs=placed,
        out_specs=placed,
        check_vma=False,
    )
```

```python
import functools

import jax
import jax.numpy as jnp
from jax import lax
from jax.experimental import pallas as pl
from jax.experimental.pallas import tpu as pltpu
from jax.sharding import Mesh, PartitionSpec as P

HEADS = 12
GROUPS = 4

NORM_EPS = 1e-05
MASK_FILL = -1e30
GELU_COEF = 0.7978845608028654
GELU_CUBE = 0.044715

SHORT = pl.CostEstimate(flops=1, bytes_accessed=1, transcendentals=0)
LONG = pl.CostEstimate(flops=8 * 10**9, bytes_accessed=1, transcendentals=0)

BF = jnp.bfloat16
F32 = jnp.float32


def in_hbm(*values):
    return [pltpu.with_memory_space_constraint(v, pltpu.HBM) for v in values]


def mm(left, right):
    return jnp.dot(left, right, preferred_element_type=F32)


def mm_lt(left, right):
    return lax.dot_general(left, right, (((0,), (0,)), ((), ())), preferred_element_type=F32)


def mm_rt(left, right):
    return lax.dot_general(left, right, (((1,), (1,)), ((), ())), preferred_element_type=F32)


def send(value, axis, flip):
    count = lax.axis_size(axis)
    return lax.ppermute(value, axis, [(s, s ^ flip) for s in range(count)])


def gather_flips(value, axis):
    return [value] + [send(value, axis, i) for i in range(1, lax.axis_size(axis))]


def swap_flips(pieces, axis):
    return [pieces[0]] + [send(p, axis, i) for i, p in enumerate(pieces) if i]


def pick(stacked, place):
    return lax.dynamic_index_in_dim(stacked, place, axis=0, keepdims=False)


def in_order(pieces, me):
    stacked = jnp.stack(pieces)
    return jnp.stack([pick(stacked, me ^ j) for j in range(len(pieces))])


def norm_stats(values):
    center = values - jnp.mean(values, axis=-1, keepdims=True)
    spread = jnp.mean(center * center, axis=-1, keepdims=True)
    rate = lax.rsqrt(spread + NORM_EPS)
    return center * rate, rate


def norm_back(slope, gain, hat, rate):
    scaled = slope * gain
    return rate * (
        scaled
        - jnp.mean(scaled, axis=-1, keepdims=True)
        - hat * jnp.mean(scaled * hat, axis=-1, keepdims=True)
    )


def total(parts):
    out = parts[0].astype(F32)
    for part in parts[1:]:
        out = out + part.astype(F32)
    return out


def cut_columns(source, cut, parts, i):
    wide = cut.shape[1] // parts
    for part in range(parts):
        low = (part * GROUPS + i) * wide
        cut[:, part * wide : (part + 1) * wide] = source[:, low : low + wide]


def cut_kernel(parts, place, source, cut):
    for i in range(GROUPS):

        @pl.when(place[0] == i)
        def _():
            cut_columns(source, cut, parts, i)


def cut_weight(weight, parts, g, k, ks):
    rows = weight.shape[0] // ks
    cols = weight.shape[1] // GROUPS
    if rows % 16 == 0:
        return pl.pallas_call(
            functools.partial(cut_kernel, parts),
            grid_spec=pltpu.PrefetchScalarGridSpec(
                num_scalar_prefetch=1,
                grid=(1,),
                in_specs=[pl.BlockSpec((rows, weight.shape[1]), lambda i, place: (place[1], 0))],
                out_specs=pl.BlockSpec((rows, cols), lambda i, place: (0, 0)),
            ),
            out_shape=jax.ShapeDtypeStruct((rows, cols), BF),
            compiler_params=pltpu.CompilerParams(vmem_limit_bytes=8 * 2**20),
        )(jnp.stack([g, k]).astype(jnp.int32), weight)
    half = pick(weight.reshape(ks, rows, -1), k)
    return lax.dynamic_index_in_dim(
        half.reshape(rows, parts, GROUPS, cols // parts), g, axis=2, keepdims=False
    ).reshape(rows, cols)


def cut_first_kernel(place, *refs):
    source, other, vectors, cut, held = refs[0], refs[1], refs[2:-2], refs[-2], refs[-1]
    rows = source.shape[0]
    third, cols = rows // 3, cut.shape[1]
    cut[rows + 16 : 2 * rows + 16, :] = other[:, :cols]
    over = other.shape[1] - cols
    for part in range(3):
        cut[2 * rows + 16 :, part * over : (part + 1) * over] = other[
            part * third : (part + 1) * third, cols:
        ]
    unit = vectors[0].shape[0]
    per = cut.shape[1] // unit
    held[...] = jnp.zeros_like(held)
    spot = 0
    for vector in vectors:
        row = vector[...].astype(F32).reshape(1, vector.shape[0])
        for part in range(vector.shape[0] // unit):
            col = spot % per * unit
            held[spot // per : spot // per + 1, col : col + unit] = row[
                :, part * unit : (part + 1) * unit
            ]
            spot += 1
    cut[rows : rows + 16, :] = held[...].astype(BF)
    for i in range(GROUPS):

        @pl.when(place[0] == i)
        def _():
            cut_columns(source, cut.at[:rows, :], 3, i)


def cut_first(weight, other, vectors, g, k, ks):
    rows, cols = weight.shape[0] // ks, weight.shape[1] // GROUPS
    tall = 2 * rows + 16 + rows // 3
    by_k = lambda i, place: (place[1], 0)
    return pl.pallas_call(
        cut_first_kernel,
        grid_spec=pltpu.PrefetchScalarGridSpec(
            num_scalar_prefetch=1,
            grid=(1,),
            in_specs=[
                pl.BlockSpec((rows, weight.shape[1]), by_k),
                pl.BlockSpec((rows, other.shape[1]), by_k),
            ]
            + [pl.BlockSpec(v.shape, lambda i, place: (0,)) for v in vectors],
            out_specs=pl.BlockSpec((tall, cols), lambda i, place: (0, 0)),
            scratch_shapes=[pltpu.VMEM((16, cols), F32)],
        ),
        out_shape=jax.ShapeDtypeStruct((tall, cols), BF),
        compiler_params=pltpu.CompilerParams(vmem_limit_bytes=8 * 2**20),
        cost_estimate=SHORT,
    )(jnp.stack([g, k]).astype(jnp.int32), *in_hbm(weight, other, *vectors))


def both_weights_kernel(rows, place, *refs):
    pieces, in_w, out_w = refs[:-2], refs[-2], refs[-1]
    zs, ks = in_w.shape[:2]
    third, cols = rows // 3, in_w.shape[3]
    over = out_w.shape[3] - cols
    low = rows + 16
    for j in range(ks):
        for i in range(zs):
            piece = pieces[j * zs + i]
            in_w[place[1] ^ i, place[2] ^ j] = piece[:rows, :]
            spot = (place[1] ^ i ^ place[0], place[2] ^ j)
            out_w[spot[0], spot[1], :, :cols] = piece[low : low + rows, :]
            for part in range(3):
                out_w[spot[0], spot[1], part * third : (part + 1) * third, cols:] = piece[
                    low + rows :, part * over : (part + 1) * over
                ]


def both_weights(pieces, g, z, k, rows, width):
    ks, zs = len(pieces), len(pieces[0])
    cols = pieces[0][0].shape[1]
    vmem = pl.BlockSpec(memory_space=pltpu.VMEM)
    shapes = [(zs, ks, rows, cols), (zs, ks, rows, width)]
    in_w, out_w = pl.pallas_call(
        functools.partial(both_weights_kernel, rows),
        grid_spec=pltpu.PrefetchScalarGridSpec(
            num_scalar_prefetch=1, in_specs=[vmem] * (zs * ks), out_specs=[vmem] * 2
        ),
        out_shape=[jax.ShapeDtypeStruct(s, BF) for s in shapes],
        compiler_params=pltpu.CompilerParams(vmem_limit_bytes=16 * 2**20),
        cost_estimate=SHORT,
    )(jnp.stack([g, z, k]).astype(jnp.int32), *[p for group in pieces for p in group])
    return in_w.reshape(width, cols), out_w.reshape(width, width)


def table_kernel(unit, place, *refs):
    pieces, out, held = refs[:-2], refs[-2], refs[-1]
    zs = len(pieces)
    per = held.shape[2] // unit
    cols = out.shape[1] // GROUPS
    for i, piece in enumerate(pieces):
        held[place[1] ^ i] = piece[...].astype(F32)

    def unpack(row, slot):
        for zz in range(zs):
            col = slot % per * unit
            out[row : row + 1, zz * unit : (zz + 1) * unit] = held[
                zz, slot // per : slot // per + 1, col : col + unit
            ]

    out[...] = jnp.zeros_like(out)
    for slot in range(8):
        unpack(slot + 8 if slot in (2, 3) else slot, slot)
    for i in range(GROUPS):

        @pl.when(place[0] == i)
        def _():
            unpack(8, 8 + i)
            out[2:4, :cols] = out[10:12, i * cols : (i + 1) * cols]


def vector_table(pieces, below, unit, width, g, z):
    cols = pieces[0].shape[1]
    return pl.pallas_call(
        functools.partial(table_kernel, unit),
        grid_spec=pltpu.PrefetchScalarGridSpec(
            num_scalar_prefetch=1,
            grid=(1,),
            in_specs=[pl.BlockSpec((16, cols), lambda i, place: (below // 16, 0))] * len(pieces),
            out_specs=pl.BlockSpec((16, width), lambda i, place: (0, 0)),
            scratch_shapes=[pltpu.VMEM((len(pieces), 16, cols), F32)],
        ),
        out_shape=jax.ShapeDtypeStruct((16, width), F32),
        compiler_params=pltpu.CompilerParams(vmem_limit_bytes=8 * 2**20),
    )(jnp.stack([g, z]).astype(jnp.int32), *pieces)


def pack_kernel(zs, stride, unit, place, sums, out_bias, gain, shift, con_bias, exp_bias, out):
    per = out.shape[1] // unit
    cols = out.shape[1] // 3

    def put(zz, slot, value):
        row, col = zz * stride + slot // per, slot % per * unit
        out[row : row + 1, col : col + unit] = value

    out[...] = jnp.zeros_like(out)
    whole = [(0, sums, 0), (1, sums, 1), (4, out_bias, 0), (5, gain, 0), (6, shift, 0), (7, con_bias, 0)]
    for slot, source, row in whole:
        for zz in range(zs):
            put(zz, slot, source[row : row + 1, zz * unit : (zz + 1) * unit])
    for i in range(GROUPS):

        @pl.when(place[0] == i)
        def _():
            for zz in range(zs):
                put(zz, 8 + i, exp_bias[:, zz * unit : (zz + 1) * unit])
            for part in range(cols // unit):
                zz = i * cols // unit + part
                low = part * unit
                put(zz, 2, sums[2:3, low : low + unit])
                put(zz, 3, sums[2:3, 2 * cols + low : 2 * cols + low + unit])


def pack_vectors(g, zs, stride, unit, sums, *vectors):
    wide = 3 * (vectors[0].shape[1] // GROUPS)
    vmem = pl.BlockSpec(memory_space=pltpu.VMEM)
    return pl.pallas_call(
        functools.partial(pack_kernel, zs, stride, unit),
        grid_spec=pltpu.PrefetchScalarGridSpec(
            num_scalar_prefetch=1, in_specs=[vmem] * (1 + len(vectors)), out_specs=vmem
        ),
        out_shape=jax.ShapeDtypeStruct((zs * stride, wide), F32),
        compiler_params=pltpu.CompilerParams(vmem_limit_bytes=8 * 2**20),
    )(jnp.stack([g]).astype(jnp.int32), sums, *vectors)


def cut_rest_kernel(parts, place, con_ref, exp_ref, cut):
    width = con_ref.shape[1]
    cut[:, :width] = con_ref[...]
    for i in range(GROUPS):

        @pl.when(place[0] == i)
        def _():
            cut_columns(exp_ref, cut.at[:, width:], parts, i)


def cut_rest(con_w, exp_w, parts, g, k, ks):
    width = con_w.shape[1]
    rows, ff_rows = exp_w.shape[0] // ks, con_w.shape[0] // (GROUPS * ks)
    wide = exp_w.shape[1] // GROUPS
    if rows % 16 == 0 and rows == ff_rows:
        return pl.pallas_call(
            functools.partial(cut_rest_kernel, parts),
            grid_spec=pltpu.PrefetchScalarGridSpec(
                num_scalar_prefetch=1,
                grid=(1,),
                in_specs=[
                    pl.BlockSpec((rows, width), lambda i, place: (place[0] * ks + place[1], 0)),
                    pl.BlockSpec((rows, exp_w.shape[1]), lambda i, place: (place[1], 0)),
                ],
                out_specs=pl.BlockSpec((rows, width + wide), lambda i, place: (0, 0)),
            ),
            out_shape=jax.ShapeDtypeStruct((rows, width + wide), BF),
            compiler_params=pltpu.CompilerParams(vmem_limit_bytes=8 * 2**20),
        )(jnp.stack([g, k]).astype(jnp.int32), *in_hbm(con_w, exp_w))
    return jnp.concatenate(
        [
            pick(con_w.reshape(GROUPS * ks, ff_rows, width), g * ks + k),
            cut_weight(exp_w, parts, g, k, ks),
        ],
        axis=1,
    )


def assemble_kernel(rows, place, *refs):
    pieces, out = refs[:-1], refs[-1]
    zs = out.shape[0]
    for j in range(out.shape[1]):
        for i in range(zs):
            out[place[0] ^ i, place[1] ^ j] = pieces[j * zs + i][:rows, :]


def assemble(pieces, first, k, rows):
    ks, zs = len(pieces), len(pieces[0])
    cols = pieces[0][0].shape[1]
    shape = (zs, ks, rows, cols)
    if rows % 16:
        parts = [in_order([p[:rows] for p in group], first) for group in pieces]
        return jnp.stack(in_order(parts, k), axis=1).reshape(zs, ks * rows, cols)
    vmem = pl.BlockSpec(memory_space=pltpu.VMEM)
    out = pl.pallas_call(
        functools.partial(assemble_kernel, rows),
        grid_spec=pltpu.PrefetchScalarGridSpec(
            num_scalar_prefetch=1, in_specs=[vmem] * (zs * ks), out_specs=vmem
        ),
        out_shape=jax.ShapeDtypeStruct(shape, BF),
        compiler_params=pltpu.CompilerParams(vmem_limit_bytes=8 * 2**20),
        cost_estimate=SHORT,
    )(jnp.stack([first, k]).astype(jnp.int32), *[p for group in pieces for p in group])
    return out.reshape(zs, ks * rows, cols)


def unfold_kernel(parts, ks, place, *refs):
    pieces, (exp_out, con_out, held) = refs[:-3], refs[-3:]
    wide = con_out.shape[3]
    part_wide = wide // parts
    for j in range(ks):
        for i in range(GROUPS):
            held[place[0] ^ i] = pieces[j * GROUPS + i][...]
        spot = place[1] ^ j
        for i in range(GROUPS):
            con_out[i, spot] = held[i, :, wide:].astype(F32)
            for part in range(parts):
                low = (part * GROUPS + i) * part_wide
                exp_out[spot, :, low : low + part_wide] = held[
                    i, :, part * part_wide : (part + 1) * part_wide
                ].astype(F32)


def unfold(pieces, parts, g, k):
    ks = len(pieces)
    rows, wide = pieces[0][0].shape[0], pieces[0][0].shape[1] // 2
    step = rows // 2 if rows % 32 == 0 else rows
    shapes = [(ks, rows, GROUPS * wide), (GROUPS, ks, rows, wide)]
    exp, con = pl.pallas_call(
        functools.partial(unfold_kernel, parts, ks),
        grid_spec=pltpu.PrefetchScalarGridSpec(
            num_scalar_prefetch=1,
            grid=(rows // step,),
            in_specs=[pl.BlockSpec((step, 2 * wide), lambda i, place: (i, 0))] * (ks * GROUPS),
            out_specs=[
                pl.BlockSpec((ks, step, GROUPS * wide), lambda i, place: (0, i, 0)),
                pl.BlockSpec((GROUPS, ks, step, wide), lambda i, place: (0, 0, i, 0)),
            ],
            scratch_shapes=[pltpu.VMEM((GROUPS, step, 2 * wide), BF)],
        ),
        out_shape=[jax.ShapeDtypeStruct(s, F32) for s in shapes],
        compiler_params=pltpu.CompilerParams(vmem_limit_bytes=20 * 2**20),
        cost_estimate=SHORT,
    )(jnp.stack([g, k]).astype(jnp.int32), *[p for group in pieces for p in group])
    return exp.reshape(ks * rows, -1), con.reshape(-1, wide)


def join_rows(pieces, joined):
    tok = joined.shape[0] // GROUPS
    for i, piece in enumerate(pieces):
        joined[i * tok : (i + 1) * tok, :] = piece[...].reshape(tok, joined.shape[1])


def hidden_kernel(*refs):
    h_rows, s_rows = refs[:GROUPS], refs[GROUPS : 2 * GROUPS]
    exp_w, con_w, bias, act_ref, inner_ref = refs[2 * GROUPS : 2 * GROUPS + 5]
    back_ref = refs[2 * GROUPS + 5 : 3 * GROUPS + 5]
    out_ref = refs[3 * GROUPS + 5 : 4 * GROUPS + 5]
    bias_ref = refs[4 * GROUPS + 5]
    h_ref, s_ref, back_sum, out_sum = refs[-4:]
    step = pl.program_id(0)
    tok = h_rows[0].shape[0]

    @pl.when(step == 0)
    def _():
        join_rows(h_rows, h_ref)
        join_rows(s_rows, s_ref)

    inner = mm(h_ref[...], exp_w[...]) + bias[8:9, :]
    square = inner * inner
    tanh = jnp.tanh(GELU_COEF * (inner + GELU_CUBE * square * inner))
    half = 0.5 + 0.5 * tanh
    act = (inner * half).astype(BF)
    gelu_slope = half + (0.5 * GELU_COEF) * inner * (1.0 - tanh * tanh) * (
        1.0 + (3.0 * GELU_CUBE) * square
    )
    slope = (mm_rt(s_ref[...], con_w[...]) * gelu_slope).astype(BF)
    act_ref[...] = act
    inner_ref[...] = slope
    bias_ref[...] = jnp.sum(slope.astype(F32), axis=0, keepdims=True)
    back = mm_rt(slope, exp_w[...])
    out = mm(act, con_w[...])

    @pl.when(step == 0)
    def _():
        back_sum[...] = back
        out_sum[...] = out

    @pl.when(step > 0)
    def _():
        back_sum[...] += back
        out_sum[...] += out

    @pl.when(step == pl.num_programs(0) - 1)
    def _():
        for i in range(GROUPS):
            back_ref[i][...] = back_sum[i * tok : (i + 1) * tok, :].astype(BF)
            out_ref[i][...] = out_sum[i * tok : (i + 1) * tok, :].astype(BF)


def hidden_part(h_rows, s_rows, weights, table):
    tok, width = h_rows[0].shape
    hidden = weights.shape[1] - width
    rows = GROUPS * tok
    step = 256
    fixed = lambda i: (0, 0)
    cols = lambda i: (0, i)
    slots = [pl.BlockSpec((tok, width), fixed)] * GROUPS
    got = pl.pallas_call(
        hidden_kernel,
        grid=(hidden // step,),
        in_specs=[pl.BlockSpec((tok, width), fixed)] * GROUPS
        + [pl.BlockSpec((1, tok, width), lambda i: (1, 0, 0))] * GROUPS
        + [
            pl.BlockSpec((width, step), lambda i: (0, width // step + i)),
            pl.BlockSpec((step, width), lambda i: (i, 0)),
            pl.BlockSpec((16, step), cols),
        ],
        out_specs=[
            pl.BlockSpec((rows, step), cols),
            pl.BlockSpec((rows, step), cols),
            *slots,
            *slots,
            pl.BlockSpec((1, step), cols),
        ],
        out_shape=[
            jax.ShapeDtypeStruct((rows, hidden), BF),
            jax.ShapeDtypeStruct((rows, hidden), BF),
            *[jax.ShapeDtypeStruct((tok, width), BF)] * GROUPS,
            *[pltpu.HBM((tok, width), BF)] * GROUPS,
            jax.ShapeDtypeStruct((1, hidden), F32),
        ],
        scratch_shapes=[pltpu.VMEM((rows, width), BF)] * 2 + [pltpu.VMEM((rows, width), F32)] * 2,
        compiler_params=pltpu.CompilerParams(vmem_limit_bytes=24 * 2**20),
        cost_estimate=SHORT,
    )(*in_hbm(*h_rows, *s_rows, weights, weights), table)
    return got[0], got[1], got[2 : 2 + GROUPS], got[2 + GROUPS : 2 + 2 * GROUPS], got[-1]


def hidden_grad_kernel(*refs):
    h_rows, s_rows = refs[:GROUPS], refs[GROUPS : 2 * GROUPS]
    inner_ref, act_ref, out_ref, h_ref, s_ref = refs[2 * GROUPS :]
    wide, step = inner_ref.shape[1], act_ref.shape[1]

    @pl.when(pl.program_id(0) == 0)
    def _():
        join_rows(s_rows, s_ref)

    join_rows(h_rows, h_ref)
    out_ref[:, :wide] = mm_lt(h_ref[...], inner_ref[...]).astype(BF)
    out_ref[:, wide:] = mm_lt(act_ref[...], s_ref[...]).astype(BF)


def hidden_grads(h_rows, s_rows, slope_inner, act):
    tok, width = h_rows[0].shape
    rows, hidden = act.shape
    step = 256
    cols = lambda i: (0, i)
    fixed = lambda i: (0, 0)
    return pl.pallas_call(
        hidden_grad_kernel,
        grid=(width // step,),
        in_specs=[pl.BlockSpec((tok, step), cols)] * GROUPS
        + [pl.BlockSpec((1, tok, width), lambda i: (1, 0, 0))] * GROUPS
        + [pl.BlockSpec((rows, hidden), fixed), pl.BlockSpec((rows, step), cols)],
        out_specs=pl.BlockSpec((step, hidden + width), lambda i: (i, 0)),
        out_shape=jax.ShapeDtypeStruct((width, hidden + width), BF),
        scratch_shapes=[pltpu.VMEM((rows, step), BF), pltpu.VMEM((rows, width), BF)],
        compiler_params=pltpu.CompilerParams(vmem_limit_bytes=16 * 2**20),
        cost_estimate=LONG,
    )(*in_hbm(*h_rows, *s_rows), slope_inner, act)


def visible(k, tok, keys):
    row = lax.broadcasted_iota(jnp.int32, (tok, keys), 0)
    col = lax.broadcasted_iota(jnp.int32, (tok, keys), 1)
    return col <= k * tok + row


def masked_scores(query, keys, seen):
    scores = mm_rt(query, keys)
    near = keys.shape[0] - seen.shape[1]
    last = jnp.where(seen, scores[:, near:], MASK_FILL)
    return last if near == 0 else jnp.concatenate([scores[:, :near], last], axis=1)


def attend_kernel(ks, head, place, *refs):
    pieces = refs[: GROUPS * ks]
    in_w, table = refs[GROUPS * ks : GROUPS * ks + 2]
    slots = refs[GROUPS * ks + 2 : GROUPS * ks + 2 + GROUPS]
    q_out, k_out, v_out, att_out, lse_out, h_out, hat_out, h_all = refs[GROUPS * ks + 2 + GROUPS :]
    g, k = place[0], place[1]
    tok, width = pieces[-1].shape
    cols = q_out.shape[1]
    gain, shift = table[0:1, :], table[1:2, :]
    for j in range(ks):
        for i in range(GROUPS):
            piece = pieces[j * GROUPS + i]
            hat, _ = norm_stats((piece[...] if j else piece[0]).astype(F32))
            normed = (hat * gain + shift).astype(BF)
            spot = pl.multiple_of(((g ^ i) * ks + (k ^ j)) * tok, tok)
            h_all[pl.ds(spot, tok), :] = normed
            if j == 0:
                spot = pl.multiple_of((g ^ i) * tok, tok)
                h_out[pl.ds(spot, tok), :] = normed
                hat_out[pl.ds(spot, tok), :] = hat.astype(BF)
    q_out[...] = (mm(h_out[...], in_w[:, :cols]) + table[2:3, :cols]).astype(BF)
    kv = mm(h_all[...], in_w[:, cols:])
    k_out[...] = kv[:, :cols].astype(BF)
    v_out[...] = (kv[:, cols:] + table[3:4, :cols]).astype(BF)
    seen = visible(k, tok, ks * tok)
    for h in range(cols // head):
        low, high = h * head, (h + 1) * head
        for i in range(GROUPS):
            rows = slice(i * tok, (i + 1) * tok)
            span = (i + 1) * ks * tok
            query = (q_out[rows, low:high].astype(F32) * head**-0.5).astype(BF)
            scores = masked_scores(query, k_out[:span, low:high], seen)
            peak = jnp.max(scores, axis=-1, keepdims=True)
            weights = jnp.exp(scores - peak)
            mass = jnp.sum(weights, axis=-1, keepdims=True)
            lse_out[rows, h : h + 1] = peak + jnp.log(mass)
            att = mm(weights.astype(BF), v_out[:span, low:high]) / mass
            att_out[rows, low:high] = att
    for i in range(GROUPS):
        slots[i][...] = att_out[pl.ds(pl.multiple_of((g ^ i) * tok, tok), tok), :].astype(BF)


def attend(g, k, ks, head, both, more, in_w, table):
    tok, width = both[0].shape[1:]
    cols = in_w.shape[1] // 3
    mine, rows = GROUPS * tok, GROUPS * ks * tok
    vmem = pl.BlockSpec(memory_space=pltpu.VMEM)
    shapes = [
        *[((tok, cols), BF)] * GROUPS,
        ((mine, cols), BF),
        ((rows, cols), BF),
        ((rows, cols), BF),
        ((mine, cols), F32),
        ((mine, 8), F32),
        ((mine, width), BF),
        ((mine, width), BF),
    ]
    return pl.pallas_call(
        functools.partial(attend_kernel, ks, head),
        grid_spec=pltpu.PrefetchScalarGridSpec(
            num_scalar_prefetch=1,
            in_specs=[pl.BlockSpec((1, tok, width), lambda i, place: (0, 0, 0))] * GROUPS
            + [vmem] * (len(more) + 2),
            grid=(1,),
            out_specs=[vmem] * len(shapes),
            scratch_shapes=[pltpu.VMEM((rows, width), BF)],
        ),
        out_shape=[jax.ShapeDtypeStruct(s, t) for s, t in shapes[:GROUPS]]
        + [pltpu.HBM(s, t) for s, t in shapes[GROUPS:]],
        compiler_params=pltpu.CompilerParams(vmem_limit_bytes=(16 if ks == 2 else 48) * 2**20),
        cost_estimate=SHORT,
    )(jnp.stack([g, k]).astype(jnp.int32), *both, *more, in_w, table)


def attend_back_kernel(ks, head, first, place, *refs):
    slopes = refs[:GROUPS]
    q_ref, k_ref, v_ref, att_ref, lse_ref, dq_out, dkv_out = refs[GROUPS : GROUPS + 7]
    dk_sum, dv_sum, slope_rows = refs[GROUPS + 7 :]
    g, k = place[0], place[1]
    tok = slopes[0].shape[0]
    heads = dq_out.shape[1] // head
    for i in range(GROUPS):
        slope_rows[pl.ds(pl.multiple_of((g ^ i) * tok, tok), tok), :] = slopes[i][...]
    seen = visible(k, tok, ks * tok)
    for i in reversed(range(GROUPS)):
        rows = slice(i * tok, (i + 1) * tok)
        span = (i + 1) * ks * tok
        for h in range(heads):
            low, high = (first + h) * head, (first + h + 1) * head
            to = slice(h * head, (h + 1) * head)
            query = (q_ref[rows, low:high].astype(F32) * head**-0.5).astype(BF)
            keys = k_ref[:span, low:high]
            slope = slope_rows[rows, low:high]
            scores = masked_scores(query, keys, seen)
            chances = jnp.exp(scores - lse_ref[rows, first + h : first + h + 1])
            diag = jnp.sum(slope.astype(F32) * att_ref[rows, low:high], axis=-1, keepdims=True)
            slope_chances = mm_rt(slope, v_ref[:span, low:high])
            slope_scores = (chances * (slope_chances - diag)).astype(BF)
            dq_out[rows, to] = (mm(slope_scores, keys) * head**-0.5).astype(BF)
            dk = mm_lt(slope_scores, query)
            dv = mm_lt(chances.astype(BF), slope)
            if i == GROUPS - 1:
                dk_sum[:, to] = dk
                dv_sum[:, to] = dv
            else:
                dk_sum[:span, to] += dk
                dv_sum[:span, to] += dv
    for i in range(GROUPS):
        for j in range(ks):
            spot = slice((i * ks + j) * tok, (i * ks + j + 1) * tok)
            dkv_out[k ^ j, i * tok : (i + 1) * tok, :] = jnp.concatenate(
                [dk_sum[spot, :], dv_sum[spot, :]], axis=1
            ).astype(BF)


def attend_back(g, k, ks, head, first, heads, slopes, q, keys, values, att, lse):
    tok, cols = slopes[0].shape
    mine, rows = GROUPS * tok, GROUPS * ks * tok
    wide = heads * head
    vmem = pl.BlockSpec(memory_space=pltpu.VMEM)
    return pl.pallas_call(
        functools.partial(attend_back_kernel, ks, head, first),
        grid_spec=pltpu.PrefetchScalarGridSpec(
            num_scalar_prefetch=1,
            in_specs=[vmem] * (len(slopes) + 5),
            out_specs=[vmem] * 2,
            scratch_shapes=[pltpu.VMEM((rows, wide), F32)] * 2 + [pltpu.VMEM((mine, cols), BF)],
        ),
        out_shape=[
            jax.ShapeDtypeStruct((mine, wide), BF),
            jax.ShapeDtypeStruct((ks, mine, 2 * wide), BF),
        ],
        compiler_params=pltpu.CompilerParams(vmem_limit_bytes=(16 if ks == 2 else 48) * 2**20),
        cost_estimate=LONG,
    )(jnp.stack([g, k]).astype(jnp.int32), *slopes, *in_hbm(q, keys, values, att, lse))


def project_back_kernel(ks, parts, place, *refs):
    count = len(parts)
    dq, dkv = refs[:count], refs[count : count + count * ks]
    h_ref, hat_ref, in_w = refs[count * (ks + 1) : count * (ks + 1) + 3]
    slots, (d_in, sums, project, back) = refs[-GROUPS - 4 : -4], refs[-4:]
    g = place[0]
    tok = slots[0].shape[0]
    cols = sum(parts)
    low = 0
    for n, wide in enumerate(parts):
        project[:, low : low + wide] = dq[n][...]
        both = total([dkv[n * ks + j][...] for j in range(ks)]).astype(BF)
        project[:, cols + low : cols + low + wide] = both[:, :wide]
        project[:, 2 * cols + low : 2 * cols + low + wide] = both[:, wide:]
        low += wide
    back[...] = mm_rt(project[...], in_w[...])
    for i in range(GROUPS):
        slots[i][...] = back[pl.ds(pl.multiple_of((g ^ i) * tok, tok), tok), :].astype(BF)
    sums[0:1, :] = jnp.sum(back[...] * hat_ref[...].astype(F32), axis=0, keepdims=True)
    sums[1:2, :] = jnp.sum(back[...], axis=0, keepdims=True)
    sums[2:3, : 3 * cols] = jnp.sum(project[...].astype(F32), axis=0, keepdims=True)
    d_in[...] = mm_lt(h_ref[...], project[...]).astype(BF)


def project_back(g, dq, dkv, h, hat, in_w):
    mine, width = h.shape
    parts = [part.shape[1] for part in dq]
    cols = sum(parts)
    ks = len(dkv[0])
    vmem = pl.BlockSpec(memory_space=pltpu.VMEM)
    got = pl.pallas_call(
        functools.partial(project_back_kernel, ks, parts),
        grid_spec=pltpu.PrefetchScalarGridSpec(
            num_scalar_prefetch=1,
            in_specs=[vmem] * (len(dq) * (ks + 1) + 3),
            out_specs=[vmem] * (GROUPS + 2),
            scratch_shapes=[pltpu.VMEM((mine, 3 * cols), BF), pltpu.VMEM((mine, width), F32)],
        ),
        out_shape=[jax.ShapeDtypeStruct((mine // GROUPS, width), BF)] * GROUPS
        + [
            jax.ShapeDtypeStruct((width, 3 * cols), BF),
            jax.ShapeDtypeStruct((8, width), F32),
        ],
        compiler_params=pltpu.CompilerParams(vmem_limit_bytes=16 * 2**20),
        cost_estimate=SHORT,
    )(
        jnp.stack([g]).astype(jnp.int32),
        *dq,
        *[p for pieces in dkv for p in pieces],
        *in_hbm(h, hat),
        in_w,
    )
    return got[:GROUPS], got[GROUPS], got[GROUPS + 1]


def finish_kernel(ks, extra, place, *refs):
    pieces, (in_out, out_out, vec_out, held) = refs[:-4], refs[-4:]
    own, cols = in_out.shape[1], held.shape[2]
    part, low = cols // 3, own + extra
    share = own // GROUPS
    third = share // 3
    over = out_out.shape[3] - cols
    for j in range(ks):
        for i in range(GROUPS):
            held[place[0] ^ i] = pieces[j * GROUPS + i][...].astype(F32)
        spot = place[1] ^ j
        for i in range(GROUPS):
            for n in range(3):
                to = (n * GROUPS + i) * part
                in_out[spot, :, to : to + part] = held[i, :own, n * part : (n + 1) * part]
                out_out[i, spot, n * third : (n + 1) * third, cols:] = held[
                    i, low + share :, n * over : (n + 1) * over
                ]
            out_out[i, spot, :, :cols] = held[i, low : low + share, :]
        vec_out[spot] = total([held[i, own:low, :] for i in range(GROUPS)])


def finish(pieces, own, extra, width, g, k):
    ks = len(pieces)
    tall, cols = pieces[0][0].shape
    vmem = pl.BlockSpec(memory_space=pltpu.VMEM)
    shapes = [(ks, own, GROUPS * cols), (GROUPS, ks, own // GROUPS, width), (ks, extra, cols)]
    in_w, out_w, vectors = pl.pallas_call(
        functools.partial(finish_kernel, ks, extra),
        grid_spec=pltpu.PrefetchScalarGridSpec(
            num_scalar_prefetch=1,
            in_specs=[vmem] * (ks * GROUPS),
            out_specs=[vmem] * 3,
            scratch_shapes=[pltpu.VMEM((GROUPS, tall, cols), F32)],
        ),
        out_shape=[jax.ShapeDtypeStruct(s, F32) for s in shapes],
        compiler_params=pltpu.CompilerParams(vmem_limit_bytes=16 * 2**20),
        cost_estimate=SHORT,
    )(jnp.stack([g, k]).astype(jnp.int32), *[p for group in pieces for p in group])
    return in_w.reshape(ks * own, -1), out_w.reshape(ks * own, width), vectors.reshape(-1)


def shards(
    inputs,
    cotangent,
    first_gain,
    first_shift,
    input_weight,
    query_bias,
    value_bias,
    output_weight,
    output_bias,
    second_gain,
    second_shift,
    expand_weight,
    expand_bias,
    contract_weight,
    contract_bias,
):
    tok, width = inputs.shape[1:]
    ks, zs = lax.axis_size("core"), lax.axis_size("fsdp")
    g, k, z = lax.axis_index("grp"), lax.axis_index("core"), lax.axis_index("fsdp")
    rows_z = width // zs
    heads_here = HEADS // GROUPS
    head = width // HEADS
    cols = width // GROUPS
    ff = expand_weight.shape[1]
    ff_z = ff // zs
    ff_g = ff_z // GROUPS
    mine = GROUPS * tok
    scale = head ** (-0.5)

    x_own = inputs[0]
    slope_own = cotangent[0]

    smalls = [first_gain, first_shift, query_bias, value_bias, output_bias]
    smalls += [second_gain, second_shift, contract_bias, expand_bias]
    own = rows_z // ks
    aligned = own % 48 == 0 and zs == GROUPS
    if aligned:
        cut = cut_first(input_weight, output_weight, smalls, g, k, ks)
    else:
        cut = cut_weight(input_weight, 3, g, k, ks)
    pieces = gather_flips(cut, "fsdp")
    rows_both = gather_flips(jnp.concatenate([inputs, cotangent]), "grp")
    rest = cut_rest(contract_weight, expand_weight, zs, g, k, ks)
    pieces, rows_both, rest = lax.optimization_barrier((pieces, rows_both, rest))
    x_more = [send(b[0], "core", j) for j in range(1, ks) for b in rows_both]
    more = [[send(b, "core", j) for b in pieces] for j in range(1, ks)]
    if aligned:
        table = vector_table(pieces, own, rows_z, width, g, z)
        in_w, out_w = both_weights([pieces] + more, g, z, k, own, width)
    else:
        in_w = assemble([pieces] + more, z, k, own).reshape(width, 3 * cols)
        out_w = gather_flips(pick(output_weight.reshape(ks, own, width), k), "fsdp")
        out_more = [[send(b, "core", j) for b in out_w] for j in range(1, ks)]
        out_w = assemble([out_w] + out_more, z, k, own).reshape(GROUPS, cols, width)
        out_w = jnp.concatenate([pick(out_w, g ^ i) for i in range(GROUPS)])
        got = in_order(gather_flips(jnp.concatenate(smalls), "fsdp"), z).astype(F32)
        vectors = [got[:, i * rows_z : (i + 1) * rows_z].reshape(width) for i in range(8)]
        for i in (2, 3):
            vectors[i] = jnp.tile(pick(vectors[i].reshape(GROUPS, cols), g), GROUPS)
        got = got[:, 8 * rows_z :].reshape(zs, GROUPS, ff_g)
        vectors.append(lax.dynamic_index_in_dim(got, g, axis=1, keepdims=False).reshape(width))
        table = jnp.pad(jnp.stack(vectors), ((0, 7), (0, 0)))
    o_bias, gain_two, shift_two, c_bias = [table[i : i + 1] for i in range(4, 8)]

    rest = lax.all_gather(rest, ("fsdp", "core"), axis=0, tiled=True)

    *slots, qs, keys, values, att_full, lse, h1, hat_one = attend(
        g, k, ks, head, rows_both, x_more, in_w, table
    )
    att = jnp.concatenate(swap_flips(slots, "grp"), axis=1)
    x_f = x_own.astype(F32)
    middle = x_f + mm(att, out_w) + o_bias
    hat_two, rate_two = norm_stats(middle)
    h2 = (hat_two * gain_two + shift_two).astype(BF)
    h2_rows = gather_flips(h2, "grp")

    act, slope_inner, sh2_part, out_part, d_exp_b = hidden_part(
        h2_rows, rows_both, rest, table
    )
    sh2 = swap_flips(sh2_part, "grp")
    d_hidden = hidden_grads(h2_rows, rows_both, slope_inner, act)
    sh2, d_hidden = lax.optimization_barrier((sh2, d_hidden))
    sh2 = total(sh2)
    d_hidden = lax.psum_scatter(d_hidden, ("fsdp", "core"), scatter_dimension=0, tiled=True)

    slope_f = slope_own.astype(F32)
    d_gain_two = jnp.sum(sh2 * hat_two, axis=0, keepdims=True)
    d_shift_two = jnp.sum(sh2, axis=0, keepdims=True)
    slope_middle = slope_f + norm_back(sh2, gain_two, hat_two, rate_two)
    slope_branch = slope_middle.astype(BF)
    slope_att = mm_rt(slope_branch, out_w).astype(BF)
    datt = swap_flips([slope_att[:, i * cols : (i + 1) * cols] for i in range(GROUPS)], "grp")

    datt, slope_late, out_part = lax.optimization_barrier((datt, slope_branch, out_part))
    out_sum = swap_flips(out_part, "grp")
    d_out = mm_lt(att, slope_late).astype(BF).reshape(GROUPS, cols, width)
    d_out = in_order([d_out[i] for i in range(GROUPS)], g)
    d_out = d_out.reshape(zs, GROUPS, ks, own // GROUPS, width)
    pieces = [lax.dynamic_index_in_dim(d_out, k ^ j, axis=2, keepdims=False) for j in range(ks)]
    datt, pieces = lax.optimization_barrier((datt, pieces))
    d_out = swap_flips(pieces, "core")

    kept = (qs, keys, values, att_full, lse)
    split = (heads_here + 1) // 2
    dq, dkv = attend_back(g, k, ks, head, 0, split, datt, *kept)
    dq, dkv = [dq], [swap_flips([dkv[j] for j in range(ks)], "core")]
    datt, d_out, out_sum = lax.optimization_barrier((datt, d_out, out_sum))
    d_out = total(d_out).astype(BF)
    pieces = [lax.dynamic_index_in_dim(d_out, g ^ i, axis=1, keepdims=False) for i in range(GROUPS)]
    datt, pieces = lax.optimization_barrier((datt, pieces))
    d_out = swap_flips(pieces, "grp")
    more = attend_back(g, k, ks, head, split, heads_here - split, datt, *kept)
    dq.append(more[0])
    dkv.append(swap_flips([more[1][j] for j in range(ks)], "core"))
    sh1_part, d_in, sums = project_back(g, dq, dkv, h1, hat_one, in_w)
    sh1, d_hidden = lax.optimization_barrier((swap_flips(sh1_part, "grp"), d_hidden))
    sh1 = total(sh1)
    hat_own, rate_own = norm_stats(x_f)
    delta_inputs = (slope_middle + norm_back(sh1, table[0:1], hat_own, rate_own)).astype(BF)[None]

    extra = -(-(12 * rows_z) // (3 * cols * ks))
    packed = pack_vectors(
        g,
        zs,
        extra * ks,
        rows_z,
        sums,
        jnp.sum(slope_branch.astype(F32), axis=0, keepdims=True),
        d_gain_two,
        d_shift_two,
        jnp.sum(slope_f, axis=0, keepdims=True),
        d_exp_b,
    )
    d_out = total(d_out).astype(BF)
    third = d_out.shape[1] // 3
    tail = d_out[..., 3 * cols :]
    tail = [tail[:, i * third : (i + 1) * third] for i in range(3)]
    d_out = jnp.concatenate([d_out[..., : 3 * cols], jnp.concatenate(tail, axis=2)], axis=1)
    d_in = jnp.concatenate(
        [
            d_in.reshape(zs, ks, own, 3 * cols),
            packed.astype(BF).reshape(zs, ks, extra, 3 * cols),
        ],
        axis=2,
    )
    pieces = [lax.dynamic_index_in_dim(d_in, k ^ j, axis=1, keepdims=False) for j in range(ks)]
    d_in = total(swap_flips(pieces, "core")).astype(BF)
    d_in = jnp.concatenate([d_in, d_out], axis=1)
    pieces = lax.optimization_barrier([pick(d_in, z ^ i) for i in range(zs)])
    d_in = swap_flips(pieces, "fsdp")
    d_hidden = gather_flips(d_hidden, "grp")
    d_in = gather_flips(total(d_in).astype(BF), "grp")
    d_hidden = [d_hidden] + [[send(p, "core", j) for p in d_hidden] for j in range(1, ks)]
    d_exp_w, d_con_w = unfold(d_hidden, zs, g, k)
    d_in, d_exp_w, d_con_w = lax.optimization_barrier((d_in, d_exp_w, d_con_w))
    outputs = (middle + total(out_sum) + c_bias).astype(BF)[None]
    d_in = [d_in] + [[send(p, "core", j) for p in d_in] for j in range(1, ks)]
    d_in_w, d_out_w, packed = finish(d_in, own, extra, width, g, k)

    def vec(i):
        return packed[i * rows_z : (i + 1) * rows_z]

    return (
        outputs,
        delta_inputs,
        vec(0),
        vec(1),
        d_in_w,
        vec(2),
        vec(3),
        d_out_w,
        vec(4),
        vec(5),
        vec(6),
        d_exp_w,
        packed[8 * rows_z : 8 * rows_z + ff_z],
        d_con_w,
        vec(7),
    )


def solution(mesh):
    ctx, zs = mesh.shape["ctx"], mesh.shape["fsdp"]
    axes = ("grp", "core", "fsdp")
    split = Mesh(mesh.devices.reshape(GROUPS, ctx // GROUPS, zs), axes)
    row, vec, mat = P("fsdp", ("grp", "core"), None), P("fsdp"), P("fsdp", None)
    placed = (row, row, vec, vec, mat, vec, vec, mat, vec, vec, vec, mat, vec, mat, vec)
    return jax.shard_map(
        shards,
        mesh=split,
        in_specs=placed,
        out_specs=placed,
        check_vma=False,
    )
```

```python
import functools

import jax
import jax.numpy as jnp
from jax import lax
from jax.experimental import pallas as pl
from jax.experimental.pallas import tpu as pltpu
from jax.sharding import Mesh, PartitionSpec as P

HEADS = 12
GROUPS = 4

NORM_EPS = 1e-05
MASK_FILL = -1e30
GELU_COEF = 0.7978845608028654
GELU_CUBE = 0.044715

SHORT = pl.CostEstimate(flops=1, bytes_accessed=1, transcendentals=0)
LONG = pl.CostEstimate(flops=8 * 10**9, bytes_accessed=1, transcendentals=0)

BF = jnp.bfloat16
F32 = jnp.float32


def in_hbm(*values):
    return [pltpu.with_memory_space_constraint(v, pltpu.HBM) for v in values]


def mm(left, right):
    return jnp.dot(left, right, preferred_element_type=F32)


def mm_lt(left, right):
    return lax.dot_general(left, right, (((0,), (0,)), ((), ())), preferred_element_type=F32)


def mm_rt(left, right):
    return lax.dot_general(left, right, (((1,), (1,)), ((), ())), preferred_element_type=F32)


def send(value, axis, flip):
    count = lax.axis_size(axis)
    return lax.ppermute(value, axis, [(s, s ^ flip) for s in range(count)])


def gather_flips(value, axis):
    return swap_flips([value] * lax.axis_size(axis), axis)


def swap_flips(pieces, axis):
    return [pieces[0]] + [send(p, axis, i) for i, p in enumerate(pieces) if i]


def pick(stacked, place):
    return lax.dynamic_index_in_dim(stacked, place, axis=0, keepdims=False)


def in_order(pieces, me):
    stacked = jnp.stack(pieces)
    return jnp.stack([pick(stacked, me ^ j) for j in range(len(pieces))])


def norm_stats(values):
    center = values - jnp.mean(values, axis=-1, keepdims=True)
    spread = jnp.mean(center * center, axis=-1, keepdims=True)
    rate = lax.rsqrt(spread + NORM_EPS)
    return center * rate, rate


def norm_back(slope, gain, hat, rate):
    scaled = slope * gain
    return rate * (
        scaled
        - jnp.mean(scaled, axis=-1, keepdims=True)
        - hat * jnp.mean(scaled * hat, axis=-1, keepdims=True)
    )


def total(parts):
    out = parts[0].astype(F32)
    for part in parts[1:]:
        out = out + part.astype(F32)
    return out


def cut_columns(source, cut, parts, i):
    wide = cut.shape[1] // parts
    for part in range(parts):
        low = (part * GROUPS + i) * wide
        cut[:, part * wide : (part + 1) * wide] = source[:, low : low + wide]


def cut_kernel(parts, place, source, cut):
    for i in range(GROUPS):

        @pl.when(place[0] == i)
        def _():
            cut_columns(source, cut, parts, i)


def cut_weight(weight, parts, g, k, ks):
    rows = weight.shape[0] // ks
    cols = weight.shape[1] // GROUPS
    if rows % 16 == 0:
        return pl.pallas_call(
            functools.partial(cut_kernel, parts),
            grid_spec=pltpu.PrefetchScalarGridSpec(
                num_scalar_prefetch=1,
                grid=(1,),
                in_specs=[pl.BlockSpec((rows, weight.shape[1]), lambda i, place: (place[1], 0))],
                out_specs=pl.BlockSpec((rows, cols), lambda i, place: (0, 0)),
            ),
            out_shape=jax.ShapeDtypeStruct((rows, cols), BF),
            compiler_params=pltpu.CompilerParams(vmem_limit_bytes=8 * 2**20),
        )(jnp.stack([g, k]).astype(jnp.int32), weight)
    half = pick(weight.reshape(ks, rows, -1), k)
    return lax.dynamic_index_in_dim(
        half.reshape(rows, parts, GROUPS, cols // parts), g, axis=2, keepdims=False
    ).reshape(rows, cols)


def cut_first_kernel(place, *refs):
    source, other, vectors, cut, held = refs[0], refs[1], refs[2:-2], refs[-2], refs[-1]
    rows = source.shape[0]
    third, cols = rows // 3, cut.shape[1]
    cut[rows + 16 : 2 * rows + 16, :] = other[:, :cols]
    over = other.shape[1] - cols
    for part in range(3):
        cut[2 * rows + 16 :, part * over : (part + 1) * over] = other[
            part * third : (part + 1) * third, cols:
        ]
    unit = vectors[0].shape[0]
    per = cut.shape[1] // unit
    held[...] = jnp.zeros_like(held)
    spot = 0
    for vector in vectors:
        row = vector[...].astype(F32).reshape(1, vector.shape[0])
        for part in range(vector.shape[0] // unit):
            col = spot % per * unit
            held[spot // per : spot // per + 1, col : col + unit] = row[
                :, part * unit : (part + 1) * unit
            ]
            spot += 1
    cut[rows : rows + 16, :] = held[...].astype(BF)
    for i in range(GROUPS):

        @pl.when(place[0] == i)
        def _():
            cut_columns(source, cut.at[:rows, :], 3, i)


def cut_first(weight, other, vectors, g, k, ks):
    rows, cols = weight.shape[0] // ks, weight.shape[1] // GROUPS
    tall = 2 * rows + 16 + rows // 3
    by_k = lambda i, place: (place[1], 0)
    return pl.pallas_call(
        cut_first_kernel,
        grid_spec=pltpu.PrefetchScalarGridSpec(
            num_scalar_prefetch=1,
            grid=(1,),
            in_specs=[
                pl.BlockSpec((rows, weight.shape[1]), by_k),
                pl.BlockSpec((rows, other.shape[1]), by_k),
            ]
            + [pl.BlockSpec(v.shape, lambda i, place: (0,)) for v in vectors],
            out_specs=pl.BlockSpec((tall, cols), lambda i, place: (0, 0)),
            scratch_shapes=[pltpu.VMEM((16, cols), F32)],
        ),
        out_shape=jax.ShapeDtypeStruct((tall, cols), BF),
        compiler_params=pltpu.CompilerParams(vmem_limit_bytes=8 * 2**20),
        cost_estimate=SHORT,
    )(jnp.stack([g, k]).astype(jnp.int32), *in_hbm(weight, other, *vectors))


def both_weights_kernel(rows, place, *refs):
    pieces, in_w, out_w = refs[:-2], refs[-2], refs[-1]
    zs, ks = in_w.shape[:2]
    third, cols = rows // 3, in_w.shape[3]
    over = out_w.shape[3] - cols
    low = rows + 16
    for j in range(ks):
        for i in range(zs):
            piece = pieces[j * zs + i]
            in_w[place[1] ^ i, place[2] ^ j] = piece[:rows, :]
            spot = (place[1] ^ i ^ place[0], place[2] ^ j)
            out_w[spot[0], spot[1], :, :cols] = piece[low : low + rows, :]
            for part in range(3):
                out_w[spot[0], spot[1], part * third : (part + 1) * third, cols:] = piece[
                    low + rows :, part * over : (part + 1) * over
                ]


def both_weights(pieces, g, z, k, rows, width):
    ks, zs = len(pieces), len(pieces[0])
    cols = pieces[0][0].shape[1]
    vmem = pl.BlockSpec(memory_space=pltpu.VMEM)
    shapes = [(zs, ks, rows, cols), (zs, ks, rows, width)]
    in_w, out_w = pl.pallas_call(
        functools.partial(both_weights_kernel, rows),
        grid_spec=pltpu.PrefetchScalarGridSpec(
            num_scalar_prefetch=1, in_specs=[vmem] * (zs * ks), out_specs=[vmem] * 2
        ),
        out_shape=[jax.ShapeDtypeStruct(s, BF) for s in shapes],
        compiler_params=pltpu.CompilerParams(vmem_limit_bytes=16 * 2**20),
        cost_estimate=SHORT,
    )(jnp.stack([g, z, k]).astype(jnp.int32), *[p for group in pieces for p in group])
    return in_w.reshape(width, cols), out_w.reshape(width, width)


def table_kernel(unit, place, *refs):
    pieces, out, held = refs[:-2], refs[-2], refs[-1]
    zs = len(pieces)
    per = held.shape[2] // unit
    cols = out.shape[1] // GROUPS
    for i, piece in enumerate(pieces):
        held[place[1] ^ i] = piece[...].astype(F32)

    def unpack(row, slot):
        for zz in range(zs):
            col = slot % per * unit
            out[row : row + 1, zz * unit : (zz + 1) * unit] = held[
                zz, slot // per : slot // per + 1, col : col + unit
            ]

    out[...] = jnp.zeros_like(out)
    for slot in range(8):
        unpack(slot + 8 if slot in (2, 3) else slot, slot)
    for i in range(GROUPS):

        @pl.when(place[0] == i)
        def _():
            unpack(8, 8 + i)
            out[2:4, :cols] = out[10:12, i * cols : (i + 1) * cols]


def vector_table(pieces, below, unit, width, g, z):
    cols = pieces[0].shape[1]
    return pl.pallas_call(
        functools.partial(table_kernel, unit),
        grid_spec=pltpu.PrefetchScalarGridSpec(
            num_scalar_prefetch=1,
            grid=(1,),
            in_specs=[pl.BlockSpec((16, cols), lambda i, place: (below // 16, 0))] * len(pieces),
            out_specs=pl.BlockSpec((16, width), lambda i, place: (0, 0)),
            scratch_shapes=[pltpu.VMEM((len(pieces), 16, cols), F32)],
        ),
        out_shape=jax.ShapeDtypeStruct((16, width), F32),
        compiler_params=pltpu.CompilerParams(vmem_limit_bytes=8 * 2**20),
    )(jnp.stack([g, z]).astype(jnp.int32), *pieces)


def pack_kernel(zs, stride, unit, place, sums, out_bias, gain, shift, con_bias, exp_bias, out):
    per = out.shape[1] // unit
    cols = out.shape[1] // 3

    def put(zz, slot, value):
        row, col = zz * stride + slot // per, slot % per * unit
        out[row : row + 1, col : col + unit] = value

    out[...] = jnp.zeros_like(out)
    whole = [(0, sums, 0), (1, sums, 1), (4, out_bias, 0), (5, gain, 0), (6, shift, 0), (7, con_bias, 0)]
    for slot, source, row in whole:
        for zz in range(zs):
            put(zz, slot, source[row : row + 1, zz * unit : (zz + 1) * unit])
    for i in range(GROUPS):

        @pl.when(place[0] == i)
        def _():
            for zz in range(zs):
                put(zz, 8 + i, exp_bias[:, zz * unit : (zz + 1) * unit])
            for part in range(cols // unit):
                zz = i * cols // unit + part
                low = part * unit
                put(zz, 2, sums[2:3, low : low + unit])
                put(zz, 3, sums[2:3, 2 * cols + low : 2 * cols + low + unit])


def pack_vectors(g, zs, stride, unit, sums, *vectors):
    wide = 3 * (vectors[0].shape[1] // GROUPS)
    vmem = pl.BlockSpec(memory_space=pltpu.VMEM)
    return pl.pallas_call(
        functools.partial(pack_kernel, zs, stride, unit),
        grid_spec=pltpu.PrefetchScalarGridSpec(
            num_scalar_prefetch=1, in_specs=[vmem] * (1 + len(vectors)), out_specs=vmem
        ),
        out_shape=jax.ShapeDtypeStruct((zs * stride, wide), F32),
        compiler_params=pltpu.CompilerParams(vmem_limit_bytes=8 * 2**20),
    )(jnp.stack([g]).astype(jnp.int32), sums, *vectors)


def cut_rest_kernel(parts, place, con_ref, exp_ref, cut):
    width = con_ref.shape[1]
    cut[:, :width] = con_ref[...]
    for i in range(GROUPS):

        @pl.when(place[0] == i)
        def _():
            cut_columns(exp_ref, cut.at[:, width:], parts, i)


def cut_rest(con_w, exp_w, parts, g, k, ks):
    width = con_w.shape[1]
    rows, ff_rows = exp_w.shape[0] // ks, con_w.shape[0] // (GROUPS * ks)
    wide = exp_w.shape[1] // GROUPS
    if rows % 16 == 0 and rows == ff_rows:
        return pl.pallas_call(
            functools.partial(cut_rest_kernel, parts),
            grid_spec=pltpu.PrefetchScalarGridSpec(
                num_scalar_prefetch=1,
                grid=(1,),
                in_specs=[
                    pl.BlockSpec((rows, width), lambda i, place: (place[0] * ks + place[1], 0)),
                    pl.BlockSpec((rows, exp_w.shape[1]), lambda i, place: (place[1], 0)),
                ],
                out_specs=pl.BlockSpec((rows, width + wide), lambda i, place: (0, 0)),
            ),
            out_shape=jax.ShapeDtypeStruct((rows, width + wide), BF),
            compiler_params=pltpu.CompilerParams(vmem_limit_bytes=8 * 2**20),
        )(jnp.stack([g, k]).astype(jnp.int32), *in_hbm(con_w, exp_w))
    return jnp.concatenate(
        [
            pick(con_w.reshape(GROUPS * ks, ff_rows, width), g * ks + k),
            cut_weight(exp_w, parts, g, k, ks),
        ],
        axis=1,
    )


def assemble_kernel(rows, place, *refs):
    pieces, out = refs[:-1], refs[-1]
    zs = out.shape[0]
    for j in range(out.shape[1]):
        for i in range(zs):
            out[place[0] ^ i, place[1] ^ j] = pieces[j * zs + i][:rows, :]


def assemble(pieces, first, k, rows):
    ks, zs = len(pieces), len(pieces[0])
    cols = pieces[0][0].shape[1]
    shape = (zs, ks, rows, cols)
    if rows % 16:
        parts = [in_order([p[:rows] for p in group], first) for group in pieces]
        return jnp.stack(in_order(parts, k), axis=1).reshape(zs, ks * rows, cols)
    vmem = pl.BlockSpec(memory_space=pltpu.VMEM)
    out = pl.pallas_call(
        functools.partial(assemble_kernel, rows),
        grid_spec=pltpu.PrefetchScalarGridSpec(
            num_scalar_prefetch=1, in_specs=[vmem] * (zs * ks), out_specs=vmem
        ),
        out_shape=jax.ShapeDtypeStruct(shape, BF),
        compiler_params=pltpu.CompilerParams(vmem_limit_bytes=8 * 2**20),
        cost_estimate=SHORT,
    )(jnp.stack([first, k]).astype(jnp.int32), *[p for group in pieces for p in group])
    return out.reshape(zs, ks * rows, cols)


def unfold_kernel(parts, ks, place, *refs):
    pieces, (exp_out, con_out, held) = refs[: GROUPS + ks - 1], refs[-3:]
    wide = con_out.shape[3]
    part_wide = wide // parts
    for j in range(ks):
        for i in range(GROUPS):
            held[place[0] ^ i] = pieces[GROUPS + j - 1][i] if j else pieces[i][...]
        spot = place[1] ^ j
        for i in range(GROUPS):
            con_out[i, spot] = held[i, :, wide:].astype(F32)
            for part in range(parts):
                low = (part * GROUPS + i) * part_wide
                exp_out[spot, :, low : low + part_wide] = held[
                    i, :, part * part_wide : (part + 1) * part_wide
                ].astype(F32)


def unfold(pieces, more, parts, g, k):
    ks = len(more) + 1
    rows, wide = pieces[0].shape[0], pieces[0].shape[1] // 2
    step = rows // 2 if rows % 32 == 0 else rows
    shapes = [(ks, rows, GROUPS * wide), (GROUPS, ks, rows, wide)]
    exp, con = pl.pallas_call(
        functools.partial(unfold_kernel, parts, ks),
        grid_spec=pltpu.PrefetchScalarGridSpec(
            num_scalar_prefetch=1,
            grid=(rows // step,),
            in_specs=[pl.BlockSpec((step, 2 * wide), lambda i, place: (i, 0))] * GROUPS
            + [pl.BlockSpec((GROUPS, step, 2 * wide), lambda i, place: (0, i, 0))] * (ks - 1),
            out_specs=[
                pl.BlockSpec((ks, step, GROUPS * wide), lambda i, place: (0, i, 0)),
                pl.BlockSpec((GROUPS, ks, step, wide), lambda i, place: (0, 0, i, 0)),
            ],
            scratch_shapes=[pltpu.VMEM((GROUPS, step, 2 * wide), BF)],
        ),
        out_shape=[jax.ShapeDtypeStruct(s, F32) for s in shapes],
        compiler_params=pltpu.CompilerParams(vmem_limit_bytes=20 * 2**20),
        cost_estimate=SHORT,
    )(jnp.stack([g, k]).astype(jnp.int32), *pieces, *more)
    return exp.reshape(ks * rows, -1), con.reshape(-1, wide)


def join_rows(pieces, joined):
    tok = joined.shape[0] // GROUPS
    for i, piece in enumerate(pieces):
        joined[i * tok : (i + 1) * tok, :] = piece[...].reshape(tok, joined.shape[1])


def hidden_kernel(*refs):
    h_rows, s_rows = refs[:GROUPS], refs[GROUPS : 2 * GROUPS]
    exp_w, con_w, bias, act_ref, inner_ref = refs[2 * GROUPS : 2 * GROUPS + 5]
    back_ref = refs[2 * GROUPS + 5 : 3 * GROUPS + 5]
    out_ref = refs[3 * GROUPS + 5 : 4 * GROUPS + 5]
    bias_ref = refs[4 * GROUPS + 5]
    h_ref, s_ref, back_sum, out_sum = refs[-4:]
    step = pl.program_id(0)
    tok = h_rows[0].shape[0]

    @pl.when(step == 0)
    def _():
        join_rows(h_rows, h_ref)
        join_rows(s_rows, s_ref)

    inner = mm(h_ref[...], exp_w[...]) + bias[8:9, :]
    square = inner * inner
    tanh = jnp.tanh(GELU_COEF * (inner + GELU_CUBE * square * inner))
    half = 0.5 + 0.5 * tanh
    act = (inner * half).astype(BF)
    gelu_slope = half + (0.5 * GELU_COEF) * inner * (1.0 - tanh * tanh) * (
        1.0 + (3.0 * GELU_CUBE) * square
    )
    slope = (mm_rt(s_ref[...], con_w[...]) * gelu_slope).astype(BF)
    act_ref[...] = act
    inner_ref[...] = slope
    bias_ref[...] = jnp.sum(slope.astype(F32), axis=0, keepdims=True)
    back = mm_rt(slope, exp_w[...])
    out = mm(act, con_w[...])

    @pl.when(step == 0)
    def _():
        back_sum[...] = back
        out_sum[...] = out

    @pl.when(step > 0)
    def _():
        back_sum[...] += back
        out_sum[...] += out

    @pl.when(step == pl.num_programs(0) - 1)
    def _():
        for i in range(GROUPS):
            back_ref[i][...] = back_sum[i * tok : (i + 1) * tok, :].astype(BF)
            out_ref[i][...] = out_sum[i * tok : (i + 1) * tok, :].astype(BF)


def hidden_part(h_rows, s_rows, weights, table):
    tok, width = h_rows[0].shape
    hidden = weights.shape[1] - width
    rows = GROUPS * tok
    step = 256
    fixed = lambda i: (0, 0)
    cols = lambda i: (0, i)
    slots = [pl.BlockSpec((tok, width), fixed)] * GROUPS
    got = pl.pallas_call(
        hidden_kernel,
        grid=(hidden // step,),
        in_specs=[pl.BlockSpec((tok, width), fixed)] * GROUPS
        + [pl.BlockSpec((1, tok, width), lambda i: (1, 0, 0))] * GROUPS
        + [
            pl.BlockSpec((width, step), lambda i: (0, width // step + i)),
            pl.BlockSpec((step, width), lambda i: (i, 0)),
            pl.BlockSpec((16, step), cols),
        ],
        out_specs=[
            pl.BlockSpec((rows, step), cols),
            pl.BlockSpec((rows, step), cols),
            *slots,
            *slots,
            pl.BlockSpec((1, step), cols),
        ],
        out_shape=[
            jax.ShapeDtypeStruct((rows, hidden), BF),
            jax.ShapeDtypeStruct((rows, hidden), BF),
            *[jax.ShapeDtypeStruct((tok, width), BF)] * GROUPS,
            *[pltpu.HBM((tok, width), BF)] * GROUPS,
            jax.ShapeDtypeStruct((1, hidden), F32),
        ],
        scratch_shapes=[pltpu.VMEM((rows, width), BF)] * 2 + [pltpu.VMEM((rows, width), F32)] * 2,
        compiler_params=pltpu.CompilerParams(vmem_limit_bytes=24 * 2**20),
        cost_estimate=SHORT,
    )(*in_hbm(*h_rows, *s_rows, weights, weights), table)
    return got[0], got[1], got[2 : 2 + GROUPS], got[2 + GROUPS : 2 + 2 * GROUPS], got[-1]


def hidden_grad_kernel(*refs):
    h_rows, s_rows = refs[:GROUPS], refs[GROUPS : 2 * GROUPS]
    inner_ref, act_ref, out_ref, h_ref, s_ref = refs[2 * GROUPS :]
    wide, step = inner_ref.shape[1], act_ref.shape[1]

    @pl.when(pl.program_id(0) == 0)
    def _():
        join_rows(s_rows, s_ref)

    join_rows(h_rows, h_ref)
    out_ref[:, :wide] = mm_lt(h_ref[...], inner_ref[...]).astype(BF)
    out_ref[:, wide:] = mm_lt(act_ref[...], s_ref[...]).astype(BF)


def hidden_grads(h_rows, s_rows, slope_inner, act):
    tok, width = h_rows[0].shape
    rows, hidden = act.shape
    step = 256
    cols = lambda i: (0, i)
    fixed = lambda i: (0, 0)
    return pl.pallas_call(
        hidden_grad_kernel,
        grid=(width // step,),
        in_specs=[pl.BlockSpec((tok, step), cols)] * GROUPS
        + [pl.BlockSpec((1, tok, width), lambda i: (1, 0, 0))] * GROUPS
        + [pl.BlockSpec((rows, hidden), fixed), pl.BlockSpec((rows, step), cols)],
        out_specs=pl.BlockSpec((step, hidden + width), lambda i: (i, 0)),
        out_shape=jax.ShapeDtypeStruct((width, hidden + width), BF),
        scratch_shapes=[pltpu.VMEM((rows, step), BF), pltpu.VMEM((rows, width), BF)],
        compiler_params=pltpu.CompilerParams(vmem_limit_bytes=16 * 2**20),
        cost_estimate=LONG,
    )(*in_hbm(*h_rows, *s_rows), slope_inner, act)


def visible(k, tok, keys):
    row = lax.broadcasted_iota(jnp.int32, (tok, keys), 0)
    col = lax.broadcasted_iota(jnp.int32, (tok, keys), 1)
    return col <= k * tok + row


def masked_scores(query, keys, seen):
    scores = mm_rt(query, keys)
    near = keys.shape[0] - seen.shape[1]
    last = jnp.where(seen, scores[:, near:], MASK_FILL)
    return last if near == 0 else jnp.concatenate([scores[:, :near], last], axis=1)


def attend_kernel(ks, head, place, *refs):
    pieces = refs[: GROUPS * ks]
    in_w, table = refs[GROUPS * ks : GROUPS * ks + 2]
    slots = refs[GROUPS * ks + 2 : GROUPS * ks + 2 + GROUPS]
    q_out, k_out, v_out, att_out, lse_out, h_out, hat_out, h_all = refs[GROUPS * ks + 2 + GROUPS :]
    g, k = place[0], place[1]
    tok, width = pieces[-1].shape
    cols = q_out.shape[1]
    gain, shift = table[0:1, :], table[1:2, :]
    for j in range(ks):
        for i in range(GROUPS):
            piece = pieces[j * GROUPS + i]
            hat, _ = norm_stats((piece[...] if j else piece[0]).astype(F32))
            normed = (hat * gain + shift).astype(BF)
            spot = pl.multiple_of(((g ^ i) * ks + (k ^ j)) * tok, tok)
            h_all[pl.ds(spot, tok), :] = normed
            if j == 0:
                spot = pl.multiple_of((g ^ i) * tok, tok)
                h_out[pl.ds(spot, tok), :] = normed
                hat_out[pl.ds(spot, tok), :] = hat.astype(BF)
    q_out[...] = (mm(h_out[...], in_w[:, :cols]) + table[2:3, :cols]).astype(BF)
    kv = mm(h_all[...], in_w[:, cols:])
    k_out[...] = kv[:, :cols].astype(BF)
    v_out[...] = (kv[:, cols:] + table[3:4, :cols]).astype(BF)
    seen = visible(k, tok, ks * tok)
    for h in range(cols // head):
        low, high = h * head, (h + 1) * head
        for i in range(GROUPS):
            rows = slice(i * tok, (i + 1) * tok)
            span = (i + 1) * ks * tok
            query = (q_out[rows, low:high].astype(F32) * head**-0.5).astype(BF)
            scores = masked_scores(query, k_out[:span, low:high], seen)
            peak = jnp.max(scores, axis=-1, keepdims=True)
            weights = jnp.exp(scores - peak)
            mass = jnp.sum(weights, axis=-1, keepdims=True)
            lse_out[rows, h : h + 1] = peak + jnp.log(mass)
            att = mm(weights.astype(BF), v_out[:span, low:high]) / mass
            att_out[rows, low:high] = att
    for i in range(GROUPS):
        slots[i][...] = att_out[pl.ds(pl.multiple_of((g ^ i) * tok, tok), tok), :].astype(BF)


def attend(g, k, ks, head, both, more, in_w, table):
    tok, width = both[0].shape[1:]
    cols = in_w.shape[1] // 3
    mine, rows = GROUPS * tok, GROUPS * ks * tok
    vmem = pl.BlockSpec(memory_space=pltpu.VMEM)
    shapes = [
        *[((tok, cols), BF)] * GROUPS,
        ((mine, cols), BF),
        ((rows, cols), BF),
        ((rows, cols), BF),
        ((mine, cols), F32),
        ((mine, 8), F32),
        ((mine, width), BF),
        ((mine, width), BF),
    ]
    return pl.pallas_call(
        functools.partial(attend_kernel, ks, head),
        grid_spec=pltpu.PrefetchScalarGridSpec(
            num_scalar_prefetch=1,
            in_specs=[pl.BlockSpec((1, tok, width), lambda i, place: (0, 0, 0))] * GROUPS
            + [vmem] * (len(more) + 2),
            grid=(1,),
            out_specs=[vmem] * len(shapes),
            scratch_shapes=[pltpu.VMEM((rows, width), BF)],
        ),
        out_shape=[jax.ShapeDtypeStruct(s, t) for s, t in shapes[:GROUPS]]
        + [pltpu.HBM(s, t) for s, t in shapes[GROUPS:]],
        compiler_params=pltpu.CompilerParams(vmem_limit_bytes=(16 if ks == 2 else 48) * 2**20),
        cost_estimate=SHORT,
    )(jnp.stack([g, k]).astype(jnp.int32), *both, *more, in_w, table)


def attend_back_kernel(ks, head, first, place, *refs):
    slopes = refs[:GROUPS]
    q_ref, k_ref, v_ref, att_ref, lse_ref, dq_out, dkv_out = refs[GROUPS : GROUPS + 7]
    dk_sum, dv_sum, slope_rows = refs[GROUPS + 7 :]
    g, k = place[0], place[1]
    tok = slopes[0].shape[0]
    heads = dq_out.shape[1] // head
    for i in range(GROUPS):
        slope_rows[pl.ds(pl.multiple_of((g ^ i) * tok, tok), tok), :] = slopes[i][...]
    seen = visible(k, tok, ks * tok)
    for i in reversed(range(GROUPS)):
        rows = slice(i * tok, (i + 1) * tok)
        span = (i + 1) * ks * tok
        for h in range(heads):
            low, high = (first + h) * head, (first + h + 1) * head
            to = slice(h * head, (h + 1) * head)
            query = (q_ref[rows, low:high].astype(F32) * head**-0.5).astype(BF)
            keys = k_ref[:span, low:high]
            slope = slope_rows[rows, low:high]
            scores = masked_scores(query, keys, seen)
            chances = jnp.exp(scores - lse_ref[rows, first + h : first + h + 1])
            diag = jnp.sum(slope.astype(F32) * att_ref[rows, low:high], axis=-1, keepdims=True)
            slope_chances = mm_rt(slope, v_ref[:span, low:high])
            slope_scores = (chances * (slope_chances - diag)).astype(BF)
            dq_out[rows, to] = (mm(slope_scores, keys) * head**-0.5).astype(BF)
            dk = mm_lt(slope_scores, query)
            dv = mm_lt(chances.astype(BF), slope)
            if i == GROUPS - 1:
                dk_sum[:, to] = dk
                dv_sum[:, to] = dv
            else:
                dk_sum[:span, to] += dk
                dv_sum[:span, to] += dv
    for i in range(GROUPS):
        for j in range(ks):
            spot = slice((i * ks + j) * tok, (i * ks + j + 1) * tok)
            dkv_out[k ^ j, i * tok : (i + 1) * tok, :] = jnp.concatenate(
                [dk_sum[spot, :], dv_sum[spot, :]], axis=1
            ).astype(BF)


def attend_back(g, k, ks, head, first, heads, slopes, q, keys, values, att, lse):
    tok, cols = slopes[0].shape
    mine, rows = GROUPS * tok, GROUPS * ks * tok
    wide = heads * head
    vmem = pl.BlockSpec(memory_space=pltpu.VMEM)
    return pl.pallas_call(
        functools.partial(attend_back_kernel, ks, head, first),
        grid_spec=pltpu.PrefetchScalarGridSpec(
            num_scalar_prefetch=1,
            in_specs=[vmem] * (len(slopes) + 5),
            out_specs=[vmem] * 2,
            scratch_shapes=[pltpu.VMEM((rows, wide), F32)] * 2 + [pltpu.VMEM((mine, cols), BF)],
        ),
        out_shape=[
            jax.ShapeDtypeStruct((mine, wide), BF),
            jax.ShapeDtypeStruct((ks, mine, 2 * wide), BF),
        ],
        compiler_params=pltpu.CompilerParams(vmem_limit_bytes=(16 if ks == 2 else 48) * 2**20),
        cost_estimate=LONG,
    )(jnp.stack([g, k]).astype(jnp.int32), *slopes, *in_hbm(q, keys, values, att, lse))


def project_back_kernel(ks, parts, place, *refs):
    count = len(parts)
    dq, dkv = refs[:count], refs[count : count + count * ks]
    h_ref, hat_ref, in_w = refs[count * (ks + 1) : count * (ks + 1) + 3]
    slots, (d_in, sums, project, back) = refs[-GROUPS - 4 : -4], refs[-4:]
    g = place[0]
    tok = slots[0].shape[0]
    cols = sum(parts)
    low = 0
    for n, wide in enumerate(parts):
        project[:, low : low + wide] = dq[n][...]
        both = total([dkv[n * ks + j][...] for j in range(ks)]).astype(BF)
        project[:, cols + low : cols + low + wide] = both[:, :wide]
        project[:, 2 * cols + low : 2 * cols + low + wide] = both[:, wide:]
        low += wide
    back[...] = mm_rt(project[...], in_w[...])
    for i in range(GROUPS):
        slots[i][...] = back[pl.ds(pl.multiple_of((g ^ i) * tok, tok), tok), :].astype(BF)
    sums[0:1, :] = jnp.sum(back[...] * hat_ref[...].astype(F32), axis=0, keepdims=True)
    sums[1:2, :] = jnp.sum(back[...], axis=0, keepdims=True)
    sums[2:3, : 3 * cols] = jnp.sum(project[...].astype(F32), axis=0, keepdims=True)
    d_in[...] = mm_lt(h_ref[...], project[...]).astype(BF)


def project_back(g, dq, dkv, h, hat, in_w):
    mine, width = h.shape
    parts = [part.shape[1] for part in dq]
    cols = sum(parts)
    ks = len(dkv[0])
    vmem = pl.BlockSpec(memory_space=pltpu.VMEM)
    got = pl.pallas_call(
        functools.partial(project_back_kernel, ks, parts),
        grid_spec=pltpu.PrefetchScalarGridSpec(
            num_scalar_prefetch=1,
            in_specs=[vmem] * (len(dq) * (ks + 1) + 3),
            out_specs=[vmem] * (GROUPS + 2),
            scratch_shapes=[pltpu.VMEM((mine, 3 * cols), BF), pltpu.VMEM((mine, width), F32)],
        ),
        out_shape=[jax.ShapeDtypeStruct((mine // GROUPS, width), BF)] * GROUPS
        + [
            jax.ShapeDtypeStruct((width, 3 * cols), BF),
            jax.ShapeDtypeStruct((8, width), F32),
        ],
        compiler_params=pltpu.CompilerParams(vmem_limit_bytes=16 * 2**20),
        cost_estimate=SHORT,
    )(
        jnp.stack([g]).astype(jnp.int32),
        *dq,
        *[p for pieces in dkv for p in pieces],
        *in_hbm(h, hat),
        in_w,
    )
    return got[:GROUPS], got[GROUPS], got[GROUPS + 1]


def finish_kernel(ks, extra, place, *refs):
    pieces, (in_out, out_out, vec_out, held) = refs[:-4], refs[-4:]
    own, cols = in_out.shape[1], held.shape[2]
    part, low = cols // 3, own + extra
    share = own // GROUPS
    third = share // 3
    over = out_out.shape[3] - cols
    for j in range(ks):
        for i in range(GROUPS):
            held[place[0] ^ i] = pieces[j * GROUPS + i][...].astype(F32)
        spot = place[1] ^ j
        for i in range(GROUPS):
            for n in range(3):
                to = (n * GROUPS + i) * part
                in_out[spot, :, to : to + part] = held[i, :own, n * part : (n + 1) * part]
                out_out[i, spot, n * third : (n + 1) * third, cols:] = held[
                    i, low + share :, n * over : (n + 1) * over
                ]
            out_out[i, spot, :, :cols] = held[i, low : low + share, :]
        vec_out[spot] = total([held[i, own:low, :] for i in range(GROUPS)])


def finish(pieces, own, extra, width, g, k):
    ks = len(pieces)
    tall, cols = pieces[0][0].shape
    vmem = pl.BlockSpec(memory_space=pltpu.VMEM)
    shapes = [(ks, own, GROUPS * cols), (GROUPS, ks, own // GROUPS, width), (ks, extra, cols)]
    in_w, out_w, vectors = pl.pallas_call(
        functools.partial(finish_kernel, ks, extra),
        grid_spec=pltpu.PrefetchScalarGridSpec(
            num_scalar_prefetch=1,
            in_specs=[vmem] * (ks * GROUPS),
            out_specs=[vmem] * 3,
            scratch_shapes=[pltpu.VMEM((GROUPS, tall, cols), F32)],
        ),
        out_shape=[jax.ShapeDtypeStruct(s, F32) for s in shapes],
        compiler_params=pltpu.CompilerParams(vmem_limit_bytes=16 * 2**20),
        cost_estimate=SHORT,
    )(jnp.stack([g, k]).astype(jnp.int32), *[p for group in pieces for p in group])
    return in_w.reshape(ks * own, -1), out_w.reshape(ks * own, width), vectors.reshape(-1)


def shards(
    inputs,
    cotangent,
    first_gain,
    first_shift,
    input_weight,
    query_bias,
    value_bias,
    output_weight,
    output_bias,
    second_gain,
    second_shift,
    expand_weight,
    expand_bias,
    contract_weight,
    contract_bias,
):
    tok, width = inputs.shape[1:]
    ks, zs = lax.axis_size("core"), lax.axis_size("fsdp")
    g, k, z = lax.axis_index("grp"), lax.axis_index("core"), lax.axis_index("fsdp")
    rows_z = width // zs
    heads_here = HEADS // GROUPS
    head = width // HEADS
    cols = width // GROUPS
    ff = expand_weight.shape[1]
    ff_z = ff // zs
    ff_g = ff_z // GROUPS
    mine = GROUPS * tok
    scale = head ** (-0.5)

    x_own = inputs[0]
    slope_own = cotangent[0]

    smalls = [first_gain, first_shift, query_bias, value_bias, output_bias]
    smalls += [second_gain, second_shift, contract_bias, expand_bias]
    own = rows_z // ks
    aligned = own % 48 == 0 and zs == GROUPS
    if aligned:
        cut = cut_first(input_weight, output_weight, smalls, g, k, ks)
    else:
        cut = cut_weight(input_weight, 3, g, k, ks)
    pieces = gather_flips(cut, "fsdp")
    rows_both = gather_flips(jnp.concatenate([inputs, cotangent]), "grp")
    rest = cut_rest(contract_weight, expand_weight, zs, g, k, ks)
    pieces.append(pieces.pop(1))
    pieces, rows_both, rest = lax.optimization_barrier((pieces, rows_both, rest))
    pieces.insert(1, pieces.pop())
    x_more = [send(b[0], "core", j) for j in range(1, ks) for b in rows_both]
    more = [[send(b, "core", j) for b in pieces] for j in range(1, ks)]
    if aligned:
        table = vector_table(pieces, own, rows_z, width, g, z)
        in_w, out_w = both_weights([pieces] + more, g, z, k, own, width)
    else:
        in_w = assemble([pieces] + more, z, k, own).reshape(width, 3 * cols)
        out_w = gather_flips(pick(output_weight.reshape(ks, own, width), k), "fsdp")
        out_more = [[send(b, "core", j) for b in out_w] for j in range(1, ks)]
        out_w = assemble([out_w] + out_more, z, k, own).reshape(GROUPS, cols, width)
        out_w = jnp.concatenate([pick(out_w, g ^ i) for i in range(GROUPS)])
        got = in_order(gather_flips(jnp.concatenate(smalls), "fsdp"), z).astype(F32)
        vectors = [got[:, i * rows_z : (i + 1) * rows_z].reshape(width) for i in range(8)]
        for i in (2, 3):
            vectors[i] = jnp.tile(pick(vectors[i].reshape(GROUPS, cols), g), GROUPS)
        got = got[:, 8 * rows_z :].reshape(zs, GROUPS, ff_g)
        vectors.append(lax.dynamic_index_in_dim(got, g, axis=1, keepdims=False).reshape(width))
        table = jnp.pad(jnp.stack(vectors), ((0, 7), (0, 0)))
    o_bias, gain_two, shift_two, c_bias = [table[i : i + 1] for i in range(4, 8)]

    rest = lax.all_gather(rest, ("fsdp", "core"), axis=0, tiled=True)

    *slots, qs, keys, values, att_full, lse, h1, hat_one = attend(
        g, k, ks, head, rows_both, x_more, in_w, table
    )
    att = jnp.concatenate(swap_flips(slots, "grp"), axis=1)
    x_f = x_own.astype(F32)
    middle = x_f + mm(att, out_w) + o_bias
    hat_two, rate_two = norm_stats(middle)
    h2 = (hat_two * gain_two + shift_two).astype(BF)
    h2_rows = gather_flips(h2, "grp")

    act, slope_inner, sh2_part, out_part, d_exp_b = hidden_part(
        h2_rows, rows_both, rest, table
    )
    sh2 = swap_flips(sh2_part, "grp")
    d_hidden = hidden_grads(h2_rows, rows_both, slope_inner, act)
    sh2, d_hidden = lax.optimization_barrier((sh2, d_hidden))
    sh2 = total(sh2)
    d_hidden = lax.psum_scatter(d_hidden, ("fsdp", "core"), scatter_dimension=0, tiled=True)

    slope_f = slope_own.astype(F32)
    d_gain_two = jnp.sum(sh2 * hat_two, axis=0, keepdims=True)
    d_shift_two = jnp.sum(sh2, axis=0, keepdims=True)
    slope_middle = slope_f + norm_back(sh2, gain_two, hat_two, rate_two)
    slope_branch = slope_middle.astype(BF)
    slope_att = mm_rt(slope_branch, out_w).astype(BF)
    datt = swap_flips([slope_att[:, i * cols : (i + 1) * cols] for i in range(GROUPS)], "grp")

    datt, slope_late, out_part = lax.optimization_barrier((datt, slope_branch, out_part))
    out_sum = swap_flips(out_part, "grp")
    d_out = mm_lt(att, slope_late).astype(BF).reshape(GROUPS, cols, width)
    d_out = in_order([d_out[i] for i in range(GROUPS)], g)
    d_out = d_out.reshape(zs, GROUPS, ks, own // GROUPS, width)
    pieces = [lax.dynamic_index_in_dim(d_out, k ^ j, axis=2, keepdims=False) for j in range(ks)]
    datt, pieces = lax.optimization_barrier((datt, pieces))
    d_out = swap_flips(pieces, "core")

    kept = (qs, keys, values, att_full, lse)
    split = (heads_here + 1) // 2
    dq, dkv = attend_back(g, k, ks, head, 0, split, datt, *kept)
    dq, dkv = [dq], [swap_flips([dkv[j] for j in range(ks)], "core")]
    datt, d_out, out_sum = lax.optimization_barrier((datt, d_out, out_sum))
    d_out = total(d_out).astype(BF)
    pieces = [lax.dynamic_index_in_dim(d_out, g ^ i, axis=1, keepdims=False) for i in range(GROUPS)]
    datt, pieces = lax.optimization_barrier((datt, pieces))
    d_out = swap_flips(pieces, "grp")
    more = attend_back(g, k, ks, head, split, heads_here - split, datt, *kept)
    dq.append(more[0])
    dkv.append(swap_flips([more[1][j] for j in range(ks)], "core"))
    sh1_part, d_in, sums = project_back(g, dq, dkv, h1, hat_one, in_w)
    sh1, d_hidden = lax.optimization_barrier((swap_flips(sh1_part, "grp"), d_hidden))
    sh1 = total(sh1)
    hat_own, rate_own = norm_stats(x_f)
    delta_inputs = (slope_middle + norm_back(sh1, table[0:1], hat_own, rate_own)).astype(BF)[None]

    extra = -(-(12 * rows_z) // (3 * cols * ks))
    packed = pack_vectors(
        g,
        zs,
        extra * ks,
        rows_z,
        sums,
        jnp.sum(slope_branch.astype(F32), axis=0, keepdims=True),
        d_gain_two,
        d_shift_two,
        jnp.sum(slope_f, axis=0, keepdims=True),
        d_exp_b,
    )
    d_out = total(d_out).astype(BF)
    third = d_out.shape[1] // 3
    tail = d_out[..., 3 * cols :]
    tail = [tail[:, i * third : (i + 1) * third] for i in range(3)]
    d_out = jnp.concatenate([d_out[..., : 3 * cols], jnp.concatenate(tail, axis=2)], axis=1)
    d_in = jnp.concatenate(
        [
            d_in.reshape(zs, ks, own, 3 * cols),
            packed.astype(BF).reshape(zs, ks, extra, 3 * cols),
        ],
        axis=2,
    )
    pieces = [lax.dynamic_index_in_dim(d_in, k ^ j, axis=1, keepdims=False) for j in range(ks)]
    d_in = total(swap_flips(pieces, "core")).astype(BF)
    d_in = jnp.concatenate([d_in, d_out], axis=1)
    pieces = lax.optimization_barrier([pick(d_in, z ^ i) for i in range(zs)])
    d_in = swap_flips(pieces, "fsdp")
    d_hidden = gather_flips(d_hidden, "grp")
    d_in.append(d_in.pop(1))
    d_in = gather_flips(total(d_in).astype(BF), "grp")
    more = jnp.stack(d_hidden)
    more = [send(more, "core", j) for j in range(1, ks)]
    d_exp_w, d_con_w = unfold(d_hidden, more, zs, g, k)
    outputs = (middle + total(out_sum) + c_bias).astype(BF)[None]
    d_in = [d_in] + [[send(p, "core", j) for p in d_in] for j in range(1, ks)]
    d_in, d_exp_w, d_con_w = lax.optimization_barrier((d_in, d_exp_w, d_con_w))
    d_in_w, d_out_w, packed = finish(d_in, own, extra, width, g, k)

    def vec(i):
        return packed[i * rows_z : (i + 1) * rows_z]

    return (
        outputs,
        delta_inputs,
        vec(0),
        vec(1),
        d_in_w,
        vec(2),
        vec(3),
        d_out_w,
        vec(4),
        vec(5),
        vec(6),
        d_exp_w,
        packed[8 * rows_z : 8 * rows_z + ff_z],
        d_con_w,
        vec(7),
    )


def solution(mesh):
    ctx, zs = mesh.shape["ctx"], mesh.shape["fsdp"]
    axes = ("grp", "core", "fsdp")
    split = Mesh(mesh.devices.reshape(GROUPS, ctx // GROUPS, zs), axes)
    row, vec, mat = P("fsdp", ("grp", "core"), None), P("fsdp"), P("fsdp", None)
    placed = (row, row, vec, vec, mat, vec, vec, mat, vec, vec, vec, mat, vec, mat, vec)
    return jax.shard_map(
        shards,
        mesh=split,
        in_specs=placed,
        out_specs=placed,
        check_vma=False,
    )
```

```python
import functools

import jax
import jax.numpy as jnp
from jax import lax
from jax.experimental import pallas as pl
from jax.experimental.pallas import tpu as pltpu
from jax.sharding import Mesh, PartitionSpec as P

HEADS = 12
GROUPS = 4

NORM_EPS = 1e-05
MASK_FILL = -1e30
GELU_COEF = 0.7978845608028654
GELU_CUBE = 0.044715

SHORT = pl.CostEstimate(flops=1, bytes_accessed=1, transcendentals=0)
LONG = pl.CostEstimate(flops=8 * 10**9, bytes_accessed=1, transcendentals=0)

BF = jnp.bfloat16
F32 = jnp.float32


def in_hbm(*values):
    return [pltpu.with_memory_space_constraint(v, pltpu.HBM) for v in values]


def mm(left, right):
    return jnp.dot(left, right, preferred_element_type=F32)


def mm_lt(left, right):
    return lax.dot_general(left, right, (((0,), (0,)), ((), ())), preferred_element_type=F32)


def mm_rt(left, right):
    return lax.dot_general(left, right, (((1,), (1,)), ((), ())), preferred_element_type=F32)


def send(value, axis, flip):
    count = lax.axis_size(axis)
    return lax.ppermute(value, axis, [(s, s ^ flip) for s in range(count)])


def gather_flips(value, axis):
    return [value] + [send(value, axis, i) for i in range(1, lax.axis_size(axis))]


def swap_flips(pieces, axis):
    return [pieces[0]] + [send(p, axis, i) for i, p in enumerate(pieces) if i]


def pick(stacked, place):
    return lax.dynamic_index_in_dim(stacked, place, axis=0, keepdims=False)


def in_order(pieces, me):
    stacked = jnp.stack(pieces)
    return jnp.stack([pick(stacked, me ^ j) for j in range(len(pieces))])


def norm_stats(values):
    center = values - jnp.mean(values, axis=-1, keepdims=True)
    spread = jnp.mean(center * center, axis=-1, keepdims=True)
    rate = lax.rsqrt(spread + NORM_EPS)
    return center * rate, rate


def norm_back(slope, gain, hat, rate):
    scaled = slope * gain
    return rate * (
        scaled
        - jnp.mean(scaled, axis=-1, keepdims=True)
        - hat * jnp.mean(scaled * hat, axis=-1, keepdims=True)
    )


def total(parts):
    out = parts[0].astype(F32)
    for part in parts[1:]:
        out = out + part.astype(F32)
    return out


def cut_columns(source, cut, parts, i):
    wide = cut.shape[1] // parts
    for part in range(parts):
        low = (part * GROUPS + i) * wide
        cut[:, part * wide : (part + 1) * wide] = source[:, low : low + wide]


def cut_kernel(parts, place, source, cut):
    for i in range(GROUPS):

        @pl.when(place[0] == i)
        def _():
            cut_columns(source, cut, parts, i)


def cut_weight(weight, parts, g, k, ks):
    rows = weight.shape[0] // ks
    cols = weight.shape[1] // GROUPS
    if rows % 16 == 0:
        return pl.pallas_call(
            functools.partial(cut_kernel, parts),
            grid_spec=pltpu.PrefetchScalarGridSpec(
                num_scalar_prefetch=1,
                grid=(1,),
                in_specs=[pl.BlockSpec((rows, weight.shape[1]), lambda i, place: (place[1], 0))],
                out_specs=pl.BlockSpec((rows, cols), lambda i, place: (0, 0)),
            ),
            out_shape=jax.ShapeDtypeStruct((rows, cols), BF),
            compiler_params=pltpu.CompilerParams(vmem_limit_bytes=8 * 2**20),
        )(jnp.stack([g, k]).astype(jnp.int32), weight)
    half = pick(weight.reshape(ks, rows, -1), k)
    return lax.dynamic_index_in_dim(
        half.reshape(rows, parts, GROUPS, cols // parts), g, axis=2, keepdims=False
    ).reshape(rows, cols)


def cut_first_kernel(place, *refs):
    source, other, vectors, cut, held = refs[0], refs[1], refs[2:-2], refs[-2], refs[-1]
    rows = source.shape[0]
    third, cols = rows // 3, cut.shape[1]
    cut[rows + 16 : 2 * rows + 16, :] = other[:, :cols]
    over = other.shape[1] - cols
    for part in range(3):
        cut[2 * rows + 16 :, part * over : (part + 1) * over] = other[
            part * third : (part + 1) * third, cols:
        ]
    unit = vectors[0].shape[0]
    per = cut.shape[1] // unit
    held[...] = jnp.zeros_like(held)
    spot = 0
    for vector in vectors:
        row = vector[...].astype(F32).reshape(1, vector.shape[0])
        for part in range(vector.shape[0] // unit):
            col = spot % per * unit
            held[spot // per : spot // per + 1, col : col + unit] = row[
                :, part * unit : (part + 1) * unit
            ]
            spot += 1
    cut[rows : rows + 16, :] = held[...].astype(BF)
    for i in range(GROUPS):

        @pl.when(place[0] == i)
        def _():
            cut_columns(source, cut.at[:rows, :], 3, i)


def cut_first(weight, other, vectors, g, k, ks):
    rows, cols = weight.shape[0] // ks, weight.shape[1] // GROUPS
    tall = 2 * rows + 16 + rows // 3
    by_k = lambda i, place: (place[1], 0)
    return pl.pallas_call(
        cut_first_kernel,
        grid_spec=pltpu.PrefetchScalarGridSpec(
            num_scalar_prefetch=1,
            grid=(1,),
            in_specs=[
                pl.BlockSpec((rows, weight.shape[1]), by_k),
                pl.BlockSpec((rows, other.shape[1]), by_k),
            ]
            + [pl.BlockSpec(v.shape, lambda i, place: (0,)) for v in vectors],
            out_specs=pl.BlockSpec((tall, cols), lambda i, place: (0, 0)),
            scratch_shapes=[pltpu.VMEM((16, cols), F32)],
        ),
        out_shape=jax.ShapeDtypeStruct((tall, cols), BF),
        compiler_params=pltpu.CompilerParams(vmem_limit_bytes=8 * 2**20),
        cost_estimate=SHORT,
    )(jnp.stack([g, k]).astype(jnp.int32), *in_hbm(weight, other, *vectors))


def both_weights_kernel(rows, place, *refs):
    pieces, in_w, out_w = refs[:-2], refs[-2], refs[-1]
    zs, ks = in_w.shape[:2]
    third, cols = rows // 3, in_w.shape[3]
    over = out_w.shape[3] - cols
    low = rows + 16
    for j in range(ks):
        for i in range(zs):
            piece = pieces[j * zs + i]
            in_w[place[1] ^ i, place[2] ^ j] = piece[:rows, :]
            spot = (place[1] ^ i ^ place[0], place[2] ^ j)
            out_w[spot[0], spot[1], :, :cols] = piece[low : low + rows, :]
            for part in range(3):
                out_w[spot[0], spot[1], part * third : (part + 1) * third, cols:] = piece[
                    low + rows :, part * over : (part + 1) * over
                ]


def both_weights(pieces, g, z, k, rows, width):
    ks, zs = len(pieces), len(pieces[0])
    cols = pieces[0][0].shape[1]
    vmem = pl.BlockSpec(memory_space=pltpu.VMEM)
    shapes = [(zs, ks, rows, cols), (zs, ks, rows, width)]
    in_w, out_w = pl.pallas_call(
        functools.partial(both_weights_kernel, rows),
        grid_spec=pltpu.PrefetchScalarGridSpec(
            num_scalar_prefetch=1, in_specs=[vmem] * (zs * ks), out_specs=[vmem] * 2
        ),
        out_shape=[jax.ShapeDtypeStruct(s, BF) for s in shapes],
        compiler_params=pltpu.CompilerParams(vmem_limit_bytes=16 * 2**20),
        cost_estimate=SHORT,
    )(jnp.stack([g, z, k]).astype(jnp.int32), *[p for group in pieces for p in group])
    return in_w.reshape(width, cols), out_w.reshape(width, width)


def table_kernel(unit, place, *refs):
    pieces, out, held = refs[:-2], refs[-2], refs[-1]
    zs = len(pieces)
    per = held.shape[2] // unit
    cols = out.shape[1] // GROUPS
    for i, piece in enumerate(pieces):
        held[place[1] ^ i] = piece[...].astype(F32)

    def unpack(row, slot):
        for zz in range(zs):
            col = slot % per * unit
            out[row : row + 1, zz * unit : (zz + 1) * unit] = held[
                zz, slot // per : slot // per + 1, col : col + unit
            ]

    out[...] = jnp.zeros_like(out)
    for slot in range(8):
        unpack(slot + 8 if slot in (2, 3) else slot, slot)
    for i in range(GROUPS):

        @pl.when(place[0] == i)
        def _():
            unpack(8, 8 + i)
            out[2:4, :cols] = out[10:12, i * cols : (i + 1) * cols]


def vector_table(pieces, below, unit, width, g, z):
    cols = pieces[0].shape[1]
    return pl.pallas_call(
        functools.partial(table_kernel, unit),
        grid_spec=pltpu.PrefetchScalarGridSpec(
            num_scalar_prefetch=1,
            grid=(1,),
            in_specs=[pl.BlockSpec((16, cols), lambda i, place: (below // 16, 0))] * len(pieces),
            out_specs=pl.BlockSpec((16, width), lambda i, place: (0, 0)),
            scratch_shapes=[pltpu.VMEM((len(pieces), 16, cols), F32)],
        ),
        out_shape=jax.ShapeDtypeStruct((16, width), F32),
        compiler_params=pltpu.CompilerParams(vmem_limit_bytes=8 * 2**20),
    )(jnp.stack([g, z]).astype(jnp.int32), *pieces)


def pack_kernel(zs, stride, unit, place, sums, out_bias, gain, shift, con_bias, exp_bias, out):
    per = out.shape[1] // unit
    cols = out.shape[1] // 3

    def put(zz, slot, value):
        row, col = zz * stride + slot // per, slot % per * unit
        out[row : row + 1, col : col + unit] = value

    out[...] = jnp.zeros_like(out)
    whole = [(0, sums, 0), (1, sums, 1), (4, out_bias, 0), (5, gain, 0), (6, shift, 0), (7, con_bias, 0)]
    for slot, source, row in whole:
        for zz in range(zs):
            put(zz, slot, source[row : row + 1, zz * unit : (zz + 1) * unit])
    for i in range(GROUPS):

        @pl.when(place[0] == i)
        def _():
            for zz in range(zs):
                put(zz, 8 + i, exp_bias[:, zz * unit : (zz + 1) * unit])
            for part in range(cols // unit):
                zz = i * cols // unit + part
                low = part * unit
                put(zz, 2, sums[2:3, low : low + unit])
                put(zz, 3, sums[2:3, 2 * cols + low : 2 * cols + low + unit])


def pack_vectors(g, zs, stride, unit, sums, *vectors):
    wide = 3 * (vectors[0].shape[1] // GROUPS)
    vmem = pl.BlockSpec(memory_space=pltpu.VMEM)
    return pl.pallas_call(
        functools.partial(pack_kernel, zs, stride, unit),
        grid_spec=pltpu.PrefetchScalarGridSpec(
            num_scalar_prefetch=1, in_specs=[vmem] * (1 + len(vectors)), out_specs=vmem
        ),
        out_shape=jax.ShapeDtypeStruct((zs * stride, wide), F32),
        compiler_params=pltpu.CompilerParams(vmem_limit_bytes=8 * 2**20),
    )(jnp.stack([g]).astype(jnp.int32), sums, *vectors)


def cut_rest_kernel(parts, place, con_ref, exp_ref, cut):
    width = con_ref.shape[1]
    cut[:, :width] = con_ref[...]
    for i in range(GROUPS):

        @pl.when(place[0] == i)
        def _():
            cut_columns(exp_ref, cut.at[:, width:], parts, i)


def cut_rest(con_w, exp_w, parts, g, k, ks):
    width = con_w.shape[1]
    rows, ff_rows = exp_w.shape[0] // ks, con_w.shape[0] // (GROUPS * ks)
    wide = exp_w.shape[1] // GROUPS
    if rows % 16 == 0 and rows == ff_rows:
        return pl.pallas_call(
            functools.partial(cut_rest_kernel, parts),
            grid_spec=pltpu.PrefetchScalarGridSpec(
                num_scalar_prefetch=1,
                grid=(1,),
                in_specs=[
                    pl.BlockSpec((rows, width), lambda i, place: (place[0] * ks + place[1], 0)),
                    pl.BlockSpec((rows, exp_w.shape[1]), lambda i, place: (place[1], 0)),
                ],
                out_specs=pl.BlockSpec((rows, width + wide), lambda i, place: (0, 0)),
            ),
            out_shape=jax.ShapeDtypeStruct((rows, width + wide), BF),
            compiler_params=pltpu.CompilerParams(vmem_limit_bytes=8 * 2**20),
        )(jnp.stack([g, k]).astype(jnp.int32), *in_hbm(con_w, exp_w))
    return jnp.concatenate(
        [
            pick(con_w.reshape(GROUPS * ks, ff_rows, width), g * ks + k),
            cut_weight(exp_w, parts, g, k, ks),
        ],
        axis=1,
    )


def assemble_kernel(rows, place, *refs):
    pieces, out = refs[:-1], refs[-1]
    zs = out.shape[0]
    for j in range(out.shape[1]):
        for i in range(zs):
            out[place[0] ^ i, place[1] ^ j] = pieces[j * zs + i][:rows, :]


def assemble(pieces, first, k, rows):
    ks, zs = len(pieces), len(pieces[0])
    cols = pieces[0][0].shape[1]
    shape = (zs, ks, rows, cols)
    if rows % 16:
        parts = [in_order([p[:rows] for p in group], first) for group in pieces]
        return jnp.stack(in_order(parts, k), axis=1).reshape(zs, ks * rows, cols)
    vmem = pl.BlockSpec(memory_space=pltpu.VMEM)
    out = pl.pallas_call(
        functools.partial(assemble_kernel, rows),
        grid_spec=pltpu.PrefetchScalarGridSpec(
            num_scalar_prefetch=1, in_specs=[vmem] * (zs * ks), out_specs=vmem
        ),
        out_shape=jax.ShapeDtypeStruct(shape, BF),
        compiler_params=pltpu.CompilerParams(vmem_limit_bytes=8 * 2**20),
        cost_estimate=SHORT,
    )(jnp.stack([first, k]).astype(jnp.int32), *[p for group in pieces for p in group])
    return out.reshape(zs, ks * rows, cols)


def unfold_kernel(parts, ks, place, *refs):
    pieces, (exp_out, con_out, held) = refs[:-3], refs[-3:]
    wide = con_out.shape[3]
    part_wide = wide // parts
    for j in range(ks):
        for i in range(GROUPS):
            held[place[0] ^ i] = pieces[j * GROUPS + i][...]
        spot = place[1] ^ j
        for i in range(GROUPS):
            con_out[i, spot] = held[i, :, wide:].astype(F32)
            for part in range(parts):
                low = (part * GROUPS + i) * part_wide
                exp_out[spot, :, low : low + part_wide] = held[
                    i, :, part * part_wide : (part + 1) * part_wide
                ].astype(F32)


def unfold(pieces, parts, g, k):
    ks = len(pieces)
    rows, wide = pieces[0][0].shape[0], pieces[0][0].shape[1] // 2
    step = rows // 2 if rows % 32 == 0 else rows
    shapes = [(ks, rows, GROUPS * wide), (GROUPS, ks, rows, wide)]
    exp, con = pl.pallas_call(
        functools.partial(unfold_kernel, parts, ks),
        grid_spec=pltpu.PrefetchScalarGridSpec(
            num_scalar_prefetch=1,
            grid=(rows // step,),
            in_specs=[pl.BlockSpec((step, 2 * wide), lambda i, place: (i, 0))] * (ks * GROUPS),
            out_specs=[
                pl.BlockSpec((ks, step, GROUPS * wide), lambda i, place: (0, i, 0)),
                pl.BlockSpec((GROUPS, ks, step, wide), lambda i, place: (0, 0, i, 0)),
            ],
            scratch_shapes=[pltpu.VMEM((GROUPS, step, 2 * wide), BF)],
        ),
        out_shape=[jax.ShapeDtypeStruct(s, F32) for s in shapes],
        compiler_params=pltpu.CompilerParams(vmem_limit_bytes=20 * 2**20),
        cost_estimate=SHORT,
    )(jnp.stack([g, k]).astype(jnp.int32), *[p for group in pieces for p in group])
    return exp.reshape(ks * rows, -1), con.reshape(-1, wide)


def join_rows(pieces, joined):
    tok = joined.shape[0] // GROUPS
    for i, piece in enumerate(pieces):
        joined[i * tok : (i + 1) * tok, :] = piece[...].reshape(tok, joined.shape[1])


def hidden_kernel(*refs):
    h_rows, s_rows = refs[:GROUPS], refs[GROUPS : 2 * GROUPS]
    exp_w, con_w, bias, act_ref, inner_ref = refs[2 * GROUPS : 2 * GROUPS + 5]
    back_ref = refs[2 * GROUPS + 5 : 3 * GROUPS + 5]
    out_ref = refs[3 * GROUPS + 5 : 4 * GROUPS + 5]
    bias_ref = refs[4 * GROUPS + 5]
    h_ref, s_ref, back_sum, out_sum = refs[-4:]
    step = pl.program_id(0)
    tok = h_rows[0].shape[0]

    @pl.when(step == 0)
    def _():
        join_rows(h_rows, h_ref)
        join_rows(s_rows, s_ref)

    inner = mm(h_ref[...], exp_w[...]) + bias[8:9, :]
    square = inner * inner
    tanh = jnp.tanh(GELU_COEF * (inner + GELU_CUBE * square * inner))
    half = 0.5 + 0.5 * tanh
    act = (inner * half).astype(BF)
    gelu_slope = half + (0.5 * GELU_COEF) * inner * (1.0 - tanh * tanh) * (
        1.0 + (3.0 * GELU_CUBE) * square
    )
    slope = (mm_rt(s_ref[...], con_w[...]) * gelu_slope).astype(BF)
    act_ref[...] = act
    inner_ref[...] = slope
    bias_ref[...] = jnp.sum(slope.astype(F32), axis=0, keepdims=True)
    back = mm_rt(slope, exp_w[...])
    out = mm(act, con_w[...])

    @pl.when(step == 0)
    def _():
        back_sum[...] = back
        out_sum[...] = out

    @pl.when(step > 0)
    def _():
        back_sum[...] += back
        out_sum[...] += out

    @pl.when(step == pl.num_programs(0) - 1)
    def _():
        for i in range(GROUPS):
            back_ref[i][...] = back_sum[i * tok : (i + 1) * tok, :].astype(BF)
            out_ref[i][...] = out_sum[i * tok : (i + 1) * tok, :].astype(BF)


def hidden_part(h_rows, s_rows, weights, table):
    tok, width = h_rows[0].shape
    hidden = weights.shape[1] - width
    rows = GROUPS * tok
    step = 256
    fixed = lambda i: (0, 0)
    cols = lambda i: (0, i)
    slots = [pl.BlockSpec((tok, width), fixed)] * GROUPS
    got = pl.pallas_call(
        hidden_kernel,
        grid=(hidden // step,),
        in_specs=[pl.BlockSpec((tok, width), fixed)] * GROUPS
        + [pl.BlockSpec((1, tok, width), lambda i: (1, 0, 0))] * GROUPS
        + [
            pl.BlockSpec((width, step), lambda i: (0, width // step + i)),
            pl.BlockSpec((step, width), lambda i: (i, 0)),
            pl.BlockSpec((16, step), cols),
        ],
        out_specs=[
            pl.BlockSpec((rows, step), cols),
            pl.BlockSpec((rows, step), cols),
            *slots,
            *slots,
            pl.BlockSpec((1, step), cols),
        ],
        out_shape=[
            jax.ShapeDtypeStruct((rows, hidden), BF),
            jax.ShapeDtypeStruct((rows, hidden), BF),
            *[jax.ShapeDtypeStruct((tok, width), BF)] * GROUPS,
            *[pltpu.HBM((tok, width), BF)] * GROUPS,
            jax.ShapeDtypeStruct((1, hidden), F32),
        ],
        scratch_shapes=[pltpu.VMEM((rows, width), BF)] * 2 + [pltpu.VMEM((rows, width), F32)] * 2,
        compiler_params=pltpu.CompilerParams(vmem_limit_bytes=24 * 2**20),
        cost_estimate=SHORT,
    )(*in_hbm(*h_rows, *s_rows, weights, weights), table)
    return got[0], got[1], got[2 : 2 + GROUPS], got[2 + GROUPS : 2 + 2 * GROUPS], got[-1]


def hidden_grad_kernel(*refs):
    h_rows, s_rows = refs[:GROUPS], refs[GROUPS : 2 * GROUPS]
    inner_ref, act_ref, out_ref, h_ref, s_ref = refs[2 * GROUPS :]
    wide, step = inner_ref.shape[1], act_ref.shape[1]

    @pl.when(pl.program_id(0) == 0)
    def _():
        join_rows(s_rows, s_ref)

    join_rows(h_rows, h_ref)
    out_ref[:, :wide] = mm_lt(h_ref[...], inner_ref[...]).astype(BF)
    out_ref[:, wide:] = mm_lt(act_ref[...], s_ref[...]).astype(BF)


def hidden_grads(h_rows, s_rows, slope_inner, act):
    tok, width = h_rows[0].shape
    rows, hidden = act.shape
    step = 256
    cols = lambda i: (0, i)
    fixed = lambda i: (0, 0)
    return pl.pallas_call(
        hidden_grad_kernel,
        grid=(width // step,),
        in_specs=[pl.BlockSpec((tok, step), cols)] * GROUPS
        + [pl.BlockSpec((1, tok, width), lambda i: (1, 0, 0))] * GROUPS
        + [pl.BlockSpec((rows, hidden), fixed), pl.BlockSpec((rows, step), cols)],
        out_specs=pl.BlockSpec((step, hidden + width), lambda i: (i, 0)),
        out_shape=jax.ShapeDtypeStruct((width, hidden + width), BF),
        scratch_shapes=[pltpu.VMEM((rows, step), BF), pltpu.VMEM((rows, width), BF)],
        compiler_params=pltpu.CompilerParams(vmem_limit_bytes=16 * 2**20),
        cost_estimate=LONG,
    )(*in_hbm(*h_rows, *s_rows), slope_inner, act)


def visible(k, tok, keys):
    row = lax.broadcasted_iota(jnp.int32, (tok, keys), 0)
    col = lax.broadcasted_iota(jnp.int32, (tok, keys), 1)
    return col <= k * tok + row


def masked_scores(query, keys, seen):
    scores = mm_rt(query, keys)
    near = keys.shape[0] - seen.shape[1]
    last = jnp.where(seen, scores[:, near:], MASK_FILL)
    return last if near == 0 else jnp.concatenate([scores[:, :near], last], axis=1)


def attend_kernel(ks, head, place, *refs):
    pieces = refs[: GROUPS * ks]
    in_w, table = refs[GROUPS * ks : GROUPS * ks + 2]
    slots = refs[GROUPS * ks + 2 : GROUPS * ks + 2 + GROUPS]
    q_out, k_out, v_out, att_out, lse_out, h_out, hat_out, h_all = refs[GROUPS * ks + 2 + GROUPS :]
    g, k = place[0], place[1]
    tok, width = pieces[-1].shape
    cols = q_out.shape[1]
    gain, shift = table[0:1, :], table[1:2, :]
    for j in range(ks):
        for i in range(GROUPS):
            piece = pieces[j * GROUPS + i]
            hat, _ = norm_stats((piece[...] if j else piece[0]).astype(F32))
            normed = (hat * gain + shift).astype(BF)
            spot = pl.multiple_of(((g ^ i) * ks + (k ^ j)) * tok, tok)
            h_all[pl.ds(spot, tok), :] = normed
            if j == 0:
                spot = pl.multiple_of((g ^ i) * tok, tok)
                h_out[pl.ds(spot, tok), :] = normed
                hat_out[pl.ds(spot, tok), :] = hat.astype(BF)
    q_out[...] = (mm(h_out[...], in_w[:, :cols]) + table[2:3, :cols]).astype(BF)
    kv = mm(h_all[...], in_w[:, cols:])
    k_out[...] = kv[:, :cols].astype(BF)
    v_out[...] = (kv[:, cols:] + table[3:4, :cols]).astype(BF)
    seen = visible(k, tok, ks * tok)
    for h in range(cols // head):
        low, high = h * head, (h + 1) * head
        for i in range(GROUPS):
            rows = slice(i * tok, (i + 1) * tok)
            span = (i + 1) * ks * tok
            query = (q_out[rows, low:high].astype(F32) * head**-0.5).astype(BF)
            scores = masked_scores(query, k_out[:span, low:high], seen)
            peak = jnp.max(scores, axis=-1, keepdims=True)
            weights = jnp.exp(scores - peak)
            mass = jnp.sum(weights, axis=-1, keepdims=True)
            lse_out[rows, h : h + 1] = peak + jnp.log(mass)
            att = mm(weights.astype(BF), v_out[:span, low:high]) / mass
            att_out[rows, low:high] = att
    for i in range(GROUPS):
        slots[i][...] = att_out[pl.ds(pl.multiple_of((g ^ i) * tok, tok), tok), :].astype(BF)


def attend(g, k, ks, head, both, more, in_w, table):
    tok, width = both[0].shape[1:]
    cols = in_w.shape[1] // 3
    mine, rows = GROUPS * tok, GROUPS * ks * tok
    vmem = pl.BlockSpec(memory_space=pltpu.VMEM)
    shapes = [
        *[((tok, cols), BF)] * GROUPS,
        ((mine, cols), BF),
        ((rows, cols), BF),
        ((rows, cols), BF),
        ((mine, cols), F32),
        ((mine, 8), F32),
        ((mine, width), BF),
        ((mine, width), BF),
    ]
    return pl.pallas_call(
        functools.partial(attend_kernel, ks, head),
        grid_spec=pltpu.PrefetchScalarGridSpec(
            num_scalar_prefetch=1,
            in_specs=[pl.BlockSpec((1, tok, width), lambda i, place: (0, 0, 0))] * GROUPS
            + [vmem] * (len(more) + 2),
            grid=(1,),
            out_specs=[vmem] * len(shapes),
            scratch_shapes=[pltpu.VMEM((rows, width), BF)],
        ),
        out_shape=[jax.ShapeDtypeStruct(s, t) for s, t in shapes[:GROUPS]]
        + [pltpu.HBM(s, t) for s, t in shapes[GROUPS:]],
        compiler_params=pltpu.CompilerParams(vmem_limit_bytes=(16 if ks == 2 else 48) * 2**20),
        cost_estimate=SHORT,
    )(jnp.stack([g, k]).astype(jnp.int32), *both, *more, in_w, table)


def attend_back_kernel(ks, head, first, place, *refs):
    slopes = refs[:GROUPS]
    q_ref, k_ref, v_ref, att_ref, lse_ref, dq_out, dkv_out = refs[GROUPS : GROUPS + 7]
    dk_sum, dv_sum, slope_rows = refs[GROUPS + 7 :]
    g, k = place[0], place[1]
    tok = slopes[0].shape[0]
    heads = dq_out.shape[1] // head
    for i in range(GROUPS):
        slope_rows[pl.ds(pl.multiple_of((g ^ i) * tok, tok), tok), :] = slopes[i][...]
    seen = visible(k, tok, ks * tok)
    for i in reversed(range(GROUPS)):
        rows = slice(i * tok, (i + 1) * tok)
        span = (i + 1) * ks * tok
        for h in range(heads):
            low, high = (first + h) * head, (first + h + 1) * head
            to = slice(h * head, (h + 1) * head)
            query = (q_ref[rows, low:high].astype(F32) * head**-0.5).astype(BF)
            keys = k_ref[:span, low:high]
            slope = slope_rows[rows, low:high]
            scores = masked_scores(query, keys, seen)
            chances = jnp.exp(scores - lse_ref[rows, first + h : first + h + 1])
            diag = jnp.sum(slope.astype(F32) * att_ref[rows, low:high], axis=-1, keepdims=True)
            slope_chances = mm_rt(slope, v_ref[:span, low:high])
            slope_scores = (chances * (slope_chances - diag)).astype(BF)
            dq_out[rows, to] = (mm(slope_scores, keys) * head**-0.5).astype(BF)
            dk = mm_lt(slope_scores, query)
            dv = mm_lt(chances.astype(BF), slope)
            if i == GROUPS - 1:
                dk_sum[:, to] = dk
                dv_sum[:, to] = dv
            else:
                dk_sum[:span, to] += dk
                dv_sum[:span, to] += dv
    for i in range(GROUPS):
        for j in range(ks):
            spot = slice((i * ks + j) * tok, (i * ks + j + 1) * tok)
            dkv_out[k ^ j, i * tok : (i + 1) * tok, :] = jnp.concatenate(
                [dk_sum[spot, :], dv_sum[spot, :]], axis=1
            ).astype(BF)


def attend_back(g, k, ks, head, first, heads, slopes, q, keys, values, att, lse):
    tok, cols = slopes[0].shape
    mine, rows = GROUPS * tok, GROUPS * ks * tok
    wide = heads * head
    vmem = pl.BlockSpec(memory_space=pltpu.VMEM)
    return pl.pallas_call(
        functools.partial(attend_back_kernel, ks, head, first),
        grid_spec=pltpu.PrefetchScalarGridSpec(
            num_scalar_prefetch=1,
            in_specs=[vmem] * (len(slopes) + 5),
            out_specs=[vmem] * 2,
            scratch_shapes=[pltpu.VMEM((rows, wide), F32)] * 2 + [pltpu.VMEM((mine, cols), BF)],
        ),
        out_shape=[
            jax.ShapeDtypeStruct((mine, wide), BF),
            jax.ShapeDtypeStruct((ks, mine, 2 * wide), BF),
        ],
        compiler_params=pltpu.CompilerParams(vmem_limit_bytes=(16 if ks == 2 else 48) * 2**20),
        cost_estimate=LONG,
    )(jnp.stack([g, k]).astype(jnp.int32), *slopes, *in_hbm(q, keys, values, att, lse))


def project_back_kernel(ks, parts, place, *refs):
    count = len(parts)
    dq, dkv = refs[:count], refs[count : count + count * ks]
    h_ref, hat_ref, in_w = refs[count * (ks + 1) : count * (ks + 1) + 3]
    slots, (d_in, sums, project, back) = refs[-GROUPS - 4 : -4], refs[-4:]
    g = place[0]
    tok = slots[0].shape[0]
    cols = sum(parts)
    low = 0
    for n, wide in enumerate(parts):
        project[:, low : low + wide] = dq[n][...]
        both = total([dkv[n * ks + j][...] for j in range(ks)]).astype(BF)
        project[:, cols + low : cols + low + wide] = both[:, :wide]
        project[:, 2 * cols + low : 2 * cols + low + wide] = both[:, wide:]
        low += wide
    back[...] = mm_rt(project[...], in_w[...])
    for i in range(GROUPS):
        slots[i][...] = back[pl.ds(pl.multiple_of((g ^ i) * tok, tok), tok), :].astype(BF)
    sums[0:1, :] = jnp.sum(back[...] * hat_ref[...].astype(F32), axis=0, keepdims=True)
    sums[1:2, :] = jnp.sum(back[...], axis=0, keepdims=True)
    sums[2:3, : 3 * cols] = jnp.sum(project[...].astype(F32), axis=0, keepdims=True)
    d_in[...] = mm_lt(h_ref[...], project[...]).astype(BF)


def project_back(g, dq, dkv, h, hat, in_w):
    mine, width = h.shape
    parts = [part.shape[1] for part in dq]
    cols = sum(parts)
    ks = len(dkv[0])
    vmem = pl.BlockSpec(memory_space=pltpu.VMEM)
    got = pl.pallas_call(
        functools.partial(project_back_kernel, ks, parts),
        grid_spec=pltpu.PrefetchScalarGridSpec(
            num_scalar_prefetch=1,
            in_specs=[vmem] * (len(dq) * (ks + 1) + 3),
            out_specs=[vmem] * (GROUPS + 2),
            scratch_shapes=[pltpu.VMEM((mine, 3 * cols), BF), pltpu.VMEM((mine, width), F32)],
        ),
        out_shape=[jax.ShapeDtypeStruct((mine // GROUPS, width), BF)] * GROUPS
        + [
            jax.ShapeDtypeStruct((width, 3 * cols), BF),
            jax.ShapeDtypeStruct((8, width), F32),
        ],
        compiler_params=pltpu.CompilerParams(vmem_limit_bytes=16 * 2**20),
        cost_estimate=SHORT,
    )(
        jnp.stack([g]).astype(jnp.int32),
        *dq,
        *[p for pieces in dkv for p in pieces],
        *in_hbm(h, hat),
        in_w,
    )
    return got[:GROUPS], got[GROUPS], got[GROUPS + 1]


def finish_kernel(ks, extra, place, *refs):
    pieces, (in_out, out_out) = refs[: ks * GROUPS], refs[ks * GROUPS : ks * GROUPS + 2]
    vectors, (held, sums) = refs[ks * GROUPS + 2 : -2], refs[-2:]
    own, cols = in_out.shape[1], held.shape[2]
    part, low = cols // 3, own + extra
    share = own // GROUPS
    third = share // 3
    over = out_out.shape[3] - cols
    for j in range(ks):
        for i in range(GROUPS):
            held[place[0] ^ i] = pieces[j * GROUPS + i][...].astype(F32)
        spot = place[1] ^ j
        for i in range(GROUPS):
            for n in range(3):
                to = (n * GROUPS + i) * part
                in_out[spot, :, to : to + part] = held[i, :own, n * part : (n + 1) * part]
                out_out[i, spot, n * third : (n + 1) * third, cols:] = held[
                    i, low + share :, n * over : (n + 1) * over
                ]
            out_out[i, spot, :, :cols] = held[i, low : low + share, :]
        sums[spot] = total([held[i, own:low, :] for i in range(GROUPS)])
    unit = vectors[0].shape[0]
    per = cols // unit

    def slot(n):
        row, col = n // per, n % per * unit
        return sums[row // extra, row % extra : row % extra + 1, col : col + unit]

    for n in range(8):
        vectors[n][...] = slot(n).reshape(unit)
    last = jnp.concatenate([slot(8 + n) for n in range(GROUPS)], axis=1)
    vectors[8][...] = last.reshape(GROUPS * unit)


def finish(pieces, own, extra, width, g, k):
    ks = len(pieces)
    tall, cols = pieces[0][0].shape
    vmem = pl.BlockSpec(memory_space=pltpu.VMEM)
    shapes = [(ks, own, GROUPS * cols), (GROUPS, ks, own // GROUPS, width)]
    shapes += [(ks * own,)] * 8 + [(GROUPS * ks * own,)]
    in_w, out_w, *vectors = pl.pallas_call(
        functools.partial(finish_kernel, ks, extra),
        grid_spec=pltpu.PrefetchScalarGridSpec(
            num_scalar_prefetch=1,
            in_specs=[vmem] * (ks * GROUPS),
            out_specs=[vmem] * len(shapes),
            scratch_shapes=[
                pltpu.VMEM((GROUPS, tall, cols), F32),
                pltpu.VMEM((ks, extra, cols), F32),
            ],
        ),
        out_shape=[jax.ShapeDtypeStruct(s, F32) for s in shapes],
        compiler_params=pltpu.CompilerParams(vmem_limit_bytes=16 * 2**20),
        cost_estimate=SHORT,
    )(jnp.stack([g, k]).astype(jnp.int32), *[p for group in pieces for p in group])
    return in_w.reshape(ks * own, -1), out_w.reshape(ks * own, width), vectors


def shards(
    inputs,
    cotangent,
    first_gain,
    first_shift,
    input_weight,
    query_bias,
    value_bias,
    output_weight,
    output_bias,
    second_gain,
    second_shift,
    expand_weight,
    expand_bias,
    contract_weight,
    contract_bias,
):
    tok, width = inputs.shape[1:]
    ks, zs = lax.axis_size("core"), lax.axis_size("fsdp")
    g, k, z = lax.axis_index("grp"), lax.axis_index("core"), lax.axis_index("fsdp")
    rows_z = width // zs
    heads_here = HEADS // GROUPS
    head = width // HEADS
    cols = width // GROUPS
    ff = expand_weight.shape[1]
    ff_z = ff // zs
    ff_g = ff_z // GROUPS
    mine = GROUPS * tok
    scale = head ** (-0.5)

    x_own = inputs[0]
    slope_own = cotangent[0]

    smalls = [first_gain, first_shift, query_bias, value_bias, output_bias]
    smalls += [second_gain, second_shift, contract_bias, expand_bias]
    own = rows_z // ks
    aligned = own % 48 == 0 and zs == GROUPS
    if aligned:
        cut = cut_first(input_weight, output_weight, smalls, g, k, ks)
    else:
        cut = cut_weight(input_weight, 3, g, k, ks)
    pieces = gather_flips(cut, "fsdp")
    rows_both = gather_flips(jnp.concatenate([inputs, cotangent]), "grp")
    rest = cut_rest(contract_weight, expand_weight, zs, g, k, ks)
    pieces, rows_both, rest = lax.optimization_barrier((pieces, rows_both, rest))
    x_more = [send(b[0], "core", j) for j in range(1, ks) for b in rows_both]
    more = [[send(b, "core", j) for b in pieces] for j in range(1, ks)]
    if aligned:
        table = vector_table(pieces, own, rows_z, width, g, z)
        in_w, out_w = both_weights([pieces] + more, g, z, k, own, width)
    else:
        in_w = assemble([pieces] + more, z, k, own).reshape(width, 3 * cols)
        out_w = gather_flips(pick(output_weight.reshape(ks, own, width), k), "fsdp")
        out_more = [[send(b, "core", j) for b in out_w] for j in range(1, ks)]
        out_w = assemble([out_w] + out_more, z, k, own).reshape(GROUPS, cols, width)
        out_w = jnp.concatenate([pick(out_w, g ^ i) for i in range(GROUPS)])
        got = in_order(gather_flips(jnp.concatenate(smalls), "fsdp"), z).astype(F32)
        vectors = [got[:, i * rows_z : (i + 1) * rows_z].reshape(width) for i in range(8)]
        for i in (2, 3):
            vectors[i] = jnp.tile(pick(vectors[i].reshape(GROUPS, cols), g), GROUPS)
        got = got[:, 8 * rows_z :].reshape(zs, GROUPS, ff_g)
        vectors.append(lax.dynamic_index_in_dim(got, g, axis=1, keepdims=False).reshape(width))
        table = jnp.pad(jnp.stack(vectors), ((0, 7), (0, 0)))
    o_bias, gain_two, shift_two, c_bias = [table[i : i + 1] for i in range(4, 8)]

    rest = lax.all_gather(rest, ("fsdp", "core"), axis=0, tiled=True)

    *slots, qs, keys, values, att_full, lse, h1, hat_one = attend(
        g, k, ks, head, rows_both, x_more, in_w, table
    )
    att = jnp.concatenate(swap_flips(slots, "grp"), axis=1)
    x_f = x_own.astype(F32)
    middle = x_f + mm(att, out_w) + o_bias
    hat_two, rate_two = norm_stats(middle)
    h2 = (hat_two * gain_two + shift_two).astype(BF)
    h2_rows = gather_flips(h2, "grp")

    act, slope_inner, sh2_part, out_part, d_exp_b = hidden_part(
        h2_rows, rows_both, rest, table
    )
    sh2 = swap_flips(sh2_part, "grp")
    d_hidden = hidden_grads(h2_rows, rows_both, slope_inner, act)
    sh2, d_hidden = lax.optimization_barrier((sh2, d_hidden))
    sh2 = total(sh2)
    d_hidden = lax.psum_scatter(d_hidden, ("fsdp", "core"), scatter_dimension=0, tiled=True)

    slope_f = slope_own.astype(F32)
    d_gain_two = jnp.sum(sh2 * hat_two, axis=0, keepdims=True)
    d_shift_two = jnp.sum(sh2, axis=0, keepdims=True)
    slope_middle = slope_f + norm_back(sh2, gain_two, hat_two, rate_two)
    slope_branch = slope_middle.astype(BF)
    slope_att = mm_rt(slope_branch, out_w).astype(BF)
    datt = swap_flips([slope_att[:, i * cols : (i + 1) * cols] for i in range(GROUPS)], "grp")

    datt, out_part = lax.optimization_barrier((datt, out_part))
    out_sum = swap_flips(out_part, "grp")
    d_out = mm_lt(att, slope_branch).astype(BF).reshape(GROUPS, cols, width)
    d_out = in_order([d_out[i] for i in range(GROUPS)], g)
    d_out = d_out.reshape(zs, GROUPS, ks, own // GROUPS, width)
    pieces = [lax.dynamic_index_in_dim(d_out, k ^ j, axis=2, keepdims=False) for j in range(ks)]
    datt, pieces = lax.optimization_barrier((datt, pieces))
    d_out = swap_flips(pieces, "core")

    kept = (qs, keys, values, att_full, lse)
    split = (heads_here + 1) // 2
    dq, dkv = attend_back(g, k, ks, head, 0, split, datt, *kept)
    dq, dkv = [dq], [swap_flips([dkv[j] for j in range(ks)], "core")]
    datt, d_out, out_sum = lax.optimization_barrier((datt, d_out, out_sum))
    d_out = total(d_out).astype(BF)
    pieces = [lax.dynamic_index_in_dim(d_out, g ^ i, axis=1, keepdims=False) for i in range(GROUPS)]
    datt, pieces = lax.optimization_barrier((datt, pieces))
    d_out = swap_flips(pieces, "grp")
    more = attend_back(g, k, ks, head, split, heads_here - split, datt, *kept)
    dq.append(more[0])
    dkv.append(swap_flips([more[1][j] for j in range(ks)], "core"))
    sh1_part, d_in, sums = project_back(g, dq, dkv, h1, hat_one, in_w)
    sh1, d_hidden = lax.optimization_barrier((swap_flips(sh1_part, "grp"), d_hidden))
    sh1 = total(sh1)
    hat_own, rate_own = norm_stats(x_f)
    delta_inputs = (slope_middle + norm_back(sh1, table[0:1], hat_own, rate_own)).astype(BF)[None]

    extra = -(-(12 * rows_z) // (3 * cols * ks))
    packed = pack_vectors(
        g,
        zs,
        extra * ks,
        rows_z,
        sums,
        jnp.sum(slope_branch.astype(F32), axis=0, keepdims=True),
        d_gain_two,
        d_shift_two,
        jnp.sum(slope_f, axis=0, keepdims=True),
        d_exp_b,
    )
    d_out = total(d_out).astype(BF)
    third = d_out.shape[1] // 3
    tail = d_out[..., 3 * cols :]
    tail = [tail[:, i * third : (i + 1) * third] for i in range(3)]
    d_out = jnp.concatenate([d_out[..., : 3 * cols], jnp.concatenate(tail, axis=2)], axis=1)
    d_in = jnp.concatenate(
        [
            d_in.reshape(zs, ks, own, 3 * cols),
            packed.astype(BF).reshape(zs, ks, extra, 3 * cols),
        ],
        axis=2,
    )
    pieces = [lax.dynamic_index_in_dim(d_in, k ^ j, axis=1, keepdims=False) for j in range(ks)]
    d_in = total(swap_flips(pieces, "core")).astype(BF)
    d_in = jnp.concatenate([d_in, d_out], axis=1)
    pieces = lax.optimization_barrier([pick(d_in, z ^ i) for i in range(zs)])
    d_in = swap_flips(pieces, "fsdp")
    d_hidden = gather_flips(d_hidden, "grp")
    d_in = gather_flips(total(d_in).astype(BF), "grp")
    d_hidden = [d_hidden] + [[send(p, "core", j) for p in d_hidden] for j in range(1, ks)]
    d_exp_w, d_con_w = unfold(d_hidden, zs, g, k)
    d_in, d_exp_w, d_con_w = lax.optimization_barrier((d_in, d_exp_w, d_con_w))
    outputs = (middle + total(out_sum) + c_bias).astype(BF)[None]
    d_in = [d_in] + [[send(p, "core", j) for p in d_in] for j in range(1, ks)]
    d_in_w, d_out_w, packed = finish(d_in, own, extra, width, g, k)

    return (
        outputs,
        delta_inputs,
        packed[0],
        packed[1],
        d_in_w,
        packed[2],
        packed[3],
        d_out_w,
        packed[4],
        packed[5],
        packed[6],
        d_exp_w,
        packed[8],
        d_con_w,
        packed[7],
    )


def solution(mesh):
    ctx, zs = mesh.shape["ctx"], mesh.shape["fsdp"]
    axes = ("grp", "core", "fsdp")
    split = Mesh(mesh.devices.reshape(GROUPS, ctx // GROUPS, zs), axes)
    row, vec, mat = P("fsdp", ("grp", "core"), None), P("fsdp"), P("fsdp", None)
    placed = (row, row, vec, vec, mat, vec, vec, mat, vec, vec, vec, mat, vec, mat, vec)
    return jax.shard_map(
        shards,
        mesh=split,
        in_specs=placed,
        out_specs=placed,
        check_vma=False,
    )
```

```python
import functools

import jax
import jax.numpy as jnp
from jax import lax
from jax.experimental import pallas as pl
from jax.experimental.pallas import tpu as pltpu
from jax.sharding import Mesh, PartitionSpec as P

HEADS = 12
GROUPS = 4

NORM_EPS = 1e-05
MASK_FILL = -1e30
GELU_COEF = 0.7978845608028654
GELU_CUBE = 0.044715

SHORT = pl.CostEstimate(flops=1, bytes_accessed=1, transcendentals=0)
LONG = pl.CostEstimate(flops=8 * 10**9, bytes_accessed=1, transcendentals=0)

BF = jnp.bfloat16
F32 = jnp.float32


def in_hbm(*values):
    return [pltpu.with_memory_space_constraint(v, pltpu.HBM) for v in values]


def mm(left, right):
    return jnp.dot(left, right, preferred_element_type=F32)


def mm_lt(left, right):
    return lax.dot_general(left, right, (((0,), (0,)), ((), ())), preferred_element_type=F32)


def mm_rt(left, right):
    return lax.dot_general(left, right, (((1,), (1,)), ((), ())), preferred_element_type=F32)


def send(value, axis, flip):
    count = lax.axis_size(axis)
    return lax.ppermute(value, axis, [(s, s ^ flip) for s in range(count)])


def gather_flips(value, axis):
    return [value] + [send(value, axis, i) for i in range(1, lax.axis_size(axis))]


def swap_flips(pieces, axis):
    return [pieces[0]] + [send(p, axis, i) for i, p in enumerate(pieces) if i]


def pick(stacked, place):
    return lax.dynamic_index_in_dim(stacked, place, axis=0, keepdims=False)


def in_order(pieces, me):
    stacked = jnp.stack(pieces)
    return jnp.stack([pick(stacked, me ^ j) for j in range(len(pieces))])


def norm_stats(values):
    center = values - jnp.mean(values, axis=-1, keepdims=True)
    spread = jnp.mean(center * center, axis=-1, keepdims=True)
    rate = lax.rsqrt(spread + NORM_EPS)
    return center * rate, rate


def norm_back(slope, gain, hat, rate):
    scaled = slope * gain
    return rate * (
        scaled
        - jnp.mean(scaled, axis=-1, keepdims=True)
        - hat * jnp.mean(scaled * hat, axis=-1, keepdims=True)
    )


def total(parts):
    out = parts[0].astype(F32)
    for part in parts[1:]:
        out = out + part.astype(F32)
    return out


def cut_columns(source, cut, parts, i):
    wide = cut.shape[1] // parts
    for part in range(parts):
        low = (part * GROUPS + i) * wide
        cut[:, part * wide : (part + 1) * wide] = source[:, low : low + wide]


def cut_kernel(parts, place, source, cut):
    for i in range(GROUPS):

        @pl.when(place[0] == i)
        def _():
            cut_columns(source, cut, parts, i)


def cut_weight(weight, parts, g, k, ks):
    rows = weight.shape[0] // ks
    cols = weight.shape[1] // GROUPS
    if rows % 16 == 0:
        return pl.pallas_call(
            functools.partial(cut_kernel, parts),
            grid_spec=pltpu.PrefetchScalarGridSpec(
                num_scalar_prefetch=1,
                grid=(1,),
                in_specs=[pl.BlockSpec((rows, weight.shape[1]), lambda i, place: (place[1], 0))],
                out_specs=pl.BlockSpec((rows, cols), lambda i, place: (0, 0)),
            ),
            out_shape=jax.ShapeDtypeStruct((rows, cols), BF),
            compiler_params=pltpu.CompilerParams(vmem_limit_bytes=8 * 2**20),
        )(jnp.stack([g, k]).astype(jnp.int32), weight)
    half = pick(weight.reshape(ks, rows, -1), k)
    return lax.dynamic_index_in_dim(
        half.reshape(rows, parts, GROUPS, cols // parts), g, axis=2, keepdims=False
    ).reshape(rows, cols)


def cut_first_kernel(place, *refs):
    source, other, vectors, cut, held = refs[0], refs[1], refs[2:-2], refs[-2], refs[-1]
    rows = source.shape[0]
    third, cols = rows // 3, cut.shape[1]
    cut[rows + 16 : 2 * rows + 16, :] = other[:, :cols]
    over = other.shape[1] - cols
    for part in range(3):
        cut[2 * rows + 16 :, part * over : (part + 1) * over] = other[
            part * third : (part + 1) * third, cols:
        ]
    unit = vectors[0].shape[0]
    per = cut.shape[1] // unit
    held[...] = jnp.zeros_like(held)
    spot = 0
    for vector in vectors:
        row = vector[...].astype(F32).reshape(1, vector.shape[0])
        for part in range(vector.shape[0] // unit):
            col = spot % per * unit
            held[spot // per : spot // per + 1, col : col + unit] = row[
                :, part * unit : (part + 1) * unit
            ]
            spot += 1
    cut[rows : rows + 16, :] = held[...].astype(BF)
    for i in range(GROUPS):

        @pl.when(place[0] == i)
        def _():
            cut_columns(source, cut.at[:rows, :], 3, i)


def cut_first(weight, other, vectors, g, k, ks):
    rows, cols = weight.shape[0] // ks, weight.shape[1] // GROUPS
    tall = 2 * rows + 16 + rows // 3
    by_k = lambda i, place: (place[1], 0)
    return pl.pallas_call(
        cut_first_kernel,
        grid_spec=pltpu.PrefetchScalarGridSpec(
            num_scalar_prefetch=1,
            grid=(1,),
            in_specs=[
                pl.BlockSpec((rows, weight.shape[1]), by_k),
                pl.BlockSpec((rows, other.shape[1]), by_k),
            ]
            + [pl.BlockSpec(v.shape, lambda i, place: (0,)) for v in vectors],
            out_specs=pl.BlockSpec((tall, cols), lambda i, place: (0, 0)),
            scratch_shapes=[pltpu.VMEM((16, cols), F32)],
        ),
        out_shape=jax.ShapeDtypeStruct((tall, cols), BF),
        compiler_params=pltpu.CompilerParams(vmem_limit_bytes=8 * 2**20),
        cost_estimate=SHORT,
    )(jnp.stack([g, k]).astype(jnp.int32), *in_hbm(weight, other, *vectors))


def both_weights_kernel(rows, place, *refs):
    pieces, in_w, out_w = refs[:-2], refs[-2], refs[-1]
    zs, ks = in_w.shape[:2]
    third, cols = rows // 3, in_w.shape[3]
    over = out_w.shape[3] - cols
    low = rows + 16
    for j in range(ks):
        for i in range(zs):
            piece = pieces[j * zs + i]
            in_w[place[1] ^ i, place[2] ^ j] = piece[:rows, :]
            spot = (place[1] ^ i ^ place[0], place[2] ^ j)
            out_w[spot[0], spot[1], :, :cols] = piece[low : low + rows, :]
            for part in range(3):
                out_w[spot[0], spot[1], part * third : (part + 1) * third, cols:] = piece[
                    low + rows :, part * over : (part + 1) * over
                ]


def both_weights(pieces, g, z, k, rows, width):
    ks, zs = len(pieces), len(pieces[0])
    cols = pieces[0][0].shape[1]
    vmem = pl.BlockSpec(memory_space=pltpu.VMEM)
    shapes = [(zs, ks, rows, cols), (zs, ks, rows, width)]
    in_w, out_w = pl.pallas_call(
        functools.partial(both_weights_kernel, rows),
        grid_spec=pltpu.PrefetchScalarGridSpec(
            num_scalar_prefetch=1, in_specs=[vmem] * (zs * ks), out_specs=[vmem] * 2
        ),
        out_shape=[jax.ShapeDtypeStruct(s, BF) for s in shapes],
        compiler_params=pltpu.CompilerParams(vmem_limit_bytes=16 * 2**20),
        cost_estimate=SHORT,
    )(jnp.stack([g, z, k]).astype(jnp.int32), *[p for group in pieces for p in group])
    return in_w.reshape(width, cols), out_w.reshape(width, width)


def table_kernel(unit, place, *refs):
    pieces, out, held = refs[:-2], refs[-2], refs[-1]
    zs = len(pieces)
    per = held.shape[2] // unit
    cols = out.shape[1] // GROUPS
    for i, piece in enumerate(pieces):
        held[place[1] ^ i] = piece[...].astype(F32)

    def unpack(row, slot):
        for zz in range(zs):
            col = slot % per * unit
            out[row : row + 1, zz * unit : (zz + 1) * unit] = held[
                zz, slot // per : slot // per + 1, col : col + unit
            ]

    out[...] = jnp.zeros_like(out)
    for slot in range(8):
        unpack(slot + 8 if slot in (2, 3) else slot, slot)
    for i in range(GROUPS):

        @pl.when(place[0] == i)
        def _():
            unpack(8, 8 + i)
            out[2:4, :cols] = out[10:12, i * cols : (i + 1) * cols]


def vector_table(pieces, below, unit, width, g, z):
    cols = pieces[0].shape[1]
    return pl.pallas_call(
        functools.partial(table_kernel, unit),
        grid_spec=pltpu.PrefetchScalarGridSpec(
            num_scalar_prefetch=1,
            grid=(1,),
            in_specs=[pl.BlockSpec((16, cols), lambda i, place: (below // 16, 0))] * len(pieces),
            out_specs=pl.BlockSpec((16, width), lambda i, place: (0, 0)),
            scratch_shapes=[pltpu.VMEM((len(pieces), 16, cols), F32)],
        ),
        out_shape=jax.ShapeDtypeStruct((16, width), F32),
        compiler_params=pltpu.CompilerParams(vmem_limit_bytes=8 * 2**20),
    )(jnp.stack([g, z]).astype(jnp.int32), *pieces)


def pack_kernel(zs, stride, unit, place, sums, out_bias, gain, shift, con_bias, exp_bias, out):
    per = out.shape[1] // unit
    cols = out.shape[1] // 3

    def put(zz, slot, value):
        row, col = zz * stride + slot // per, slot % per * unit
        out[row : row + 1, col : col + unit] = value

    out[...] = jnp.zeros_like(out)
    whole = [(0, sums, 0), (1, sums, 1), (4, out_bias, 0), (5, gain, 0), (6, shift, 0), (7, con_bias, 0)]
    for slot, source, row in whole:
        for zz in range(zs):
            put(zz, slot, source[row : row + 1, zz * unit : (zz + 1) * unit])
    for i in range(GROUPS):

        @pl.when(place[0] == i)
        def _():
            for zz in range(zs):
                put(zz, 8 + i, exp_bias[:, zz * unit : (zz + 1) * unit])
            for part in range(cols // unit):
                zz = i * cols // unit + part
                low = part * unit
                put(zz, 2, sums[2:3, low : low + unit])
                put(zz, 3, sums[2:3, 2 * cols + low : 2 * cols + low + unit])


def pack_vectors(g, zs, stride, unit, sums, *vectors):
    wide = 3 * (vectors[0].shape[1] // GROUPS)
    vmem = pl.BlockSpec(memory_space=pltpu.VMEM)
    return pl.pallas_call(
        functools.partial(pack_kernel, zs, stride, unit),
        grid_spec=pltpu.PrefetchScalarGridSpec(
            num_scalar_prefetch=1, in_specs=[vmem] * (1 + len(vectors)), out_specs=vmem
        ),
        out_shape=jax.ShapeDtypeStruct((zs * stride, wide), F32),
        compiler_params=pltpu.CompilerParams(vmem_limit_bytes=8 * 2**20),
    )(jnp.stack([g]).astype(jnp.int32), sums, *vectors)


def cut_rest_kernel(parts, place, con_ref, exp_ref, cut):
    width = con_ref.shape[1]
    cut[:, :width] = con_ref[...]
    for i in range(GROUPS):

        @pl.when(place[0] == i)
        def _():
            cut_columns(exp_ref, cut.at[:, width:], parts, i)


def cut_rest(con_w, exp_w, parts, g, k, ks):
    width = con_w.shape[1]
    rows, ff_rows = exp_w.shape[0] // ks, con_w.shape[0] // (GROUPS * ks)
    wide = exp_w.shape[1] // GROUPS
    if rows % 16 == 0 and rows == ff_rows:
        return pl.pallas_call(
            functools.partial(cut_rest_kernel, parts),
            grid_spec=pltpu.PrefetchScalarGridSpec(
                num_scalar_prefetch=1,
                grid=(1,),
                in_specs=[
                    pl.BlockSpec((rows, width), lambda i, place: (place[0] * ks + place[1], 0)),
                    pl.BlockSpec((rows, exp_w.shape[1]), lambda i, place: (place[1], 0)),
                ],
                out_specs=pl.BlockSpec((rows, width + wide), lambda i, place: (0, 0)),
            ),
            out_shape=jax.ShapeDtypeStruct((rows, width + wide), BF),
            compiler_params=pltpu.CompilerParams(vmem_limit_bytes=8 * 2**20),
        )(jnp.stack([g, k]).astype(jnp.int32), *in_hbm(con_w, exp_w))
    return jnp.concatenate(
        [
            pick(con_w.reshape(GROUPS * ks, ff_rows, width), g * ks + k),
            cut_weight(exp_w, parts, g, k, ks),
        ],
        axis=1,
    )


def assemble_kernel(rows, place, *refs):
    pieces, out = refs[:-1], refs[-1]
    zs = out.shape[0]
    for j in range(out.shape[1]):
        for i in range(zs):
            out[place[0] ^ i, place[1] ^ j] = pieces[j * zs + i][:rows, :]


def assemble(pieces, first, k, rows):
    ks, zs = len(pieces), len(pieces[0])
    cols = pieces[0][0].shape[1]
    shape = (zs, ks, rows, cols)
    if rows % 16:
        parts = [in_order([p[:rows] for p in group], first) for group in pieces]
        return jnp.stack(in_order(parts, k), axis=1).reshape(zs, ks * rows, cols)
    vmem = pl.BlockSpec(memory_space=pltpu.VMEM)
    out = pl.pallas_call(
        functools.partial(assemble_kernel, rows),
        grid_spec=pltpu.PrefetchScalarGridSpec(
            num_scalar_prefetch=1, in_specs=[vmem] * (zs * ks), out_specs=vmem
        ),
        out_shape=jax.ShapeDtypeStruct(shape, BF),
        compiler_params=pltpu.CompilerParams(vmem_limit_bytes=8 * 2**20),
        cost_estimate=SHORT,
    )(jnp.stack([first, k]).astype(jnp.int32), *[p for group in pieces for p in group])
    return out.reshape(zs, ks * rows, cols)


def unfold_kernel(parts, ks, place, *refs):
    pieces, (exp_out, con_out, held) = refs[:-3], refs[-3:]
    wide = con_out.shape[3]
    part_wide = wide // parts
    for j in range(ks):
        for i in range(GROUPS):
            held[place[0] ^ i] = pieces[j * GROUPS + i][...]
        spot = place[1] ^ j
        for i in range(GROUPS):
            con_out[i, spot] = held[i, :, wide:].astype(F32)
            for part in range(parts):
                low = (part * GROUPS + i) * part_wide
                exp_out[spot, :, low : low + part_wide] = held[
                    i, :, part * part_wide : (part + 1) * part_wide
                ].astype(F32)


def unfold(pieces, parts, g, k):
    ks = len(pieces)
    rows, wide = pieces[0][0].shape[0], pieces[0][0].shape[1] // 2
    step = rows // 2 if rows % 32 == 0 else rows
    shapes = [(ks, rows, GROUPS * wide), (GROUPS, ks, rows, wide)]
    exp, con = pl.pallas_call(
        functools.partial(unfold_kernel, parts, ks),
        grid_spec=pltpu.PrefetchScalarGridSpec(
            num_scalar_prefetch=1,
            grid=(rows // step,),
            in_specs=[pl.BlockSpec((step, 2 * wide), lambda i, place: (i, 0))] * (ks * GROUPS),
            out_specs=[
                pl.BlockSpec((ks, step, GROUPS * wide), lambda i, place: (0, i, 0)),
                pl.BlockSpec((GROUPS, ks, step, wide), lambda i, place: (0, 0, i, 0)),
            ],
            scratch_shapes=[pltpu.VMEM((GROUPS, step, 2 * wide), BF)],
        ),
        out_shape=[jax.ShapeDtypeStruct(s, F32) for s in shapes],
        compiler_params=pltpu.CompilerParams(vmem_limit_bytes=20 * 2**20),
        cost_estimate=SHORT,
    )(jnp.stack([g, k]).astype(jnp.int32), *[p for group in pieces for p in group])
    return exp.reshape(ks * rows, -1), con.reshape(-1, wide)


def join_rows(pieces, joined):
    tok = joined.shape[0] // GROUPS
    for i, piece in enumerate(pieces):
        joined[i * tok : (i + 1) * tok, :] = piece[...].reshape(tok, joined.shape[1])


def hidden_kernel(*refs):
    h_rows, s_rows = refs[:GROUPS], refs[GROUPS : 2 * GROUPS]
    exp_w, con_w, bias, act_ref, inner_ref = refs[2 * GROUPS : 2 * GROUPS + 5]
    back_ref = refs[2 * GROUPS + 5 : 3 * GROUPS + 5]
    out_ref = refs[3 * GROUPS + 5 : 4 * GROUPS + 5]
    bias_ref = refs[4 * GROUPS + 5]
    h_ref, s_ref, back_sum, out_sum = refs[-4:]
    step = pl.program_id(0)
    tok = h_rows[0].shape[0]

    @pl.when(step == 0)
    def _():
        join_rows(h_rows, h_ref)
        join_rows(s_rows, s_ref)

    inner = mm(h_ref[...], exp_w[...]) + bias[8:9, :]
    square = inner * inner
    tanh = jnp.tanh(GELU_COEF * (inner + GELU_CUBE * square * inner))
    half = 0.5 + 0.5 * tanh
    act = (inner * half).astype(BF)
    gelu_slope = half + (0.5 * GELU_COEF) * inner * (1.0 - tanh * tanh) * (
        1.0 + (3.0 * GELU_CUBE) * square
    )
    slope = (mm_rt(s_ref[...], con_w[...]) * gelu_slope).astype(BF)
    act_ref[...] = act
    inner_ref[...] = slope
    bias_ref[...] = jnp.sum(slope.astype(F32), axis=0, keepdims=True)
    back = mm_rt(slope, exp_w[...])
    out = mm(act, con_w[...])

    @pl.when(step == 0)
    def _():
        back_sum[...] = back
        out_sum[...] = out

    @pl.when(step > 0)
    def _():
        back_sum[...] += back
        out_sum[...] += out

    @pl.when(step == pl.num_programs(0) - 1)
    def _():
        for i in range(GROUPS):
            back_ref[i][...] = back_sum[i * tok : (i + 1) * tok, :].astype(BF)
            out_ref[i][...] = out_sum[i * tok : (i + 1) * tok, :].astype(BF)


def hidden_part(h_rows, s_rows, weights, table):
    tok, width = h_rows[0].shape
    hidden = weights.shape[1] - width
    rows = GROUPS * tok
    step = 256
    fixed = lambda i: (0, 0)
    cols = lambda i: (0, i)
    slots = [pl.BlockSpec((tok, width), fixed)] * GROUPS
    got = pl.pallas_call(
        hidden_kernel,
        grid=(hidden // step,),
        in_specs=[pl.BlockSpec((tok, width), fixed)] * GROUPS
        + [pl.BlockSpec((1, tok, width), lambda i: (1, 0, 0))] * GROUPS
        + [
            pl.BlockSpec((width, step), lambda i: (0, width // step + i)),
            pl.BlockSpec((step, width), lambda i: (i, 0)),
            pl.BlockSpec((16, step), cols),
        ],
        out_specs=[
            pl.BlockSpec((rows, step), cols),
            pl.BlockSpec((rows, step), cols),
            *slots,
            *slots,
            pl.BlockSpec((1, step), cols),
        ],
        out_shape=[
            jax.ShapeDtypeStruct((rows, hidden), BF),
            jax.ShapeDtypeStruct((rows, hidden), BF),
            *[jax.ShapeDtypeStruct((tok, width), BF)] * GROUPS,
            *[pltpu.HBM((tok, width), BF)] * GROUPS,
            jax.ShapeDtypeStruct((1, hidden), F32),
        ],
        scratch_shapes=[pltpu.VMEM((rows, width), BF)] * 2 + [pltpu.VMEM((rows, width), F32)] * 2,
        compiler_params=pltpu.CompilerParams(vmem_limit_bytes=24 * 2**20),
        cost_estimate=SHORT,
    )(*in_hbm(*h_rows, *s_rows, weights, weights), table)
    return got[0], got[1], got[2 : 2 + GROUPS], got[2 + GROUPS : 2 + 2 * GROUPS], got[-1]


def hidden_grad_kernel(*refs):
    h_rows, s_rows = refs[:GROUPS], refs[GROUPS : 2 * GROUPS]
    inner_ref, act_ref, out_ref, h_ref, s_ref = refs[2 * GROUPS :]
    wide, step = inner_ref.shape[1], act_ref.shape[1]

    @pl.when(pl.program_id(0) == 0)
    def _():
        join_rows(s_rows, s_ref)

    join_rows(h_rows, h_ref)
    out_ref[:, :wide] = mm_lt(h_ref[...], inner_ref[...]).astype(BF)
    out_ref[:, wide:] = mm_lt(act_ref[...], s_ref[...]).astype(BF)


def hidden_grads(h_rows, s_rows, slope_inner, act):
    tok, width = h_rows[0].shape
    rows, hidden = act.shape
    step = 256
    cols = lambda i: (0, i)
    fixed = lambda i: (0, 0)
    return pl.pallas_call(
        hidden_grad_kernel,
        grid=(width // step,),
        in_specs=[pl.BlockSpec((tok, step), cols)] * GROUPS
        + [pl.BlockSpec((1, tok, width), lambda i: (1, 0, 0))] * GROUPS
        + [pl.BlockSpec((rows, hidden), fixed), pl.BlockSpec((rows, step), cols)],
        out_specs=pl.BlockSpec((step, hidden + width), lambda i: (i, 0)),
        out_shape=jax.ShapeDtypeStruct((width, hidden + width), BF),
        scratch_shapes=[pltpu.VMEM((rows, step), BF), pltpu.VMEM((rows, width), BF)],
        compiler_params=pltpu.CompilerParams(vmem_limit_bytes=16 * 2**20),
        cost_estimate=LONG,
    )(*in_hbm(*h_rows, *s_rows), slope_inner, act)


def visible(k, tok, keys):
    row = lax.broadcasted_iota(jnp.int32, (tok, keys), 0)
    col = lax.broadcasted_iota(jnp.int32, (tok, keys), 1)
    return col <= k * tok + row


def masked_scores(query, keys, seen):
    scores = mm_rt(query, keys)
    near = keys.shape[0] - seen.shape[1]
    last = jnp.where(seen, scores[:, near:], MASK_FILL)
    return last if near == 0 else jnp.concatenate([scores[:, :near], last], axis=1)


def attend_kernel(ks, head, place, *refs):
    pieces = refs[: GROUPS * ks]
    in_w, table = refs[GROUPS * ks : GROUPS * ks + 2]
    slots = refs[GROUPS * ks + 2 : GROUPS * ks + 2 + GROUPS]
    q_out, k_out, v_out, att_out, lse_out, h_out, hat_out, h_all = refs[GROUPS * ks + 2 + GROUPS :]
    g, k = place[0], place[1]
    tok, width = pieces[-1].shape
    cols = q_out.shape[1]
    gain, shift = table[0:1, :], table[1:2, :]
    for j in range(ks):
        for i in range(GROUPS):
            piece = pieces[j * GROUPS + i]
            hat, _ = norm_stats((piece[...] if j else piece[0]).astype(F32))
            normed = (hat * gain + shift).astype(BF)
            spot = pl.multiple_of(((g ^ i) * ks + (k ^ j)) * tok, tok)
            h_all[pl.ds(spot, tok), :] = normed
            if j == 0:
                spot = pl.multiple_of((g ^ i) * tok, tok)
                h_out[pl.ds(spot, tok), :] = normed
                hat_out[pl.ds(spot, tok), :] = hat.astype(BF)
    q_out[...] = (mm(h_out[...], in_w[:, :cols]) + table[2:3, :cols]).astype(BF)
    kv = mm(h_all[...], in_w[:, cols:])
    k_out[...] = kv[:, :cols].astype(BF)
    v_out[...] = (kv[:, cols:] + table[3:4, :cols]).astype(BF)
    seen = visible(k, tok, ks * tok)
    for h in range(cols // head):
        low, high = h * head, (h + 1) * head
        for i in range(GROUPS):
            rows = slice(i * tok, (i + 1) * tok)
            span = (i + 1) * ks * tok
            query = (q_out[rows, low:high].astype(F32) * head**-0.5).astype(BF)
            scores = masked_scores(query, k_out[:span, low:high], seen)
            peak = jnp.max(scores, axis=-1, keepdims=True)
            weights = jnp.exp(scores - peak)
            mass = jnp.sum(weights, axis=-1, keepdims=True)
            lse_out[rows, h : h + 1] = peak + jnp.log(mass)
            att = mm(weights.astype(BF), v_out[:span, low:high]) / mass
            att_out[rows, low:high] = att
    for i in range(GROUPS):
        slots[i][...] = att_out[pl.ds(pl.multiple_of((g ^ i) * tok, tok), tok), :].astype(BF)


def attend(g, k, ks, head, both, more, in_w, table):
    tok, width = both[0].shape[1:]
    cols = in_w.shape[1] // 3
    mine, rows = GROUPS * tok, GROUPS * ks * tok
    vmem = pl.BlockSpec(memory_space=pltpu.VMEM)
    shapes = [
        *[((tok, cols), BF)] * GROUPS,
        ((mine, cols), BF),
        ((rows, cols), BF),
        ((rows, cols), BF),
        ((mine, cols), F32),
        ((mine, 8), F32),
        ((mine, width), BF),
        ((mine, width), BF),
    ]
    return pl.pallas_call(
        functools.partial(attend_kernel, ks, head),
        grid_spec=pltpu.PrefetchScalarGridSpec(
            num_scalar_prefetch=1,
            in_specs=[pl.BlockSpec((1, tok, width), lambda i, place: (0, 0, 0))] * GROUPS
            + [vmem] * (len(more) + 2),
            grid=(1,),
            out_specs=[vmem] * len(shapes),
            scratch_shapes=[pltpu.VMEM((rows, width), BF)],
        ),
        out_shape=[jax.ShapeDtypeStruct(s, t) for s, t in shapes[:GROUPS]]
        + [pltpu.HBM(s, t) for s, t in shapes[GROUPS:]],
        compiler_params=pltpu.CompilerParams(vmem_limit_bytes=(16 if ks == 2 else 48) * 2**20),
        cost_estimate=SHORT,
    )(jnp.stack([g, k]).astype(jnp.int32), *both, *more, in_w, table)


def attend_back_kernel(ks, head, first, place, *refs):
    slopes = refs[:GROUPS]
    q_ref, k_ref, v_ref, att_ref, lse_ref, dq_out, dkv_out = refs[GROUPS : GROUPS + 7]
    dk_sum, dv_sum, slope_rows = refs[GROUPS + 7 :]
    g, k = place[0], place[1]
    tok = slopes[0].shape[0]
    heads = dq_out.shape[1] // head
    for i in range(GROUPS):
        slope_rows[pl.ds(pl.multiple_of((g ^ i) * tok, tok), tok), :] = slopes[i][...]
    seen = visible(k, tok, ks * tok)
    for i in reversed(range(GROUPS)):
        rows = slice(i * tok, (i + 1) * tok)
        span = (i + 1) * ks * tok
        for h in range(heads):
            low, high = (first + h) * head, (first + h + 1) * head
            to = slice(h * head, (h + 1) * head)
            query = (q_ref[rows, low:high].astype(F32) * head**-0.5).astype(BF)
            keys = k_ref[:span, low:high]
            slope = slope_rows[rows, low:high]
            scores = masked_scores(query, keys, seen)
            chances = jnp.exp(scores - lse_ref[rows, first + h : first + h + 1])
            diag = jnp.sum(slope.astype(F32) * att_ref[rows, low:high], axis=-1, keepdims=True)
            slope_chances = mm_rt(slope, v_ref[:span, low:high])
            slope_scores = (chances * (slope_chances - diag)).astype(BF)
            dq_out[rows, to] = (mm(slope_scores, keys) * head**-0.5).astype(BF)
            dk = mm_lt(slope_scores, query)
            dv = mm_lt(chances.astype(BF), slope)
            if i == GROUPS - 1:
                dk_sum[:, to] = dk
                dv_sum[:, to] = dv
            else:
                dk_sum[:span, to] += dk
                dv_sum[:span, to] += dv
    for i in range(GROUPS):
        for j in range(ks):
            spot = slice((i * ks + j) * tok, (i * ks + j + 1) * tok)
            dkv_out[k ^ j, i * tok : (i + 1) * tok, :] = jnp.concatenate(
                [dk_sum[spot, :], dv_sum[spot, :]], axis=1
            ).astype(BF)


def attend_back(g, k, ks, head, first, heads, slopes, q, keys, values, att, lse):
    tok, cols = slopes[0].shape
    mine, rows = GROUPS * tok, GROUPS * ks * tok
    wide = heads * head
    vmem = pl.BlockSpec(memory_space=pltpu.VMEM)
    return pl.pallas_call(
        functools.partial(attend_back_kernel, ks, head, first),
        grid_spec=pltpu.PrefetchScalarGridSpec(
            num_scalar_prefetch=1,
            in_specs=[vmem] * (len(slopes) + 5),
            out_specs=[vmem] * 2,
            scratch_shapes=[pltpu.VMEM((rows, wide), F32)] * 2 + [pltpu.VMEM((mine, cols), BF)],
        ),
        out_shape=[
            jax.ShapeDtypeStruct((mine, wide), BF),
            jax.ShapeDtypeStruct((ks, mine, 2 * wide), BF),
        ],
        compiler_params=pltpu.CompilerParams(vmem_limit_bytes=(16 if ks == 2 else 48) * 2**20),
        cost_estimate=LONG,
    )(jnp.stack([g, k]).astype(jnp.int32), *slopes, *in_hbm(q, keys, values, att, lse))


def project_back_kernel(ks, parts, place, *refs):
    count = len(parts)
    dq, dkv = refs[:count], refs[count : count + count * ks]
    h_ref, hat_ref, in_w = refs[count * (ks + 1) : count * (ks + 1) + 3]
    slots, (d_in, sums, project, back) = refs[-GROUPS - 4 : -4], refs[-4:]
    g = place[0]
    tok = slots[0].shape[0]
    cols = sum(parts)
    low = 0
    for n, wide in enumerate(parts):
        project[:, low : low + wide] = dq[n][...]
        both = total([dkv[n * ks + j][...] for j in range(ks)]).astype(BF)
        project[:, cols + low : cols + low + wide] = both[:, :wide]
        project[:, 2 * cols + low : 2 * cols + low + wide] = both[:, wide:]
        low += wide
    back[...] = mm_rt(project[...], in_w[...])
    for i in range(GROUPS):
        slots[i][...] = back[pl.ds(pl.multiple_of((g ^ i) * tok, tok), tok), :].astype(BF)
    sums[0:1, :] = jnp.sum(back[...] * hat_ref[...].astype(F32), axis=0, keepdims=True)
    sums[1:2, :] = jnp.sum(back[...], axis=0, keepdims=True)
    sums[2:3, : 3 * cols] = jnp.sum(project[...].astype(F32), axis=0, keepdims=True)
    d_in[...] = mm_lt(h_ref[...], project[...]).astype(BF)


def project_back(g, dq, dkv, h, hat, in_w):
    mine, width = h.shape
    parts = [part.shape[1] for part in dq]
    cols = sum(parts)
    ks = len(dkv[0])
    vmem = pl.BlockSpec(memory_space=pltpu.VMEM)
    got = pl.pallas_call(
        functools.partial(project_back_kernel, ks, parts),
        grid_spec=pltpu.PrefetchScalarGridSpec(
            num_scalar_prefetch=1,
            in_specs=[vmem] * (len(dq) * (ks + 1) + 3),
            out_specs=[vmem] * (GROUPS + 2),
            scratch_shapes=[pltpu.VMEM((mine, 3 * cols), BF), pltpu.VMEM((mine, width), F32)],
        ),
        out_shape=[jax.ShapeDtypeStruct((mine // GROUPS, width), BF)] * GROUPS
        + [
            jax.ShapeDtypeStruct((width, 3 * cols), BF),
            jax.ShapeDtypeStruct((8, width), F32),
        ],
        compiler_params=pltpu.CompilerParams(vmem_limit_bytes=16 * 2**20),
        cost_estimate=SHORT,
    )(
        jnp.stack([g]).astype(jnp.int32),
        *dq,
        *[p for pieces in dkv for p in pieces],
        *in_hbm(h, hat),
        in_w,
    )
    return got[:GROUPS], got[GROUPS], got[GROUPS + 1]


def finish_kernel(ks, extra, place, *refs):
    pieces, (in_out, out_out) = refs[: ks * GROUPS], refs[ks * GROUPS : ks * GROUPS + 2]
    vectors, (held, sums) = refs[ks * GROUPS + 2 : -2], refs[-2:]
    own, cols = in_out.shape[1], held.shape[2]
    part, low = cols // 3, own + extra
    share = own // GROUPS
    third = share // 3
    over = out_out.shape[3] - cols
    for j in range(ks):
        for i in range(GROUPS):
            held[place[0] ^ i] = pieces[j * GROUPS + i][...].astype(F32)
        spot = place[1] ^ j
        for i in range(GROUPS):
            for n in range(3):
                to = (n * GROUPS + i) * part
                in_out[spot, :, to : to + part] = held[i, :own, n * part : (n + 1) * part]
                out_out[i, spot, n * third : (n + 1) * third, cols:] = held[
                    i, low + share :, n * over : (n + 1) * over
                ]
            out_out[i, spot, :, :cols] = held[i, low : low + share, :]
        sums[spot] = total([held[i, own:low, :] for i in range(GROUPS)])
    unit = vectors[0].shape[0]
    per = cols // unit

    def slot(n):
        row, col = n // per, n % per * unit
        return sums[row // extra, row % extra : row % extra + 1, col : col + unit]

    for n in range(8):
        vectors[n][...] = slot(n).reshape(unit)
    last = jnp.concatenate([slot(8 + n) for n in range(GROUPS)], axis=1)
    vectors[8][...] = last.reshape(GROUPS * unit)


def finish(pieces, own, extra, width, g, k):
    ks = len(pieces)
    tall, cols = pieces[0][0].shape
    vmem = pl.BlockSpec(memory_space=pltpu.VMEM)
    shapes = [(ks, own, GROUPS * cols), (GROUPS, ks, own // GROUPS, width)]
    shapes += [(ks * own,)] * 8 + [(GROUPS * ks * own,)]
    in_w, out_w, *vectors = pl.pallas_call(
        functools.partial(finish_kernel, ks, extra),
        grid_spec=pltpu.PrefetchScalarGridSpec(
            num_scalar_prefetch=1,
            in_specs=[vmem] * (ks * GROUPS),
            out_specs=[vmem] * len(shapes),
            scratch_shapes=[
                pltpu.VMEM((GROUPS, tall, cols), F32),
                pltpu.VMEM((ks, extra, cols), F32),
            ],
        ),
        out_shape=[jax.ShapeDtypeStruct(s, F32) for s in shapes],
        compiler_params=pltpu.CompilerParams(vmem_limit_bytes=16 * 2**20),
        cost_estimate=SHORT,
    )(jnp.stack([g, k]).astype(jnp.int32), *[p for group in pieces for p in group])
    return in_w.reshape(ks * own, -1), out_w.reshape(ks * own, width), vectors


def shards(
    inputs,
    cotangent,
    first_gain,
    first_shift,
    input_weight,
    query_bias,
    value_bias,
    output_weight,
    output_bias,
    second_gain,
    second_shift,
    expand_weight,
    expand_bias,
    contract_weight,
    contract_bias,
):
    tok, width = inputs.shape[1:]
    ks, zs = lax.axis_size("core"), lax.axis_size("fsdp")
    g, k, z = lax.axis_index("grp"), lax.axis_index("core"), lax.axis_index("fsdp")
    rows_z = width // zs
    heads_here = HEADS // GROUPS
    head = width // HEADS
    cols = width // GROUPS
    ff = expand_weight.shape[1]
    ff_z = ff // zs
    ff_g = ff_z // GROUPS
    mine = GROUPS * tok
    scale = head ** (-0.5)

    x_own = inputs[0]
    slope_own = cotangent[0]

    smalls = [first_gain, first_shift, query_bias, value_bias, output_bias]
    smalls += [second_gain, second_shift, contract_bias, expand_bias]
    own = rows_z // ks
    aligned = own % 48 == 0 and zs == GROUPS
    if aligned:
        cut = cut_first(input_weight, output_weight, smalls, g, k, ks)
    else:
        cut = cut_weight(input_weight, 3, g, k, ks)
    pieces = gather_flips(cut, "fsdp")
    rows_both = gather_flips(jnp.concatenate([inputs, cotangent]), "grp")
    rest = cut_rest(contract_weight, expand_weight, zs, g, k, ks)
    pieces, rows_both, rest = lax.optimization_barrier((pieces, rows_both, rest))
    x_more = [send(b[0], "core", j) for j in range(1, ks) for b in rows_both]
    more = [[send(b, "core", j) for b in pieces] for j in range(1, ks)]
    if aligned:
        table = vector_table(pieces, own, rows_z, width, g, z)
        in_w, out_w = both_weights([pieces] + more, g, z, k, own, width)
    else:
        in_w = assemble([pieces] + more, z, k, own).reshape(width, 3 * cols)
        out_w = gather_flips(pick(output_weight.reshape(ks, own, width), k), "fsdp")
        out_more = [[send(b, "core", j) for b in out_w] for j in range(1, ks)]
        out_w = assemble([out_w] + out_more, z, k, own).reshape(GROUPS, cols, width)
        out_w = jnp.concatenate([pick(out_w, g ^ i) for i in range(GROUPS)])
        got = in_order(gather_flips(jnp.concatenate(smalls), "fsdp"), z).astype(F32)
        vectors = [got[:, i * rows_z : (i + 1) * rows_z].reshape(width) for i in range(8)]
        for i in (2, 3):
            vectors[i] = jnp.tile(pick(vectors[i].reshape(GROUPS, cols), g), GROUPS)
        got = got[:, 8 * rows_z :].reshape(zs, GROUPS, ff_g)
        vectors.append(lax.dynamic_index_in_dim(got, g, axis=1, keepdims=False).reshape(width))
        table = jnp.pad(jnp.stack(vectors), ((0, 7), (0, 0)))
    o_bias, gain_two, shift_two, c_bias = [table[i : i + 1] for i in range(4, 8)]

    rest = lax.all_gather(rest, ("fsdp", "core"), axis=0, tiled=True)

    *slots, qs, keys, values, att_full, lse, h1, hat_one = attend(
        g, k, ks, head, rows_both, x_more, in_w, table
    )
    att = jnp.concatenate(swap_flips(slots, "grp"), axis=1)
    x_f = x_own.astype(F32)
    middle = x_f + mm(att, out_w) + o_bias
    hat_two, rate_two = norm_stats(middle)
    h2 = (hat_two * gain_two + shift_two).astype(BF)
    h2_rows = gather_flips(h2, "grp")

    act, slope_inner, sh2_part, out_part, d_exp_b = hidden_part(
        h2_rows, rows_both, rest, table
    )
    sh2 = swap_flips(sh2_part, "grp")
    d_hidden = hidden_grads(h2_rows, rows_both, slope_inner, act)
    sh2, d_hidden = lax.optimization_barrier((sh2, d_hidden))
    sh2 = total(sh2)
    d_hidden = lax.psum_scatter(d_hidden, ("fsdp", "core"), scatter_dimension=0, tiled=True)

    slope_f = slope_own.astype(F32)
    d_gain_two = jnp.sum(sh2 * hat_two, axis=0, keepdims=True)
    d_shift_two = jnp.sum(sh2, axis=0, keepdims=True)
    slope_middle = slope_f + norm_back(sh2, gain_two, hat_two, rate_two)
    slope_branch = slope_middle.astype(BF)
    slope_att = mm_rt(slope_branch, out_w).astype(BF)
    datt = swap_flips([slope_att[:, i * cols : (i + 1) * cols] for i in range(GROUPS)], "grp")

    datt, out_part = lax.optimization_barrier((datt, out_part))
    out_sum = swap_flips(out_part, "grp")
    d_out = mm_lt(att, slope_branch).astype(BF).reshape(GROUPS, cols, width)
    d_out = in_order([d_out[i] for i in range(GROUPS)], g)
    d_out = d_out.reshape(zs, GROUPS, ks, own // GROUPS, width)
    pieces = [lax.dynamic_index_in_dim(d_out, k ^ j, axis=2, keepdims=False) for j in range(ks)]
    datt, pieces = lax.optimization_barrier((datt, pieces))
    d_out = swap_flips(pieces, "core")

    kept = (qs, keys, values, att_full, lse)
    split = (heads_here + 1) // 2
    dq, dkv = attend_back(g, k, ks, head, 0, split, datt, *kept)
    dq, dkv = [dq], [swap_flips([dkv[j] for j in range(ks)], "core")]
    datt, d_out, out_sum = lax.optimization_barrier((datt, d_out, out_sum))
    outputs = (middle + total(out_sum) + c_bias).astype(BF)[None]
    datt, outputs = lax.optimization_barrier((datt, outputs))
    d_out = total(d_out).astype(BF)
    pieces = [lax.dynamic_index_in_dim(d_out, g ^ i, axis=1, keepdims=False) for i in range(GROUPS)]
    datt, pieces = lax.optimization_barrier((datt, pieces))
    d_out = swap_flips(pieces, "grp")
    more = attend_back(g, k, ks, head, split, heads_here - split, datt, *kept)
    dq.append(more[0])
    dkv.append(swap_flips([more[1][j] for j in range(ks)], "core"))
    sh1_part, d_in, sums = project_back(g, dq, dkv, h1, hat_one, in_w)
    sh1, d_hidden = lax.optimization_barrier((swap_flips(sh1_part, "grp"), d_hidden))
    sh1 = total(sh1)
    hat_own, rate_own = norm_stats(x_f)
    delta_inputs = (slope_middle + norm_back(sh1, table[0:1], hat_own, rate_own)).astype(BF)[None]

    extra = -(-(12 * rows_z) // (3 * cols * ks))
    packed = pack_vectors(
        g,
        zs,
        extra * ks,
        rows_z,
        sums,
        jnp.sum(slope_branch.astype(F32), axis=0, keepdims=True),
        d_gain_two,
        d_shift_two,
        jnp.sum(slope_f, axis=0, keepdims=True),
        d_exp_b,
    )
    d_out = total(d_out).astype(BF)
    third = d_out.shape[1] // 3
    tail = d_out[..., 3 * cols :]
    tail = [tail[:, i * third : (i + 1) * third] for i in range(3)]
    d_out = jnp.concatenate([d_out[..., : 3 * cols], jnp.concatenate(tail, axis=2)], axis=1)
    d_in = jnp.concatenate(
        [
            d_in.reshape(zs, ks, own, 3 * cols),
            packed.astype(BF).reshape(zs, ks, extra, 3 * cols),
        ],
        axis=2,
    )
    pieces = [lax.dynamic_index_in_dim(d_in, k ^ j, axis=1, keepdims=False) for j in range(ks)]
    d_in = total(swap_flips(pieces, "core")).astype(BF)
    d_in = jnp.concatenate([d_in, d_out], axis=1)
    pieces = lax.optimization_barrier([pick(d_in, z ^ i) for i in range(zs)])
    d_in = swap_flips(pieces, "fsdp")
    d_hidden = gather_flips(d_hidden, "grp")
    d_in = gather_flips(total(d_in).astype(BF), "grp")
    d_hidden = [d_hidden] + [[send(p, "core", j) for p in d_hidden] for j in range(1, ks)]
    d_exp_w, d_con_w = unfold(d_hidden, zs, g, k)
    d_in, d_exp_w, d_con_w = lax.optimization_barrier((d_in, d_exp_w, d_con_w))
    d_in = [d_in] + [[send(p, "core", j) for p in d_in] for j in range(1, ks)]
    d_in_w, d_out_w, packed = finish(d_in, own, extra, width, g, k)

    return (
        outputs,
        delta_inputs,
        packed[0],
        packed[1],
        d_in_w,
        packed[2],
        packed[3],
        d_out_w,
        packed[4],
        packed[5],
        packed[6],
        d_exp_w,
        packed[8],
        d_con_w,
        packed[7],
    )


def solution(mesh):
    ctx, zs = mesh.shape["ctx"], mesh.shape["fsdp"]
    axes = ("grp", "core", "fsdp")
    split = Mesh(mesh.devices.reshape(GROUPS, ctx // GROUPS, zs), axes)
    row, vec, mat = P("fsdp", ("grp", "core"), None), P("fsdp"), P("fsdp", None)
    placed = (row, row, vec, vec, mat, vec, vec, mat, vec, vec, vec, mat, vec, mat, vec)
    return jax.shard_map(
        shards,
        mesh=split,
        in_specs=placed,
        out_specs=placed,
        check_vma=False,
    )
```
